32 devices in a mesh: section: 2 (over core), dp: 8 (over z, x), tensor: 2 (over y).
Axes of the slice: x: 2, y: 2, z: 4, core: 2. Of those that a mesh axis runs over, the one named last changes fastest.
Arguments:
- x_input: bfloat16 [2, 8192, 768], P(None, ('dp', 'tensor')), may hold values from -6 to 6
- teacher: float32 [2, 8192, 768], P(None, ('dp', 'tensor')), may hold values from -6 to 6
- segment_ids: int32 [2, 8, 1024], P(None, 'dp'), may hold values from 0 to 2, as said below
- valid_len: int32 [2, 8], replicated, may hold values from 256 to 1024
- norm_gain: bfloat16 [2, 768], P('section', 'dp'), may hold values from 0.5 to 1.5
- w_zx: bfloat16 [2, 768, 2, 1536], P('section', 'dp', None, 'tensor'), may hold values from -0.21875 to 0.21875
- w_bc: bfloat16 [2, 768, 256], P('section', 'dp'), may hold values from -0.21875 to 0.21875
- w_dt: bfloat16 [2, 768, 24], P('section', 'dp', 'tensor'), may hold values from -0.21875 to 0.21875
- conv_x: bfloat16 [2, 5, 1536], P('section', None, 'tensor'), may hold values from -3 to 3
- conv_bc: bfloat16 [2, 5, 256], P('section'), may hold values from -3 to 3
- dt_bias: float32 [2, 24], P('section'), may hold values from -4.5 to -1.5
- a_log: float32 [2, 24], P('section'), may hold values from -4 to 2.5
- d_skip: float32 [2, 24], P('section'), may hold values from 0.5 to 1.5
- gnorm_gain: bfloat16 [2, 1536], P('section', 'tensor'), may hold values from 0.5 to 1.5
- w_out: bfloat16 [2, 1536, 768], P('section', 'tensor', 'dp'), may hold values from -0.15625 to 0.15625
Outputs:
- layer_outputs: bfloat16 [2, 2, 8192, 768], P('section', None, ('dp', 'tensor'))
- boundary_grads: float32 [2, 2, 8192, 768], P('section', None, ('dp', 'tensor'))
- grad_norm_gain: float32 [2, 768], P('section', 'dp')
- grad_w_zx: float32 [2, 768, 2, 1536], P('section', 'dp', None, 'tensor')
- grad_w_bc: float32 [2, 768, 256], P('section', 'dp')
- grad_w_dt: float32 [2, 768, 24], P('section', 'dp', 'tensor')
- grad_conv_x: float32 [2, 5, 1536], P('section', None, 'tensor')
- grad_conv_bc: float32 [2, 5, 256], P('section')
- grad_dt_bias: float32 [2, 24], P('section', 'tensor')
- grad_a_log: float32 [2, 24], P('section', 'tensor')
- grad_d_skip: float32 [2, 24], P('section', 'tensor')
- grad_gnorm_gain: float32 [2, 1536], P('section', 'tensor')
- grad_w_out: float32 [2, 1536, 768], P('section', 'tensor', 'dp')
The draws below stay inside these ranges and needn't reach their ends.
Inputs may be any that keep to these rules, and one draw needn't show every extreme that they name: `segment_ids`: within each sequence the ids start at 0 at the first token, never fall, and rise by at most one from a token to the next; the last document is cut at the sequence's end.
All inputs are finite; a program needn't handle non-finite values.
Results may differ from the reference program's by a relative error of at most 0.019.
Values may be sent and summed in bfloat16 or wider, within the bound.
No kernel may reach another device: no remote copies, remote signals or barrier semaphores. Data moves between devices by JAX's collectives and lax.ppermute only.
A program may use at most 256 MiB of HBM per device.

```python
import jax
import jax.numpy as jnp
from jax import lax

D = 768
INNER = 1536
HEADS = 24
HEAD_DIM = 64
STATE = 128
CONV = 4
SPAN = 256
LEN = 1024
MICRO = 2
MINDOC = 200
MAXDOC = 2000
SEQS = 8
TOKENS = 8192


def draw_segment_ids(key, part):
    key = jax.random.fold_in(key, 11)
    rows = MICRO * SEQS
    number = LEN // MINDOC + 2
    middle = LEN // 2
    first_key, rest_key, kind_key, span_key, whole_key, pick_key = jax.random.split(key, 6)
    first = jax.random.randint(first_key, (rows, 1), 1, LEN)
    lengths = jax.random.randint(rest_key, (rows, number), MINDOC, MAXDOC + 1)
    kind = jax.random.randint(kind_key, (rows, 1), 0, 4)
    beyond = jax.random.randint(span_key, (rows, 1), middle + 1, LEN)
    spanning = jax.random.randint(whole_key, (1, SEQS), 0, MICRO)
    chosen = (jnp.arange(MICRO)[:, None] == spanning).reshape(rows, 1)
    first = jnp.where(kind == 1, middle, first)
    first = jnp.where(kind == 2, middle - 1, first)
    first = jnp.where((kind == 3) | chosen, beyond, first)
    picked = jax.random.randint(pick_key, (), 0, rows)
    dense_row = (jnp.arange(rows) == picked)[:, None]
    first = jnp.where(dense_row, 1, first)
    lengths = jnp.where(dense_row, MINDOC, lengths)
    offsets = jnp.concatenate([jnp.zeros((rows, 1), jnp.int32), jnp.cumsum(lengths, axis=1)[:, :-1]], axis=1)
    bounds = first + offsets
    positions = jnp.arange(LEN)
    ids = jnp.sum((bounds[:, :, None] <= positions[None, None, :]).astype(jnp.int32), axis=1)
    ids = jnp.minimum(ids, LEN // (2 * MINDOC))
    return ids.reshape(MICRO, SEQS, LEN).astype(jnp.int32)


def draw_valid_len(key, part):
    key = jax.random.fold_in(key, 23)
    order = jnp.arange(SEQS)[None, :]
    base = LEN // 4 + order * (3 * LEN // 4) // (SEQS - 1)
    noise = jax.random.randint(key, (MICRO, SEQS), 0, LEN // 16 + 1)
    value = jnp.minimum(base + noise, LEN)
    value = jnp.where(order == 0, LEN // 4, value)
    return value.astype(jnp.int32)


def level_of(rng, dims, shards, low, high):
    level = 1.0
    for axis_at, shards_of in shards:
        heights = jax.random.uniform(jax.random.fold_in(jax.random.fold_in(rng, 6), axis_at), (shards_of,), jnp.float32, low / len(shards), high / len(shards))
        level = level * jnp.repeat(jnp.exp(heights), dims[axis_at] // shards_of).reshape((-1,) + (1,) * (len(dims) - 1 - axis_at))
    return level


def scatter_about(own_key, dims, scale, most, cuts=(), kind=jnp.bfloat16):
    values = scale * jax.random.normal(own_key, dims, jnp.float32)
    if cuts:
        values = values * level_of(own_key, dims, cuts, -0.22, 0.18)
    return jnp.clip(values, -most, most).astype(kind)


def setup_inputs(seed: int = 0) -> dict:
    streams_of = jax.random.split(jax.random.key(seed), 16)
    x_input = scatter_about(streams_of[0], (MICRO, TOKENS, D), 1.0, 6.0, ((1, 16),))
    teacher = scatter_about(streams_of[1], (MICRO, TOKENS, D), 1.0, 6.0, ((1, 16),), jnp.float32)
    segment_ids = draw_segment_ids(jax.random.fold_in(streams_of[15], 71), 0)
    valid_len = draw_valid_len(jax.random.fold_in(streams_of[15], 71), 0)
    norm_gain = jnp.clip(1.0 + 0.1 * jax.random.normal(streams_of[4], (2, D), jnp.float32), 0.5, 1.5).astype(jnp.bfloat16)
    w_zx = scatter_about(streams_of[5], (2, D, 2, INNER), D ** -0.5, 0.21875, ((0, 2), (1, 8), (3, 2)))
    w_bc = scatter_about(streams_of[6], (2, D, 2 * STATE), D ** -0.5, 0.21875, ((0, 2), (1, 8)))
    w_dt = scatter_about(streams_of[7], (2, D, HEADS), D ** -0.5, 0.21875, ((0, 2), (1, 8), (2, 2)))
    conv_x = scatter_about(streams_of[8], (2, CONV + 1, INNER), CONV ** -0.5, 3.0, ((0, 2), (2, 2)))
    conv_bc = scatter_about(streams_of[9], (2, CONV + 1, 2 * STATE), CONV ** -0.5, 3.0, ((0, 2),))
    dt_bias = jnp.clip(-4.5 + 3.0 * jax.random.uniform(streams_of[10], (2, HEADS), jnp.float32) ** level_of(streams_of[10], (2, HEADS), ((0, 2),), -0.2, 0.2), -4.5, -1.5)
    a_log = jnp.clip(-4.0 + 6.5 * jax.random.uniform(streams_of[11], (2, HEADS), jnp.float32) ** level_of(streams_of[11], (2, HEADS), ((0, 2),), -0.2, 0.2), -4.0, 2.5)
    d_skip = jnp.clip(0.5 + 1.0 * jax.random.uniform(streams_of[12], (2, HEADS), jnp.float32) ** level_of(streams_of[12], (2, HEADS), ((0, 2),), -0.2, 0.2), 0.5, 1.5)
    gnorm_gain = jnp.clip(1.0 + 0.1 * jax.random.normal(streams_of[13], (2, INNER), jnp.float32), 0.5, 1.5).astype(jnp.bfloat16)
    w_out = scatter_about(streams_of[14], (2, INNER, D), INNER ** -0.5, 0.15625, ((0, 2), (1, 2), (2, 8)))
    return {"x_input": x_input, "teacher": teacher, "segment_ids": segment_ids, "valid_len": valid_len, "norm_gain": norm_gain, "w_zx": w_zx, "w_bc": w_bc, "w_dt": w_dt, "conv_x": conv_x, "conv_bc": conv_bc, "dt_bias": dt_bias, "a_log": a_log, "d_skip": d_skip, "gnorm_gain": gnorm_gain, "w_out": w_out}


@jax.custom_vjp
def low(v):
    return lax.optimization_barrier(v.astype(jnp.bfloat16)).astype(jnp.float32)

@jax.custom_vjp
def low_back(v):
    return v

def low_keep(v):
    return (low(v), None)

def low_pass(kept, grad):
    return (grad,)

def back_keep(v):
    return (v, None)

def back_low(kept, grad):
    return (low(grad),)
low.defvjp(low_keep, low_pass)
low_back.defvjp(back_keep, back_low)
epsilon = 1e-05

def exact_dot(left, right):
    return jnp.dot(left, right, precision=lax.Precision.HIGHEST, preferred_element_type=jnp.float32)

def causal_conv(signal, taps, segment):
    reach = taps.shape[0] - 1
    length = signal.shape[0]
    result = taps[reach] + taps[reach - 1] * signal
    for lag in range(1, reach):
        moved = jnp.pad(signal, ((lag, 0), (0, 0)))[:length]
        moved_segment = jnp.pad(segment, (lag, 0), constant_values=-1)[:length]
        same = (moved_segment == segment).astype(jnp.float32)
        result = result + taps[reach - 1 - lag] * moved * same[:, None]
    return result

def block_scan(values, b_rows, c_rows, steps_dt, rates, segment):
    length, heads, head_width = values.shape
    blocks = length // SPAN
    values = values.reshape(blocks, SPAN, heads, head_width)
    b_rows = b_rows.reshape(blocks, SPAN, -1)
    c_rows = c_rows.reshape(blocks, SPAN, -1)
    steps_dt = steps_dt.reshape(blocks, SPAN, heads)
    segment = segment.reshape(blocks, SPAN)
    log_decay = jnp.cumsum(-steps_dt * rates, axis=1)
    scaled = values * steps_dt[..., None]
    lower = jnp.arange(SPAN)[:, None] >= jnp.arange(SPAN)[None, :]
    linked = lower[None] & (segment[:, :, None] == segment[:, None, :])
    decay_heads = jnp.transpose(log_decay, (0, 2, 1))
    gaps = decay_heads[:, :, :, None] - decay_heads[:, :, None, :]
    keep = linked[:, None]
    factors = jnp.where(keep, jnp.exp(jnp.where(keep, gaps, 0.0)), 0.0)
    scores = jnp.einsum('cis,cjs->cij', c_rows, b_rows, precision=lax.Precision.HIGHEST)
    inside = jnp.einsum('chij,cjhp->cihp', factors * scores[:, None], scaled, precision=lax.Precision.HIGHEST)
    same_end = (segment == segment[:, -1:]).astype(jnp.float32)
    tail = jnp.exp(log_decay[:, -1:, :] - log_decay) * same_end[:, :, None]
    states = jnp.einsum('cjhp,cjs->chps', tail[..., None] * scaled, b_rows, precision=lax.Precision.HIGHEST)

    def carry_step(carried, item):
        state, previous = carried
        log_block, c_block, segment_block, new_state = item
        entry = jnp.exp(log_block) * (segment_block == previous).astype(jnp.float32)[:, None]
        across = jnp.einsum('is,hps->ihp', c_block, state, precision=lax.Precision.HIGHEST) * entry[:, :, None]
        through = jnp.exp(log_block[-1]) * (segment_block[-1] == previous).astype(jnp.float32)
        state = through[:, None, None] * state + new_state
        return ((state, segment_block[-1]), across)
    start_state = jnp.zeros((heads, head_width, b_rows.shape[-1]), jnp.float32)
    start_segment = jnp.array(-1, jnp.int32)
    _, across = lax.scan(carry_step, (start_state, start_segment), (log_decay, c_rows, segment, states))
    return (inside + across).reshape(length, heads, head_width)

def mixer(projected, conv_x, conv_bc, dt_bias, a_log, d_skip, segment):
    inner_width = conv_x.shape[1]
    gate_part = projected[:, :inner_width]
    value_part = projected[:, inner_width:2 * inner_width]
    state_part = projected[:, 2 * inner_width:2 * inner_width + 2 * STATE]
    step_part = projected[:, 2 * inner_width + 2 * STATE:]
    values = jax.nn.silu(causal_conv(value_part, conv_x, segment))
    states_in = jax.nn.silu(causal_conv(state_part, conv_bc, segment))
    steps_dt = jax.nn.softplus(step_part + dt_bias)
    length = values.shape[0]
    heads = steps_dt.shape[1]
    shaped = values.reshape(length, heads, HEAD_DIM)
    result = block_scan(shaped, states_in[:, :STATE], states_in[:, STATE:], steps_dt, jnp.exp(a_log), segment)
    result = result + d_skip[:, None] * shaped
    return result.reshape(length, inner_width) * jax.nn.silu(gate_part)

def layer(hidden, segment, params):
    gain, w_zx, w_bc, w_dt, conv_x, conv_bc, dt_bias, a_log, d_skip, gate_gain, w_out = params
    scale = lax.rsqrt(lax.optimization_barrier(jnp.mean(hidden * hidden, axis=1, keepdims=True)) + epsilon)
    normed = low(hidden * scale * gain)
    w_in = jnp.concatenate([w_zx[:, 0], w_zx[:, 1], w_bc, w_dt], axis=1)
    projected = low_back(exact_dot(normed, w_in))
    gated = mixer(projected, conv_x, conv_bc, dt_bias, a_log, d_skip, segment)
    mean_square = lax.optimization_barrier(jnp.mean(gated * gated, axis=1, keepdims=True))
    mixed = low(gated * lax.rsqrt(mean_square + epsilon) * gate_gain)
    branch = low_back(exact_dot(mixed, w_out))
    return hidden + branch

def sequence_loss(params_first, params_second, x_rows, extra, segment, counted, target, loss_weight):
    first_out = layer(x_rows, segment, params_first)
    sent = low(first_out)
    second_in = low_back(sent) + extra
    second_out = layer(second_in, segment, params_second)
    miss = second_out - target
    loss = jnp.sum(counted[:, None] * miss * miss) * loss_weight
    return (loss, (sent, second_out))

def reference(x_input, teacher, segment_ids, valid_len, norm_gain, w_zx, w_bc, w_dt, conv_x, conv_bc, dt_bias, a_log, d_skip, gnorm_gain, w_out):
    params = tuple((value.astype(jnp.float32) for value in (norm_gain, w_zx, w_bc, w_dt, conv_x, conv_bc, dt_bias, a_log, d_skip, gnorm_gain, w_out)))
    params_first = tuple((value[0] for value in params))
    params_second = tuple((value[1] for value in params))
    counted_total = jnp.sum(valid_len).astype(jnp.float32)
    loss_weight = MICRO * TOKENS / counted_total
    rows_x = x_input.astype(jnp.float32).reshape(MICRO * SEQS, LEN, D)
    rows_t = teacher.reshape(MICRO * SEQS, LEN, D)
    rows_seg = segment_ids.reshape(MICRO * SEQS, LEN)
    rows_len = valid_len.reshape(MICRO * SEQS)
    positions = jnp.arange(LEN)

    def one_sequence(totals, item):
        x_rows, target, segment, length = item
        counted = (positions < length).astype(jnp.float32)
        extra = jnp.zeros_like(x_rows)

        def wrapped(first, second, rows_in, rows_extra):
            return sequence_loss(first, second, rows_in, rows_extra, segment, counted, target, loss_weight)
        _, pull, outputs = jax.vjp(wrapped, params_first, params_second, x_rows, extra, has_aux=True)
        grad_first, grad_second, grad_x, grad_extra = pull(jnp.ones((), jnp.float32))
        totals = jax.tree.map(lambda left, right: left + right, totals, (grad_first, grad_second))
        return (totals, (outputs[0], outputs[1], grad_x, grad_extra))
    start = jax.tree.map(jnp.zeros_like, (params_first, params_second))
    totals, stacked = lax.scan(one_sequence, start, (rows_x, rows_t, rows_seg, rows_len))
    sent_all, final_all, grad_x_all, grad_extra_all = stacked
    layer_outputs = jnp.stack([sent_all, final_all]).reshape(2, MICRO, TOKENS, D).astype(jnp.bfloat16)
    boundary_grads = jnp.stack([grad_x_all, grad_extra_all]).reshape(2, MICRO, TOKENS, D)
    grads = tuple((jnp.stack([first, second]) for first, second in zip(totals[0], totals[1])))
    return (layer_outputs, boundary_grads, grads[0], grads[1], grads[2], grads[3], grads[4], grads[5], grads[6], grads[7], grads[8], grads[9], grads[10])
```

```python
import functools

import jax
import jax.numpy as jnp
import numpy as np
from jax import lax
from jax.experimental import pallas as pl
from jax.experimental.pallas import tpu as pltpu
from jax.sharding import PartitionSpec as P

HEAD_DIM = 64
STATE = 128
SPAN = 256
LANES = 128

epsilon = 1e-05
f32 = jnp.float32
bf16 = jnp.bfloat16


def nn(left, right):
    return lax.dot_general(left, right, (((1,), (0,)), ((), ())), preferred_element_type=f32)


def nt(left, right):
    return lax.dot_general(left, right, (((1,), (1,)), ((), ())), preferred_element_type=f32)


def tn(left, right):
    return lax.dot_general(left, right, (((0,), (0,)), ((), ())), preferred_element_type=f32)


def high_low(value):
    high = value.astype(bf16)
    return high, (value - high.astype(f32)).astype(bf16)


def spread(per_head, spreader):
    return nn(jnp.concatenate(high_low(per_head), axis=1), spreader)


def gathered_heads(units, spreader):
    high, low = high_low(units)
    once = spreader[:LANES]
    return nt(high, once) + nt(low, once)


def running_sum(triangle, value):
    high = value.astype(bf16)
    rest = value - high.astype(f32)
    middle = rest.astype(bf16)
    low = (rest - middle.astype(f32)).astype(bf16)
    sums = nn(triangle, jnp.concatenate([high, middle, low], axis=1))
    return sums[:, :LANES] + sums[:, LANES : 2 * LANES] + sums[:, 2 * LANES :]


def softplus(value):
    return jnp.maximum(value, 0.0) + jnp.log1p(jnp.exp(-jnp.abs(value)))


def moved_down(block, edge, lag):
    return jnp.concatenate([edge, block], axis=0)[8 - lag : 8 - lag + block.shape[0]]


def moved_up(block, edge, lag):
    return jnp.concatenate([block, edge], axis=0)[lag : lag + block.shape[0]]


def decay_parts(steps_in, head_rows, marks, heads):
    lane = lax.broadcasted_iota(jnp.int32, (1, LANES), 1)
    live = lane < heads
    shifted = steps_in + head_rows[0:1, :LANES]
    steps = jnp.where(live, softplus(shifted), 0.0)
    rates = head_rows[1:2, :LANES]
    log_steps = -steps * rates
    row = lax.broadcasted_iota(jnp.int32, (SPAN, SPAN), 0)
    column = lax.broadcasted_iota(jnp.int32, (SPAN, SPAN), 1)
    lower = (row >= column).astype(bf16)
    logs = running_sum(lower, log_steps)
    last = logs[SPAN - 1 : SPAN]
    entry = jnp.exp(logs) * marks[:, 3:4]
    tail = jnp.exp(last - logs) * marks[:, 4:5]
    through = jnp.exp(last) * marks[SPAN - 1 : SPAN, 3:4]
    entry = jnp.where(live, entry, 0.0)
    tail = jnp.where(live, tail, 0.0)
    through = jnp.where(live, through, 0.0)
    return shifted, steps, log_steps, logs, entry, tail, through, row, column


def linked_mask(row, column, marks, segment_row):
    linked = (row >= column) & (marks[:, 5:6] == segment_row)
    return jnp.where(linked, 0.0, -1e30)


def gain_row(weights):
    return jnp.transpose(weights[:, 384:512].astype(f32))[64:65, :]


def forward_kernel(second, heads, *refs):
    if second:
        (h_ref, own_ref, other_ref), refs = refs[:3], refs[3:]
    else:
        (h_ref,), refs = refs[:1], refs[1:]
    (a0, a1, b0, b1, o0, o1, marks_ref, segment_ref, small_ref, states_small_ref, head_ref, spread_ref), refs = refs[:12], refs[12:]
    if second:
        h_out, refs = refs[0], refs[1:]
    gate_ref, raw_ref, conv_ref, y_ref, raw_states_ref, conv_states_ref, steps_ref, entry_state_ref, part_ref = refs[:9]
    state, raw_edge, states_edge, gain = refs[9:]
    chunk = pl.program_id(0)
    half = gate_ref.shape[1] // 2

    @pl.when(chunk == 0)
    def _():
        state[...] = jnp.zeros_like(state)
        raw_edge[...] = jnp.zeros_like(raw_edge)
        states_edge[...] = jnp.zeros_like(states_edge)
        gain[0:1, :] = gain_row(b0[...])

    hidden = h_ref[...].astype(f32)
    if second:
        hidden = hidden + branch_of(own_ref, other_ref, 2 * half)[0]
        rounded = hidden.astype(bf16)
        h_out[...] = rounded
        hidden = rounded.astype(f32)
    scale = lax.rsqrt(jnp.mean(hidden * hidden, axis=1, keepdims=True) + epsilon)
    normed = (hidden * scale * gain[0:1, :]).astype(bf16)
    first_a = nn(normed, a0[...])
    second_a = nn(normed, a1[...])
    first_b = nn(normed, b0[...])
    second_b = nn(normed, b1[...])
    gate = jnp.concatenate([first_a[:, :half], second_a[:, :half]], axis=1)
    raw = jnp.concatenate([first_b[:, :half], second_b[:, :half]], axis=1)
    marks = marks_ref[...]
    turned = marks[0:1, 10:11] > 0.5
    first_states, second_states = first_a[:, half:], second_a[:, half:]
    raw_states = jnp.concatenate(
        [jnp.where(turned, second_states, first_states), jnp.where(turned, first_states, second_states)], axis=1
    )
    lane = lax.broadcasted_iota(jnp.int32, (1, LANES), 1)
    steps_in = jnp.where(lane < heads // 2, first_b[:, half:], pltpu.roll(second_b[:, half:], heads // 2, 1))
    gate_ref[...] = gate
    raw_ref[...] = raw
    raw_states_ref[...] = raw_states
    steps_ref[...] = steps_in

    def conv(block, edge, taps):
        total = taps[4:5] + taps[3:4] * block
        for lag in (1, 2, 3):
            total = total + taps[3 - lag : 4 - lag] * (moved_down(block, edge, lag) * marks[:, lag - 1 : lag])
        return total

    taps = small_ref[...]
    conved = conv(raw, raw_edge[...], taps)
    conv_ref[...] = conved
    conved_states = conv(raw_states, states_edge[...], states_small_ref[...])
    conv_states_ref[...] = conved_states
    raw_edge[...] = raw[SPAN - 8 :]
    states_edge[...] = raw_states[SPAN - 8 :]
    values = conved * jax.nn.sigmoid(conved)
    states_in = conved_states * jax.nn.sigmoid(conved_states)
    b_rows = states_in[:, :STATE].astype(bf16)
    c_rows = states_in[:, STATE:].astype(bf16)
    _, steps, _, logs, entry, tail, through, row, column = decay_parts(steps_in, head_ref[...], marks, heads)
    spreader = spread_ref[...]
    spread_steps = spread(steps, spreader)
    scaled = values * spread_steps
    mask = linked_mask(row, column, marks, segment_ref[...])
    scores = nt(c_rows, b_rows)
    logs_across = jnp.transpose(logs)
    pieces = []
    for pair in range(heads // 2):
        mixes = []
        for head in (2 * pair, 2 * pair + 1):
            factor = jnp.exp(logs[:, head : head + 1] - logs_across[head : head + 1, :] + mask)
            mixes.append((factor * scores).astype(bf16))
        block = scaled[:, pair * LANES : (pair + 1) * LANES]
        left = jnp.where(lane < HEAD_DIM, block, 0.0).astype(bf16)
        right = jnp.where(lane < HEAD_DIM, 0.0, block).astype(bf16)
        pieces.append(nn(jnp.concatenate(mixes, axis=1), jnp.concatenate([left, right], axis=0)))
    inside = jnp.concatenate(pieces, axis=1)
    held = state[...]
    entry_state_ref[0] = held
    across = nn(c_rows, held.astype(bf16)) * spread(entry, spreader)
    through_row = spread(jnp.broadcast_to(through, (8, LANES)), spreader)[0:1]
    state[...] = through_row * held + tn(b_rows, (spread(tail, spreader) * scaled).astype(bf16))
    y = inside + across + taps[6:7] * values
    y_ref[...] = y
    gated = y * (gate * jax.nn.sigmoid(gate))
    squares = jnp.sum(gated * gated, axis=1, keepdims=True)
    weighted = (gated * taps[5:6]).astype(bf16)
    part = nt(weighted[:, :half], o0[...]) + nt(weighted[:, half:], o1[...])
    width = part.shape[1]
    part_ref[:, :width] = part.astype(bf16)
    high, low = high_low(squares)
    part_ref[:, width:] = jnp.where(lane == 0, high, jnp.where(lane == 1, low, jnp.zeros_like(low)))


def branch_of(own_ref, other_ref, units):
    width = own_ref.shape[1] - LANES
    own = own_ref[...].astype(f32)
    other = other_ref[...].astype(f32)
    total = own[:, :width] + other[:, :width]
    own_squares = own[:, width : width + 1] + own[:, width + 1 : width + 2]
    other_squares = other[:, width : width + 1] + other[:, width + 1 : width + 2]
    inverse = lax.rsqrt((own_squares + other_squares) / (2 * units) + epsilon)
    return total * inverse, total, inverse


def backward_kernel(second, heads, *refs):
    if second:
        (h_ref, own_ref, other_ref, target_ref), refs = refs[:4], refs[4:]
    else:
        (h_ref, own_ref, other_ref, next_h_ref, next_out_ref, grad_own_ref, grad_other_ref, next_gain_ref), refs = refs[:8], refs[8:]
    (a0, a1, b0, b1, o0, o1, marks_ref, segment_ref, small_ref, states_small_ref, head_ref, spread_ref), refs = refs[:12], refs[12:]
    (gate_ref, raw_ref, conv_ref, y_ref, raw_states_ref, conv_states_ref, steps_ref, entry_state_ref), refs = refs[:8], refs[8:]
    if second:
        (out_ref, grad_out_ref), refs = refs[:2], refs[2:]
    else:
        (grad_out_ref,), refs = refs[:1], refs[1:]
    (da0, da1, db0, db1, do0, do1, part_ref, sums_ref, states_sums_ref), refs = refs[:9], refs[9:]
    (acc_a0, acc_a1, acc_b0, acc_b1, acc_o0, acc_o1, dstate, next_state, conv_edge, states_edge, gain, sums, states_sums) = refs
    step = pl.program_id(0)
    half = gate_ref.shape[1] // 2
    units = 2 * half

    @pl.when(step == 0)
    def _():
        for ref in (acc_a0, acc_a1, acc_b0, acc_b1, acc_o0, acc_o1, dstate, next_state, conv_edge, states_edge, sums, states_sums):
            ref[...] = jnp.zeros_like(ref)
        gain[0:1, :] = gain_row(b0[...])

    marks = marks_ref[...]
    hidden = h_ref[...].astype(f32)
    branch, total, inverse = branch_of(own_ref, other_ref, units)
    if second:
        produced = hidden + branch
        out_ref[...] = produced.astype(bf16)
        grad_out = marks[:, 9:10] * (produced - target_ref[...])
        grad_out_ref[...] = grad_out
    else:
        next_gain = next_gain_ref[0:1, :]
        grad_normed = grad_own_ref[...].astype(f32) + grad_other_ref[...].astype(f32)
        grad_out, gain_term = norm_backward(grad_normed, next_h_ref[...].astype(f32), next_out_ref[...], next_gain)
        sums[7:8, :] += jnp.sum(gain_term, axis=0, keepdims=True)
        grad_out_ref[...] = grad_out
    grad = grad_out.astype(bf16)
    inner = jnp.sum(grad.astype(f32) * total, axis=1, keepdims=True) * (inverse * inverse * inverse) / (2 * units)
    taps = small_ref[...]
    gate = gate_ref[...]
    y = y_ref[...]
    gate_sig = jax.nn.sigmoid(gate)
    gate_silu = gate * gate_sig
    gated = y * gate_silu
    gated_unit = gated * inverse
    grad_mixed = jnp.concatenate([nn(grad, o0[...]), nn(grad, o1[...])], axis=1)
    mixed = (gated_unit * taps[5:6]).astype(bf16)
    acc_o0[...] += tn(grad, mixed[:, :half])
    acc_o1[...] += tn(grad, mixed[:, half:])
    sums[5:6, :] += jnp.sum(grad_mixed * gated_unit, axis=0, keepdims=True)
    grad_gated = grad_mixed * taps[5:6] * inverse - gated * inner
    grad_gate = grad_gated * y * (gate_sig * (1.0 + gate * (1.0 - gate_sig)))
    grad_y_low = (grad_gated * gate_silu).astype(bf16)
    grad_y = grad_y_low.astype(f32)

    conved = conv_ref[...]
    value_sig = jax.nn.sigmoid(conved)
    values = conved * value_sig
    conved_states = conv_states_ref[...]
    states_sig = jax.nn.sigmoid(conved_states)
    states_in = conved_states * states_sig
    b_rows = states_in[:, :STATE].astype(bf16)
    c_rows = states_in[:, STATE:].astype(bf16)
    shifted, steps, log_steps, logs, entry, tail, through, row, column = decay_parts(steps_ref[...], head_ref[...], marks, heads)
    spreader = spread_ref[...]
    spread_steps = spread(steps, spreader)
    spread_entry = spread(entry, spreader)
    spread_tail = spread(tail, spreader)
    through_row = spread(jnp.broadcast_to(through, (8, LANES)), spreader)[0:1]
    scaled_low = (values * spread_steps).astype(bf16)
    scaled = scaled_low.astype(f32)
    mask = linked_mask(row, column, marks, segment_ref[...])
    scores = nt(c_rows, b_rows)
    logs_across = jnp.transpose(logs)
    lane = lax.broadcasted_iota(jnp.int32, (1, LANES), 1)
    grad_scores = jnp.zeros((SPAN, SPAN), f32)
    pieces = []
    zero = jnp.zeros((), bf16)
    for pair in range(heads // 2):
        block = scaled_low[:, pair * LANES : (pair + 1) * LANES]
        grad_block = grad_y_low[:, pair * LANES : (pair + 1) * LANES]
        grad_left = jnp.where(lane < HEAD_DIM, grad_block, zero)
        grad_right = jnp.where(lane < HEAD_DIM, zero, grad_block)
        mixes = []
        for head, grad_one in ((2 * pair, grad_left), (2 * pair + 1, grad_right)):
            factor = jnp.exp(logs[:, head : head + 1] - logs_across[head : head + 1, :] + mask)
            mixes.append((factor * scores).astype(bf16))
            grad_scores = grad_scores + nt(grad_one, block) * factor
        pieces.append(tn(jnp.concatenate(mixes, axis=0), jnp.concatenate([grad_left, grad_right], axis=0)))
    held = entry_state_ref[0]
    held_low = held.astype(bf16)
    gradient = dstate[...]
    gradient_low = gradient.astype(bf16)
    grad_scaled = jnp.concatenate(pieces, axis=1) + spread_tail * nn(b_rows, gradient_low)
    grad_entry = (spread_entry * grad_y).astype(bf16)
    grad_scores_low = grad_scores.astype(bf16)
    grad_c = nn(grad_scores_low, b_rows) + nt(grad_entry, held_low)
    grad_b = tn(grad_scores_low, c_rows) + nt((spread_tail * scaled).astype(bf16), gradient_low)
    state_term = jnp.sum(gradient * next_state[...], axis=0, keepdims=True)
    dstate[...] = through_row * gradient + tn(c_rows, grad_entry)
    next_state[...] = held
    skip = taps[6:7]
    sums[6:7, :] += jnp.sum(grad_y * values, axis=0, keepdims=True)
    grad_logs = gathered_heads(grad_y * (y - skip * values) - scaled * grad_scaled, spreader)
    state_heads = gathered_heads(jnp.broadcast_to(state_term, (8, units)), spreader)[0:1]
    last_row = lax.broadcasted_iota(jnp.int32, (SPAN, 1), 0) == SPAN - 1
    grad_logs = grad_logs + jnp.where(last_row, state_heads, 0.0)
    upper = (row <= column).astype(bf16)
    grad_log_steps = running_sum(upper, grad_logs)
    grad_steps = gathered_heads(grad_scaled * values, spreader) - head_ref[1:2, :LANES] * grad_log_steps
    grad_steps_in = jnp.where(lane < heads, grad_steps * jax.nn.sigmoid(shifted), 0.0)
    states_sums[5:6, :] += jnp.concatenate(
        [
            jnp.sum(grad_steps_in, axis=0, keepdims=True),
            jnp.sum(grad_log_steps * log_steps, axis=0, keepdims=True),
        ],
        axis=1,
    )
    grad_values = grad_scaled * spread_steps + skip * grad_y
    grad_conved = grad_values * (value_sig * (1.0 + conved * (1.0 - value_sig)))
    grad_states = jnp.concatenate([grad_b, grad_c], axis=1)
    grad_conved_states = grad_states * (states_sig * (1.0 + conved_states * (1.0 - states_sig)))

    def conv_backward(block, edge, tap_rows, raw, total_ref):
        result = tap_rows[3:4] * block
        total_ref[3:4, :] += jnp.sum(block * raw, axis=0, keepdims=True)
        total_ref[4:5, :] += jnp.sum(block, axis=0, keepdims=True)
        for lag in (1, 2, 3):
            term = moved_up(block, edge, lag) * marks[:, 5 + lag : 6 + lag]
            result = result + tap_rows[3 - lag : 4 - lag] * term
            total_ref[3 - lag : 4 - lag, :] += jnp.sum(term * raw, axis=0, keepdims=True)
        return result

    grad_raw = conv_backward(grad_conved, conv_edge[...], taps, raw_ref[...], sums).astype(bf16)
    grad_raw_states = conv_backward(
        grad_conved_states, states_edge[...], states_small_ref[...], raw_states_ref[...], states_sums
    )
    conv_edge[...] = grad_conved[:8]
    states_edge[...] = grad_conved_states[:8]
    grad_gate = grad_gate.astype(bf16)
    scale = lax.rsqrt(jnp.mean(hidden * hidden, axis=1, keepdims=True) + epsilon)
    normed = (hidden * scale * gain[0:1, :]).astype(bf16)
    turned = marks[0:1, 10:11] > 0.5
    first_states = jnp.where(turned, grad_raw_states[:, STATE:], grad_raw_states[:, :STATE])
    second_states = jnp.where(turned, grad_raw_states[:, :STATE], grad_raw_states[:, STATE:])
    grad_a0 = jnp.concatenate([grad_gate[:, :half], first_states.astype(bf16)], axis=1)
    grad_a1 = jnp.concatenate([grad_gate[:, half:], second_states.astype(bf16)], axis=1)
    own_steps = jnp.where(lane < heads // 2, grad_steps_in, 0.0)
    other_steps = pltpu.roll(grad_steps_in, LANES - heads // 2, 1)
    other_steps = jnp.where(lane < heads // 2, other_steps, 0.0)
    grad_b0 = jnp.concatenate([grad_raw[:, :half], own_steps.astype(bf16)], axis=1)
    grad_b1 = jnp.concatenate([grad_raw[:, half:], other_steps.astype(bf16)], axis=1)
    acc_a0[...] += tn(normed, grad_a0)
    acc_a1[...] += tn(normed, grad_a1)
    acc_b0[...] += tn(normed, grad_b0)
    acc_b1[...] += tn(normed, grad_b1)
    part = nt(grad_a0, a0[...]) + nt(grad_a1, a1[...]) + nt(grad_b0, b0[...]) + nt(grad_b1, b1[...])
    part_ref[...] = part.astype(bf16)

    @pl.when(step == pl.num_programs(0) - 1)
    def _():
        for out, acc in ((da0, acc_a0), (da1, acc_a1), (db0, acc_b0), (db1, acc_b1), (do0, acc_o0), (do1, acc_o1)):
            out[...] = acc[...].astype(out.dtype)
        sums_ref[...] = sums[...]
        states_sums_ref[...] = states_sums[...]


def norm_backward(grad_normed, hidden, grad_out, gain):
    scale = lax.rsqrt(jnp.mean(hidden * hidden, axis=1, keepdims=True) + epsilon)
    weighted = grad_normed * gain
    shared = jnp.mean(weighted * hidden, axis=1, keepdims=True) * (scale * scale * scale)
    return grad_out + scale * weighted - hidden * shared, grad_normed * hidden * scale


VMEM_LIMIT = 60 * 1024 * 1024


def spreader_of(units):
    one = (np.arange(LANES)[:, None] == np.arange(units)[None, :] // HEAD_DIM).astype(np.float32)
    return jnp.asarray(np.concatenate([one, one], axis=0), bf16)


def rows_spec(width, last=None):
    if last is None:
        return pl.BlockSpec((SPAN, width), lambda i: (i, 0))
    return pl.BlockSpec((SPAN, width), lambda i: (last - i, 0))


def whole_spec(array):
    return pl.BlockSpec(array.shape, lambda i: (0,) * array.ndim)


def common_args(weights, marks, segment_row, params, chunks, reverse):
    last = chunks - 1
    spreader = spreader_of(params[0].shape[1])
    arrays = list(weights) + [marks, segment_row] + list(params) + [spreader]
    specs = [whole_spec(w) for w in weights]
    specs.append(rows_spec(LANES, last if reverse else None))
    specs.append(pl.BlockSpec((1, SPAN), (lambda i: (0, last - i)) if reverse else (lambda i: (0, i))))
    specs += [whole_spec(p) for p in params] + [whole_spec(spreader)]
    return arrays, specs


def forward_layer(h, parts, weights, marks, segment_row, params):
    length, width = h.shape
    units = params[0].shape[1]
    heads = units // HEAD_DIM
    chunks = length // SPAN
    second = parts is not None
    shared, shared_specs = common_args(weights, marks, segment_row, params, chunks, False)
    inputs, specs = [h], [rows_spec(width)]
    outs, out_specs = [], []
    if second:
        inputs += list(parts)
        specs += [rows_spec(width + LANES)] * 2
        outs.append(jax.ShapeDtypeStruct((length, width), bf16))
        out_specs.append(rows_spec(width))
    for columns in (units, units, units, units, 2 * STATE, 2 * STATE, LANES):
        outs.append(jax.ShapeDtypeStruct((length, columns), f32))
        out_specs.append(rows_spec(columns))
    outs.append(jax.ShapeDtypeStruct((chunks, STATE, units), f32))
    out_specs.append(pl.BlockSpec((1, STATE, units), lambda i: (i, 0, 0)))
    outs.append(jax.ShapeDtypeStruct((length, width + LANES), bf16))
    out_specs.append(rows_spec(width + LANES))
    results = pl.pallas_call(
        functools.partial(forward_kernel, second, heads),
        grid=(chunks,),
        in_specs=specs + shared_specs,
        out_specs=out_specs,
        out_shape=outs,
        scratch_shapes=[
            pltpu.VMEM((STATE, units), f32),
            pltpu.VMEM((8, units), f32),
            pltpu.VMEM((8, 2 * STATE), f32),
            pltpu.VMEM((8, width), f32),
        ],
        compiler_params=pltpu.CompilerParams(vmem_limit_bytes=VMEM_LIMIT, dimension_semantics=("arbitrary",)),
        cost_estimate=pl.CostEstimate(flops=6_000_000_000, bytes_accessed=30_000_000, transcendentals=6_000_000),
    )(*inputs, *shared)
    if second:
        return results[0], results[1:9], results[9]
    return h, results[:8], results[8]


def backward_layer(h, parts, extra, weights, marks, segment_row, params, saved):
    length, width = h.shape
    units = params[0].shape[1]
    heads = units // HEAD_DIM
    chunks = length // SPAN
    last = chunks - 1
    second = len(extra) == 1
    shared, shared_specs = common_args(weights, marks, segment_row, params, chunks, True)
    inputs = [h] + list(parts) + list(extra)
    specs = [rows_spec(width, last)] + [rows_spec(width + LANES, last)] * 2
    if second:
        specs += [rows_spec(width, last)]
    else:
        specs += [rows_spec(width, last)] * 4 + [whole_spec(extra[4])]
    saved_specs = [rows_spec(s.shape[1], last) for s in saved[:7]]
    saved_specs.append(pl.BlockSpec((1, STATE, units), lambda i: (last - i, 0, 0)))
    outs, out_specs = [], []
    if second:
        outs.append(jax.ShapeDtypeStruct((length, width), bf16))
        out_specs.append(rows_spec(width, last))
    outs.append(jax.ShapeDtypeStruct((length, width), f32))
    out_specs.append(rows_spec(width, last))
    for w in weights:
        outs.append(jax.ShapeDtypeStruct(w.shape, bf16))
        out_specs.append(whole_spec(w))
    outs.append(jax.ShapeDtypeStruct((length, width), bf16))
    out_specs.append(rows_spec(width, last))
    for columns in (units, 2 * STATE):
        outs.append(jax.ShapeDtypeStruct((8, columns), f32))
        out_specs.append(pl.BlockSpec((8, columns), lambda i: (0, 0)))
    return pl.pallas_call(
        functools.partial(backward_kernel, second, heads),
        grid=(chunks,),
        in_specs=specs + shared_specs + saved_specs,
        out_specs=out_specs,
        out_shape=outs,
        scratch_shapes=[pltpu.VMEM(w.shape, f32) for w in weights]
        + [
            pltpu.VMEM((STATE, units), f32),
            pltpu.VMEM((STATE, units), f32),
            pltpu.VMEM((8, units), f32),
            pltpu.VMEM((8, 2 * STATE), f32),
            pltpu.VMEM((8, width), f32),
            pltpu.VMEM((8, units), f32),
            pltpu.VMEM((8, 2 * STATE), f32),
        ],
        compiler_params=pltpu.CompilerParams(vmem_limit_bytes=VMEM_LIMIT, dimension_semantics=("arbitrary",)),
        cost_estimate=pl.CostEstimate(flops=20_000_000_000, bytes_accessed=50_000_000, transcendentals=9_000_000),
    )(*inputs, *shared, *saved)


def token_marks(segment, counted, turned):
    length = segment.shape[0]
    blocks = segment.reshape(-1, SPAN)
    ends = blocks[:, -1]
    before = jnp.concatenate([jnp.full((1,), -1, segment.dtype), ends[:-1]])
    columns = [jnp.pad(segment, (lag, 0), constant_values=-1)[:length] == segment for lag in (1, 2, 3)]
    columns += [(blocks == before[:, None]).reshape(-1), (blocks == ends[:, None]).reshape(-1), segment]
    columns += [jnp.pad(segment, (0, lag), constant_values=-1)[lag:] == segment for lag in (1, 2, 3)]
    columns += [counted, jnp.broadcast_to(turned, segment.shape)]
    stacked = jnp.stack([c.astype(f32) for c in columns], axis=1)
    return jnp.pad(stacked, ((0, 0), (0, LANES - stacked.shape[1])))


def factors_of(number):
    found = []
    while number > 1:
        size = 2 if number % 4 or not found else 4
        size = size if number % size == 0 else number
        found.append(size)
        number //= size
    return found[::-1] or [1]


def digit_pairs(size, stride, total, moves):
    pairs = []
    for index in range(total):
        place = index // stride % size
        for start, end in moves:
            if start == place:
                pairs.append((index, index + (end - start) * stride))
    return pairs


class Line:
    def __init__(self, size, stride, total):
        self.size, self.stride, self.total = size, stride, total

    def place(self):
        return lax.axis_index("dp") // self.stride % self.size

    def send(self, block, moves):
        return lax.ppermute(block, "dp", digit_pairs(self.size, self.stride, self.total, moves))

    def gather(self, block):
        size, place = self.size, self.place()
        if size == 1:
            return block[None]
        if size == 2:
            other = self.send(block, [(0, 1), (1, 0)])
            first = place == 0
            return jnp.stack([jnp.where(first, block, other), jnp.where(first, other, block)])
        ups, downs = [], []
        up = down = block
        for hop in range(1, size):
            up = self.send(up, [(p, p + 1) for p in range(size - 1) if p >= hop - 1])
            down = self.send(down, [(p, p - 1) for p in range(1, size) if p <= size - hop])
            ups.append(up)
            downs.append(down)
        row = jnp.stack(ups[::-1] + [block] + downs)
        return lax.dynamic_slice_in_dim(row, size - 1 - place, size, 0)

    def reduce(self, blocks):
        size, place = self.size, self.place()
        if size == 1:
            return blocks[0]
        at = lambda index: lax.dynamic_index_in_dim(blocks, jnp.clip(index, 0, size - 1), 0, keepdims=False).astype(f32)
        own = at(place)
        if size == 2:
            other = self.send(at(1 - place).astype(bf16), [(0, 1), (1, 0)])
            return (own + other.astype(f32)).astype(bf16)
        up = down = None
        for far in range(size - 1, 0, -1):
            up_block, down_block = at(place + far), at(place - far)
            if up is not None:
                up_block, down_block = up_block + up.astype(f32), down_block + down.astype(f32)
            up = self.send(up_block.astype(bf16), [(p, p + 1) for p in range(size - far)])
            down = self.send(down_block.astype(bf16), [(p, p - 1) for p in range(far, size)])
        return (own + up.astype(f32) + down.astype(f32)).astype(bf16)

    def total_of(self, block):
        size = self.size
        if size == 1:
            return block
        if size == 2:
            return block + self.send(block, [(0, 1), (1, 0)])
        result = up = block
        down = block
        for hop in range(1, size):
            up = self.send(up, [(p, p + 1) for p in range(size - 1) if p >= hop - 1])
            down = self.send(down, [(p, p - 1) for p in range(1, size) if p <= size - hop])
            result = result + up + down
        return result


def swapped(block, axis):
    return lax.ppermute(block, axis, [(0, 1), (1, 0)])


def chosen_swap(block, section):
    size = lax.axis_size("tensor")
    pairs = [(section * size + i, section * size + 1 - i) for i in range(size)]
    return lax.ppermute(block, ("section", "tensor"), pairs)


def body(
    x_input,
    teacher,
    segment_ids,
    valid_len,
    norm_gain,
    w_zx,
    w_bc,
    w_dt,
    conv_x,
    conv_bc,
    dt_bias,
    a_log,
    d_skip,
    gnorm_gain,
    w_out,
):
    micro, local_rows, width = x_input.shape
    seq_length = segment_ids.shape[2]
    ranks = lax.axis_size("dp")
    core = lax.axis_index("section")
    turn = lax.axis_index("tensor")
    rank = lax.axis_index("dp")
    on_first = core == 0
    block_rows = w_zx.shape[1]
    half = w_zx.shape[3] // 2
    heads_half = w_dt.shape[2] // 2
    sizes = factors_of(ranks)
    lines = []
    stride = ranks
    for size in sizes:
        stride //= size
        lines.append(Line(size, stride, ranks))

    def pick(pair, index):
        return lax.dynamic_index_in_dim(pair, index, 0, keepdims=False)

    def by_layer(kept, received):
        return jnp.where(on_first, kept, received), jnp.where(on_first, received, kept)

    bc_half = lax.dynamic_slice_in_dim(w_bc[0], turn * STATE, STATE, 1)
    gain_column = jnp.pad(norm_gain[0][:, None], ((0, 0), (LANES // 2, LANES // 2 - 1)))

    def in_pack(part):
        steps = w_dt[0][:, part * heads_half : (part + 1) * heads_half]
        steps = jnp.pad(steps, ((0, 0), (0, LANES - heads_half))) + gain_column
        columns = slice(part * half, (part + 1) * half)
        return jnp.concatenate([w_zx[0][:, 0, columns], bc_half, w_zx[0][:, 1, columns], steps], axis=1)

    in_packs = jnp.stack([in_pack(0), in_pack(1)])
    in_layers = by_layer(pick(in_packs, core), swapped(pick(in_packs, 1 - core), "section"))
    out_packs = jnp.transpose(w_out[0].reshape(2, half, block_rows), (0, 2, 1))
    out_layers = by_layer(pick(out_packs, core), swapped(pick(out_packs, 1 - core), "section"))

    def lines_over(block, chosen):
        for line in reversed(chosen):
            block = line.gather(block)
        return block

    def gathered_in(block):
        first = lines[0].gather(block)
        columns = half + STATE
        rest = lines[1:]
        a_rows = lines_over(first[..., :columns], rest)
        b_part = first[..., columns:]
        b_both = lines_over(jnp.stack([b_part, swapped(b_part, "tensor")]), rest)
        a_rows = jnp.moveaxis(a_rows, len(rest), 0).reshape(width, columns)
        b_both = jnp.moveaxis(b_both, (len(rest), len(rest) + 1), (0, 1)).reshape(2, width, half + LANES)
        return a_rows, swapped(a_rows, "tensor"), b_both[0], b_both[1]

    def gathered_out(block):
        rows = lines_over(lines[0].gather(block), lines[1:])
        rows = jnp.moveaxis(rows, len(lines) - 1, 0).reshape(width, half)
        return rows, swapped(rows, "tensor")

    def whole_rows(rows):
        quarter = local_rows // 2
        own = pick(rows, turn)
        away = lax.dynamic_slice_in_dim(pick(rows, 1 - turn), core * quarter, quarter, 0)
        here = swapped(away, "tensor")
        beside = swapped(here, "section")
        first, second = jnp.where(on_first, here, beside), jnp.where(on_first, beside, here)
        other = jnp.concatenate([first, second], axis=0)
        return jnp.where(turn == 0, jnp.concatenate([own, other]), jnp.concatenate([other, own]))

    x_rows = whole_rows(x_input)
    target = whole_rows(teacher)
    segment = pick(segment_ids[:, 0], turn)
    length = pick(pick(valid_len, turn), rank)
    loss_weight = micro * seq_length * ranks / jnp.sum(valid_len).astype(f32)
    counted = jnp.where(jnp.arange(seq_length) < length, 2.0 * loss_weight, 0.0)
    marks = token_marks(segment, counted, turn)
    segment_row = segment.astype(f32)[None]

    channels = jnp.concatenate([conv_x[0].astype(f32), gnorm_gain.astype(f32)], axis=0)
    channels = jnp.stack([channels[:, :half], channels[:, half:]])
    channels = jnp.stack(by_layer(pick(channels, core), swapped(pick(channels, 1 - core), "section")))
    channels = jnp.concatenate([channels, swapped(channels, "tensor")], axis=2)
    shared = jnp.concatenate(
        [conv_bc[0].astype(f32), jnp.pad(jnp.concatenate([dt_bias, a_log, d_skip]), ((0, 0), (0, 2 * STATE - dt_bias.shape[1])))]
    )
    shared = jnp.stack(by_layer(shared, swapped(shared, "section")))

    def own_heads(row):
        starts = turn * 2 * heads_half + core * heads_half, (1 - turn) * 2 * heads_half + core * heads_half
        return jnp.concatenate([lax.dynamic_slice_in_dim(row, start, heads_half) for start in starts])

    def params_of(layer):
        skips = jnp.repeat(own_heads(shared[layer, 7]), HEAD_DIM)
        small = jnp.concatenate([channels[layer], skips[None], jnp.zeros_like(skips)[None]])
        states_small = jnp.pad(shared[layer, :5], ((0, 3), (0, 0)))
        head_rows = jnp.stack([own_heads(shared[layer, 5]), jnp.exp(own_heads(shared[layer, 6]))])
        head_rows = jnp.pad(head_rows, ((0, 6), (0, LANES - head_rows.shape[1])))
        return small, states_small, head_rows

    params = [params_of(0), params_of(1)]
    weights = [gathered_in(in_layers[0]) + gathered_out(out_layers[0])]
    weights.append(gathered_in(in_layers[1]) + gathered_out(out_layers[1]))

    _, saved_first, part = forward_layer(x_rows, None, weights[0], marks, segment_row, params[0])
    parts_first = (part, swapped(part, "section"))
    hidden, saved_second, part = forward_layer(x_rows, parts_first, weights[1], marks, segment_row, params[1])
    parts_second = (part, swapped(part, "section"))

    results = backward_layer(hidden, parts_second, (target,), weights[1], marks, segment_row, params[1], saved_second)
    produced, grad_out = results[:2]
    grads_second = results[2:8]
    sums_second = results[9:]
    gain_next = jnp.broadcast_to(weights[1][2][:, half + LANES // 2].astype(f32)[None], (8, width))
    extra = (hidden, grad_out, results[8], swapped(results[8], "section"), gain_next)
    results = backward_layer(x_rows, parts_first, extra, weights[0], marks, segment_row, params[0], saved_first)
    grad_hidden = results[0]
    grads_first = results[1:7]
    sums_first = results[8:]
    gain_first = weights[0][2][:, half + LANES // 2].astype(f32)[None]
    grad_normed = results[7].astype(f32) + swapped(results[7], "section").astype(f32)
    grad_out_low = grad_hidden.astype(bf16).astype(f32)
    grad_x, gain_term = norm_backward(grad_normed, x_rows.astype(f32), grad_out_low, gain_first)
    grad_gain_first = jnp.sum(gain_term, axis=0)

    def halves(rows):
        own = lax.dynamic_slice_in_dim(rows, turn * local_rows, local_rows, 0)
        away = lax.dynamic_slice_in_dim(rows, (1 - turn) * local_rows, local_rows, 0)
        return own, away

    def placed(own, received):
        return jnp.where(turn == 0, jnp.stack([own, received]), jnp.stack([received, own]))

    own, away = halves(jnp.where(on_first, hidden, produced))
    layer_outputs = placed(own, swapped(away, "tensor"))
    own_second, away = halves(grad_hidden)
    received_second = chosen_swap(away.astype(bf16), 1)
    own_first, away = halves(grad_x)
    received_first = chosen_swap(away.astype(bf16), 0)
    boundary = placed(
        jnp.where(on_first, own_first, own_second),
        jnp.where(on_first, received_first, received_second).astype(f32),
    )

    def add(left, right):
        return (left.astype(f32) + right.astype(f32)).astype(bf16)

    def reduced(grads):
        a_own, a_other, b_own, b_other, o_own, o_other = grads
        shape = tuple(sizes) + (block_rows,)

        def over_rest(block):
            lead = block.shape[0]
            for line in reversed(lines[1:]):
                index = lines.index(line) + 1
                block = line.reduce(jnp.moveaxis(block, index, 0))
            return block

        a_sum = add(a_own, swapped(a_other, "tensor")).reshape((1,) + shape + (-1,))
        a_sum = over_rest(a_sum)[0]
        b_sum = over_rest(jnp.stack([b_own, b_other]).reshape((2,) + shape + (-1,)))
        b_sum = add(b_sum[0], swapped(b_sum[1], "tensor"))
        o_sum = over_rest(add(o_own, swapped(o_other, "tensor")).reshape((1,) + shape + (-1,)))[0]
        return lines[0].reduce(jnp.concatenate([a_sum, b_sum, o_sum], axis=-1))

    owned_second = reduced(grads_second)
    owned_first = reduced(grads_first)
    mine, others = by_layer(owned_first, owned_second)
    beside = swapped(others, "section").astype(f32)
    mine = mine.astype(f32)

    def both(columns):
        start, size = columns
        here, there = mine[:, start : start + size], beside[:, start : start + size]
        return jnp.where(on_first, jnp.concatenate([here, there], 1), jnp.concatenate([there, here], 1))

    b_start = half + STATE
    o_start = b_start + half + LANES
    grad_zx = jnp.stack([both((0, half)), both((b_start, half))], axis=1)
    bc_own = mine[:, half:b_start] + beside[:, half:b_start]
    bc_other = swapped(bc_own, "tensor")
    grad_bc = jnp.where(turn == 0, jnp.concatenate([bc_own, bc_other], 1), jnp.concatenate([bc_other, bc_own], 1))
    grad_dt = both((b_start + half, heads_half))
    grad_out_w = jnp.transpose(both((o_start, half)))

    def split_pack(sums, states_sums):
        skips = jnp.sum(sums[6].reshape(2 * heads_half, HEAD_DIM), axis=1)
        heads = jnp.stack([skips, states_sums[5, : 2 * heads_half], states_sums[5, STATE : STATE + 2 * heads_half]])
        heads = heads.reshape(3, 2, heads_half)
        heads = jnp.pad(heads, ((0, 0), (0, 0), (0, half - heads_half))).reshape(3, 2 * half)
        return jnp.concatenate([sums[:6], heads], axis=0)

    split_first, split_second = split_pack(*sums_first), split_pack(*sums_second)
    mine, others = by_layer(split_first, split_second)
    beside = swapped(others, "section")
    packed = jnp.concatenate([mine, beside])
    packed = packed[:, :half] + swapped(packed[:, half:], "tensor")
    mine, others = by_layer(sums_first[1][:5], sums_second[1][:5])
    states_total = mine + swapped(others, "section")
    gain_total = jnp.where(on_first, grad_gain_first, sums_first[0][7])
    total = jnp.concatenate([states_total.reshape(-1), gain_total]).reshape(-1, 2 * STATE)
    total = total + swapped(total, "tensor")
    for line in lines:
        packed = line.total_of(packed)
        total = line.total_of(total)
    rows = packed.shape[0] // 2
    here, there = packed[:rows], packed[rows:]

    def in_order(here, there):
        return jnp.where(on_first, jnp.concatenate([here, there], -1), jnp.concatenate([there, here], -1))

    channel_grads = in_order(here[:6], there[:6])
    head_grads = in_order(here[6:9, :heads_half], there[6:9, :heads_half])
    states_total = total[:5]
    gain_total = lax.dynamic_slice_in_dim(total[5:].reshape(-1), rank * block_rows, block_rows)
    return (
        layer_outputs[None],
        boundary[None],
        gain_total[None],
        grad_zx[None],
        grad_bc[None],
        grad_dt[None],
        channel_grads[None, :5],
        states_total[None],
        head_grads[1][None],
        head_grads[2][None],
        head_grads[0][None],
        channel_grads[5][None],
        grad_out_w[None],
    )


def solution(mesh):
    placed = (
        P(None, ("dp", "tensor"), None),
        P(None, ("dp", "tensor"), None),
        P(None, "dp", None),
        P(),
        P("section", "dp"),
        P("section", "dp", None, "tensor"),
        P("section", "dp", None),
        P("section", "dp", "tensor"),
        P("section", None, "tensor"),
        P("section", None, None),
        P("section", None),
        P("section", None),
        P("section", None),
        P("section", "tensor"),
        P("section", "tensor", "dp"),
    )
    return jax.shard_map(
        body,
        mesh=mesh,
        in_specs=placed,
        out_specs=(
            P("section", None, ("dp", "tensor"), None),
            P("section", None, ("dp", "tensor"), None),
            P("section", "dp"),
            P("section", "dp", None, "tensor"),
            P("section", "dp", None),
            P("section", "dp", "tensor"),
            P("section", None, "tensor"),
            P("section", None, None),
            P("section", "tensor"),
            P("section", "tensor"),
            P("section", "tensor"),
            P("section", "tensor"),
            P("section", "tensor", "dp"),
        ),
        check_vma=False,
    )
```

```python
import functools

import jax
import jax.numpy as jnp
import numpy as np
from jax import lax
from jax.experimental import pallas as pl
from jax.experimental.pallas import tpu as pltpu
from jax.sharding import PartitionSpec as P

HEAD_DIM = 64
STATE = 128
SPAN = 256
LANES = 128

epsilon = 1e-05
f32 = jnp.float32
bf16 = jnp.bfloat16


def nn(left, right):
    return lax.dot_general(left, right, (((1,), (0,)), ((), ())), preferred_element_type=f32)


def nt(left, right):
    return lax.dot_general(left, right, (((1,), (1,)), ((), ())), preferred_element_type=f32)


def tn(left, right):
    return lax.dot_general(left, right, (((0,), (0,)), ((), ())), preferred_element_type=f32)


def high_low(value):
    high = value.astype(bf16)
    return high, (value - high.astype(f32)).astype(bf16)


def spread(per_head, spreader):
    return nn(jnp.concatenate(high_low(per_head), axis=1), spreader)


def gathered_heads(units, spreader):
    high, low = high_low(units)
    once = spreader[:LANES]
    return nt(high, once) + nt(low, once)


def running_sum(triangle, value):
    high = value.astype(bf16)
    rest = value - high.astype(f32)
    middle = rest.astype(bf16)
    low = (rest - middle.astype(f32)).astype(bf16)
    sums = nn(triangle, jnp.concatenate([high, middle, low], axis=1))
    return sums[:, :LANES] + sums[:, LANES : 2 * LANES] + sums[:, 2 * LANES :]


def softplus(value):
    return jnp.maximum(value, 0.0) + jnp.log1p(jnp.exp(-jnp.abs(value)))


def moved_down(block, edge, lag):
    return jnp.concatenate([edge, block], axis=0)[8 - lag : 8 - lag + block.shape[0]]


def moved_up(block, edge, lag):
    return jnp.concatenate([block, edge], axis=0)[lag : lag + block.shape[0]]


def decay_parts(steps_in, head_rows, marks, heads):
    lane = lax.broadcasted_iota(jnp.int32, (1, LANES), 1)
    live = lane < heads
    shifted = steps_in + head_rows[0:1, :LANES]
    steps = jnp.where(live, softplus(shifted), 0.0)
    rates = head_rows[1:2, :LANES]
    log_steps = -steps * rates
    row = lax.broadcasted_iota(jnp.int32, (SPAN, SPAN), 0)
    column = lax.broadcasted_iota(jnp.int32, (SPAN, SPAN), 1)
    lower = (row >= column).astype(bf16)
    logs = running_sum(lower, log_steps)
    last = logs[SPAN - 1 : SPAN]
    entry = jnp.exp(logs) * marks[:, 3:4]
    tail = jnp.exp(last - logs) * marks[:, 4:5]
    through = jnp.exp(last) * marks[SPAN - 1 : SPAN, 3:4]
    entry = jnp.where(live, entry, 0.0)
    tail = jnp.where(live, tail, 0.0)
    through = jnp.where(live, through, 0.0)
    return shifted, steps, log_steps, logs, entry, tail, through, row, column


def linked_mask(row, column, marks, segment_row):
    linked = (row >= column) & (marks[:, 5:6] == segment_row)
    return jnp.where(linked, 0.0, -1e30)


def branch_of(own_ref, other_ref, units):
    width = own_ref.shape[1] - LANES
    own = own_ref[...].astype(f32)
    other = other_ref[...].astype(f32)
    total = own[:, :width] + other[:, :width]
    own_squares = own[:, width : width + 1] + own[:, width + 1 : width + 2]
    other_squares = other[:, width : width + 1] + other[:, width + 1 : width + 2]
    inverse = lax.rsqrt((own_squares + other_squares) / (2 * units) + epsilon)
    return total * inverse, total, inverse


def load_weights(weights, start, sources, place_ref):
    rows, columns = sources[0].shape[1:]
    mine = place_ref[0]
    for source, place, offset in zip(sources, (mine, 1 - mine, mine, 1 - mine), (0, 0, columns, columns)):
        for index in range(source.shape[0]):
            first = pl.multiple_of((2 * index + place) * rows, 32)
            weights[pl.ds(first, rows), start + offset : start + offset + columns] = source[index]


def store_grads(targets, acc, start, place_ref):
    rows, columns = targets[0].shape[1:]
    mine = place_ref[0]
    for target, place, offset in zip(targets, (mine, 1 - mine, mine, 1 - mine), (0, 0, columns, columns)):
        for index in range(target.shape[0]):
            first = pl.multiple_of((2 * index + place) * rows, 32)
            target[index] = acc[pl.ds(first, rows), start + offset : start + offset + columns].astype(bf16)


def scan_forward_kernel(second, heads, *refs):
    place_ref, refs = refs[0], refs[1:]
    if second:
        (h_ref, own_ref, other_ref), refs = refs[:3], refs[3:]
    else:
        (h_ref,), refs = refs[:1], refs[1:]
    x_parts, s_parts, refs = refs[:4], refs[4:8], refs[8:]
    (marks_ref, segment_ref, small_ref, states_small_ref, head_ref, spread_ref), refs = refs[:6], refs[6:]
    if second:
        h_out, refs = refs[0], refs[1:]
    gain_ref, refs = refs[0], refs[1:]
    normed_ref, raw_ref, conv_ref, y_ref, raw_states_ref, conv_states_ref, steps_ref, entry_state_ref = refs[:8]
    state, raw_edge, states_edge, gain, weights = refs[8:]
    units = raw_ref.shape[1]

    @pl.when(pl.program_id(0) == 0)
    def _():
        state[...] = jnp.zeros_like(state)
        raw_edge[...] = jnp.zeros_like(raw_edge)
        states_edge[...] = jnp.zeros_like(states_edge)
        load_weights(weights, 0, x_parts, place_ref)
        load_weights(weights, units, s_parts, place_ref)
        steps_columns = weights[:, units + STATE : units + STATE + LANES].astype(f32)
        gain[...] = jnp.broadcast_to(jnp.transpose(steps_columns)[LANES // 2 : LANES // 2 + 1, :], gain.shape)
        gain_ref[...] = gain[...]

    hidden = h_ref[...].astype(f32)
    if second:
        rounded = (hidden + branch_of(own_ref, other_ref, units)[0]).astype(bf16)
        h_out[...] = rounded
        hidden = rounded.astype(f32)
    scale = lax.rsqrt(jnp.mean(hidden * hidden, axis=1, keepdims=True) + epsilon)
    normed = (hidden * scale * gain[0:1, :]).astype(bf16)
    normed_ref[...] = normed
    projected = nn(normed, weights[...])
    raw = projected[:, :units]
    first, second_part = projected[:, units : units + 2 * STATE], projected[:, units + 2 * STATE :]
    marks = marks_ref[...]
    turned = marks[0:1, 10:11] > 0.5
    raw_states = jnp.concatenate(
        [
            jnp.where(turned, second_part[:, :STATE], first[:, :STATE]),
            jnp.where(turned, first[:, :STATE], second_part[:, :STATE]),
        ],
        axis=1,
    )
    lane = lax.broadcasted_iota(jnp.int32, (1, LANES), 1)
    steps_in = jnp.where(lane < heads // 2, first[:, STATE:], pltpu.roll(second_part[:, STATE:], heads // 2, 1))
    raw_ref[...] = raw
    raw_states_ref[...] = raw_states
    steps_ref[...] = steps_in

    def conv(block, edge, taps):
        total = taps[4:5] + taps[3:4] * block
        for lag in (1, 2, 3):
            total = total + taps[3 - lag : 4 - lag] * (moved_down(block, edge, lag) * marks[:, lag - 1 : lag])
        return total

    taps = small_ref[...]
    conved = conv(raw, raw_edge[...], taps)
    conv_ref[...] = conved
    conved_states = conv(raw_states, states_edge[...], states_small_ref[...])
    conv_states_ref[...] = conved_states
    raw_edge[...] = raw[SPAN - 8 :]
    states_edge[...] = raw_states[SPAN - 8 :]
    values = conved * jax.nn.sigmoid(conved)
    states_in = conved_states * jax.nn.sigmoid(conved_states)
    b_rows = states_in[:, :STATE].astype(bf16)
    c_rows = states_in[:, STATE:].astype(bf16)
    _, steps, _, logs, entry, tail, through, row, column = decay_parts(steps_in, head_ref[...], marks, heads)
    spreader = spread_ref[...]
    scaled = values * spread(steps, spreader)
    mask = linked_mask(row, column, marks, segment_ref[...])
    scores = nt(c_rows, b_rows)
    logs_across = jnp.transpose(logs)
    pieces = []
    for pair in range(heads // 2):
        mixes = []
        for head in (2 * pair, 2 * pair + 1):
            factor = jnp.exp(logs[:, head : head + 1] - logs_across[head : head + 1, :] + mask)
            mixes.append((factor * scores).astype(bf16))
        block = scaled[:, pair * LANES : (pair + 1) * LANES]
        left = jnp.where(lane < HEAD_DIM, block, 0.0).astype(bf16)
        right = jnp.where(lane < HEAD_DIM, 0.0, block).astype(bf16)
        pieces.append(nn(jnp.concatenate(mixes, axis=1), jnp.concatenate([left, right], axis=0)))
    inside = jnp.concatenate(pieces, axis=1)
    held = state[...]
    entry_state_ref[0] = held
    across = nn(c_rows, held.astype(bf16)) * spread(entry, spreader)
    through_row = spread(jnp.broadcast_to(through, (8, LANES)), spreader)[0:1]
    state[...] = through_row * held + tn(b_rows, (spread(tail, spreader) * scaled).astype(bf16))
    y_ref[...] = inside + across + taps[6:7] * values


def gate_forward_kernel(place_ref, normed_ref, y_ref, *refs):
    z_parts, o_parts, refs = refs[:4], refs[4:8], refs[8:]
    small_ref, gate_ref, part_ref, weights, out_weights = refs

    @pl.when(pl.program_id(0) == 0)
    def _():
        load_weights(weights, 0, z_parts, place_ref)
        load_weights(out_weights, 0, o_parts, place_ref)

    gate = nn(normed_ref[...], weights[...])
    gate_ref[...] = gate
    gated = y_ref[...] * (gate * jax.nn.sigmoid(gate))
    squares = jnp.sum(gated * gated, axis=1, keepdims=True)
    part = nt((gated * small_ref[5:6]).astype(bf16), out_weights[...])
    width = part.shape[1]
    part_ref[:, :width] = part.astype(bf16)
    high, low = high_low(squares)
    lane = lax.broadcasted_iota(jnp.int32, (1, LANES), 1)
    part_ref[:, width:] = jnp.where(lane == 0, high, jnp.where(lane == 1, low, jnp.zeros_like(low)))


def gate_backward_kernel(second, *refs):
    place_ref, refs = refs[0], refs[1:]
    if second:
        (h_ref, own_ref, other_ref, target_ref), refs = refs[:4], refs[4:]
    else:
        (own_ref, other_ref, next_h_ref, next_out_ref, grad_own_ref, grad_other_ref, next_gain_ref), refs = refs[:7], refs[7:]
    (normed_ref, gate_ref, y_ref), z_parts, o_parts, (marks_ref, small_ref), refs = refs[:3], refs[3:7], refs[7:11], refs[11:13], refs[13:]
    if second:
        out_ref, refs = refs[0], refs[1:]
    (grad_out_ref, grad_y_ref, part_ref), dz_parts, do_parts, sums_ref, refs = refs[:3], refs[3:7], refs[7:11], refs[11], refs[12:]
    weights, out_weights, acc_z, acc_o, sums = refs
    units = y_ref.shape[1]

    @pl.when(pl.program_id(0) == 0)
    def _():
        load_weights(weights, 0, z_parts, place_ref)
        load_weights(out_weights, 0, o_parts, place_ref)
        for ref in (acc_z, acc_o, sums):
            ref[...] = jnp.zeros_like(ref)

    branch, total, inverse = branch_of(own_ref, other_ref, units)
    if second:
        produced = h_ref[...].astype(f32) + branch
        out_ref[...] = produced.astype(bf16)
        grad_out = marks_ref[:, 9:10] * (produced - target_ref[...])
    else:
        grad_normed = grad_own_ref[...].astype(f32) + grad_other_ref[...].astype(f32)
        grad_out, gain_term = norm_backward(grad_normed, next_h_ref[...].astype(f32), next_out_ref[...], next_gain_ref[0:1, :])
        sums[7:8, :] += jnp.sum(gain_term, axis=0, keepdims=True)
    grad_out_ref[...] = grad_out
    grad = grad_out.astype(bf16)
    inner = jnp.sum(grad.astype(f32) * total, axis=1, keepdims=True) * (inverse * inverse * inverse) / (2 * units)
    gain = small_ref[5:6]
    gate = gate_ref[...]
    y = y_ref[...]
    gate_sig = jax.nn.sigmoid(gate)
    gate_silu = gate * gate_sig
    gated = y * gate_silu
    gated_unit = gated * inverse
    grad_mixed = nn(grad, out_weights[...])
    acc_o[...] += tn(grad, (gated_unit * gain).astype(bf16))
    sums[5:6, :] += jnp.sum(grad_mixed * gated_unit, axis=0, keepdims=True)
    grad_gated = grad_mixed * gain * inverse - gated * inner
    grad_gate = (grad_gated * y * (gate_sig * (1.0 + gate * (1.0 - gate_sig)))).astype(bf16)
    grad_y_ref[...] = (grad_gated * gate_silu).astype(bf16)
    acc_z[...] += tn(normed_ref[...], grad_gate)
    part_ref[...] = nt(grad_gate, weights[...])

    @pl.when(pl.program_id(0) == pl.num_programs(0) - 1)
    def _():
        store_grads(dz_parts, acc_z, 0, place_ref)
        store_grads(do_parts, acc_o, 0, place_ref)
        sums_ref[...] = sums[...]


def scan_backward_kernel(heads, *refs):
    (place_ref, grad_y_ref, gate_part_ref, normed_ref), x_parts, s_parts, refs = refs[:4], refs[4:8], refs[8:12], refs[12:]
    (marks_ref, segment_ref, small_ref, states_small_ref, head_ref, spread_ref), refs = refs[:6], refs[6:]
    (raw_ref, conv_ref, y_ref, raw_states_ref, conv_states_ref, steps_ref, entry_state_ref), refs = refs[:7], refs[7:]
    dx_parts, ds_parts, (part_ref, sums_ref, states_sums_ref), refs = refs[:4], refs[4:8], refs[8:11], refs[11:]
    weights, acc, dstate, next_state, conv_edge, states_edge, sums, states_sums = refs
    step = pl.program_id(0)
    units = raw_ref.shape[1]

    @pl.when(step == 0)
    def _():
        for ref in (acc, dstate, next_state, conv_edge, states_edge, sums, states_sums):
            ref[...] = jnp.zeros_like(ref)
        load_weights(weights, 0, x_parts, place_ref)
        load_weights(weights, units, s_parts, place_ref)

    marks = marks_ref[...]
    taps = small_ref[...]
    y = y_ref[...]
    grad_y_low = grad_y_ref[...]
    grad_y = grad_y_low.astype(f32)
    conved = conv_ref[...]
    value_sig = jax.nn.sigmoid(conved)
    values = conved * value_sig
    conved_states = conv_states_ref[...]
    states_sig = jax.nn.sigmoid(conved_states)
    states_in = conved_states * states_sig
    b_rows = states_in[:, :STATE].astype(bf16)
    c_rows = states_in[:, STATE:].astype(bf16)
    shifted, steps, log_steps, logs, entry, tail, through, row, column = decay_parts(steps_ref[...], head_ref[...], marks, heads)
    spreader = spread_ref[...]
    spread_steps = spread(steps, spreader)
    spread_entry = spread(entry, spreader)
    spread_tail = spread(tail, spreader)
    through_row = spread(jnp.broadcast_to(through, (8, LANES)), spreader)[0:1]
    scaled_low = (values * spread_steps).astype(bf16)
    scaled = scaled_low.astype(f32)
    mask = linked_mask(row, column, marks, segment_ref[...])
    scores = nt(c_rows, b_rows)
    logs_across = jnp.transpose(logs)
    lane = lax.broadcasted_iota(jnp.int32, (1, LANES), 1)
    is_left = lane < HEAD_DIM
    zero = jnp.zeros((), bf16)
    grad_scores = jnp.zeros((SPAN, SPAN), f32)
    pieces = []
    for pair in range(heads // 2):
        columns = slice(pair * LANES, (pair + 1) * LANES)
        block, grad = scaled_low[:, columns], grad_y_low[:, columns]
        grad_left = jnp.where(is_left, grad, zero)
        grad_right = jnp.where(is_left, zero, grad)
        mixes = []
        for head, grad_one in ((2 * pair, grad_left), (2 * pair + 1, grad_right)):
            factor = jnp.exp(logs[:, head : head + 1] - logs_across[head : head + 1, :] + mask)
            mixes.append((factor * scores).astype(bf16))
            grad_scores = grad_scores + nt(grad_one, block) * factor
        pieces.append(tn(jnp.concatenate(mixes, axis=0), jnp.concatenate([grad_left, grad_right], axis=0)))
    held = entry_state_ref[0]
    held_low = held.astype(bf16)
    gradient = dstate[...]
    gradient_low = gradient.astype(bf16)
    grad_scaled = jnp.concatenate(pieces, axis=1) + spread_tail * nn(b_rows, gradient_low)
    grad_entry = (spread_entry * grad_y).astype(bf16)
    grad_scores_low = grad_scores.astype(bf16)
    grad_c = nn(grad_scores_low, b_rows) + nt(grad_entry, held_low)
    grad_b = tn(grad_scores_low, c_rows) + nt((spread_tail * scaled).astype(bf16), gradient_low)
    state_term = jnp.sum(gradient * next_state[...], axis=0, keepdims=True)
    dstate[...] = through_row * gradient + tn(c_rows, grad_entry)
    next_state[...] = held
    skip = taps[6:7]
    sums[6:7, :] += jnp.sum(grad_y * values, axis=0, keepdims=True)
    grad_logs = gathered_heads(grad_y * (y - skip * values) - scaled * grad_scaled, spreader)
    state_heads = gathered_heads(jnp.broadcast_to(state_term, (8, units)), spreader)[0:1]
    last_row = lax.broadcasted_iota(jnp.int32, (SPAN, 1), 0) == SPAN - 1
    grad_logs = grad_logs + jnp.where(last_row, state_heads, 0.0)
    grad_log_steps = running_sum((row <= column).astype(bf16), grad_logs)
    grad_steps = gathered_heads(grad_scaled * values, spreader) - head_ref[1:2, :LANES] * grad_log_steps
    grad_steps_in = jnp.where(lane < heads, grad_steps * jax.nn.sigmoid(shifted), 0.0)
    states_sums[5:6, :] += jnp.concatenate(
        [
            jnp.sum(grad_steps_in, axis=0, keepdims=True),
            jnp.sum(grad_log_steps * log_steps, axis=0, keepdims=True),
        ],
        axis=1,
    )
    grad_values = grad_scaled * spread_steps + skip * grad_y
    grad_conved = grad_values * (value_sig * (1.0 + conved * (1.0 - value_sig)))
    grad_states = jnp.concatenate([grad_b, grad_c], axis=1)
    grad_conved_states = grad_states * (states_sig * (1.0 + conved_states * (1.0 - states_sig)))

    def conv_backward(block, edge, tap_rows, raw, total_ref):
        result = tap_rows[3:4] * block
        total_ref[3:4, :] += jnp.sum(block * raw, axis=0, keepdims=True)
        total_ref[4:5, :] += jnp.sum(block, axis=0, keepdims=True)
        for lag in (1, 2, 3):
            term = moved_up(block, edge, lag) * marks[:, 5 + lag : 6 + lag]
            result = result + tap_rows[3 - lag : 4 - lag] * term
            total_ref[3 - lag : 4 - lag, :] += jnp.sum(term * raw, axis=0, keepdims=True)
        return result

    grad_raw = conv_backward(grad_conved, conv_edge[...], taps, raw_ref[...], sums)
    grad_raw_states = conv_backward(
        grad_conved_states, states_edge[...], states_small_ref[...], raw_states_ref[...], states_sums
    )
    conv_edge[...] = grad_conved[:8]
    states_edge[...] = grad_conved_states[:8]
    turned = marks[0:1, 10:11] > 0.5
    first_states = jnp.where(turned, grad_raw_states[:, STATE:], grad_raw_states[:, :STATE])
    second_states = jnp.where(turned, grad_raw_states[:, :STATE], grad_raw_states[:, STATE:])
    own_steps = jnp.where(lane < heads // 2, grad_steps_in, 0.0)
    other_steps = jnp.where(lane < heads // 2, pltpu.roll(grad_steps_in, LANES - heads // 2, 1), 0.0)
    grads = jnp.concatenate([grad_raw, first_states, own_steps, second_states, other_steps], axis=1).astype(bf16)
    acc[...] += tn(normed_ref[...], grads)
    part_ref[...] = (nt(grads, weights[...]) + gate_part_ref[...]).astype(bf16)

    @pl.when(step == pl.num_programs(0) - 1)
    def _():
        store_grads(dx_parts, acc, 0, place_ref)
        store_grads(ds_parts, acc, units, place_ref)
        skips = gathered_heads(sums[...], spreader)[6:7]
        states_sums[6:7, :] = jnp.concatenate([skips, jnp.zeros_like(skips)], axis=1)
        sums_ref[...] = sums[...]
        states_sums_ref[...] = states_sums[...]


def norm_backward(grad_normed, hidden, grad_out, gain):
    scale = lax.rsqrt(jnp.mean(hidden * hidden, axis=1, keepdims=True) + epsilon)
    weighted = grad_normed * gain
    shared = jnp.mean(weighted * hidden, axis=1, keepdims=True) * (scale * scale * scale)
    return grad_out + scale * weighted - hidden * shared, grad_normed * hidden * scale


VMEM_LIMIT = 60 * 1024 * 1024


def spreader_of(units):
    one = (np.arange(LANES)[:, None] == np.arange(units)[None, :] // HEAD_DIM).astype(np.float32)
    return jnp.asarray(np.concatenate([one, one], axis=0), bf16)


def rows_spec(width, last=None):
    if last is None:
        return pl.BlockSpec((SPAN, width), lambda i: (i, 0))
    return pl.BlockSpec((SPAN, width), lambda i: (last - i, 0))


def whole_spec(array):
    return pl.BlockSpec(array.shape, lambda i: (0,) * array.ndim)


def call(kernel, inputs, outputs, scratch, chunks, flops):
    return pl.pallas_call(
        kernel,
        grid=(chunks,),
        in_specs=[spec for _, spec in inputs],
        out_specs=[spec for _, _, spec in outputs],
        out_shape=[jax.ShapeDtypeStruct(shape, dtype) for shape, dtype, _ in outputs],
        scratch_shapes=[pltpu.VMEM(shape, dtype) for shape, dtype in scratch],
        compiler_params=pltpu.CompilerParams(vmem_limit_bytes=VMEM_LIMIT, dimension_semantics=("arbitrary",)),
        cost_estimate=pl.CostEstimate(flops=flops, bytes_accessed=20_000_000, transcendentals=0),
    )(*[array for array, _ in inputs])


def fixed(array):
    return array, whole_spec(array)


def scalars(array):
    return array, pl.BlockSpec(memory_space=pltpu.SMEM)


def scan_forward(place, h, parts, weights, marks, segment_row, params):
    length, width = h.shape
    units = params[0].shape[1]
    chunks = length // SPAN
    second = parts is not None
    inputs = [scalars(place), (h, rows_spec(width))]
    outputs = []
    if second:
        inputs += [(part, rows_spec(width + LANES)) for part in parts]
        outputs.append(((length, width), bf16, rows_spec(width)))
    inputs += [fixed(w) for w in weights]
    inputs += [(marks, rows_spec(LANES)), (segment_row, pl.BlockSpec((1, SPAN), lambda i: (0, i)))]
    inputs += [fixed(p) for p in params] + [fixed(spreader_of(units))]
    outputs.append(((8, width), f32, pl.BlockSpec((8, width), lambda i: (0, 0))))
    outputs.append(((length, width), bf16, rows_spec(width)))
    for columns in (units, units, units, 2 * STATE, 2 * STATE, LANES):
        outputs.append(((length, columns), f32, rows_spec(columns)))
    outputs.append(((chunks, STATE, units), f32, pl.BlockSpec((1, STATE, units), lambda i: (i, 0, 0))))
    scratch = [
        ((STATE, units), f32),
        ((8, units), f32),
        ((8, 2 * STATE), f32),
        ((8, width), f32),
        ((width, units + 4 * STATE), bf16),
    ]
    kernel = functools.partial(scan_forward_kernel, second, units // HEAD_DIM)
    results = call(kernel, inputs, outputs, scratch, chunks, 10_000_000_000)
    if not second:
        results = [h] + list(results)
    return results[0], results[1], results[2], results[3:]


def gate_forward(place, normed, y, weights, params):
    length, width = normed.shape
    units = params[0].shape[1]
    inputs = [scalars(place), (normed, rows_spec(width)), (y, rows_spec(units))] + [fixed(w) for w in weights] + [fixed(params[0])]
    outputs = [((length, units), f32, rows_spec(units)), ((length, width + LANES), bf16, rows_spec(width + LANES))]
    scratch = [((width, units), bf16)] * 2
    return call(gate_forward_kernel, inputs, outputs, scratch, length // SPAN, 2_500_000_000)


def gate_backward(place, h, parts, extra, normed, gate, y, weights, marks, params):
    length, width = normed.shape
    units = params[0].shape[1]
    second = len(extra) == 1
    inputs = [scalars(place)] + ([(h, rows_spec(width))] if second else [])
    inputs += [(part, rows_spec(width + LANES)) for part in parts]
    inputs += [(rows, rows_spec(width)) for rows in extra[:4]] + [fixed(gain) for gain in extra[4:]]
    inputs += [(normed, rows_spec(width)), (gate, rows_spec(units)), (y, rows_spec(units))]
    inputs += [fixed(w) for w in weights] + [(marks, rows_spec(LANES)), fixed(params[0])]
    outputs = [((length, width), bf16, rows_spec(width))] if second else []
    outputs += [((length, width), f32, rows_spec(width)), ((length, units), bf16, rows_spec(units)), ((length, width), f32, rows_spec(width))]
    outputs += [(w.shape, bf16, whole_spec(w)) for w in weights]
    outputs.append(((8, units), f32, pl.BlockSpec((8, units), lambda i: (0, 0))))
    scratch = [((width, units), bf16)] * 2 + [((width, units), f32)] * 2 + [((8, units), f32)]
    results = call(functools.partial(gate_backward_kernel, second), inputs, outputs, scratch, length // SPAN, 8_000_000_000)
    if not second:
        results = [None] + list(results)
    return results


def scan_backward(place, grad_y, gate_part, normed, weights, marks, segment_row, params, saved):
    length, width = normed.shape
    units = params[0].shape[1]
    chunks = length // SPAN
    last = chunks - 1
    inputs = [scalars(place), (grad_y, rows_spec(units, last)), (gate_part, rows_spec(width, last)), (normed, rows_spec(width, last))]
    inputs += [fixed(w) for w in weights]
    inputs += [(marks, rows_spec(LANES, last)), (segment_row, pl.BlockSpec((1, SPAN), lambda i: (0, last - i)))]
    inputs += [fixed(p) for p in params] + [fixed(spreader_of(units))]
    inputs += [(s, rows_spec(s.shape[1], last)) for s in saved[:6]]
    inputs.append((saved[6], pl.BlockSpec((1, STATE, units), lambda i: (last - i, 0, 0))))
    outputs = [(w.shape, bf16, whole_spec(w)) for w in weights]
    outputs.append(((length, width), bf16, rows_spec(width, last)))
    for columns in (units, 2 * STATE):
        outputs.append(((8, columns), f32, pl.BlockSpec((8, columns), lambda i: (0, 0))))
    scratch = [
        ((width, units + 4 * STATE), bf16),
        ((width, units + 4 * STATE), f32),
        ((STATE, units), f32),
        ((STATE, units), f32),
        ((8, units), f32),
        ((8, 2 * STATE), f32),
        ((8, units), f32),
        ((8, 2 * STATE), f32),
    ]
    kernel = functools.partial(scan_backward_kernel, units // HEAD_DIM)
    return call(kernel, inputs, outputs, scratch, chunks, 20_000_000_000)


def finish_kernel(own_ref, other_ref, h_ref, grad_out_ref, gain_ref, grad_ref, sums_ref, sums):
    @pl.when(pl.program_id(0) == 0)
    def _():
        sums[...] = jnp.zeros_like(sums)

    grad_normed = own_ref[...].astype(f32) + other_ref[...].astype(f32)
    grad_out = grad_out_ref[...].astype(bf16).astype(f32)
    grad_ref[...], gain_term = norm_backward(grad_normed, h_ref[...].astype(f32), grad_out, gain_ref[0:1, :])
    sums[0:1, :] += jnp.sum(gain_term, axis=0, keepdims=True)
    sums_ref[...] = sums[...]


def finish(own, other, h, grad_out, gain):
    length, width = h.shape
    inputs = [(rows, rows_spec(width)) for rows in (own, other, h, grad_out)] + [fixed(gain)]
    outputs = [((length, width), f32, rows_spec(width)), ((8, width), f32, pl.BlockSpec((8, width), lambda i: (0, 0)))]
    return call(finish_kernel, inputs, outputs, [((8, width), f32)], length // SPAN, 30_000_000)


def marks_kernel(place_ref, lengths_ref, segments_ref, marks_ref, row_ref):
    turn, rank = place_ref[1], place_ref[2]
    micro, sequences = lengths_ref.shape
    length = segments_ref.shape[1]
    total = jnp.int32(0)
    for batch in range(micro):
        total = lax.fori_loop(0, sequences, lambda i, t: t + lengths_ref[batch, i], total)
    weight = 2.0 * (micro * sequences * length) / jnp.full((1, length), total, jnp.int32).astype(f32)
    position = lax.broadcasted_iota(jnp.int32, (1, length), 1)
    segment = jnp.where(turn == 0, segments_ref[0:1, :], segments_ref[1:2, :])
    wide = jnp.broadcast_to(segment, (8, length))

    def same(lag):
        moved = pltpu.roll(wide, lag % length, 1)[0:1]
        inside = (position >= lag) & (position < length + lag)
        return jnp.where(inside & (moved == segment), 1.0, 0.0)

    before = jnp.full((1, length), -1, jnp.int32)
    end = before
    for block in range(length // SPAN):
        here = (position >= block * SPAN) & (position < (block + 1) * SPAN)
        end = jnp.where(here, segment[:, (block + 1) * SPAN - 1 : (block + 1) * SPAN], end)
        if block:
            before = jnp.where(here, segment[:, block * SPAN - 1 : block * SPAN], before)
    as_float = segment.astype(f32)
    rows = [same(1), same(2), same(3)]
    rows += [jnp.where(segment == before, 1.0, 0.0), jnp.where(segment == end, 1.0, 0.0), as_float]
    rows += [same(-1), same(-2), same(-3)]
    rows += [jnp.where(position < lengths_ref[turn, rank], weight, 0.0), jnp.full((1, length), turn, jnp.int32).astype(f32)]
    rows.append(jnp.zeros((LANES - len(rows), length), f32))
    marks_ref[...] = jnp.transpose(jnp.concatenate(rows, axis=0))
    row_ref[...] = as_float


def token_marks(place, lengths, segments):
    length = segments.shape[1]
    return pl.pallas_call(
        marks_kernel,
        in_specs=[pl.BlockSpec(memory_space=pltpu.SMEM)] * 2 + [pl.BlockSpec(memory_space=pltpu.VMEM)],
        out_shape=[jax.ShapeDtypeStruct((length, LANES), f32), jax.ShapeDtypeStruct((1, length), f32)],
        compiler_params=pltpu.CompilerParams(vmem_limit_bytes=VMEM_LIMIT),
    )(place, lengths, segments)


def three_parts(value):
    high = value.astype(bf16)
    rest = value - high.astype(f32)
    middle = rest.astype(bf16)
    return high, middle, (rest - middle.astype(f32)).astype(bf16)


PARAM_ROWS = 16


def pack_kernel(place_ref, zx_ref, bc_ref, dt_ref, gain_ref, out_ref, conv_ref, gate_gain_ref, states_conv_ref, heads_ref, kept_ref, sent_ref):
    turn, core = place_ref[1], place_ref[3]
    rows = zx_ref.shape[0]
    units = zx_ref.shape[1] // 2
    half = units // 2
    heads_half = dt_ref.shape[1] // 2
    lane = lax.broadcasted_iota(jnp.int32, (1, LANES), 1)
    bc = jnp.where(turn == 0, bc_ref[:, :STATE], bc_ref[:, STATE:])
    diagonal = lax.broadcasted_iota(jnp.int32, (rows, rows), 0) == lax.broadcasted_iota(jnp.int32, (rows, rows), 1)
    gain = jnp.sum(jnp.where(diagonal, gain_ref[...].astype(f32), 0.0), axis=1, keepdims=True)
    steps = jnp.concatenate([dt_ref[...].astype(f32), jnp.zeros((rows, LANES - 2 * heads_half), f32)], axis=1)
    later_steps = pltpu.roll(steps, LANES - heads_half, 1)
    shared = jnp.concatenate([states_conv_ref[...], jnp.zeros((PARAM_ROWS - 5, 2 * STATE), bf16)], axis=0)
    split = [part for row in range(3) for part in three_parts(heads_ref[row : row + 1, :])]
    heads = jnp.concatenate(split + [jnp.zeros((PARAM_ROWS - 9, LANES), bf16)], axis=0)
    for ref, part in ((kept_ref, core), (sent_ref, 1 - core)):
        first = part == 0

        def chosen(array, start):
            return jnp.where(first, array[:, start : start + half], array[:, start + half : start + 2 * half])

        ref[:rows, :half] = chosen(zx_ref, units)
        ref[:rows, half : half + STATE] = bc
        own_steps = jnp.where(lane < heads_half, jnp.where(first, steps, later_steps), 0.0)
        ref[:rows, half + STATE : half + 2 * STATE] = jnp.where(lane == LANES // 2, gain, own_steps).astype(bf16)
        ref[:rows, half + 2 * STATE : 2 * half + 2 * STATE] = chosen(zx_ref, 0)
        ref[:rows, 2 * half + 2 * STATE :] = chosen(out_ref, 0)
        ref[rows:, :] = jnp.zeros((PARAM_ROWS, ref.shape[1]), bf16)
        channels = jnp.concatenate([chosen(conv_ref, 0), chosen(gate_gain_ref, 0)], axis=0)
        ref[rows:, :half] = jnp.concatenate([channels, jnp.zeros((PARAM_ROWS - 6, half), bf16)], axis=0)
        ref[rows:, half : half + 2 * STATE] = shared
        ref[rows:, half + 2 * STATE : half + 2 * STATE + LANES] = heads


def plain_call(kernel, place, inputs, outputs):
    return pl.pallas_call(
        kernel,
        in_specs=[pl.BlockSpec(memory_space=pltpu.SMEM)] + [pl.BlockSpec(memory_space=pltpu.VMEM)] * len(inputs),
        out_shape=[jax.ShapeDtypeStruct(shape, dtype) for shape, dtype in outputs],
        compiler_params=pltpu.CompilerParams(vmem_limit_bytes=VMEM_LIMIT),
    )(place, *inputs)


def unpack_kernel(place_ref, kept_ref, received_ref, *refs):
    scan_ref, middle_ref, gate_ref, out_ref, params_ref, channels_ref = refs
    kept_first = place_ref[3] == 0
    kept, received = kept_ref[...], received_ref[...]
    first = jnp.where(kept_first, kept, received)
    second = jnp.where(kept_first, received, kept)
    rows, half = gate_ref.shape
    scan = scan_ref.shape[1]
    scan_ref[...] = first[:rows, :scan]
    middle_ref[:, : 2 * half] = first[:rows, scan:]
    middle_ref[:, 2 * half :] = second[:rows, :scan]
    gate_ref[...] = second[:rows, scan : scan + half]
    out_ref[...] = second[:rows, scan + half :]
    params_ref[0] = first[rows:, : scan + LANES]
    params_ref[1] = second[rows:, : scan + LANES]
    channels_ref[:PARAM_ROWS] = first[rows:, :half]
    channels_ref[PARAM_ROWS:] = second[rows:, :half]


def params_kernel(heads_half, place_ref, params_ref, channels_ref, spread_ref, *refs):
    turn, core = place_ref[1], place_ref[3]
    half = channels_ref.shape[1]
    lane = lax.broadcasted_iota(jnp.int32, (1, LANES), 1)
    for layer in range(2):
        small_ref, states_ref, head_ref = refs[3 * layer : 3 * layer + 3]
        rows = params_ref[layer].astype(f32)
        split = rows[:, half + 2 * STATE :]
        heads = [split[3 * i : 3 * i + 1] + split[3 * i + 1 : 3 * i + 2] + split[3 * i + 2 : 3 * i + 3] for i in range(3)]
        heads = jnp.concatenate(heads + [jnp.zeros((5, LANES), f32)], axis=0)
        moved = [pltpu.roll(heads, (LANES - start * heads_half) % LANES, 1) for start in range(4)]

        def of(index):
            return jnp.where(index == 0, moved[0], jnp.where(index == 1, moved[1], jnp.where(index == 2, moved[2], moved[3])))

        own, other = of(2 * turn + core), pltpu.roll(of(2 * (1 - turn) + core), heads_half, 1)
        heads = jnp.where(lane < heads_half, own, jnp.where(lane < 2 * heads_half, other, 0.0))
        head_ref[...] = jnp.concatenate([heads[0:1], jnp.exp(heads[1:2]), jnp.zeros((6, LANES), f32)], axis=0)
        high, middle, low = three_parts(jnp.broadcast_to(heads[2:3], (8, LANES)))
        once = spread_ref[:LANES]
        skips = (nn(high, once) + nn(middle, once) + nn(low, once))[0:1]
        own_rows = rows[0:6, :half]
        other_rows = channels_ref[PARAM_ROWS * layer : PARAM_ROWS * layer + 6].astype(f32)
        channels = jnp.concatenate([own_rows, other_rows], axis=1)
        small_ref[...] = jnp.concatenate([channels, skips, jnp.zeros_like(skips)], axis=0)
        states_ref[...] = jnp.concatenate([rows[0:5, half : half + 2 * STATE], jnp.zeros((3, 2 * STATE), f32)], axis=0)


def line_kernel(widths, place_ref, own_ref, up_ref, down_ref, up2_ref, down2_ref, far_ref, *outs):
    place = place_ref[0]
    above = {-1: up_ref, -2: up2_ref, -3: far_ref, 0: own_ref, 1: down_ref, 2: down2_ref, 3: far_ref}
    for here in range(4):

        @pl.when(place == here)
        def _():
            for index in range(4):
                start = 0
                for out, columns in zip(outs, widths):
                    out[index] = above[index - here][:, start : start + columns]
                    start += columns


def pick_kernel(place_ref, blocks_ref, *outs):
    place = place_ref[0]
    wanted = (place - 2, place + 2, 3 - place, place - 1, place + 1, place)
    for out, index in zip(outs, wanted):
        out[...] = blocks_ref[jnp.clip(index, 0, 3)]


def factors_of(number):
    found = []
    while number > 1:
        size = 4 if number % 4 == 0 else 2 if number % 2 == 0 else number
        found.append(size)
        number //= size
    return found[::-1]


def digit_pairs(size, stride, total, moves):
    pairs = []
    for index in range(total):
        place = index // stride % size
        for start, end in moves:
            if start == place:
                pairs.append((index, index + (end - start) * stride))
    return pairs


def after(block, *others):
    return lax.optimization_barrier((block,) + others)[0]


class Line:
    def __init__(self, size, stride, total):
        self.size, self.stride, self.total = size, stride, total

    def place(self):
        return lax.axis_index("dp") // self.stride % self.size

    def send(self, block, moves):
        return lax.ppermute(block, "dp", digit_pairs(self.size, self.stride, self.total, moves))

    def neighbours(self, block):
        size = self.size
        up = self.send(block, [(p, p + 1) for p in range(size - 1)])
        return up, self.send(block, [(p, p - 1) for p in range(1, size)])

    def second(self, up, down):
        up2 = self.send(up, [(1, 2), (2, 3)])
        down2 = self.send(down, [(2, 1), (1, 0)])
        return up2, down2, self.send(jnp.where(self.place() == 1, up, down), [(1, 3), (2, 0)])

    def gather(self, block, widths):
        size, place = self.size, self.place()
        if size == 4:
            up, down = self.neighbours(block)
            outs = [((size, block.shape[0], columns), block.dtype) for columns in widths]
            scalar = jnp.stack([place]).astype(jnp.int32)
            kernel = functools.partial(line_kernel, widths)
            return plain_call(kernel, scalar, (block, up, down) + self.second(up, down), outs)
        if size == 2:
            other = self.send(block, [(0, 1), (1, 0)])
            first = place == 0
            row = jnp.stack([jnp.where(first, block, other), jnp.where(first, other, block)])
        else:
            ups, downs = [], []
            up = down = block
            for hop in range(1, size):
                up = self.send(up, [(p, p + 1) for p in range(size - 1) if p >= hop - 1])
                down = self.send(down, [(p, p - 1) for p in range(1, size) if p <= size - hop])
                ups.append(up)
                downs.append(down)
            row = lax.dynamic_slice_in_dim(jnp.stack(ups[::-1] + [block] + downs), size - 1 - place, size, 0)
        starts = [sum(widths[:i]) for i in range(len(widths))]
        return [row[..., start : start + columns] for start, columns in zip(starts, widths)]

    def reduce(self, blocks):
        size, place = self.size, self.place()
        if size == 4:
            scalar = jnp.stack([place]).astype(jnp.int32)
            below2, above2, mirrored, below, above, own = plain_call(
                pick_kernel, scalar, (blocks,), [(blocks.shape[1:], bf16)] * 6
            )
            from_above = self.send(below2, [(2, 1), (3, 2)])
            from_below = self.send(above2, [(1, 2), (0, 1)])
            far = self.send(mirrored, [(3, 1), (0, 2)])
            zero = jnp.zeros((), bf16)
            below = below.astype(f32) + from_above.astype(f32) + jnp.where(place == 1, far, zero).astype(f32)
            above = above.astype(f32) + from_below.astype(f32) + jnp.where(place == 2, far, zero).astype(f32)
            down = self.send(below.astype(bf16), [(p, p - 1) for p in range(1, size)])
            up = self.send(above.astype(bf16), [(p, p + 1) for p in range(size - 1)])
            return (own.astype(f32) + up.astype(f32) + down.astype(f32)).astype(bf16)
        at = lambda index: lax.dynamic_index_in_dim(blocks, jnp.clip(index, 0, size - 1), 0, keepdims=False).astype(f32)
        own = at(place)
        up = down = None
        for far in range(size - 1, 0, -1):
            up_block, down_block = at(place + far), at(place - far)
            if up is not None:
                up_block, down_block = up_block + up.astype(f32), down_block + down.astype(f32)
            up = self.send(up_block.astype(bf16), [(p, p + 1) for p in range(size - far)])
            down = self.send(down_block.astype(bf16), [(p, p - 1) for p in range(far, size)])
        return (own + up.astype(f32) + down.astype(f32)).astype(bf16)

    def total_of(self, block):
        size = self.size
        up, down = self.neighbours(block)
        if size == 4:
            return block + up + down + sum(self.second(up, down))
        result = block + up + down
        for hop in range(2, size):
            up = self.send(up, [(p, p + 1) for p in range(size - 1) if p >= hop - 1])
            down = self.send(down, [(p, p - 1) for p in range(1, size) if p <= size - hop])
            result = result + up + down
        return result


def swapped(block, axis):
    return lax.ppermute(block, axis, [(0, 1), (1, 0)])


def chosen_swap(block, section):
    size = lax.axis_size("tensor")
    pairs = [(section * size + i, section * size + 1 - i) for i in range(size)]
    return lax.ppermute(block, ("section", "tensor"), pairs)


def body(
    x_input,
    teacher,
    segment_ids,
    valid_len,
    norm_gain,
    w_zx,
    w_bc,
    w_dt,
    conv_x,
    conv_bc,
    dt_bias,
    a_log,
    d_skip,
    gnorm_gain,
    w_out,
):
    local_rows, width = x_input.shape[1:]
    ranks = lax.axis_size("dp")
    core = lax.axis_index("section")
    turn = lax.axis_index("tensor")
    rank = lax.axis_index("dp")
    place = jnp.stack([rank % 2, turn, rank, core]).astype(jnp.int32)
    on_first = core == 0
    block_rows = w_zx.shape[1]
    half = w_zx.shape[3] // 2
    units = 2 * half
    heads_half = w_dt.shape[2] // 2
    scan_columns = half + 2 * STATE
    lines = []
    stride = ranks
    for size in factors_of(ranks // 2):
        stride //= size
        lines.append(Line(size, stride, ranks))

    def pick(pair, index):
        return lax.dynamic_index_in_dim(pair, index, 0, keepdims=False)

    def by_layer(kept, received):
        return jnp.where(on_first, kept, received), jnp.where(on_first, received, kept)

    def x_swapped(block):
        return lax.ppermute(block, "dp", [(i, i ^ 1) for i in range(ranks)])

    def y_swapped(block):
        return swapped(block, "tensor")

    pack_shape = (block_rows + PARAM_ROWS, scan_columns + units)
    heads = jnp.pad(jnp.concatenate([dt_bias, a_log, d_skip]), ((0, 5), (0, LANES - dt_bias.shape[1])))
    kept, sent = plain_call(
        pack_kernel,
        place,
        (w_zx[0].reshape(block_rows, -1), w_bc[0], w_dt[0], norm_gain, w_out[0].T, conv_x[0], gnorm_gain, conv_bc[0], heads),
        [(pack_shape, bf16)] * 2,
    )
    received = swapped(sent, "section")
    scan_block, middle_block, gate_block, out_block, params_both, channels = plain_call(
        unpack_kernel,
        place,
        (kept, received),
        [
            ((block_rows, scan_columns), bf16),
            ((block_rows, units + scan_columns), bf16),
            ((block_rows, half), bf16),
            ((block_rows, half), bf16),
            ((2, PARAM_ROWS, scan_columns + LANES), bf16),
            ((2 * PARAM_ROWS, half), bf16),
        ],
    )

    def line_gather(block, widths):
        rows = block.shape[0]
        for line in lines[:0:-1]:
            block = line.gather(block, (block.shape[1],))[0].reshape(-1, block.shape[1])
        parts = lines[0].gather(block, widths)
        return [part.reshape(-1, rows, part.shape[-1]) for part in parts]

    def plane_start(left, right):
        return (left, x_swapped(left), y_swapped(left)), (right, x_swapped(right), y_swapped(right))

    def plane_end(lefts, rights):
        return lefts + (y_swapped(lefts[1]),), rights + (x_swapped(rights[2]),)

    def whole_rows(rows):
        quarter = local_rows // 2
        own = pick(rows, turn)
        away = lax.dynamic_slice_in_dim(pick(rows, 1 - turn), core * quarter, quarter, 0)
        here = y_swapped(away)
        beside = swapped(here, "section")
        first, second = jnp.where(on_first, here, beside), jnp.where(on_first, beside, here)
        other = jnp.concatenate([first, second], axis=0)
        return jnp.where(turn == 0, jnp.concatenate([own, other]), jnp.concatenate([other, own]))

    scan_line = line_gather(scan_block, (half, 2 * STATE))
    x_rows = whole_rows(x_input)
    spreader = spreader_of(units)
    channels = y_swapped(after(channels, scan_line[0]))
    params = plain_call(
        functools.partial(params_kernel, heads_half),
        place,
        (params_both, channels, spreader),
        [((8, units), f32), ((8, 2 * STATE), f32), ((8, LANES), f32)] * 2,
    )
    params = [params[:3], params[3:]]
    marks, segment_row = token_marks(place, valid_len, segment_ids[:, 0])

    scan_half = plane_start(*scan_line)
    plane = plane_end(*plane_start(after(gate_block, scan_line[0]), after(out_block, scan_line[0])))
    middle_line = line_gather(after(middle_block, scan_line[0]), (half, half, half, 2 * STATE))
    scan_weights = [sum(plane_end(*scan_half), ())]
    gate_half = plane_start(*[after(part, scan_weights[0][7]) for part in middle_line[:2]])
    gate_weights = [sum(plane_end(*gate_half), ())]
    scan_half = plane_start(*[after(part, gate_half[0][1]) for part in middle_line[2:]])
    scan_weights.append(sum(plane_end(*scan_half), ()))
    plane = jnp.concatenate(plane[0] + plane[1], axis=1)
    gate_weights.append(line_gather(after(plane, middle_line[0]), (half,) * 8))
    target = whole_rows(after(teacher, scan_weights[0][7]))

    _, gain_first, normed_first, saved_first = scan_forward(
        place, x_rows, None, scan_weights[0], marks, segment_row, params[0]
    )
    gate_first, part = gate_forward(place, normed_first, saved_first[2], gate_weights[0], params[0])
    parts_first = (part, swapped(part, "section"))
    hidden, gain_second, normed_second, saved_second = scan_forward(
        place, x_rows, parts_first, scan_weights[1], marks, segment_row, params[1]
    )
    gate_second, part = gate_forward(place, normed_second, saved_second[2], gate_weights[1], params[1])
    parts_second = (part, swapped(part, "section"))

    def add(*blocks):
        return sum(block.astype(f32) for block in blocks).astype(bf16)

    def reduce_start(left, right):
        return (left, y_swapped(left[3]), y_swapped(left[2])), (right, x_swapped(right[3]), x_swapped(right[1]))

    def reduce_end(lefts, rights):
        left, left_on, left_y = lefts
        right, right_on, right_x = rights
        left_x = x_swapped(add(left[1], left_on))
        right_y = y_swapped(add(right[2], right_on))
        return add(left[0], left_x, left_y), add(right[0], right_x, right_y)

    def line_reduce(*blocks):
        total = jnp.concatenate(blocks, axis=-1)
        columns = total.shape[-1]
        for line in lines:
            total = line.reduce(total.reshape(line.size, -1, columns))
        return total

    results = gate_backward(
        place, hidden, parts_second, (target,), normed_second, gate_second, saved_second[2], gate_weights[1], marks, params[1]
    )
    produced, grad_out, grad_y, gate_part = results[:4]
    gate_reduce = reduce_start(results[4:8], results[8:12])
    gate_sums_second = results[12]
    results = scan_backward(
        place, grad_y, gate_part, normed_second, scan_weights[1], marks, segment_row, params[1], saved_second
    )
    grad_parts = (results[8], swapped(results[8], "section"))
    sums_second = (gate_sums_second, results[9], results[10])
    scan_reduce = reduce_start(
        [after(block, grad_parts[1]) for block in results[:4]], [after(block, grad_parts[1]) for block in results[4:8]]
    )
    extra = (hidden, grad_out) + grad_parts + (gain_second,)
    results = gate_backward(
        place, x_rows, parts_first, extra, normed_first, gate_first, saved_first[2], gate_weights[0], marks, params[0]
    )
    _, grad_hidden, grad_y, gate_part = results[:4]
    blocks_second = reduce_end(*scan_reduce) + reduce_end(*gate_reduce)
    gate_reduce = reduce_start(results[4:8], results[8:12])
    gate_sums_first = results[12]
    results = scan_backward(
        place, grad_y, gate_part, normed_first, scan_weights[0], marks, segment_row, params[0], saved_first
    )
    sums_first = (gate_sums_first, results[9], results[10])
    scan_reduce = reduce_start(results[:4], results[4:8])
    owned_second = line_reduce(*blocks_second)
    grad_x, gain_sums = finish(results[8], swapped(results[8], "section"), x_rows, grad_hidden, gain_first)
    owned_first = line_reduce(*(reduce_end(*scan_reduce) + reduce_end(*gate_reduce)))

    def halves(rows):
        own = lax.dynamic_slice_in_dim(rows, turn * local_rows, local_rows, 0)
        away = lax.dynamic_slice_in_dim(rows, (1 - turn) * local_rows, local_rows, 0)
        return own, away

    def placed(own, received):
        return jnp.where(turn == 0, jnp.stack([own, received]), jnp.stack([received, own]))

    own, away = halves(jnp.where(on_first, hidden, produced))
    layer_outputs = placed(own, y_swapped(away))
    own_second, away = halves(grad_hidden)
    received_second = chosen_swap(away.astype(bf16), 1)
    own_first, away = halves(grad_x)
    received_first = chosen_swap(away.astype(bf16), 0)
    boundary = placed(
        jnp.where(on_first, own_first, own_second),
        jnp.where(on_first, received_first, received_second).astype(f32),
    )

    mine, others = by_layer(owned_first, owned_second)
    beside = swapped(others, "section").astype(f32)
    mine = mine.astype(f32)

    def both(start, size):
        here, there = mine[:, start : start + size], beside[:, start : start + size]
        return jnp.where(on_first, jnp.concatenate([here, there], 1), jnp.concatenate([there, here], 1))

    grad_zx = jnp.stack([both(scan_columns, half), both(0, half)], axis=1)
    bc_own = mine[:, half : half + STATE] + beside[:, half : half + STATE]
    bc_other = y_swapped(bc_own)
    grad_bc = jnp.where(turn == 0, jnp.concatenate([bc_own, bc_other], 1), jnp.concatenate([bc_other, bc_own], 1))
    grad_dt = both(half + STATE, heads_half)
    grad_out_w = jnp.transpose(both(scan_columns + half, half))

    def small_pack(sums):
        gate, scan, states = sums
        wide = jnp.pad(states, ((0, 0), (0, units - 2 * STATE)))
        return jnp.concatenate([scan[:5], gate[5:6], gate[7:8], jnp.zeros((1, units), f32), wide])

    first, second = small_pack(sums_first), small_pack(sums_second)
    mine, others = by_layer(first, second)
    there = swapped(others, "section")
    both_cores = jnp.concatenate([mine, there])
    away = y_swapped(both_cores)
    rows = mine.shape[0]
    here_sum = jnp.concatenate([mine[:, :half] + away[:rows, half:], there[:, :half] + away[rows:, half:]], axis=1)
    gain_total = jnp.where(on_first, gain_sums[0:1], first[6:7])
    gain_total = gain_total + y_swapped(gain_total)
    states_total = mine[8:, : 2 * STATE] + there[8:, : 2 * STATE]
    states_total = states_total + y_swapped(states_total)

    def own_heads(pack, others):
        lanes = jnp.stack([pack[14, :LANES], pack[13, :LANES], pack[13, STATE : STATE + LANES]])
        away = jnp.stack([others[14, :LANES], others[13, :LANES], others[13, STATE : STATE + LANES]])
        return lanes[:, :heads_half] + away[:, heads_half : 2 * heads_half]

    heads = jnp.concatenate([own_heads(mine, away[:rows]), own_heads(there, away[rows:])], axis=1)
    heads = jnp.pad(heads, ((0, 5), (0, units - heads.shape[1])))
    total = jnp.concatenate(
        [here_sum[:6], gain_total, jnp.zeros((1, units), f32), jnp.pad(states_total, ((0, 0), (0, units - 2 * STATE))), heads]
    )
    total = total + x_swapped(total)
    for line in lines:
        total = line.total_of(total)

    def in_order(rows, columns):
        here, there = rows[..., :columns], rows[..., columns : 2 * columns]
        return jnp.where(on_first, rows[..., : 2 * columns], jnp.concatenate([there, here], -1))

    channel_grads = in_order(total[:6], half)
    head_grads = in_order(total[16:19], heads_half)
    gain_own = lax.dynamic_slice_in_dim(total[6], rank * block_rows, block_rows)
    return (
        layer_outputs[None],
        boundary[None],
        gain_own[None],
        grad_zx[None],
        grad_bc[None],
        grad_dt[None],
        channel_grads[None, :5],
        total[None, 8:13, : 2 * STATE],
        head_grads[1][None],
        head_grads[2][None],
        head_grads[0][None],
        channel_grads[5][None],
        grad_out_w[None],
    )


def solution(mesh):
    placed = (
        P(None, ("dp", "tensor"), None),
        P(None, ("dp", "tensor"), None),
        P(None, "dp", None),
        P(),
        P("section", "dp"),
        P("section", "dp", None, "tensor"),
        P("section", "dp", None),
        P("section", "dp", "tensor"),
        P("section", None, "tensor"),
        P("section", None, None),
        P("section", None),
        P("section", None),
        P("section", None),
        P("section", "tensor"),
        P("section", "tensor", "dp"),
    )
    return jax.shard_map(
        body,
        mesh=mesh,
        in_specs=placed,
        out_specs=(
            P("section", None, ("dp", "tensor"), None),
            P("section", None, ("dp", "tensor"), None),
            P("section", "dp"),
            P("section", "dp", None, "tensor"),
            P("section", "dp", None),
            P("section", "dp", "tensor"),
            P("section", None, "tensor"),
            P("section", None, None),
            P("section", "tensor"),
            P("section", "tensor"),
            P("section", "tensor"),
            P("section", "tensor"),
            P("section", "tensor", "dp"),
        ),
        check_vma=False,
    )
```

```python
import functools

import jax
import jax.numpy as jnp
import numpy as np
from jax import lax
from jax.experimental import pallas as pl
from jax.experimental.pallas import tpu as pltpu
from jax.sharding import PartitionSpec as P

HEAD_DIM = 64
STATE = 128
SPAN = 256
LANES = 128

epsilon = 1e-05
f32 = jnp.float32
bf16 = jnp.bfloat16


def nn(left, right):
    return lax.dot_general(left, right, (((1,), (0,)), ((), ())), preferred_element_type=f32)


def nt(left, right):
    return lax.dot_general(left, right, (((1,), (1,)), ((), ())), preferred_element_type=f32)


def tn(left, right):
    return lax.dot_general(left, right, (((0,), (0,)), ((), ())), preferred_element_type=f32)


def high_low(value):
    high = value.astype(bf16)
    return high, (value - high.astype(f32)).astype(bf16)


def spread(per_head, spreader):
    return nn(jnp.concatenate(high_low(per_head), axis=1), spreader)


def gathered_heads(units, spreader):
    high, low = high_low(units)
    once = spreader[:LANES]
    return nt(high, once) + nt(low, once)


def running_sum(triangle, value):
    high = value.astype(bf16)
    rest = value - high.astype(f32)
    middle = rest.astype(bf16)
    low = (rest - middle.astype(f32)).astype(bf16)
    sums = nn(triangle, jnp.concatenate([high, middle, low], axis=1))
    return sums[:, :LANES] + sums[:, LANES : 2 * LANES] + sums[:, 2 * LANES :]


def softplus(value):
    return jnp.maximum(value, 0.0) + jnp.log1p(jnp.exp(-jnp.abs(value)))


def moved_down(block, edge, lag):
    return jnp.concatenate([edge, block], axis=0)[8 - lag : 8 - lag + block.shape[0]]


def moved_up(block, edge, lag):
    return jnp.concatenate([block, edge], axis=0)[lag : lag + block.shape[0]]


def decay_parts(steps_in, head_rows, marks, heads):
    lane = lax.broadcasted_iota(jnp.int32, (1, LANES), 1)
    live = lane < heads
    shifted = steps_in + head_rows[0:1, :LANES]
    steps = jnp.where(live, softplus(shifted), 0.0)
    rates = head_rows[1:2, :LANES]
    log_steps = -steps * rates
    row = lax.broadcasted_iota(jnp.int32, (SPAN, SPAN), 0)
    column = lax.broadcasted_iota(jnp.int32, (SPAN, SPAN), 1)
    lower = (row >= column).astype(bf16)
    logs = running_sum(lower, log_steps)
    last = logs[SPAN - 1 : SPAN]
    entry = jnp.exp(logs) * marks[:, 3:4]
    tail = jnp.exp(last - logs) * marks[:, 4:5]
    through = jnp.exp(last) * marks[SPAN - 1 : SPAN, 3:4]
    entry = jnp.where(live, entry, 0.0)
    tail = jnp.where(live, tail, 0.0)
    through = jnp.where(live, through, 0.0)
    return shifted, steps, log_steps, logs, entry, tail, through, row, column


def linked_mask(row, column, marks, segment_row):
    linked = (row >= column) & (marks[:, 5:6] == segment_row)
    return jnp.where(linked, 0.0, -1e30)


def branch_of(own_ref, other_ref, units):
    width = own_ref.shape[1] - LANES
    own = own_ref[...].astype(f32)
    other = other_ref[...].astype(f32)
    total = own[:, :width] + other[:, :width]
    own_squares = own[:, width : width + 1] + own[:, width + 1 : width + 2]
    other_squares = other[:, width : width + 1] + other[:, width + 1 : width + 2]
    inverse = lax.rsqrt((own_squares + other_squares) / (2 * units) + epsilon)
    return total * inverse, total, inverse


def pieces_of(rows, places):
    half = places // 2
    return ((False, False, 0, places), (True, False, 0, places), (False, True, 0, places), (True, True, 0, half), (True, True, half, places - half))


def load_weights(weights, start, refs, columns, rows, place_ref):
    first, last = columns
    places = weights.shape[0] // (2 * rows)
    mine = place_ref[0]
    size = refs[0].shape[1] // 4
    for index, (moved, turned, base, count) in enumerate(pieces_of(rows, places)):
        if len(refs) == 1:
            if index == 4:
                break
            ref, offset, base, count = refs[0], index * size, 0, places
        else:
            ref, offset = refs[index], 0
        place = 1 - mine if moved else mine
        target = start + (last - first if turned else 0)
        for step in range(count):
            row = pl.multiple_of((2 * (base + step) + place) * rows, 32)
            weights[pl.ds(row, rows), target : target + last - first] = ref[step * rows : (step + 1) * rows, offset + first : offset + last]


def store_grads(refs, columns, acc, start, rows, place_ref):
    first, last = columns
    mine = place_ref[0]
    for ref, (moved, turned, base, count) in zip(refs, pieces_of(rows, acc.shape[0] // (2 * rows))):
        place = 1 - mine if moved else mine
        source = start + (last - first if turned else 0)
        for step in range(count):
            row = pl.multiple_of((2 * (base + step) + place) * rows, 32)
            ref[step * rows : (step + 1) * rows, first:last] = acc[pl.ds(row, rows), source : source + last - first].astype(bf16)


def scan_forward_kernel(second, heads, rows, pieces, *refs):
    place_ref, refs = refs[0], refs[1:]
    if second:
        (h_ref, own_ref, other_ref), refs = refs[:3], refs[3:]
    else:
        (h_ref,), refs = refs[:1], refs[1:]
    parts, refs = refs[:pieces], refs[pieces:]
    (marks_ref, segment_ref, small_ref, states_small_ref, head_ref, spread_ref), refs = refs[:6], refs[6:]
    if second:
        h_out, refs = refs[0], refs[1:]
    gain_ref, refs = refs[0], refs[1:]
    normed_ref, raw_ref, conv_ref, y_ref, raw_states_ref, conv_states_ref, steps_ref, entry_state_ref = refs[:8]
    state, raw_edge, states_edge, gain, weights = refs[8:]
    units = raw_ref.shape[1]

    @pl.when(pl.program_id(0) == 0)
    def _():
        state[...] = jnp.zeros_like(state)
        raw_edge[...] = jnp.zeros_like(raw_edge)
        states_edge[...] = jnp.zeros_like(states_edge)
        load_weights(weights, 0, parts, (0, units // 2), rows, place_ref)
        load_weights(weights, units, parts, (units // 2, units // 2 + 2 * STATE), rows, place_ref)
        steps_columns = weights[:, units + STATE : units + STATE + LANES].astype(f32)
        gain[...] = jnp.broadcast_to(jnp.transpose(steps_columns)[LANES // 2 : LANES // 2 + 1, :], gain.shape)
        gain_ref[...] = gain[...]

    hidden = h_ref[...].astype(f32)
    if second:
        rounded = (hidden + branch_of(own_ref, other_ref, units)[0]).astype(bf16)
        h_out[...] = rounded
        hidden = rounded.astype(f32)
    scale = lax.rsqrt(jnp.mean(hidden * hidden, axis=1, keepdims=True) + epsilon)
    normed = (hidden * scale * gain[0:1, :]).astype(bf16)
    normed_ref[...] = normed
    projected = nn(normed, weights[...])
    raw = projected[:, :units]
    first, second_part = projected[:, units : units + 2 * STATE], projected[:, units + 2 * STATE :]
    marks = marks_ref[...]
    turned = marks[0:1, 10:11] > 0.5
    raw_states = jnp.concatenate(
        [
            jnp.where(turned, second_part[:, :STATE], first[:, :STATE]),
            jnp.where(turned, first[:, :STATE], second_part[:, :STATE]),
        ],
        axis=1,
    )
    lane = lax.broadcasted_iota(jnp.int32, (1, LANES), 1)
    steps_in = jnp.where(lane < heads // 2, first[:, STATE:], pltpu.roll(second_part[:, STATE:], heads // 2, 1))
    raw_ref[...] = raw
    raw_states_ref[...] = raw_states
    steps_ref[...] = steps_in

    def conv(block, edge, taps):
        total = taps[4:5] + taps[3:4] * block
        for lag in (1, 2, 3):
            total = total + taps[3 - lag : 4 - lag] * (moved_down(block, edge, lag) * marks[:, lag - 1 : lag])
        return total

    taps = small_ref[...]
    conved = conv(raw, raw_edge[...], taps)
    conv_ref[...] = conved
    conved_states = conv(raw_states, states_edge[...], states_small_ref[...])
    conv_states_ref[...] = conved_states
    raw_edge[...] = raw[SPAN - 8 :]
    states_edge[...] = raw_states[SPAN - 8 :]
    values = conved * jax.nn.sigmoid(conved)
    states_in = conved_states * jax.nn.sigmoid(conved_states)
    b_rows = states_in[:, :STATE].astype(bf16)
    c_rows = states_in[:, STATE:].astype(bf16)
    _, steps, _, logs, entry, tail, through, row, column = decay_parts(steps_in, head_ref[...], marks, heads)
    spreader = spread_ref[...]
    scaled = values * spread(steps, spreader)
    mask = linked_mask(row, column, marks, segment_ref[...])
    scores = nt(c_rows, b_rows)
    logs_across = jnp.transpose(logs)
    pieces = []
    for pair in range(heads // 2):
        mixes = []
        for head in (2 * pair, 2 * pair + 1):
            factor = jnp.exp(logs[:, head : head + 1] - logs_across[head : head + 1, :] + mask)
            mixes.append((factor * scores).astype(bf16))
        block = scaled[:, pair * LANES : (pair + 1) * LANES]
        left = jnp.where(lane < HEAD_DIM, block, 0.0).astype(bf16)
        right = jnp.where(lane < HEAD_DIM, 0.0, block).astype(bf16)
        pieces.append(nn(jnp.concatenate(mixes, axis=1), jnp.concatenate([left, right], axis=0)))
    inside = jnp.concatenate(pieces, axis=1)
    held = state[...]
    entry_state_ref[0] = held
    across = nn(c_rows, held.astype(bf16)) * spread(entry, spreader)
    through_row = spread(jnp.broadcast_to(through, (8, LANES)), spreader)[0:1]
    state[...] = through_row * held + tn(b_rows, (spread(tail, spreader) * scaled).astype(bf16))
    y_ref[...] = inside + across + taps[6:7] * values


def gate_forward_kernel(rows, pieces, place_ref, normed_ref, y_ref, *refs):
    parts, refs = refs[:pieces], refs[pieces:]
    small_ref, gate_ref, part_ref, weights, out_weights = refs

    @pl.when(pl.program_id(0) == 0)
    def _():
        half = weights.shape[1] // 2
        load_weights(weights, 0, parts, (0, half), rows, place_ref)
        load_weights(out_weights, 0, parts, (half, 2 * half), rows, place_ref)

    gate = nn(normed_ref[...], weights[...])
    gate_ref[...] = gate
    gated = y_ref[...] * (gate * jax.nn.sigmoid(gate))
    squares = jnp.sum(gated * gated, axis=1, keepdims=True)
    part = nt((gated * small_ref[5:6]).astype(bf16), out_weights[...])
    width = part.shape[1]
    part_ref[:, :width] = part.astype(bf16)
    high, low = high_low(squares)
    lane = lax.broadcasted_iota(jnp.int32, (1, LANES), 1)
    part_ref[:, width:] = jnp.where(lane == 0, high, jnp.where(lane == 1, low, jnp.zeros_like(low)))


def gate_backward_kernel(second, rows, pieces, *refs):
    place_ref, refs = refs[0], refs[1:]
    if second:
        (h_ref, own_ref, other_ref, target_ref), refs = refs[:4], refs[4:]
    else:
        (own_ref, other_ref, next_h_ref, next_out_ref, grad_own_ref, grad_other_ref, next_gain_ref), refs = refs[:7], refs[7:]
    (normed_ref, gate_ref, y_ref), parts, refs = refs[:3], refs[3 : 3 + pieces], refs[3 + pieces :]
    (marks_ref, small_ref), refs = refs[:2], refs[2:]
    if second:
        out_ref, refs = refs[0], refs[1:]
    (grad_out_ref, grad_y_ref, part_ref), grads, sums_ref, refs = refs[:3], refs[3:8], refs[8], refs[9:]
    weights, out_weights, acc_z, acc_o, sums = refs
    units = y_ref.shape[1]

    @pl.when(pl.program_id(0) == 0)
    def _():
        load_weights(weights, 0, parts, (0, units // 2), rows, place_ref)
        load_weights(out_weights, 0, parts, (units // 2, units), rows, place_ref)
        for ref in (acc_z, acc_o, sums):
            ref[...] = jnp.zeros_like(ref)

    branch, total, inverse = branch_of(own_ref, other_ref, units)
    if second:
        produced = h_ref[...].astype(f32) + branch
        out_ref[...] = jnp.where(place_ref[3] == 0, h_ref[...].astype(f32), produced).astype(bf16)
        grad_out = marks_ref[:, 9:10] * (produced - target_ref[...])
    else:
        grad_normed = grad_own_ref[...].astype(f32) + grad_other_ref[...].astype(f32)
        grad_out, gain_term = norm_backward(grad_normed, next_h_ref[...].astype(f32), next_out_ref[...], next_gain_ref[0:1, :])
        sums[7:8, :] += jnp.sum(gain_term, axis=0, keepdims=True)
    grad_out_ref[...] = grad_out
    grad = grad_out.astype(bf16)
    inner = jnp.sum(grad.astype(f32) * total, axis=1, keepdims=True) * (inverse * inverse * inverse) / (2 * units)
    gain = small_ref[5:6]
    gate = gate_ref[...]
    y = y_ref[...]
    gate_sig = jax.nn.sigmoid(gate)
    gate_silu = gate * gate_sig
    gated = y * gate_silu
    gated_unit = gated * inverse
    grad_mixed = nn(grad, out_weights[...])
    acc_o[...] += tn(grad, (gated_unit * gain).astype(bf16))
    sums[5:6, :] += jnp.sum(grad_mixed * gated_unit, axis=0, keepdims=True)
    grad_gated = grad_mixed * gain * inverse - gated * inner
    grad_gate = (grad_gated * y * (gate_sig * (1.0 + gate * (1.0 - gate_sig)))).astype(bf16)
    grad_y_ref[...] = (grad_gated * gate_silu).astype(bf16)
    acc_z[...] += tn(normed_ref[...], grad_gate)
    part_ref[...] = nt(grad_gate, weights[...])

    @pl.when(pl.program_id(0) == pl.num_programs(0) - 1)
    def _():
        store_grads(grads, (0, units // 2), acc_z, 0, rows, place_ref)
        store_grads(grads, (units // 2, units), acc_o, 0, rows, place_ref)
        sums_ref[...] = sums[...]


def scan_backward_kernel(heads, rows, pieces, *refs):
    (place_ref, grad_y_ref, gate_part_ref), parts, refs = refs[:3], refs[3 : 3 + pieces], refs[3 + pieces :]
    (marks_ref, segment_ref, small_ref, states_small_ref, head_ref, spread_ref), refs = refs[:6], refs[6:]
    (raw_ref, conv_ref, y_ref, raw_states_ref, conv_states_ref, steps_ref, entry_state_ref), refs = refs[:7], refs[7:]
    (grads_ref, part_ref, sums_ref, states_sums_ref), refs = refs[:4], refs[4:]
    weights, dstate, next_state, conv_edge, states_edge, sums, states_sums = refs
    step = pl.program_id(0)
    units = raw_ref.shape[1]

    @pl.when(step == 0)
    def _():
        for ref in (dstate, next_state, conv_edge, states_edge, sums, states_sums):
            ref[...] = jnp.zeros_like(ref)
        load_weights(weights, 0, parts, (0, units // 2), rows, place_ref)
        load_weights(weights, units, parts, (units // 2, units // 2 + 2 * STATE), rows, place_ref)

    marks = marks_ref[...]
    taps = small_ref[...]
    y = y_ref[...]
    grad_y_low = grad_y_ref[...]
    grad_y = grad_y_low.astype(f32)
    conved = conv_ref[...]
    value_sig = jax.nn.sigmoid(conved)
    values = conved * value_sig
    conved_states = conv_states_ref[...]
    states_sig = jax.nn.sigmoid(conved_states)
    states_in = conved_states * states_sig
    b_rows = states_in[:, :STATE].astype(bf16)
    c_rows = states_in[:, STATE:].astype(bf16)
    shifted, steps, log_steps, logs, entry, tail, through, row, column = decay_parts(steps_ref[...], head_ref[...], marks, heads)
    spreader = spread_ref[...]
    spread_steps = spread(steps, spreader)
    spread_entry = spread(entry, spreader)
    spread_tail = spread(tail, spreader)
    through_row = spread(jnp.broadcast_to(through, (8, LANES)), spreader)[0:1]
    scaled_low = (values * spread_steps).astype(bf16)
    scaled = scaled_low.astype(f32)
    mask = linked_mask(row, column, marks, segment_ref[...])
    scores = nt(c_rows, b_rows)
    logs_across = jnp.transpose(logs)
    lane = lax.broadcasted_iota(jnp.int32, (1, LANES), 1)
    is_left = lane < HEAD_DIM
    zero = jnp.zeros((), bf16)
    grad_scores = jnp.zeros((SPAN, SPAN), f32)
    pieces = []
    for pair in range(heads // 2):
        columns = slice(pair * LANES, (pair + 1) * LANES)
        block, grad = scaled_low[:, columns], grad_y_low[:, columns]
        grad_left = jnp.where(is_left, grad, zero)
        grad_right = jnp.where(is_left, zero, grad)
        mixes = []
        for head, grad_one in ((2 * pair, grad_left), (2 * pair + 1, grad_right)):
            factor = jnp.exp(logs[:, head : head + 1] - logs_across[head : head + 1, :] + mask)
            mixes.append((factor * scores).astype(bf16))
            grad_scores = grad_scores + nt(grad_one, block) * factor
        pieces.append(tn(jnp.concatenate(mixes, axis=0), jnp.concatenate([grad_left, grad_right], axis=0)))
    held = entry_state_ref[0]
    held_low = held.astype(bf16)
    gradient = dstate[...]
    gradient_low = gradient.astype(bf16)
    grad_scaled = jnp.concatenate(pieces, axis=1) + spread_tail * nn(b_rows, gradient_low)
    grad_entry = (spread_entry * grad_y).astype(bf16)
    grad_scores_low = grad_scores.astype(bf16)
    grad_c = nn(grad_scores_low, b_rows) + nt(grad_entry, held_low)
    grad_b = tn(grad_scores_low, c_rows) + nt((spread_tail * scaled).astype(bf16), gradient_low)
    state_term = jnp.sum(gradient * next_state[...], axis=0, keepdims=True)
    dstate[...] = through_row * gradient + tn(c_rows, grad_entry)
    next_state[...] = held
    skip = taps[6:7]
    sums[6:7, :] += jnp.sum(grad_y * values, axis=0, keepdims=True)
    grad_logs = gathered_heads(grad_y * (y - skip * values) - scaled * grad_scaled, spreader)
    state_heads = gathered_heads(jnp.broadcast_to(state_term, (8, units)), spreader)[0:1]
    last_row = lax.broadcasted_iota(jnp.int32, (SPAN, 1), 0) == SPAN - 1
    grad_logs = grad_logs + jnp.where(last_row, state_heads, 0.0)
    grad_log_steps = running_sum((row <= column).astype(bf16), grad_logs)
    grad_steps = gathered_heads(grad_scaled * values, spreader) - head_ref[1:2, :LANES] * grad_log_steps
    grad_steps_in = jnp.where(lane < heads, grad_steps * jax.nn.sigmoid(shifted), 0.0)
    states_sums[5:6, :] += jnp.concatenate(
        [
            jnp.sum(grad_steps_in, axis=0, keepdims=True),
            jnp.sum(grad_log_steps * log_steps, axis=0, keepdims=True),
        ],
        axis=1,
    )
    grad_values = grad_scaled * spread_steps + skip * grad_y
    grad_conved = grad_values * (value_sig * (1.0 + conved * (1.0 - value_sig)))
    grad_states = jnp.concatenate([grad_b, grad_c], axis=1)
    grad_conved_states = grad_states * (states_sig * (1.0 + conved_states * (1.0 - states_sig)))

    def conv_backward(block, edge, tap_rows, raw, total_ref):
        result = tap_rows[3:4] * block
        total_ref[3:4, :] += jnp.sum(block * raw, axis=0, keepdims=True)
        total_ref[4:5, :] += jnp.sum(block, axis=0, keepdims=True)
        for lag in (1, 2, 3):
            term = moved_up(block, edge, lag) * marks[:, 5 + lag : 6 + lag]
            result = result + tap_rows[3 - lag : 4 - lag] * term
            total_ref[3 - lag : 4 - lag, :] += jnp.sum(term * raw, axis=0, keepdims=True)
        return result

    grad_raw = conv_backward(grad_conved, conv_edge[...], taps, raw_ref[...], sums)
    grad_raw_states = conv_backward(
        grad_conved_states, states_edge[...], states_small_ref[...], raw_states_ref[...], states_sums
    )
    conv_edge[...] = grad_conved[:8]
    states_edge[...] = grad_conved_states[:8]
    turned = marks[0:1, 10:11] > 0.5
    first_states = jnp.where(turned, grad_raw_states[:, STATE:], grad_raw_states[:, :STATE])
    second_states = jnp.where(turned, grad_raw_states[:, :STATE], grad_raw_states[:, STATE:])
    own_steps = jnp.where(lane < heads // 2, grad_steps_in, 0.0)
    other_steps = jnp.where(lane < heads // 2, pltpu.roll(grad_steps_in, LANES - heads // 2, 1), 0.0)
    grads = jnp.concatenate([grad_raw, first_states, own_steps, second_states, other_steps], axis=1).astype(bf16)
    grads_ref[...] = grads
    part_ref[...] = (nt(grads, weights[...]) + gate_part_ref[...]).astype(bf16)

    @pl.when(step == pl.num_programs(0) - 1)
    def _():
        skips = gathered_heads(sums[...], spreader)[6:7]
        states_sums[6:7, :] = jnp.concatenate([skips, jnp.zeros_like(skips)], axis=1)
        sums_ref[...] = sums[...]
        states_sums_ref[...] = states_sums[...]


def weight_grads_kernel(rows, place_ref, normed_ref, grads_ref, *refs):
    outs, acc = refs[-6:-1], refs[-1]
    units = acc.shape[1] - 4 * STATE

    @pl.when(pl.program_id(0) == 0)
    def _():
        acc[...] = jnp.zeros_like(acc)

    acc[...] += tn(normed_ref[...], grads_ref[...])

    @pl.when(pl.program_id(0) == pl.num_programs(0) - 1)
    def _():
        store_grads(outs, (0, units // 2), acc, 0, rows, place_ref)
        store_grads(outs, (units // 2, units // 2 + 2 * STATE), acc, units, rows, place_ref)


def norm_backward(grad_normed, hidden, grad_out, gain):
    scale = lax.rsqrt(jnp.mean(hidden * hidden, axis=1, keepdims=True) + epsilon)
    weighted = grad_normed * gain
    shared = jnp.mean(weighted * hidden, axis=1, keepdims=True) * (scale * scale * scale)
    return grad_out + scale * weighted - hidden * shared, grad_normed * hidden * scale


VMEM_LIMIT = 60 * 1024 * 1024


def spreader_of(units):
    one = (np.arange(LANES)[:, None] == np.arange(units)[None, :] // HEAD_DIM).astype(np.float32)
    return jnp.asarray(np.concatenate([one, one], axis=0), bf16)


def rows_spec(width, last=None):
    if last is None:
        return pl.BlockSpec((SPAN, width), lambda i: (i, 0))
    return pl.BlockSpec((SPAN, width), lambda i: (last - i, 0))


def whole_spec(array):
    return pl.BlockSpec(array.shape, lambda i: (0,) * array.ndim)


def call(kernel, inputs, outputs, scratch, chunks, flops):
    return pl.pallas_call(
        kernel,
        grid=(chunks,),
        in_specs=[spec for _, spec in inputs],
        out_specs=[spec for _, _, spec in outputs],
        out_shape=[jax.ShapeDtypeStruct(shape, dtype) for shape, dtype, _ in outputs],
        scratch_shapes=[pltpu.VMEM(shape, dtype) for shape, dtype in scratch],
        compiler_params=pltpu.CompilerParams(vmem_limit_bytes=VMEM_LIMIT, dimension_semantics=("arbitrary",)),
        cost_estimate=pl.CostEstimate(flops=flops, bytes_accessed=500_000, transcendentals=0),
    )(*[array for array, _ in inputs])


def fixed(array):
    return array, whole_spec(array)


def scalars(array):
    return array, pl.BlockSpec(memory_space=pltpu.SMEM)


def grad_outputs(width, rows, columns):
    outputs = []
    for _, _, _, count in pieces_of(rows, width // (2 * rows)):
        shape = (count * rows, columns)
        outputs.append((shape, bf16, pl.BlockSpec(shape, lambda i: (0, 0))))
    return outputs


def awaited(arrays):
    return [(array, pl.BlockSpec(memory_space=pl.ANY)) for array in arrays]


def scan_forward(place, rows, h, parts, weights, marks, segment_row, params):
    length, width = h.shape
    units = params[0].shape[1]
    chunks = length // SPAN
    second = parts is not None
    inputs = [scalars(place), (h, rows_spec(width))]
    outputs = []
    if second:
        inputs += [(part, rows_spec(width + LANES)) for part in parts]
        outputs.append(((length, width), bf16, rows_spec(width)))
    inputs += [fixed(w) for w in weights]
    inputs += [(marks, rows_spec(LANES)), (segment_row, pl.BlockSpec((1, SPAN), lambda i: (0, i)))]
    inputs += [fixed(p) for p in params] + [fixed(spreader_of(units))]
    outputs.append(((8, width), f32, pl.BlockSpec((8, width), lambda i: (0, 0))))
    outputs.append(((length, width), bf16, rows_spec(width)))
    for columns in (units, units, units, 2 * STATE, 2 * STATE, LANES):
        outputs.append(((length, columns), f32, rows_spec(columns)))
    outputs.append(((chunks, STATE, units), f32, pl.BlockSpec((1, STATE, units), lambda i: (i, 0, 0))))
    scratch = [
        ((STATE, units), f32),
        ((8, units), f32),
        ((8, 2 * STATE), f32),
        ((8, width), f32),
        ((width, units + 4 * STATE), bf16),
    ]
    kernel = functools.partial(scan_forward_kernel, second, units // HEAD_DIM, rows, len(weights))
    results = call(kernel, inputs, outputs, scratch, chunks, 2_000_000_000)
    if not second:
        results = [h] + list(results)
    return results[0], results[1], results[2], results[3:]


def gate_forward(place, rows, normed, y, weights, params):
    length, width = normed.shape
    units = params[0].shape[1]
    inputs = [scalars(place), (normed, rows_spec(width)), (y, rows_spec(units))] + [fixed(w) for w in weights] + [fixed(params[0])]
    outputs = [((length, units), f32, rows_spec(units)), ((length, width + LANES), bf16, rows_spec(width + LANES))]
    scratch = [((width, units), bf16)] * 2
    return call(functools.partial(gate_forward_kernel, rows, len(weights)), inputs, outputs, scratch, length // SPAN, 1_000_000_000)


def gate_backward(place, rows, h, parts, extra, normed, gate, y, weights, marks, params):
    length, width = normed.shape
    units = params[0].shape[1]
    second = len(extra) == 1
    inputs = [scalars(place)] + ([(h, rows_spec(width))] if second else [])
    inputs += [(part, rows_spec(width + LANES)) for part in parts]
    inputs += [(array, rows_spec(width)) for array in extra[:4]] + [fixed(gain) for gain in extra[4:]]
    inputs += [(normed, rows_spec(width)), (gate, rows_spec(units)), (y, rows_spec(units))]
    inputs += [fixed(w) for w in weights] + [(marks, rows_spec(LANES)), fixed(params[0])]
    outputs = [((length, width), bf16, rows_spec(width))] if second else []
    outputs += [((length, width), f32, rows_spec(width)), ((length, units), bf16, rows_spec(units)), ((length, width), f32, rows_spec(width))]
    outputs += grad_outputs(width, rows, units)
    outputs.append(((8, units), f32, pl.BlockSpec((8, units), lambda i: (0, 0))))
    scratch = [((width, units), bf16)] * 2 + [((width, units), f32)] * 2 + [((8, units), f32)]
    results = call(functools.partial(gate_backward_kernel, second, rows, len(weights)), inputs, outputs, scratch, length // SPAN, 2_000_000_000)
    if not second:
        results = [None] + list(results)
    return results


def scan_backward(place, rows, grad_y, gate_part, weights, marks, segment_row, params, saved):
    length, width = gate_part.shape
    units = params[0].shape[1]
    chunks = length // SPAN
    last = chunks - 1
    inputs = [scalars(place), (grad_y, rows_spec(units, last)), (gate_part, rows_spec(width, last))]
    inputs += [fixed(w) for w in weights]
    inputs += [(marks, rows_spec(LANES, last)), (segment_row, pl.BlockSpec((1, SPAN), lambda i: (0, last - i)))]
    inputs += [fixed(p) for p in params] + [fixed(spreader_of(units))]
    inputs += [(s, rows_spec(s.shape[1], last)) for s in saved[:6]]
    inputs.append((saved[6], pl.BlockSpec((1, STATE, units), lambda i: (last - i, 0, 0))))
    columns = units + 4 * STATE
    outputs = [((length, columns), bf16, rows_spec(columns, last)), ((length, width), bf16, rows_spec(width, last))]
    for columns in (units, 2 * STATE):
        outputs.append(((8, columns), f32, pl.BlockSpec((8, columns), lambda i: (0, 0))))
    scratch = [
        ((width, units + 4 * STATE), bf16),
        ((STATE, units), f32),
        ((STATE, units), f32),
        ((8, units), f32),
        ((8, 2 * STATE), f32),
        ((8, units), f32),
        ((8, 2 * STATE), f32),
    ]
    kernel = functools.partial(scan_backward_kernel, units // HEAD_DIM, rows, len(weights))
    return call(kernel, inputs, outputs, scratch, chunks, 3_000_000_000)


def weight_grads(place, rows, normed, grads, ready):
    length, width = normed.shape
    columns = grads.shape[1]
    inputs = [scalars(place), (normed, rows_spec(width)), (grads, rows_spec(columns))] + awaited(ready)
    outputs = grad_outputs(width, rows, columns // 2)
    scratch = [((width, columns), f32)]
    return call(functools.partial(weight_grads_kernel, rows), inputs, outputs, scratch, length // SPAN, 500_000_000)


def finish_kernel(place_ref, own_ref, other_ref, h_ref, grad_out_ref, gain_ref, *refs):
    grad_ref, low_ref, sums_ref, sums = refs[-4:]

    @pl.when(pl.program_id(0) == 0)
    def _():
        sums[...] = jnp.zeros_like(sums)

    grad_normed = own_ref[...].astype(f32) + other_ref[...].astype(f32)
    next_grad = grad_out_ref[...]
    grad, gain_term = norm_backward(grad_normed, h_ref[...].astype(f32), next_grad.astype(bf16).astype(f32), gain_ref[0:1, :])
    rows = jnp.where(place_ref[3] == 0, grad, next_grad)
    grad_ref[...] = rows
    low_ref[...] = rows.astype(bf16)
    sums[0:1, :] += jnp.sum(gain_term, axis=0, keepdims=True)
    sums_ref[...] = sums[...]


def finish(place, own, other, h, grad_out, gain, ready):
    length, width = h.shape
    inputs = [scalars(place)] + [(rows, rows_spec(width)) for rows in (own, other, h, grad_out)] + [fixed(gain)]
    inputs += awaited(ready)
    outputs = [((length, width), f32, rows_spec(width)), ((length, width), bf16, rows_spec(width))]
    outputs.append(((8, width), f32, pl.BlockSpec((8, width), lambda i: (0, 0))))
    return call(finish_kernel, inputs, outputs, [((8, width), f32)], length // SPAN, 30_000_000)


def placed_kernel(place_ref, own_ref, away_ref, *refs):
    out_ref = refs[-1]
    own = pl.program_id(0) == place_ref[1]
    out_ref[0] = jnp.where(own, own_ref[...].astype(f32), away_ref[...].astype(f32)).astype(out_ref.dtype)


def placed_rows(place, rows, away, ready=()):
    half, width = away.shape
    return pl.pallas_call(
        placed_kernel,
        grid_spec=pltpu.PrefetchScalarGridSpec(
            num_scalar_prefetch=1,
            grid=(2,),
            in_specs=[
                pl.BlockSpec((half, width), lambda m, place: (place[1], 0)),
                pl.BlockSpec((half, width), lambda m, place: (0, 0)),
            ]
            + [pl.BlockSpec(memory_space=pl.ANY)] * len(ready),
            out_specs=pl.BlockSpec((1, half, width), lambda m, place: (m, 0, 0)),
        ),
        out_shape=jax.ShapeDtypeStruct((2, half, width), rows.dtype),
        compiler_params=pltpu.CompilerParams(vmem_limit_bytes=VMEM_LIMIT, dimension_semantics=("arbitrary",)),
        cost_estimate=pl.CostEstimate(flops=0, bytes_accessed=500_000, transcendentals=0),
    )(place, rows, away, *ready)


def marks_kernel(place_ref, lengths_ref, segments_ref, marks_ref, row_ref):
    turn, rank = place_ref[1], place_ref[2]
    micro, sequences = lengths_ref.shape
    length = segments_ref.shape[1]
    total = jnp.int32(0)
    for batch in range(micro):
        total = lax.fori_loop(0, sequences, lambda i, t: t + lengths_ref[batch, i], total)
    weight = 2.0 * (micro * sequences * length) / jnp.full((1, length), total, jnp.int32).astype(f32)
    position = lax.broadcasted_iota(jnp.int32, (1, length), 1)
    segment = jnp.where(turn == 0, segments_ref[0:1, :], segments_ref[1:2, :])
    wide = jnp.broadcast_to(segment, (8, length))

    def same(lag):
        moved = pltpu.roll(wide, lag % length, 1)[0:1]
        inside = (position >= lag) & (position < length + lag)
        return jnp.where(inside & (moved == segment), 1.0, 0.0)

    before = jnp.full((1, length), -1, jnp.int32)
    end = before
    for block in range(length // SPAN):
        here = (position >= block * SPAN) & (position < (block + 1) * SPAN)
        end = jnp.where(here, segment[:, (block + 1) * SPAN - 1 : (block + 1) * SPAN], end)
        if block:
            before = jnp.where(here, segment[:, block * SPAN - 1 : block * SPAN], before)
    as_float = segment.astype(f32)
    rows = [same(1), same(2), same(3)]
    rows += [jnp.where(segment == before, 1.0, 0.0), jnp.where(segment == end, 1.0, 0.0), as_float]
    rows += [same(-1), same(-2), same(-3)]
    rows += [jnp.where(position < lengths_ref[turn, rank], weight, 0.0), jnp.full((1, length), turn, jnp.int32).astype(f32)]
    rows.append(jnp.zeros((LANES - len(rows), length), f32))
    marks_ref[...] = jnp.transpose(jnp.concatenate(rows, axis=0))
    row_ref[...] = as_float


def token_marks(place, lengths, segments):
    length = segments.shape[1]
    return pl.pallas_call(
        marks_kernel,
        in_specs=[pl.BlockSpec(memory_space=pltpu.SMEM)] * 2 + [pl.BlockSpec(memory_space=pltpu.VMEM)],
        out_shape=[jax.ShapeDtypeStruct((length, LANES), f32), jax.ShapeDtypeStruct((1, length), f32)],
        compiler_params=pltpu.CompilerParams(vmem_limit_bytes=VMEM_LIMIT),
        cost_estimate=pl.CostEstimate(flops=0, bytes_accessed=500_000, transcendentals=0),
    )(place, lengths, segments)


def three_parts(value):
    high = value.astype(bf16)
    rest = value - high.astype(f32)
    middle = rest.astype(bf16)
    return high, middle, (rest - middle.astype(f32)).astype(bf16)


PARAM_ROWS = 16


def pack_kernel(
    place_ref, zx_ref, bc_ref, dt_ref, gain_ref, out_ref, conv_ref, gate_gain_ref, states_conv_ref, bias_ref, rate_ref, skip_ref, kept_ref, sent_ref
):
    turn, core = place_ref[1], place_ref[3]
    rows = zx_ref.shape[0]
    half = zx_ref.shape[2] // 2
    heads_half = dt_ref.shape[0] // 2
    lane = lax.broadcasted_iota(jnp.int32, (1, LANES), 1)
    bc = jnp.where(turn == 0, bc_ref[:, :STATE], bc_ref[:, STATE:])
    diagonal = lax.broadcasted_iota(jnp.int32, (rows, rows), 0) == lax.broadcasted_iota(jnp.int32, (rows, rows), 1)
    gain = jnp.sum(jnp.where(diagonal, gain_ref[...].astype(f32), 0.0), axis=1, keepdims=True)
    head = lax.broadcasted_iota(jnp.int32, (2 * heads_half, LANES), 0)
    column = lax.broadcasted_iota(jnp.int32, (2 * heads_half, LANES), 1)
    shared = jnp.concatenate([states_conv_ref[...], jnp.zeros((PARAM_ROWS - 5, 2 * STATE), bf16)], axis=0)
    split = [part.astype(f32) for ref in (bias_ref, rate_ref, skip_ref) for part in three_parts(ref[...])]
    heads = jnp.concatenate(split + [jnp.zeros((PARAM_ROWS - 9, split[0].shape[1]), f32)], axis=0)
    heads = jnp.concatenate([heads, jnp.zeros((PARAM_ROWS, LANES - heads.shape[1]), f32)], axis=1).astype(bf16)
    for ref, part in ((kept_ref, core), (sent_ref, 1 - core)):
        first = part == 0

        def chosen(array, start):
            return jnp.where(first, array[:, start : start + half], array[:, start + half : start + 2 * half])

        ref[:rows, :half] = chosen(zx_ref[:, 1, :], 0)
        ref[:rows, half : half + STATE] = bc
        taken = (head == column + part * heads_half) & (column < heads_half)
        own_steps = tn(dt_ref[...], jnp.where(taken, 1.0, 0.0).astype(bf16))
        ref[:rows, half + STATE : half + 2 * STATE] = jnp.where(lane == LANES // 2, gain, own_steps).astype(bf16)
        ref[:rows, half + 2 * STATE : 2 * half + 2 * STATE] = chosen(zx_ref[:, 0, :], 0)
        ref[:rows, 2 * half + 2 * STATE :] = chosen(out_ref, 0)
        ref[rows:, :] = jnp.zeros((PARAM_ROWS, ref.shape[1]), bf16)
        channels = jnp.concatenate([chosen(conv_ref, 0), chosen(gate_gain_ref, 0)], axis=0)
        ref[rows:, :half] = jnp.concatenate([channels, jnp.zeros((PARAM_ROWS - 6, half), bf16)], axis=0)
        ref[rows:, half : half + 2 * STATE] = shared
        ref[rows:, half + 2 * STATE : half + 2 * STATE + LANES] = heads


def plain_call(kernel, place, inputs, outputs, ready=()):
    count = len(ready)
    body = kernel if not count else lambda place_ref, *refs: kernel(place_ref, *refs[count:])
    return pl.pallas_call(
        body,
        in_specs=[pl.BlockSpec(memory_space=pltpu.SMEM)]
        + [pl.BlockSpec(memory_space=pl.ANY)] * count
        + [pl.BlockSpec(memory_space=pltpu.VMEM)] * len(inputs),
        out_shape=[jax.ShapeDtypeStruct(shape, dtype) for shape, dtype in outputs],
        compiler_params=pltpu.CompilerParams(vmem_limit_bytes=VMEM_LIMIT),
        cost_estimate=pl.CostEstimate(flops=0, bytes_accessed=500_000, transcendentals=0),
    )(place, *ready, *inputs)


def unpack_kernel(place_ref, kept_ref, received_ref, *refs):
    scan_ref, middle_ref, gate_ref, params_ref, channels_ref = refs
    kept_first = place_ref[3] == 0
    kept, received = kept_ref[...], received_ref[...]
    first = jnp.where(kept_first, kept, received)
    second = jnp.where(kept_first, received, kept)
    rows, scan = scan_ref.shape
    half = channels_ref.shape[1]
    scan_ref[...] = first[:rows, :scan]
    middle_ref[:, : 2 * half] = first[:rows, scan:]
    middle_ref[:, 2 * half :] = second[:rows, :scan]
    gate_ref[...] = second[:rows, scan:]
    params_ref[0] = first[rows:, : scan + LANES]
    params_ref[1] = second[rows:, : scan + LANES]
    channels_ref[:PARAM_ROWS] = first[rows:, :half]
    channels_ref[PARAM_ROWS:] = second[rows:, :half]


def params_kernel(heads_half, place_ref, params_ref, channels_ref, spread_ref, *refs):
    turn, core = place_ref[1], place_ref[3]
    half = channels_ref.shape[1]
    lane = lax.broadcasted_iota(jnp.int32, (1, LANES), 1)
    for layer in range(2):
        small_ref, states_ref, head_ref = refs[3 * layer : 3 * layer + 3]
        rows = params_ref[layer].astype(f32)
        split = rows[:, half + 2 * STATE :]
        heads = [split[3 * i : 3 * i + 1] + split[3 * i + 1 : 3 * i + 2] + split[3 * i + 2 : 3 * i + 3] for i in range(3)]
        heads = jnp.concatenate(heads + [jnp.zeros((5, LANES), f32)], axis=0)
        moved = [pltpu.roll(heads, (LANES - start * heads_half) % LANES, 1) for start in range(4)]

        def of(index):
            return jnp.where(index == 0, moved[0], jnp.where(index == 1, moved[1], jnp.where(index == 2, moved[2], moved[3])))

        own, other = of(2 * turn + core), pltpu.roll(of(2 * (1 - turn) + core), heads_half, 1)
        heads = jnp.where(lane < heads_half, own, jnp.where(lane < 2 * heads_half, other, 0.0))
        head_ref[...] = jnp.concatenate([heads[0:1], jnp.exp(heads[1:2]), jnp.zeros((6, LANES), f32)], axis=0)
        high, middle, low = three_parts(jnp.broadcast_to(heads[2:3], (8, LANES)))
        once = spread_ref[:LANES]
        skips = (nn(high, once) + nn(middle, once) + nn(low, once))[0:1]
        own_rows = rows[0:6, :half]
        other_rows = channels_ref[PARAM_ROWS * layer : PARAM_ROWS * layer + 6].astype(f32)
        channels = jnp.concatenate([own_rows, other_rows], axis=1)
        small_ref[...] = jnp.concatenate([channels, skips, jnp.zeros_like(skips)], axis=0)
        states_ref[...] = jnp.concatenate([rows[0:5, half : half + 2 * STATE], jnp.zeros((3, 2 * STATE), f32)], axis=0)


def beside_kernel(place_ref, *refs):
    out = refs[-1]
    start = 0
    for ref in refs[:-1]:
        out[:, start : start + ref.shape[1]] = ref[...]
        start += ref.shape[1]


def split_kernel(place_ref, whole_ref, *outs):
    start = 0
    for out in outs:
        out[...] = whole_ref[:, start : start + out.shape[1]]
        start += out.shape[1]


def cross_kernel(place_ref, *refs):
    over_x, over_tensor = refs[-2:]
    start = 0
    for group in range(len(refs[:-2]) // 4):
        x_ref, y_ref, first_ref, second_ref = refs[4 * group : 4 * group + 4]
        columns = slice(start, start + x_ref.shape[1])
        start += x_ref.shape[1]
        half = first_ref.shape[0]
        over_x[:half, columns] = (x_ref[:half].astype(f32) + first_ref[...].astype(f32)).astype(bf16)
        over_x[half:, columns] = x_ref[half:]
        over_tensor[:half, columns] = y_ref[:half]
        over_tensor[half:, columns] = (y_ref[half:].astype(f32) + second_ref[...].astype(f32)).astype(bf16)


def join_kernel(groups, place_ref, *refs):
    out = refs[-1]
    start = 0
    for own, over_x, over_tensor, offset in groups:
        width = refs[own].shape[1]
        there = slice(offset, offset + width)
        total = refs[own][...].astype(f32) + refs[over_x][:, there].astype(f32) + refs[over_tensor][:, there].astype(f32)
        out[:, start : start + width] = total.astype(bf16)
        start += width


def owned_kernel(place_ref, first_ref, second_ref, beside_ref, across_ref, both_ref, zx_ref, bc_ref, dt_ref, out_ref):
    first = place_ref[3] == 0
    half = out_ref.shape[1] // 2
    heads_half = dt_ref.shape[1] // 2
    mine = jnp.where(first, first_ref[...], second_ref[...]).astype(f32)
    beside = beside_ref[...].astype(f32)
    lower, upper = jnp.where(first, mine, beside), jnp.where(first, beside, mine)
    gate = half + 2 * STATE
    for index, part in enumerate((lower, upper)):
        columns = slice(index * half, (index + 1) * half)
        zx_ref[:, 0, columns] = part[:, gate : gate + half]
        zx_ref[:, 1, columns] = part[:, :half]
        out_ref[:, columns] = part[:, gate + half :]
    own = mine[:, half : half + STATE] + beside[:, half : half + STATE]
    other = across_ref[...].astype(f32) + both_ref[...].astype(f32)
    straight = place_ref[1] == 0
    bc_ref[:, :STATE] = jnp.where(straight, own, other)
    bc_ref[:, STATE:] = jnp.where(straight, other, own)
    lane = lax.broadcasted_iota(jnp.int32, (1, LANES), 1)
    steps = slice(half + STATE, half + 2 * STATE)
    both = jnp.where(lane < heads_half, lower[:, steps], pltpu.roll(upper[:, steps], heads_half, 1))
    dt_ref[...] = both[:, : 2 * heads_half]


def small_kernel(gate0, scan0, states0, gate1, scan1, states1, gain_ref, out_ref):
    for layer, (gate, scan, states, gain) in enumerate(
        ((gate0, scan0, states0, gain_ref[0:1, :]), (gate1, scan1, states1, gate0[7:8, :]))
    ):
        start = 16 * layer
        out_ref[start : start + 5, :] = scan[0:5, :]
        out_ref[start + 5 : start + 6, :] = gate[5:6, :]
        out_ref[start + 6 : start + 7, :] = gain
        out_ref[start + 7 : start + 16, :] = jnp.zeros((9, out_ref.shape[1]), f32)
        out_ref[start + 8 : start + 15, : 2 * STATE] = states[0:7, :]


def fold_kernel(heads_half, place_ref, own_ref, away_ref, mine_ref, others_ref):
    first = place_ref[3] == 0
    half = mine_ref.shape[1]
    folded = []
    for layer in range(2):
        own, away = own_ref[16 * layer : 16 * layer + 16], away_ref[16 * layer : 16 * layer + 16]
        units = own[0:6, :half] + away[0:6, half:]
        gain = own[6:7] + away[6:7]
        total = own[8:16, :half] + away[8:16, :half]
        own_heads = jnp.concatenate([own[14:15, :LANES], own[13:14, : 2 * LANES]], axis=1)
        away_heads = jnp.concatenate([away[14:15, :LANES], away[13:14, : 2 * LANES]], axis=1)
        moved = pltpu.roll(jnp.broadcast_to(away_heads, (8, 3 * LANES)), 3 * LANES - heads_half, 1)[0:1]
        heads = jnp.concatenate([own_heads + moved, jnp.zeros((1, half - 3 * LANES), f32)], axis=1) if half > 3 * LANES else own_heads + moved
        zeros = jnp.zeros((2, half), f32)
        folded.append(jnp.concatenate([units, gain[:, :half], gain[:, half:], total[0:5], heads, zeros], axis=0))
    mine_ref[...] = jnp.where(first, folded[0], folded[1])
    others_ref[...] = jnp.where(first, folded[1], folded[0])


def small_outputs_kernel(heads_half, place_ref, total_ref, conv_ref, states_conv_ref, gate_gain_ref, heads_ref, gain_ref):
    first = place_ref[3] == 0
    half = total_ref.shape[1]
    here, there = total_ref[0:16], total_ref[16:32]
    lower, upper = jnp.where(first, here, there), jnp.where(first, there, here)
    conv_ref[:, :half] = lower[0:5]
    conv_ref[:, half:] = upper[0:5]
    gate_gain_ref[:, :half] = lower[5:6]
    gate_gain_ref[:, half:] = upper[5:6]
    states_conv_ref[...] = here[8:13, : 2 * STATE] + there[8:13, : 2 * STATE]
    lane = lax.broadcasted_iota(jnp.int32, (1, LANES), 1)
    for row in range(3):
        own = lower[13:14, row * LANES : (row + 1) * LANES]
        other = pltpu.roll(jnp.broadcast_to(upper[13:14, row * LANES : (row + 1) * LANES], (8, LANES)), heads_half, 1)[0:1]
        heads_ref[row : row + 1, :] = jnp.where(lane < heads_half, own, other)[:, : 2 * heads_half]
    gain_ref[:, :half] = here[6:7]
    gain_ref[:, half:] = here[7:8]


def tied(*values):
    return lax.optimization_barrier(values)


def swapped(block, axis):
    return lax.ppermute(block, axis, [(0, 1), (1, 0)])


def far_swapped(block):
    size = lax.axis_size("tensor")
    return lax.ppermute(block, ("section", "tensor"), [(i, 2 * size - 1 - i) for i in range(2 * size)])


def body(
    x_input,
    teacher,
    segment_ids,
    valid_len,
    norm_gain,
    w_zx,
    w_bc,
    w_dt,
    conv_x,
    conv_bc,
    dt_bias,
    a_log,
    d_skip,
    gnorm_gain,
    w_out,
):
    local_rows, width = x_input.shape[1:]
    ranks = lax.axis_size("dp")
    places = ranks // 2
    core = lax.axis_index("section")
    turn = lax.axis_index("tensor")
    rank = lax.axis_index("dp")
    place = jnp.stack([rank % 2, turn, rank, core]).astype(jnp.int32)
    on_first = core == 0
    block_rows = w_zx.shape[1]
    half = w_zx.shape[3] // 2
    units = 2 * half
    heads_half = w_dt.shape[2] // 2
    scan_columns = half + 2 * STATE
    line_groups = [[2 * index + start for index in range(places)] for start in range(2)]

    def by_layer(kept, received):
        return jnp.where(on_first, kept, received), jnp.where(on_first, received, kept)

    def x_swapped(block):
        return lax.ppermute(block, "dp", [(i, i ^ 1) for i in range(ranks)])

    def y_swapped(block):
        return swapped(block, "tensor")

    def line_gather(block):
        return lax.all_gather(block, "dp", axis_index_groups=line_groups, axis=0, tiled=True)

    def line_reduce(block):
        return lax.psum_scatter(block, "dp", axis_index_groups=line_groups, scatter_dimension=0, tiled=True)

    def line_total(block):
        if places != 4:
            return lax.psum(block, "dp", axis_index_groups=line_groups)

        def send(rows, moves):
            return lax.ppermute(rows, "dp", [(2 * a + start, 2 * b + start) for a, b in moves for start in range(2)])

        up, down = send(block, [(0, 1), (1, 2), (2, 3)]), send(block, [(1, 0), (2, 1), (3, 2)])
        up2, down2 = send(up, [(1, 2), (2, 3)]), send(down, [(2, 1), (1, 0)])
        far = send(jnp.where(rank // 2 == 1, up, down), [(1, 3), (2, 0)])
        return block + up + down + up2 + down2 + far

    pack_shape = (block_rows + PARAM_ROWS, scan_columns + units)
    kept, sent = plain_call(
        pack_kernel,
        place,
        (w_zx[0], w_bc[0], w_dt[0].T, norm_gain, w_out[0].T, conv_x[0], gnorm_gain, conv_bc[0], dt_bias, a_log, d_skip),
        [(pack_shape, bf16)] * 2,
    )
    received = swapped(sent, "section")
    scan_block, middle_block, gate_block, params_both, channels = plain_call(
        unpack_kernel,
        place,
        (kept, received),
        [
            ((block_rows, scan_columns), bf16),
            ((block_rows, units + scan_columns), bf16),
            ((block_rows, units), bf16),
            ((2, PARAM_ROWS, scan_columns + LANES), bf16),
            ((2 * PARAM_ROWS, half), bf16),
        ],
    )

    def plane_end(block, over_x, over_tensor):
        cut = places // 2 * block_rows
        return block, over_x, over_tensor, y_swapped(over_x[:cut]), x_swapped(over_tensor[cut:])

    def quarter(rows):
        away = lax.dynamic_index_in_dim(rows, 1 - turn, 0, keepdims=False)
        return lax.dynamic_slice_in_dim(away, core * (local_rows // 2), local_rows // 2, 0)

    def whole_rows(rows, here, beside):
        own = lax.dynamic_index_in_dim(rows, turn, 0, keepdims=False)
        other = jnp.concatenate(by_layer(here, beside), axis=0)
        return jnp.where(turn == 0, jnp.concatenate([own, other]), jnp.concatenate([other, own]))

    scan_line, here, channels = tied(line_gather(scan_block), y_swapped(quarter(x_input)), y_swapped(channels))
    scan_line, middle_block = tied(scan_line, middle_block)
    middle_line = line_gather(middle_block)
    scan_half = scan_line, x_swapped(scan_line), y_swapped(scan_line)
    x_rows = whole_rows(x_input, here, swapped(here, "section"))
    params = plain_call(
        functools.partial(params_kernel, heads_half),
        place,
        (params_both, channels, spreader_of(units)),
        [((8, units), f32), ((8, 2 * STATE), f32), ((8, LANES), f32)] * 2,
    )
    params = [params[:3], params[3:]]
    marks, segment_row = token_marks(place, valid_len, segment_ids[:, 0])
    over_x = x_swapped(gate_block)
    side = (gate_block, over_x, y_swapped(gate_block), y_swapped(over_x))
    side = plain_call(beside_kernel, place, side, [((block_rows, 4 * units), bf16)], (x_rows, marks, params[0][0]))[0]
    scan_first, side = tied(plane_end(*scan_half), side)
    middle_line, side = tied(middle_line, side)
    gate_second = (line_gather(side),)
    gate_line, next_line = plain_call(
        split_kernel,
        place,
        (middle_line,),
        [((places * block_rows, units), bf16), ((places * block_rows, scan_columns), bf16)],
        (scan_first[4],),
    )

    gate_half = gate_line, x_swapped(gate_line), y_swapped(gate_line)
    next_half = next_line, x_swapped(next_line), y_swapped(next_line)
    results = scan_forward(place, block_rows, x_rows, None, scan_first, marks, segment_row, params[0])
    results, gate_half, next_half = tied(results, gate_half, next_half)
    _, gain_first, normed_first, saved_first = results
    gate_first = plane_end(*gate_half)
    gated_first, part = gate_forward(place, block_rows, normed_first, saved_first[2], gate_first, params[0])
    part, next_half = tied(part, next_half)
    scan_second = plane_end(*next_half)
    parts_first = (part, swapped(part, "section"))
    parts_first, teacher = tied(parts_first, teacher)
    results = scan_forward(place, block_rows, x_rows, parts_first, scan_second, marks, segment_row, params[1])
    results, here = tied(results, y_swapped(quarter(teacher)))
    hidden, gain_second, normed_second, saved_second = results
    results = gate_forward(place, block_rows, normed_second, saved_second[2], gate_second, params[1])
    (gated_second, part), here, beside = tied(results, here, swapped(here, "section"))
    parts_second = (part, swapped(part, "section"))
    target = whole_rows(teacher, here, beside)

    def plane_start(pieces):
        return tuple(pieces[:3]), (y_swapped(pieces[3]), x_swapped(pieces[4]))

    def crossed(*groups):
        arrays = [array for pieces, came in groups for array in pieces[1:] + came]
        columns = sum(pieces[0].shape[1] for pieces, _ in groups)
        over_x, over_tensor = plain_call(cross_kernel, place, arrays, [((places * block_rows, columns), bf16)] * 2)
        return [pieces[0] for pieces, _ in groups], x_swapped(over_x), y_swapped(over_tensor)

    def joined(*groups, ready=()):
        arrays, spans = [], []
        for owns, over_x, over_tensor in groups:
            base = len(arrays)
            arrays += list(owns) + [over_x, over_tensor]
            offset = 0
            for index, own in enumerate(owns):
                spans.append((base + index, base + len(owns), base + len(owns) + 1, offset))
                offset += own.shape[1]
        columns = sum(arrays[span[0]].shape[1] for span in spans)
        kernel = functools.partial(join_kernel, spans)
        return plain_call(kernel, place, arrays, [((places * block_rows, columns), bf16)], ready)[0]

    results = gate_backward(
        place,
        block_rows,
        hidden,
        parts_second,
        (target,),
        normed_second,
        gated_second,
        saved_second[2],
        gate_second,
        marks,
        params[1],
    )
    produced, grad_out, grad_y, gate_part = results[:4]
    gate_reduce = plane_start(results[4:9])
    gate_sums_second = results[9]

    def away_rows(rows):
        return y_swapped(lax.dynamic_slice_in_dim(rows, (1 - turn) * local_rows, local_rows, 0))

    results = scan_backward(
        place, block_rows, grad_y, gate_part, scan_second, marks, segment_row, params[1], saved_second
    )
    results, gate_reduce, produced_away = tied(results, gate_reduce, away_rows(produced))
    grads, part, sums, states_sums = results
    sums_second = (gate_sums_second, sums, states_sums)
    results = weight_grads(place, block_rows, normed_second, grads, ())
    results, grad_parts = tied(results, (part, swapped(part, "section")))
    scan_reduce = plane_start(results)
    results = gate_backward(
        place,
        block_rows,
        x_rows,
        parts_first,
        (hidden, grad_out) + grad_parts + (gain_second,),
        normed_first,
        gated_first,
        saved_first[2],
        gate_first,
        marks,
        params[0],
    )
    results, scan_reduce = tied(results[1:], scan_reduce)
    grad_hidden, grad_y, gate_part = results[:3]
    crossed_second = crossed(scan_reduce, gate_reduce)
    gate_reduce = plane_start(results[3:8])
    gate_sums_first = results[8]
    results = scan_backward(
        place, block_rows, grad_y, gate_part, scan_first, marks, segment_row, params[0], saved_first
    )
    results, crossed_second, gate_reduce = tied(results, crossed_second, gate_reduce)
    grads, part, sums, states_sums = results
    sums_first = (gate_sums_first, sums, states_sums)
    results = weight_grads(place, block_rows, normed_first, grads, ())
    results, grad_parts = tied(results, (part, swapped(part, "section")))
    scan_reduce = plane_start(results)
    owned_second = line_reduce(joined(crossed_second, ready=(results[0],)))
    crossed_gate = crossed(gate_reduce)
    results = finish(place, *grad_parts, x_rows, grad_hidden, gain_first, (crossed_gate[0][0],))
    (grad_rows, grad_low, gain_sums), scan_reduce = tied(results, scan_reduce)
    crossed_scan = crossed(scan_reduce)
    layer_outputs = placed_rows(place, produced, produced_away, (crossed_scan[0][0],))
    smalls = plain_call(
        lambda place_ref, *refs: small_kernel(*refs), place, sums_first + sums_second + (gain_sums,), [((32, units), f32)]
    )[0]
    smalls_away = y_swapped(smalls)
    mine, others = plain_call(
        functools.partial(fold_kernel, heads_half), place, (smalls, smalls_away), [((16, half), f32)] * 2
    )
    total = jnp.concatenate([mine, swapped(others, "section")])
    total = total + x_swapped(total)
    blocks = joined(crossed_scan, crossed_gate, ready=(total,))
    grad_low, blocks = tied(grad_low, blocks)
    owned_first = line_reduce(blocks)
    boundary = placed_rows(place, grad_rows, away_rows(grad_low))
    total = line_total(total)
    grad_conv, grad_states_conv, grad_gate_gain, grad_heads, gain_total = plain_call(
        functools.partial(small_outputs_kernel, heads_half),
        place,
        (total,),
        [((5, units), f32), ((5, 2 * STATE), f32), ((1, units), f32), ((3, 2 * heads_half), f32), ((1, width), f32)],
    )

    others = jnp.where(on_first, owned_second, owned_first)
    own_states, other_states = by_layer(owned_first[:, half : half + STATE], owned_second[:, half : half + STATE])
    grad_zx, grad_bc, grad_dt, grad_out_w = plain_call(
        owned_kernel,
        place,
        (owned_first, owned_second, swapped(others, "section"), y_swapped(own_states), far_swapped(other_states)),
        [((block_rows, 2, units), f32)] + [((block_rows, columns), f32) for columns in (2 * STATE, 2 * heads_half, units)],
        (boundary, layer_outputs, grad_conv),
    )
    return (
        layer_outputs[None],
        boundary[None],
        lax.dynamic_slice_in_dim(gain_total, rank * block_rows, block_rows, 1),
        grad_zx[None],
        grad_bc[None],
        grad_dt[None],
        grad_conv[None],
        grad_states_conv[None],
        grad_heads[1:2],
        grad_heads[2:3],
        grad_heads[0:1],
        grad_gate_gain,
        grad_out_w.T[None],
    )


def solution(mesh):
    placed = (
        P(None, ("dp", "tensor"), None),
        P(None, ("dp", "tensor"), None),
        P(None, "dp", None),
        P(),
        P("section", "dp"),
        P("section", "dp", None, "tensor"),
        P("section", "dp", None),
        P("section", "dp", "tensor"),
        P("section", None, "tensor"),
        P("section", None, None),
        P("section", None),
        P("section", None),
        P("section", None),
        P("section", "tensor"),
        P("section", "tensor", "dp"),
    )
    return jax.shard_map(
        body,
        mesh=mesh,
        in_specs=placed,
        out_specs=(
            P("section", None, ("dp", "tensor"), None),
            P("section", None, ("dp", "tensor"), None),
            P("section", "dp"),
            P("section", "dp", None, "tensor"),
            P("section", "dp", None),
            P("section", "dp", "tensor"),
            P("section", None, "tensor"),
            P("section", None, None),
            P("section", "tensor"),
            P("section", "tensor"),
            P("section", "tensor"),
            P("section", "tensor"),
            P("section", "tensor", "dp"),
        ),
        check_vma=False,
    )
```

```python
import functools

import jax
import jax.numpy as jnp
import numpy as np
from jax import lax
from jax.experimental import pallas as pl
from jax.experimental.pallas import tpu as pltpu
from jax.sharding import PartitionSpec as P

HEAD_DIM = 64
STATE = 128
SPAN = 256
LANES = 128

epsilon = 1e-05
f32 = jnp.float32
bf16 = jnp.bfloat16


def nn(left, right):
    return lax.dot_general(left, right, (((1,), (0,)), ((), ())), preferred_element_type=f32)


def nt(left, right):
    return lax.dot_general(left, right, (((1,), (1,)), ((), ())), preferred_element_type=f32)


def tn(left, right):
    return lax.dot_general(left, right, (((0,), (0,)), ((), ())), preferred_element_type=f32)


def high_low(value):
    high = value.astype(bf16)
    return high, (value - high.astype(f32)).astype(bf16)


def spread(per_head, spreader):
    return nn(jnp.concatenate(high_low(per_head), axis=1), spreader)


def gathered_heads(units, spreader):
    high, low = high_low(units)
    once = spreader[:LANES]
    return nt(high, once) + nt(low, once)


def running_sum(triangle, value):
    high = value.astype(bf16)
    rest = value - high.astype(f32)
    middle = rest.astype(bf16)
    low = (rest - middle.astype(f32)).astype(bf16)
    sums = nn(triangle, jnp.concatenate([high, middle, low], axis=1))
    return sums[:, :LANES] + sums[:, LANES : 2 * LANES] + sums[:, 2 * LANES :]


def softplus(value):
    return jnp.maximum(value, 0.0) + jnp.log1p(jnp.exp(-jnp.abs(value)))


def moved_down(block, edge, lag):
    return jnp.concatenate([edge, block], axis=0)[8 - lag : 8 - lag + block.shape[0]]


def moved_up(block, edge, lag):
    return jnp.concatenate([block, edge], axis=0)[lag : lag + block.shape[0]]


def decay_parts(steps_in, head_rows, marks, heads):
    lane = lax.broadcasted_iota(jnp.int32, (1, LANES), 1)
    live = lane < heads
    shifted = steps_in + head_rows[0:1, :LANES]
    steps = jnp.where(live, softplus(shifted), 0.0)
    rates = head_rows[1:2, :LANES]
    log_steps = -steps * rates
    row = lax.broadcasted_iota(jnp.int32, (SPAN, SPAN), 0)
    column = lax.broadcasted_iota(jnp.int32, (SPAN, SPAN), 1)
    lower = (row >= column).astype(bf16)
    logs = running_sum(lower, log_steps)
    last = logs[SPAN - 1 : SPAN]
    entry = jnp.exp(logs) * marks[:, 3:4]
    tail = jnp.exp(last - logs) * marks[:, 4:5]
    through = jnp.exp(last) * marks[SPAN - 1 : SPAN, 3:4]
    entry = jnp.where(live, entry, 0.0)
    tail = jnp.where(live, tail, 0.0)
    through = jnp.where(live, through, 0.0)
    return shifted, steps, log_steps, logs, entry, tail, through, row, column


def linked_mask(row, column, marks, segment_row):
    linked = (row >= column) & (marks[:, 5:6] == segment_row)
    return jnp.where(linked, 0.0, -1e30)


def branch_of(own_ref, other_ref, units):
    width = own_ref.shape[1] - LANES
    own = own_ref[...].astype(f32)
    other = other_ref[...].astype(f32)
    total = own[:, :width] + other[:, :width]
    own_squares = own[:, width : width + 1] + own[:, width + 1 : width + 2]
    other_squares = other[:, width : width + 1] + other[:, width + 1 : width + 2]
    inverse = lax.rsqrt((own_squares + other_squares) / (2 * units) + epsilon)
    return total * inverse, total, inverse


def pieces_of(rows, places):
    half = places // 2
    return ((False, False, 0, places), (True, False, 0, places), (False, True, 0, places), (True, True, 0, half), (True, True, half, places - half))


def load_weights(weights, start, refs, columns, rows, place_ref):
    first, last = columns
    places = weights.shape[0] // (2 * rows)
    mine = place_ref[0]
    size = refs[0].shape[1] // 4
    for index, (moved, turned, base, count) in enumerate(pieces_of(rows, places)):
        if len(refs) == 1:
            if index == 4:
                break
            ref, offset, base, count = refs[0], index * size, 0, places
        else:
            ref, offset = refs[index], 0
        place = 1 - mine if moved else mine
        target = start + (last - first if turned else 0)
        for step in range(count):
            row = pl.multiple_of((2 * (base + step) + place) * rows, 32)
            weights[pl.ds(row, rows), target : target + last - first] = ref[step * rows : (step + 1) * rows, offset + first : offset + last]


def store_grads(refs, columns, acc, start, rows, place_ref):
    first, last = columns
    mine = place_ref[0]
    for ref, (moved, turned, base, count) in zip(refs, pieces_of(rows, acc.shape[0] // (2 * rows))):
        place = 1 - mine if moved else mine
        source = start + (last - first if turned else 0)
        for step in range(count):
            row = pl.multiple_of((2 * (base + step) + place) * rows, 32)
            ref[step * rows : (step + 1) * rows, first:last] = acc[pl.ds(row, rows), source : source + last - first].astype(bf16)


def scan_forward_kernel(second, heads, rows, pieces, *refs):
    place_ref, refs = refs[0], refs[1:]
    if second:
        (h_ref, own_ref, other_ref), refs = refs[:3], refs[3:]
    else:
        (h_ref,), refs = refs[:1], refs[1:]
    parts, refs = refs[:pieces], refs[pieces:]
    (marks_ref, segment_ref, small_ref, states_small_ref, head_ref, spread_ref), refs = refs[:6], refs[6:]
    if second:
        h_out, refs = refs[0], refs[1:]
    gain_ref, refs = refs[0], refs[1:]
    normed_ref, raw_ref, conv_ref, y_ref, raw_states_ref, conv_states_ref, steps_ref, entry_state_ref = refs[:8]
    state, raw_edge, states_edge, gain, weights = refs[8:]
    units = raw_ref.shape[1]

    @pl.when(pl.program_id(0) == 0)
    def _():
        state[...] = jnp.zeros_like(state)
        raw_edge[...] = jnp.zeros_like(raw_edge)
        states_edge[...] = jnp.zeros_like(states_edge)
        load_weights(weights, 0, parts, (0, units // 2), rows, place_ref)
        load_weights(weights, units, parts, (units // 2, units // 2 + 2 * STATE), rows, place_ref)
        steps_columns = weights[:, units + STATE : units + STATE + LANES].astype(f32)
        gain[...] = jnp.broadcast_to(jnp.transpose(steps_columns)[LANES // 2 : LANES // 2 + 1, :], gain.shape)
        gain_ref[...] = gain[...]

    hidden = h_ref[...].astype(f32)
    if second:
        rounded = (hidden + branch_of(own_ref, other_ref, units)[0]).astype(bf16)
        h_out[...] = rounded
        hidden = rounded.astype(f32)
    scale = lax.rsqrt(jnp.mean(hidden * hidden, axis=1, keepdims=True) + epsilon)
    normed = (hidden * scale * gain[0:1, :]).astype(bf16)
    normed_ref[...] = normed
    projected = nn(normed, weights[...])
    raw = projected[:, :units]
    first, second_part = projected[:, units : units + 2 * STATE], projected[:, units + 2 * STATE :]
    marks = marks_ref[...]
    turned = marks[0:1, 10:11] > 0.5
    raw_states = jnp.concatenate(
        [
            jnp.where(turned, second_part[:, :STATE], first[:, :STATE]),
            jnp.where(turned, first[:, :STATE], second_part[:, :STATE]),
        ],
        axis=1,
    )
    lane = lax.broadcasted_iota(jnp.int32, (1, LANES), 1)
    steps_in = jnp.where(lane < heads // 2, first[:, STATE:], pltpu.roll(second_part[:, STATE:], heads // 2, 1))
    raw_ref[...] = raw
    raw_states_ref[...] = raw_states
    steps_ref[...] = steps_in

    def conv(block, edge, taps):
        total = taps[4:5] + taps[3:4] * block
        for lag in (1, 2, 3):
            total = total + taps[3 - lag : 4 - lag] * (moved_down(block, edge, lag) * marks[:, lag - 1 : lag])
        return total

    taps = small_ref[...]
    conved = conv(raw, raw_edge[...], taps)
    conv_ref[...] = conved
    conved_states = conv(raw_states, states_edge[...], states_small_ref[...])
    conv_states_ref[...] = conved_states
    raw_edge[...] = raw[SPAN - 8 :]
    states_edge[...] = raw_states[SPAN - 8 :]
    values = conved * jax.nn.sigmoid(conved)
    states_in = conved_states * jax.nn.sigmoid(conved_states)
    b_rows = states_in[:, :STATE].astype(bf16)
    c_rows = states_in[:, STATE:].astype(bf16)
    _, steps, _, logs, entry, tail, through, row, column = decay_parts(steps_in, head_ref[...], marks, heads)
    spreader = spread_ref[...]
    scaled = values * spread(steps, spreader)
    mask = linked_mask(row, column, marks, segment_ref[...])
    scores = nt(c_rows, b_rows)
    logs_across = jnp.transpose(logs)
    pieces = []
    for pair in range(heads // 2):
        mixes = []
        for head in (2 * pair, 2 * pair + 1):
            factor = jnp.exp(logs[:, head : head + 1] - logs_across[head : head + 1, :] + mask)
            mixes.append((factor * scores).astype(bf16))
        block = scaled[:, pair * LANES : (pair + 1) * LANES]
        left = jnp.where(lane < HEAD_DIM, block, 0.0).astype(bf16)
        right = jnp.where(lane < HEAD_DIM, 0.0, block).astype(bf16)
        pieces.append(nn(jnp.concatenate(mixes, axis=1), jnp.concatenate([left, right], axis=0)))
    inside = jnp.concatenate(pieces, axis=1)
    held = state[...]
    entry_state_ref[0] = held
    across = nn(c_rows, held.astype(bf16)) * spread(entry, spreader)
    through_row = spread(jnp.broadcast_to(through, (8, LANES)), spreader)[0:1]
    state[...] = through_row * held + tn(b_rows, (spread(tail, spreader) * scaled).astype(bf16))
    y_ref[...] = inside + across + taps[6:7] * values


def gate_forward_kernel(rows, pieces, place_ref, normed_ref, y_ref, *refs):
    parts, refs = refs[:pieces], refs[pieces:]
    small_ref, gate_ref, part_ref, weights, out_weights = refs

    @pl.when(pl.program_id(0) == 0)
    def _():
        half = weights.shape[1] // 2
        load_weights(weights, 0, parts, (0, half), rows, place_ref)
        load_weights(out_weights, 0, parts, (half, 2 * half), rows, place_ref)

    gate = nn(normed_ref[...], weights[...])
    gate_ref[...] = gate
    gated = y_ref[...] * (gate * jax.nn.sigmoid(gate))
    squares = jnp.sum(gated * gated, axis=1, keepdims=True)
    part = nt((gated * small_ref[5:6]).astype(bf16), out_weights[...])
    width = part.shape[1]
    part_ref[:, :width] = part.astype(bf16)
    high, low = high_low(squares)
    lane = lax.broadcasted_iota(jnp.int32, (1, LANES), 1)
    part_ref[:, width:] = jnp.where(lane == 0, high, jnp.where(lane == 1, low, jnp.zeros_like(low)))


def gate_backward_kernel(second, rows, pieces, *refs):
    place_ref, refs = refs[0], refs[1:]
    if second:
        (h_ref, own_ref, other_ref, target_ref), refs = refs[:4], refs[4:]
    else:
        (own_ref, other_ref, next_h_ref, next_out_ref, grad_own_ref, grad_other_ref, next_gain_ref), refs = refs[:7], refs[7:]
    (normed_ref, gate_ref, y_ref), parts, refs = refs[:3], refs[3 : 3 + pieces], refs[3 + pieces :]
    (marks_ref, small_ref), refs = refs[:2], refs[2:]
    if second:
        out_ref, refs = refs[0], refs[1:]
    (grad_out_ref, grad_y_ref, part_ref), grads, sums_ref, refs = refs[:3], refs[3:8], refs[8], refs[9:]
    weights, out_weights, acc_z, acc_o, sums = refs
    units = y_ref.shape[1]

    @pl.when(pl.program_id(0) == 0)
    def _():
        load_weights(weights, 0, parts, (0, units // 2), rows, place_ref)
        load_weights(out_weights, 0, parts, (units // 2, units), rows, place_ref)
        for ref in (acc_z, acc_o, sums):
            ref[...] = jnp.zeros_like(ref)

    branch, total, inverse = branch_of(own_ref, other_ref, units)
    if second:
        produced = h_ref[...].astype(f32) + branch
        out_ref[...] = jnp.where(place_ref[3] == 0, h_ref[...].astype(f32), produced).astype(bf16)
        grad_out = marks_ref[:, 9:10] * (produced - target_ref[...])
    else:
        grad_normed = grad_own_ref[...].astype(f32) + grad_other_ref[...].astype(f32)
        grad_out, gain_term = norm_backward(grad_normed, next_h_ref[...].astype(f32), next_out_ref[...], next_gain_ref[0:1, :])
        sums[7:8, :] += jnp.sum(gain_term, axis=0, keepdims=True)
    grad_out_ref[...] = grad_out
    grad = grad_out.astype(bf16)
    inner = jnp.sum(grad.astype(f32) * total, axis=1, keepdims=True) * (inverse * inverse * inverse) / (2 * units)
    gain = small_ref[5:6]
    gate = gate_ref[...]
    y = y_ref[...]
    gate_sig = jax.nn.sigmoid(gate)
    gate_silu = gate * gate_sig
    gated = y * gate_silu
    gated_unit = gated * inverse
    grad_mixed = nn(grad, out_weights[...])
    acc_o[...] += tn(grad, (gated_unit * gain).astype(bf16))
    sums[5:6, :] += jnp.sum(grad_mixed * gated_unit, axis=0, keepdims=True)
    grad_gated = grad_mixed * gain * inverse - gated * inner
    grad_gate = (grad_gated * y * (gate_sig * (1.0 + gate * (1.0 - gate_sig)))).astype(bf16)
    grad_y_ref[...] = (grad_gated * gate_silu).astype(bf16)
    acc_z[...] += tn(normed_ref[...], grad_gate)
    part_ref[...] = nt(grad_gate, weights[...])

    @pl.when(pl.program_id(0) == pl.num_programs(0) - 1)
    def _():
        store_grads(grads, (0, units // 2), acc_z, 0, rows, place_ref)
        store_grads(grads, (units // 2, units), acc_o, 0, rows, place_ref)
        sums_ref[...] = sums[...]


def scan_backward_kernel(heads, rows, pieces, *refs):
    (place_ref, grad_y_ref, gate_part_ref), parts, refs = refs[:3], refs[3 : 3 + pieces], refs[3 + pieces :]
    (marks_ref, segment_ref, small_ref, states_small_ref, head_ref, spread_ref), refs = refs[:6], refs[6:]
    (raw_ref, conv_ref, y_ref, raw_states_ref, conv_states_ref, steps_ref, entry_state_ref), refs = refs[:7], refs[7:]
    (grads_ref, part_ref, sums_ref, states_sums_ref), refs = refs[:4], refs[4:]
    weights, dstate, next_state, conv_edge, states_edge, sums, states_sums = refs
    step = pl.program_id(0)
    units = raw_ref.shape[1]

    @pl.when(step == 0)
    def _():
        for ref in (dstate, next_state, conv_edge, states_edge, sums, states_sums):
            ref[...] = jnp.zeros_like(ref)
        load_weights(weights, 0, parts, (0, units // 2), rows, place_ref)
        load_weights(weights, units, parts, (units // 2, units // 2 + 2 * STATE), rows, place_ref)

    marks = marks_ref[...]
    taps = small_ref[...]
    y = y_ref[...]
    grad_y_low = grad_y_ref[...]
    grad_y = grad_y_low.astype(f32)
    conved = conv_ref[...]
    value_sig = jax.nn.sigmoid(conved)
    values = conved * value_sig
    conved_states = conv_states_ref[...]
    states_sig = jax.nn.sigmoid(conved_states)
    states_in = conved_states * states_sig
    b_rows = states_in[:, :STATE].astype(bf16)
    c_rows = states_in[:, STATE:].astype(bf16)
    shifted, steps, log_steps, logs, entry, tail, through, row, column = decay_parts(steps_ref[...], head_ref[...], marks, heads)
    spreader = spread_ref[...]
    spread_steps = spread(steps, spreader)
    spread_entry = spread(entry, spreader)
    spread_tail = spread(tail, spreader)
    through_row = spread(jnp.broadcast_to(through, (8, LANES)), spreader)[0:1]
    scaled_low = (values * spread_steps).astype(bf16)
    scaled = scaled_low.astype(f32)
    mask = linked_mask(row, column, marks, segment_ref[...])
    scores = nt(c_rows, b_rows)
    logs_across = jnp.transpose(logs)
    lane = lax.broadcasted_iota(jnp.int32, (1, LANES), 1)
    is_left = lane < HEAD_DIM
    zero = jnp.zeros((), bf16)
    grad_scores = jnp.zeros((SPAN, SPAN), f32)
    pieces = []
    for pair in range(heads // 2):
        columns = slice(pair * LANES, (pair + 1) * LANES)
        block, grad = scaled_low[:, columns], grad_y_low[:, columns]
        grad_left = jnp.where(is_left, grad, zero)
        grad_right = jnp.where(is_left, zero, grad)
        mixes = []
        for head, grad_one in ((2 * pair, grad_left), (2 * pair + 1, grad_right)):
            factor = jnp.exp(logs[:, head : head + 1] - logs_across[head : head + 1, :] + mask)
            mixes.append((factor * scores).astype(bf16))
            grad_scores = grad_scores + nt(grad_one, block) * factor
        pieces.append(tn(jnp.concatenate(mixes, axis=0), jnp.concatenate([grad_left, grad_right], axis=0)))
    held = entry_state_ref[0]
    held_low = held.astype(bf16)
    gradient = dstate[...]
    gradient_low = gradient.astype(bf16)
    grad_scaled = jnp.concatenate(pieces, axis=1) + spread_tail * nn(b_rows, gradient_low)
    grad_entry = (spread_entry * grad_y).astype(bf16)
    grad_scores_low = grad_scores.astype(bf16)
    grad_c = nn(grad_scores_low, b_rows) + nt(grad_entry, held_low)
    grad_b = tn(grad_scores_low, c_rows) + nt((spread_tail * scaled).astype(bf16), gradient_low)
    state_term = jnp.sum(gradient * next_state[...], axis=0, keepdims=True)
    dstate[...] = through_row * gradient + tn(c_rows, grad_entry)
    next_state[...] = held
    skip = taps[6:7]
    sums[6:7, :] += jnp.sum(grad_y * values, axis=0, keepdims=True)
    grad_logs = gathered_heads(grad_y * (y - skip * values) - scaled * grad_scaled, spreader)
    state_heads = gathered_heads(jnp.broadcast_to(state_term, (8, units)), spreader)[0:1]
    last_row = lax.broadcasted_iota(jnp.int32, (SPAN, 1), 0) == SPAN - 1
    grad_logs = grad_logs + jnp.where(last_row, state_heads, 0.0)
    grad_log_steps = running_sum((row <= column).astype(bf16), grad_logs)
    grad_steps = gathered_heads(grad_scaled * values, spreader) - head_ref[1:2, :LANES] * grad_log_steps
    grad_steps_in = jnp.where(lane < heads, grad_steps * jax.nn.sigmoid(shifted), 0.0)
    states_sums[5:6, :] += jnp.concatenate(
        [
            jnp.sum(grad_steps_in, axis=0, keepdims=True),
            jnp.sum(grad_log_steps * log_steps, axis=0, keepdims=True),
        ],
        axis=1,
    )
    grad_values = grad_scaled * spread_steps + skip * grad_y
    grad_conved = grad_values * (value_sig * (1.0 + conved * (1.0 - value_sig)))
    grad_states = jnp.concatenate([grad_b, grad_c], axis=1)
    grad_conved_states = grad_states * (states_sig * (1.0 + conved_states * (1.0 - states_sig)))

    def conv_backward(block, edge, tap_rows, raw, total_ref):
        result = tap_rows[3:4] * block
        total_ref[3:4, :] += jnp.sum(block * raw, axis=0, keepdims=True)
        total_ref[4:5, :] += jnp.sum(block, axis=0, keepdims=True)
        for lag in (1, 2, 3):
            term = moved_up(block, edge, lag) * marks[:, 5 + lag : 6 + lag]
            result = result + tap_rows[3 - lag : 4 - lag] * term
            total_ref[3 - lag : 4 - lag, :] += jnp.sum(term * raw, axis=0, keepdims=True)
        return result

    grad_raw = conv_backward(grad_conved, conv_edge[...], taps, raw_ref[...], sums)
    grad_raw_states = conv_backward(
        grad_conved_states, states_edge[...], states_small_ref[...], raw_states_ref[...], states_sums
    )
    conv_edge[...] = grad_conved[:8]
    states_edge[...] = grad_conved_states[:8]
    turned = marks[0:1, 10:11] > 0.5
    first_states = jnp.where(turned, grad_raw_states[:, STATE:], grad_raw_states[:, :STATE])
    second_states = jnp.where(turned, grad_raw_states[:, :STATE], grad_raw_states[:, STATE:])
    own_steps = jnp.where(lane < heads // 2, grad_steps_in, 0.0)
    other_steps = jnp.where(lane < heads // 2, pltpu.roll(grad_steps_in, LANES - heads // 2, 1), 0.0)
    grads = jnp.concatenate([grad_raw, first_states, own_steps, second_states, other_steps], axis=1).astype(bf16)
    grads_ref[...] = grads
    part_ref[...] = (nt(grads, weights[...]) + gate_part_ref[...]).astype(bf16)

    @pl.when(step == pl.num_programs(0) - 1)
    def _():
        skips = gathered_heads(sums[...], spreader)[6:7]
        states_sums[6:7, :] = jnp.concatenate([skips, jnp.zeros_like(skips)], axis=1)
        sums_ref[...] = sums[...]
        states_sums_ref[...] = states_sums[...]


def weight_grads_kernel(rows, place_ref, normed_ref, grads_ref, *refs):
    outs, acc = refs[-6:-1], refs[-1]
    units = acc.shape[1] - 4 * STATE

    @pl.when(pl.program_id(0) == 0)
    def _():
        acc[...] = jnp.zeros_like(acc)

    acc[...] += tn(normed_ref[...], grads_ref[...])

    @pl.when(pl.program_id(0) == pl.num_programs(0) - 1)
    def _():
        store_grads(outs, (0, units // 2), acc, 0, rows, place_ref)
        store_grads(outs, (units // 2, units // 2 + 2 * STATE), acc, units, rows, place_ref)


def norm_backward(grad_normed, hidden, grad_out, gain):
    scale = lax.rsqrt(jnp.mean(hidden * hidden, axis=1, keepdims=True) + epsilon)
    weighted = grad_normed * gain
    shared = jnp.mean(weighted * hidden, axis=1, keepdims=True) * (scale * scale * scale)
    return grad_out + scale * weighted - hidden * shared, grad_normed * hidden * scale


VMEM_LIMIT = 60 * 1024 * 1024


def spreader_of(units):
    one = (np.arange(LANES)[:, None] == np.arange(units)[None, :] // HEAD_DIM).astype(np.float32)
    return jnp.asarray(np.concatenate([one, one], axis=0), bf16)


def rows_spec(width, last=None):
    if last is None:
        return pl.BlockSpec((SPAN, width), lambda i: (i, 0))
    return pl.BlockSpec((SPAN, width), lambda i: (last - i, 0))


def whole_spec(array):
    return pl.BlockSpec(array.shape, lambda i: (0,) * array.ndim)


def call(kernel, inputs, outputs, scratch, chunks, flops):
    return pl.pallas_call(
        kernel,
        grid=(chunks,),
        in_specs=[spec for _, spec in inputs],
        out_specs=[spec for _, _, spec in outputs],
        out_shape=[jax.ShapeDtypeStruct(shape, dtype) for shape, dtype, _ in outputs],
        scratch_shapes=[pltpu.VMEM(shape, dtype) for shape, dtype in scratch],
        compiler_params=pltpu.CompilerParams(vmem_limit_bytes=VMEM_LIMIT, dimension_semantics=("arbitrary",)),
        cost_estimate=pl.CostEstimate(flops=flops, bytes_accessed=500_000, transcendentals=0),
    )(*[array for array, _ in inputs])


def fixed(array):
    return array, whole_spec(array)


def scalars(array):
    return array, pl.BlockSpec(memory_space=pltpu.SMEM)


def grad_outputs(width, rows, columns):
    outputs = []
    for _, _, _, count in pieces_of(rows, width // (2 * rows)):
        shape = (count * rows, columns)
        outputs.append((shape, bf16, pl.BlockSpec(shape, lambda i: (0, 0))))
    return outputs


def awaited(arrays):
    return [(array, pl.BlockSpec(memory_space=pl.ANY)) for array in arrays]


def scan_forward(place, rows, h, parts, weights, marks, segment_row, params):
    length, width = h.shape
    units = params[0].shape[1]
    chunks = length // SPAN
    second = parts is not None
    inputs = [scalars(place), (h, rows_spec(width))]
    outputs = []
    if second:
        inputs += [(part, rows_spec(width + LANES)) for part in parts]
        outputs.append(((length, width), bf16, rows_spec(width)))
    inputs += [fixed(w) for w in weights]
    inputs += [(marks, rows_spec(LANES)), (segment_row, pl.BlockSpec((1, SPAN), lambda i: (0, i)))]
    inputs += [fixed(p) for p in params] + [fixed(spreader_of(units))]
    outputs.append(((8, width), f32, pl.BlockSpec((8, width), lambda i: (0, 0))))
    outputs.append(((length, width), bf16, rows_spec(width)))
    for columns in (units, units, units, 2 * STATE, 2 * STATE, LANES):
        outputs.append(((length, columns), f32, rows_spec(columns)))
    outputs.append(((chunks, STATE, units), f32, pl.BlockSpec((1, STATE, units), lambda i: (i, 0, 0))))
    scratch = [
        ((STATE, units), f32),
        ((8, units), f32),
        ((8, 2 * STATE), f32),
        ((8, width), f32),
        ((width, units + 4 * STATE), bf16),
    ]
    kernel = functools.partial(scan_forward_kernel, second, units // HEAD_DIM, rows, len(weights))
    results = call(kernel, inputs, outputs, scratch, chunks, 2_000_000_000)
    if not second:
        results = [h] + list(results)
    return results[0], results[1], results[2], results[3:]


def gate_forward(place, rows, normed, y, weights, params):
    length, width = normed.shape
    units = params[0].shape[1]
    inputs = [scalars(place), (normed, rows_spec(width)), (y, rows_spec(units))] + [fixed(w) for w in weights] + [fixed(params[0])]
    outputs = [((length, units), f32, rows_spec(units)), ((length, width + LANES), bf16, rows_spec(width + LANES))]
    scratch = [((width, units), bf16)] * 2
    return call(functools.partial(gate_forward_kernel, rows, len(weights)), inputs, outputs, scratch, length // SPAN, 1_000_000_000)


def gate_backward(place, rows, h, parts, extra, normed, gate, y, weights, marks, params):
    length, width = normed.shape
    units = params[0].shape[1]
    second = len(extra) == 1
    inputs = [scalars(place)] + ([(h, rows_spec(width))] if second else [])
    inputs += [(part, rows_spec(width + LANES)) for part in parts]
    inputs += [(array, rows_spec(width)) for array in extra[:4]] + [fixed(gain) for gain in extra[4:]]
    inputs += [(normed, rows_spec(width)), (gate, rows_spec(units)), (y, rows_spec(units))]
    inputs += [fixed(w) for w in weights] + [(marks, rows_spec(LANES)), fixed(params[0])]
    outputs = [((length, width), bf16, rows_spec(width))] if second else []
    outputs += [((length, width), f32, rows_spec(width)), ((length, units), bf16, rows_spec(units)), ((length, width), f32, rows_spec(width))]
    outputs += grad_outputs(width, rows, units)
    outputs.append(((8, units), f32, pl.BlockSpec((8, units), lambda i: (0, 0))))
    scratch = [((width, units), bf16)] * 2 + [((width, units), f32)] * 2 + [((8, units), f32)]
    results = call(functools.partial(gate_backward_kernel, second, rows, len(weights)), inputs, outputs, scratch, length // SPAN, 2_000_000_000)
    if not second:
        results = [None] + list(results)
    return results


def scan_backward(place, rows, grad_y, gate_part, weights, marks, segment_row, params, saved):
    length, width = gate_part.shape
    units = params[0].shape[1]
    chunks = length // SPAN
    last = chunks - 1
    inputs = [scalars(place), (grad_y, rows_spec(units, last)), (gate_part, rows_spec(width, last))]
    inputs += [fixed(w) for w in weights]
    inputs += [(marks, rows_spec(LANES, last)), (segment_row, pl.BlockSpec((1, SPAN), lambda i: (0, last - i)))]
    inputs += [fixed(p) for p in params] + [fixed(spreader_of(units))]
    inputs += [(s, rows_spec(s.shape[1], last)) for s in saved[:6]]
    inputs.append((saved[6], pl.BlockSpec((1, STATE, units), lambda i: (last - i, 0, 0))))
    columns = units + 4 * STATE
    outputs = [((length, columns), bf16, rows_spec(columns, last)), ((length, width), bf16, rows_spec(width, last))]
    for columns in (units, 2 * STATE):
        outputs.append(((8, columns), f32, pl.BlockSpec((8, columns), lambda i: (0, 0))))
    scratch = [
        ((width, units + 4 * STATE), bf16),
        ((STATE, units), f32),
        ((STATE, units), f32),
        ((8, units), f32),
        ((8, 2 * STATE), f32),
        ((8, units), f32),
        ((8, 2 * STATE), f32),
    ]
    kernel = functools.partial(scan_backward_kernel, units // HEAD_DIM, rows, len(weights))
    return call(kernel, inputs, outputs, scratch, chunks, 3_000_000_000)


def weight_grads(place, rows, normed, grads, ready):
    length, width = normed.shape
    columns = grads.shape[1]
    inputs = [scalars(place), (normed, rows_spec(width)), (grads, rows_spec(columns))] + awaited(ready)
    outputs = grad_outputs(width, rows, columns // 2)
    scratch = [((width, columns), f32)]
    return call(functools.partial(weight_grads_kernel, rows), inputs, outputs, scratch, length // SPAN, 500_000_000)


def finish_kernel(place_ref, own_ref, other_ref, h_ref, grad_out_ref, gain_ref, *refs):
    grad_ref, low_ref, sums_ref, sums = refs[-4:]

    @pl.when(pl.program_id(0) == 0)
    def _():
        sums[...] = jnp.zeros_like(sums)

    grad_normed = own_ref[...].astype(f32) + other_ref[...].astype(f32)
    next_grad = grad_out_ref[...]
    grad, gain_term = norm_backward(grad_normed, h_ref[...].astype(f32), next_grad.astype(bf16).astype(f32), gain_ref[0:1, :])
    rows = jnp.where(place_ref[3] == 0, grad, next_grad)
    grad_ref[...] = rows
    low_ref[...] = rows.astype(bf16)
    sums[0:1, :] += jnp.sum(gain_term, axis=0, keepdims=True)
    sums_ref[...] = sums[...]


def finish(place, own, other, h, grad_out, gain, ready):
    length, width = h.shape
    inputs = [scalars(place)] + [(rows, rows_spec(width)) for rows in (own, other, h, grad_out)] + [fixed(gain)]
    inputs += awaited(ready)
    outputs = [((length, width), f32, rows_spec(width)), ((length, width), bf16, rows_spec(width))]
    outputs.append(((8, width), f32, pl.BlockSpec((8, width), lambda i: (0, 0))))
    return call(finish_kernel, inputs, outputs, [((8, width), f32)], length // SPAN, 30_000_000)


def placed_kernel(place_ref, own_ref, away_ref, *refs):
    out_ref = refs[-1]
    own = pl.program_id(0) == place_ref[1]
    out_ref[0] = jnp.where(own, own_ref[...].astype(f32), away_ref[...].astype(f32)).astype(out_ref.dtype)


def placed_rows(place, rows, away, ready=()):
    half, width = away.shape
    return pl.pallas_call(
        placed_kernel,
        grid_spec=pltpu.PrefetchScalarGridSpec(
            num_scalar_prefetch=1,
            grid=(2,),
            in_specs=[
                pl.BlockSpec((half, width), lambda m, place: (place[1], 0)),
                pl.BlockSpec((half, width), lambda m, place: (0, 0)),
            ]
            + [pl.BlockSpec(memory_space=pl.ANY)] * len(ready),
            out_specs=pl.BlockSpec((1, half, width), lambda m, place: (m, 0, 0)),
        ),
        out_shape=jax.ShapeDtypeStruct((2, half, width), rows.dtype),
        compiler_params=pltpu.CompilerParams(vmem_limit_bytes=VMEM_LIMIT, dimension_semantics=("arbitrary",)),
        cost_estimate=pl.CostEstimate(flops=0, bytes_accessed=500_000, transcendentals=0),
    )(place, rows, away, *ready)


def marks_kernel(place_ref, lengths_ref, segments_ref, marks_ref, row_ref):
    turn, rank = place_ref[1], place_ref[2]
    micro, sequences = lengths_ref.shape
    length = segments_ref.shape[1]
    total = jnp.int32(0)
    for batch in range(micro):
        total = lax.fori_loop(0, sequences, lambda i, t: t + lengths_ref[batch, i], total)
    weight = 2.0 * (micro * sequences * length) / jnp.full((1, length), total, jnp.int32).astype(f32)
    position = lax.broadcasted_iota(jnp.int32, (1, length), 1)
    segment = jnp.where(turn == 0, segments_ref[0:1, :], segments_ref[1:2, :])
    wide = jnp.broadcast_to(segment, (8, length))

    def same(lag):
        moved = pltpu.roll(wide, lag % length, 1)[0:1]
        inside = (position >= lag) & (position < length + lag)
        return jnp.where(inside & (moved == segment), 1.0, 0.0)

    before = jnp.full((1, length), -1, jnp.int32)
    end = before
    for block in range(length // SPAN):
        here = (position >= block * SPAN) & (position < (block + 1) * SPAN)
        end = jnp.where(here, segment[:, (block + 1) * SPAN - 1 : (block + 1) * SPAN], end)
        if block:
            before = jnp.where(here, segment[:, block * SPAN - 1 : block * SPAN], before)
    as_float = segment.astype(f32)
    rows = [same(1), same(2), same(3)]
    rows += [jnp.where(segment == before, 1.0, 0.0), jnp.where(segment == end, 1.0, 0.0), as_float]
    rows += [same(-1), same(-2), same(-3)]
    rows += [jnp.where(position < lengths_ref[turn, rank], weight, 0.0), jnp.full((1, length), turn, jnp.int32).astype(f32)]
    rows.append(jnp.zeros((LANES - len(rows), length), f32))
    marks_ref[...] = jnp.transpose(jnp.concatenate(rows, axis=0))
    row_ref[...] = as_float


def token_marks(place, lengths, segments):
    length = segments.shape[1]
    return pl.pallas_call(
        marks_kernel,
        in_specs=[pl.BlockSpec(memory_space=pltpu.SMEM)] * 2 + [pl.BlockSpec(memory_space=pltpu.VMEM)],
        out_shape=[jax.ShapeDtypeStruct((length, LANES), f32), jax.ShapeDtypeStruct((1, length), f32)],
        compiler_params=pltpu.CompilerParams(vmem_limit_bytes=VMEM_LIMIT),
        cost_estimate=pl.CostEstimate(flops=0, bytes_accessed=500_000, transcendentals=0),
    )(place, lengths, segments)


def three_parts(value):
    high = value.astype(bf16)
    rest = value - high.astype(f32)
    middle = rest.astype(bf16)
    return high, middle, (rest - middle.astype(f32)).astype(bf16)


PARAM_ROWS = 16


def pack_kernel(
    place_ref, zx_ref, bc_ref, dt_ref, gain_ref, out_ref, conv_ref, gate_gain_ref, states_conv_ref, bias_ref, rate_ref, skip_ref, kept_ref, sent_ref
):
    turn, core = place_ref[1], place_ref[3]
    rows = zx_ref.shape[0]
    half = zx_ref.shape[2] // 2
    heads_half = dt_ref.shape[0] // 2
    lane = lax.broadcasted_iota(jnp.int32, (1, LANES), 1)
    bc = jnp.where(turn == 0, bc_ref[:, :STATE], bc_ref[:, STATE:])
    diagonal = lax.broadcasted_iota(jnp.int32, (rows, rows), 0) == lax.broadcasted_iota(jnp.int32, (rows, rows), 1)
    gain = jnp.sum(jnp.where(diagonal, gain_ref[...].astype(f32), 0.0), axis=1, keepdims=True)
    head = lax.broadcasted_iota(jnp.int32, (2 * heads_half, LANES), 0)
    column = lax.broadcasted_iota(jnp.int32, (2 * heads_half, LANES), 1)
    shared = jnp.concatenate([states_conv_ref[...], jnp.zeros((PARAM_ROWS - 5, 2 * STATE), bf16)], axis=0)
    split = [part.astype(f32) for ref in (bias_ref, rate_ref, skip_ref) for part in three_parts(ref[...])]
    heads = jnp.concatenate(split + [jnp.zeros((PARAM_ROWS - 9, split[0].shape[1]), f32)], axis=0)
    heads = jnp.concatenate([heads, jnp.zeros((PARAM_ROWS, LANES - heads.shape[1]), f32)], axis=1).astype(bf16)
    for ref, part in ((kept_ref, core), (sent_ref, 1 - core)):
        first = part == 0

        def chosen(array, start):
            return jnp.where(first, array[:, start : start + half], array[:, start + half : start + 2 * half])

        ref[:rows, :half] = chosen(zx_ref[:, 1, :], 0)
        ref[:rows, half : half + STATE] = bc
        taken = (head == column + part * heads_half) & (column < heads_half)
        own_steps = tn(dt_ref[...], jnp.where(taken, 1.0, 0.0).astype(bf16))
        ref[:rows, half + STATE : half + 2 * STATE] = jnp.where(lane == LANES // 2, gain, own_steps).astype(bf16)
        ref[:rows, half + 2 * STATE : 2 * half + 2 * STATE] = chosen(zx_ref[:, 0, :], 0)
        ref[:rows, 2 * half + 2 * STATE :] = chosen(out_ref, 0)
        ref[rows:, :] = jnp.zeros((PARAM_ROWS, ref.shape[1]), bf16)
        channels = jnp.concatenate([chosen(conv_ref, 0), chosen(gate_gain_ref, 0)], axis=0)
        ref[rows:, :half] = jnp.concatenate([channels, jnp.zeros((PARAM_ROWS - 6, half), bf16)], axis=0)
        ref[rows:, half : half + 2 * STATE] = shared
        ref[rows:, half + 2 * STATE : half + 2 * STATE + LANES] = heads


def plain_call(kernel, place, inputs, outputs, ready=()):
    count = len(ready)
    body = kernel if not count else lambda place_ref, *refs: kernel(place_ref, *refs[count:])
    return pl.pallas_call(
        body,
        in_specs=[pl.BlockSpec(memory_space=pltpu.SMEM)]
        + [pl.BlockSpec(memory_space=pl.ANY)] * count
        + [pl.BlockSpec(memory_space=pltpu.VMEM)] * len(inputs),
        out_shape=[jax.ShapeDtypeStruct(shape, dtype) for shape, dtype in outputs],
        compiler_params=pltpu.CompilerParams(vmem_limit_bytes=VMEM_LIMIT),
        cost_estimate=pl.CostEstimate(flops=0, bytes_accessed=500_000, transcendentals=0),
    )(place, *ready, *inputs)


def unpack_kernel(place_ref, kept_ref, received_ref, *refs):
    scan_ref, middle_ref, gate_ref, params_ref, channels_ref = refs
    kept_first = place_ref[3] == 0
    kept, received = kept_ref[...], received_ref[...]
    first = jnp.where(kept_first, kept, received)
    second = jnp.where(kept_first, received, kept)
    rows, scan = scan_ref.shape
    half = channels_ref.shape[1]
    scan_ref[...] = first[:rows, :scan]
    middle_ref[:, : 2 * half] = first[:rows, scan:]
    middle_ref[:, 2 * half :] = second[:rows, :scan]
    gate_ref[...] = second[:rows, scan:]
    params_ref[0] = first[rows:, : scan + LANES]
    params_ref[1] = second[rows:, : scan + LANES]
    channels_ref[:PARAM_ROWS] = first[rows:, :half]
    channels_ref[PARAM_ROWS:] = second[rows:, :half]


def params_kernel(heads_half, place_ref, params_ref, channels_ref, spread_ref, *refs):
    turn, core = place_ref[1], place_ref[3]
    half = channels_ref.shape[1]
    lane = lax.broadcasted_iota(jnp.int32, (1, LANES), 1)
    for layer in range(2):
        small_ref, states_ref, head_ref = refs[3 * layer : 3 * layer + 3]
        rows = params_ref[layer].astype(f32)
        split = rows[:, half + 2 * STATE :]
        heads = [split[3 * i : 3 * i + 1] + split[3 * i + 1 : 3 * i + 2] + split[3 * i + 2 : 3 * i + 3] for i in range(3)]
        heads = jnp.concatenate(heads + [jnp.zeros((5, LANES), f32)], axis=0)
        moved = [pltpu.roll(heads, (LANES - start * heads_half) % LANES, 1) for start in range(4)]

        def of(index):
            return jnp.where(index == 0, moved[0], jnp.where(index == 1, moved[1], jnp.where(index == 2, moved[2], moved[3])))

        own, other = of(2 * turn + core), pltpu.roll(of(2 * (1 - turn) + core), heads_half, 1)
        heads = jnp.where(lane < heads_half, own, jnp.where(lane < 2 * heads_half, other, 0.0))
        head_ref[...] = jnp.concatenate([heads[0:1], jnp.exp(heads[1:2]), jnp.zeros((6, LANES), f32)], axis=0)
        high, middle, low = three_parts(jnp.broadcast_to(heads[2:3], (8, LANES)))
        once = spread_ref[:LANES]
        skips = (nn(high, once) + nn(middle, once) + nn(low, once))[0:1]
        own_rows = rows[0:6, :half]
        other_rows = channels_ref[PARAM_ROWS * layer : PARAM_ROWS * layer + 6].astype(f32)
        channels = jnp.concatenate([own_rows, other_rows], axis=1)
        small_ref[...] = jnp.concatenate([channels, skips, jnp.zeros_like(skips)], axis=0)
        states_ref[...] = jnp.concatenate([rows[0:5, half : half + 2 * STATE], jnp.zeros((3, 2 * STATE), f32)], axis=0)


def beside_kernel(place_ref, *refs):
    out = refs[-1]
    start = 0
    for ref in refs[:-1]:
        out[:, start : start + ref.shape[1]] = ref[...]
        start += ref.shape[1]


def split_kernel(place_ref, whole_ref, *outs):
    start = 0
    for out in outs:
        out[...] = whole_ref[:, start : start + out.shape[1]]
        start += out.shape[1]


def cross_kernel(place_ref, *refs):
    over_x, over_tensor = refs[-2:]
    start = 0
    for group in range(len(refs[:-2]) // 4):
        x_ref, y_ref, first_ref, second_ref = refs[4 * group : 4 * group + 4]
        columns = slice(start, start + x_ref.shape[1])
        start += x_ref.shape[1]
        half = first_ref.shape[0]
        over_x[:half, columns] = (x_ref[:half].astype(f32) + first_ref[...].astype(f32)).astype(bf16)
        over_x[half:, columns] = x_ref[half:]
        over_tensor[:half, columns] = y_ref[:half]
        over_tensor[half:, columns] = (y_ref[half:].astype(f32) + second_ref[...].astype(f32)).astype(bf16)


def join_kernel(groups, place_ref, *refs):
    out = refs[-1]
    start = 0
    for own, over_x, over_tensor, offset in groups:
        width = refs[own].shape[1]
        there = slice(offset, offset + width)
        total = refs[own][...].astype(f32) + refs[over_x][:, there].astype(f32) + refs[over_tensor][:, there].astype(f32)
        out[:, start : start + width] = total.astype(bf16)
        start += width


def owned_kernel(place_ref, first_ref, second_ref, beside_ref, across_ref, both_ref, zx_ref, bc_ref, dt_ref, out_ref):
    first = place_ref[3] == 0
    half = out_ref.shape[1] // 2
    heads_half = dt_ref.shape[1] // 2
    mine = jnp.where(first, first_ref[...], second_ref[...]).astype(f32)
    beside = beside_ref[...].astype(f32)
    lower, upper = jnp.where(first, mine, beside), jnp.where(first, beside, mine)
    gate = half + 2 * STATE
    for index, part in enumerate((lower, upper)):
        columns = slice(index * half, (index + 1) * half)
        zx_ref[:, 0, columns] = part[:, gate : gate + half]
        zx_ref[:, 1, columns] = part[:, :half]
        out_ref[:, columns] = part[:, gate + half :]
    own = mine[:, half : half + STATE] + beside[:, half : half + STATE]
    other = across_ref[...].astype(f32) + both_ref[...].astype(f32)
    straight = place_ref[1] == 0
    bc_ref[:, :STATE] = jnp.where(straight, own, other)
    bc_ref[:, STATE:] = jnp.where(straight, other, own)
    lane = lax.broadcasted_iota(jnp.int32, (1, LANES), 1)
    steps = slice(half + STATE, half + 2 * STATE)
    both = jnp.where(lane < heads_half, lower[:, steps], pltpu.roll(upper[:, steps], heads_half, 1))
    dt_ref[...] = both[:, : 2 * heads_half]


def small_kernel(gate0, scan0, states0, gate1, scan1, states1, gain_ref, out_ref):
    for layer, (gate, scan, states, gain) in enumerate(
        ((gate0, scan0, states0, gain_ref[0:1, :]), (gate1, scan1, states1, gate0[7:8, :]))
    ):
        start = 16 * layer
        out_ref[start : start + 5, :] = scan[0:5, :]
        out_ref[start + 5 : start + 6, :] = gate[5:6, :]
        out_ref[start + 6 : start + 7, :] = gain
        out_ref[start + 7 : start + 16, :] = jnp.zeros((9, out_ref.shape[1]), f32)
        out_ref[start + 8 : start + 15, : 2 * STATE] = states[0:7, :]


def fold_kernel(heads_half, place_ref, own_ref, away_ref, mine_ref, others_ref):
    first = place_ref[3] == 0
    half = mine_ref.shape[1]
    folded = []
    for layer in range(2):
        own, away = own_ref[16 * layer : 16 * layer + 16], away_ref[16 * layer : 16 * layer + 16]
        units = own[0:6, :half] + away[0:6, half:]
        gain = own[6:7] + away[6:7]
        total = own[8:16, :half] + away[8:16, :half]
        own_heads = jnp.concatenate([own[14:15, :LANES], own[13:14, : 2 * LANES]], axis=1)
        away_heads = jnp.concatenate([away[14:15, :LANES], away[13:14, : 2 * LANES]], axis=1)
        moved = pltpu.roll(jnp.broadcast_to(away_heads, (8, 3 * LANES)), 3 * LANES - heads_half, 1)[0:1]
        heads = jnp.concatenate([own_heads + moved, jnp.zeros((1, half - 3 * LANES), f32)], axis=1) if half > 3 * LANES else own_heads + moved
        zeros = jnp.zeros((2, half), f32)
        folded.append(jnp.concatenate([units, gain[:, :half], gain[:, half:], total[0:5], heads, zeros], axis=0))
    mine_ref[...] = jnp.where(first, folded[0], folded[1])
    others_ref[...] = jnp.where(first, folded[1], folded[0])


def small_outputs_kernel(heads_half, place_ref, total_ref, conv_ref, states_conv_ref, gate_gain_ref, heads_ref, gain_ref):
    first = place_ref[3] == 0
    half = total_ref.shape[1]
    here, there = total_ref[0:16], total_ref[16:32]
    lower, upper = jnp.where(first, here, there), jnp.where(first, there, here)
    conv_ref[:, :half] = lower[0:5]
    conv_ref[:, half:] = upper[0:5]
    gate_gain_ref[:, :half] = lower[5:6]
    gate_gain_ref[:, half:] = upper[5:6]
    states_conv_ref[...] = here[8:13, : 2 * STATE] + there[8:13, : 2 * STATE]
    lane = lax.broadcasted_iota(jnp.int32, (1, LANES), 1)
    for row in range(3):
        own = lower[13:14, row * LANES : (row + 1) * LANES]
        other = pltpu.roll(jnp.broadcast_to(upper[13:14, row * LANES : (row + 1) * LANES], (8, LANES)), heads_half, 1)[0:1]
        heads_ref[row : row + 1, :] = jnp.where(lane < heads_half, own, other)[:, : 2 * heads_half]
    gain_ref[:, :half] = here[6:7]
    gain_ref[:, half:] = here[7:8]


def tied(*values):
    return lax.optimization_barrier(values)


def swapped(block, axis):
    return lax.ppermute(block, axis, [(0, 1), (1, 0)])


def far_swapped(block):
    size = lax.axis_size("tensor")
    return lax.ppermute(block, ("section", "tensor"), [(i, 2 * size - 1 - i) for i in range(2 * size)])


def body(
    x_input,
    teacher,
    segment_ids,
    valid_len,
    norm_gain,
    w_zx,
    w_bc,
    w_dt,
    conv_x,
    conv_bc,
    dt_bias,
    a_log,
    d_skip,
    gnorm_gain,
    w_out,
):
    local_rows, width = x_input.shape[1:]
    ranks = lax.axis_size("dp")
    places = ranks // 2
    core = lax.axis_index("section")
    turn = lax.axis_index("tensor")
    rank = lax.axis_index("dp")
    place = jnp.stack([rank % 2, turn, rank, core]).astype(jnp.int32)
    on_first = core == 0
    block_rows = w_zx.shape[1]
    half = w_zx.shape[3] // 2
    units = 2 * half
    heads_half = w_dt.shape[2] // 2
    scan_columns = half + 2 * STATE
    line_groups = [[2 * index + start for index in range(places)] for start in range(2)]

    def by_layer(kept, received):
        return jnp.where(on_first, kept, received), jnp.where(on_first, received, kept)

    def x_swapped(block):
        return lax.ppermute(block, "dp", [(i, i ^ 1) for i in range(ranks)])

    def y_swapped(block):
        return swapped(block, "tensor")

    def line_gather(block):
        return lax.all_gather(block, "dp", axis_index_groups=line_groups, axis=0, tiled=True)

    def line_reduce(block):
        return lax.psum_scatter(block, "dp", axis_index_groups=line_groups, scatter_dimension=0, tiled=True)

    def line_total(block):
        if places != 4:
            return lax.psum(block, "dp", axis_index_groups=line_groups)

        def send(rows, moves):
            return lax.ppermute(rows, "dp", [(2 * a + start, 2 * b + start) for a, b in moves for start in range(2)])

        up, down = send(block, [(0, 1), (1, 2), (2, 3)]), send(block, [(1, 0), (2, 1), (3, 2)])
        up2, down2 = send(up, [(1, 2), (2, 3)]), send(down, [(2, 1), (1, 0)])
        far = send(jnp.where(rank // 2 == 1, up, down), [(1, 3), (2, 0)])
        return block + up + down + up2 + down2 + far

    pack_shape = (block_rows + PARAM_ROWS, scan_columns + units)
    kept, sent = plain_call(
        pack_kernel,
        place,
        (w_zx[0], w_bc[0], w_dt[0].T, norm_gain, w_out[0].T, conv_x[0], gnorm_gain, conv_bc[0], dt_bias, a_log, d_skip),
        [(pack_shape, bf16)] * 2,
    )
    received = swapped(sent, "section")
    scan_block, middle_block, gate_block, params_both, channels = plain_call(
        unpack_kernel,
        place,
        (kept, received),
        [
            ((block_rows, scan_columns), bf16),
            ((block_rows, units + scan_columns), bf16),
            ((block_rows, units), bf16),
            ((2, PARAM_ROWS, scan_columns + LANES), bf16),
            ((2 * PARAM_ROWS, half), bf16),
        ],
    )

    def plane_end(block, over_x, over_tensor):
        cut = places // 2 * block_rows
        return block, over_x, over_tensor, y_swapped(over_x[:cut]), x_swapped(over_tensor[cut:])

    def quarter(rows):
        away = lax.dynamic_index_in_dim(rows, 1 - turn, 0, keepdims=False)
        return lax.dynamic_slice_in_dim(away, core * (local_rows // 2), local_rows // 2, 0)

    def whole_rows(rows, here, beside):
        own = lax.dynamic_index_in_dim(rows, turn, 0, keepdims=False)
        other = jnp.concatenate(by_layer(here, beside), axis=0)
        return jnp.where(turn == 0, jnp.concatenate([own, other]), jnp.concatenate([other, own]))

    scan_line, here, channels = tied(line_gather(scan_block), y_swapped(quarter(x_input)), y_swapped(channels))
    scan_line, middle_block = tied(scan_line, middle_block)
    middle_line = line_gather(middle_block)
    scan_half = scan_line, x_swapped(scan_line), y_swapped(scan_line)
    x_rows = whole_rows(x_input, here, swapped(here, "section"))
    params = plain_call(
        functools.partial(params_kernel, heads_half),
        place,
        (params_both, channels, spreader_of(units)),
        [((8, units), f32), ((8, 2 * STATE), f32), ((8, LANES), f32)] * 2,
    )
    params = [params[:3], params[3:]]
    marks, segment_row = token_marks(place, valid_len, segment_ids[:, 0])
    over_x = x_swapped(gate_block)
    side = (gate_block, over_x, y_swapped(gate_block), y_swapped(over_x))
    side = plain_call(beside_kernel, place, side, [((block_rows, 4 * units), bf16)], (x_rows, marks, params[0][0]))[0]
    scan_first, side = tied(plane_end(*scan_half), side)
    middle_line, side = tied(middle_line, side)
    gate_second = (line_gather(side),)
    gate_line, next_line = plain_call(
        split_kernel,
        place,
        (middle_line,),
        [((places * block_rows, units), bf16), ((places * block_rows, scan_columns), bf16)],
        (scan_first[4],),
    )

    gate_half = gate_line, x_swapped(gate_line), y_swapped(gate_line)
    next_half = next_line, x_swapped(next_line), y_swapped(next_line)
    results = scan_forward(place, block_rows, x_rows, None, scan_first, marks, segment_row, params[0])
    results, gate_half, next_half = tied(results, gate_half, next_half)
    _, gain_first, normed_first, saved_first = results
    gate_first = plane_end(*gate_half)
    results = gate_forward(place, block_rows, normed_first, saved_first[2], gate_first, params[0])
    (gated_first, part), scan_second = tied(results, plane_end(*next_half))
    parts_first = (part, swapped(part, "section"))
    parts_first, teacher, gate_second = tied(parts_first, teacher, gate_second)
    results = scan_forward(place, block_rows, x_rows, parts_first, scan_second, marks, segment_row, params[1])
    results, here = tied(results, y_swapped(quarter(teacher)))
    hidden, gain_second, normed_second, saved_second = results
    results = gate_forward(place, block_rows, normed_second, saved_second[2], gate_second, params[1])
    (gated_second, part), here, beside = tied(results, here, swapped(here, "section"))
    parts_second = (part, swapped(part, "section"))
    target = whole_rows(teacher, here, beside)

    def plane_start(pieces):
        return tuple(pieces[:3]), (y_swapped(pieces[3]), x_swapped(pieces[4]))

    def crossed(*groups):
        arrays = [array for pieces, came in groups for array in pieces[1:] + came]
        columns = sum(pieces[0].shape[1] for pieces, _ in groups)
        over_x, over_tensor = plain_call(cross_kernel, place, arrays, [((places * block_rows, columns), bf16)] * 2)
        return [pieces[0] for pieces, _ in groups], x_swapped(over_x), y_swapped(over_tensor)

    def joined(*groups, ready=()):
        arrays, spans = [], []
        for owns, over_x, over_tensor in groups:
            base = len(arrays)
            arrays += list(owns) + [over_x, over_tensor]
            offset = 0
            for index, own in enumerate(owns):
                spans.append((base + index, base + len(owns), base + len(owns) + 1, offset))
                offset += own.shape[1]
        columns = sum(arrays[span[0]].shape[1] for span in spans)
        kernel = functools.partial(join_kernel, spans)
        return plain_call(kernel, place, arrays, [((places * block_rows, columns), bf16)], ready)[0]

    results = gate_backward(
        place,
        block_rows,
        hidden,
        parts_second,
        (target,),
        normed_second,
        gated_second,
        saved_second[2],
        gate_second,
        marks,
        params[1],
    )
    produced, grad_out, grad_y, gate_part = results[:4]
    gate_reduce = plane_start(results[4:9])
    gate_sums_second = results[9]

    def away_rows(rows):
        return y_swapped(lax.dynamic_slice_in_dim(rows, (1 - turn) * local_rows, local_rows, 0))

    results = scan_backward(
        place, block_rows, grad_y, gate_part, scan_second, marks, segment_row, params[1], saved_second
    )
    results, gate_reduce, produced_away = tied(results, gate_reduce, away_rows(produced))
    grads, part, sums, states_sums = results
    sums_second = (gate_sums_second, sums, states_sums)
    results = weight_grads(place, block_rows, normed_second, grads, ())
    results, grad_parts = tied(results, (part, swapped(part, "section")))
    scan_reduce = plane_start(results)
    results = gate_backward(
        place,
        block_rows,
        x_rows,
        parts_first,
        (hidden, grad_out) + grad_parts + (gain_second,),
        normed_first,
        gated_first,
        saved_first[2],
        gate_first,
        marks,
        params[0],
    )
    results, scan_reduce = tied(results[1:], scan_reduce)
    grad_hidden, grad_y, gate_part = results[:3]
    crossed_second = crossed(scan_reduce, gate_reduce)
    gate_reduce = plane_start(results[3:8])
    gate_sums_first = results[8]
    results = scan_backward(
        place, block_rows, grad_y, gate_part, scan_first, marks, segment_row, params[0], saved_first
    )
    results, crossed_second, gate_reduce = tied(results, crossed_second, gate_reduce)
    grads, part, sums, states_sums = results
    sums_first = (gate_sums_first, sums, states_sums)
    results = weight_grads(place, block_rows, normed_first, grads, ())
    results, grad_parts = tied(results, (part, swapped(part, "section")))
    scan_reduce = plane_start(results)
    blocks_second = joined(crossed_second, ready=(results[0],))
    owned_second = line_reduce(blocks_second)
    gate_reduce, blocks_second = tied(gate_reduce, blocks_second)
    crossed_gate = crossed(gate_reduce)
    results = finish(place, *grad_parts, x_rows, grad_hidden, gain_first, (crossed_gate[0][0],))
    (grad_rows, grad_low, gain_sums), scan_reduce = tied(results, scan_reduce)
    crossed_scan = crossed(scan_reduce)
    layer_outputs = placed_rows(place, produced, produced_away, (crossed_scan[0][0],))
    blocks = joined(crossed_scan, crossed_gate, ready=(layer_outputs, owned_second))
    owned_first = line_reduce(blocks)
    smalls = plain_call(
        lambda place_ref, *refs: small_kernel(*refs),
        place,
        sums_first + sums_second + (gain_sums,),
        [((32, units), f32)],
        (blocks,),
    )[0]
    smalls_away = y_swapped(smalls)
    grad_low, smalls = tied(grad_low, smalls)
    mine, others = plain_call(
        functools.partial(fold_kernel, heads_half), place, (smalls, smalls_away), [((16, half), f32)] * 2
    )
    total = jnp.concatenate([mine, swapped(others, "section")])
    total = total + x_swapped(total)
    owned_first, boundary = tied(owned_first, placed_rows(place, grad_rows, away_rows(grad_low)))
    total = line_total(total)
    grad_conv, grad_states_conv, grad_gate_gain, grad_heads, gain_total = plain_call(
        functools.partial(small_outputs_kernel, heads_half),
        place,
        (total,),
        [((5, units), f32), ((5, 2 * STATE), f32), ((1, units), f32), ((3, 2 * heads_half), f32), ((1, width), f32)],
    )

    others = jnp.where(on_first, owned_second, owned_first)
    own_states, other_states = by_layer(owned_first[:, half : half + STATE], owned_second[:, half : half + STATE])
    grad_zx, grad_bc, grad_dt, grad_out_w = plain_call(
        owned_kernel,
        place,
        (owned_first, owned_second, swapped(others, "section"), y_swapped(own_states), far_swapped(other_states)),
        [((block_rows, 2, units), f32)] + [((block_rows, columns), f32) for columns in (2 * STATE, 2 * heads_half, units)],
        (boundary, layer_outputs, grad_conv),
    )
    return (
        layer_outputs[None],
        boundary[None],
        lax.dynamic_slice_in_dim(gain_total, rank * block_rows, block_rows, 1),
        grad_zx[None],
        grad_bc[None],
        grad_dt[None],
        grad_conv[None],
        grad_states_conv[None],
        grad_heads[1:2],
        grad_heads[2:3],
        grad_heads[0:1],
        grad_gate_gain,
        grad_out_w.T[None],
    )


def solution(mesh):
    placed = (
        P(None, ("dp", "tensor"), None),
        P(None, ("dp", "tensor"), None),
        P(None, "dp", None),
        P(),
        P("section", "dp"),
        P("section", "dp", None, "tensor"),
        P("section", "dp", None),
        P("section", "dp", "tensor"),
        P("section", None, "tensor"),
        P("section", None, None),
        P("section", None),
        P("section", None),
        P("section", None),
        P("section", "tensor"),
        P("section", "tensor", "dp"),
    )
    return jax.shard_map(
        body,
        mesh=mesh,
        in_specs=placed,
        out_specs=(
            P("section", None, ("dp", "tensor"), None),
            P("section", None, ("dp", "tensor"), None),
            P("section", "dp"),
            P("section", "dp", None, "tensor"),
            P("section", "dp", None),
            P("section", "dp", "tensor"),
            P("section", None, "tensor"),
            P("section", None, None),
            P("section", "tensor"),
            P("section", "tensor"),
            P("section", "tensor"),
            P("section", "tensor"),
            P("section", "tensor", "dp"),
        ),
        check_vma=False,
    )
```

```python
import functools

import jax
import jax.numpy as jnp
import numpy as np
from jax import lax
from jax.experimental import pallas as pl
from jax.experimental.pallas import tpu as pltpu
from jax.sharding import PartitionSpec as P

HEAD_DIM = 64
STATE = 128
SPAN = 256
WIDE = 512
LANES = 128

epsilon = 1e-05
f32 = jnp.float32
bf16 = jnp.bfloat16


def nn(left, right):
    return lax.dot_general(left, right, (((1,), (0,)), ((), ())), preferred_element_type=f32)


def nt(left, right):
    return lax.dot_general(left, right, (((1,), (1,)), ((), ())), preferred_element_type=f32)


def tn(left, right):
    return lax.dot_general(left, right, (((0,), (0,)), ((), ())), preferred_element_type=f32)


def high_low(value):
    high = value.astype(bf16)
    return high, (value - high.astype(f32)).astype(bf16)


def spread(per_head, spreader):
    return nn(jnp.concatenate(high_low(per_head), axis=1), spreader)


def gathered_heads(units, spreader):
    high, low = high_low(units)
    once = spreader[:LANES]
    return nt(high, once) + nt(low, once)


def running_sum(triangle, value):
    high = value.astype(bf16)
    rest = value - high.astype(f32)
    middle = rest.astype(bf16)
    low = (rest - middle.astype(f32)).astype(bf16)
    sums = nn(triangle, jnp.concatenate([high, middle, low], axis=1))
    return sums[:, :LANES] + sums[:, LANES : 2 * LANES] + sums[:, 2 * LANES :]


def softplus(value):
    return jnp.maximum(value, 0.0) + jnp.log1p(jnp.exp(-jnp.abs(value)))


def moved_down(block, edge, lag):
    return jnp.concatenate([edge, block], axis=0)[8 - lag : 8 - lag + block.shape[0]]


def moved_up(block, edge, lag):
    return jnp.concatenate([block, edge], axis=0)[lag : lag + block.shape[0]]


def decay_parts(steps_in, head_rows, marks, heads):
    lane = lax.broadcasted_iota(jnp.int32, (1, LANES), 1)
    live = lane < heads
    shifted = steps_in + head_rows[0:1, :LANES]
    steps = jnp.where(live, softplus(shifted), 0.0)
    rates = head_rows[1:2, :LANES]
    log_steps = -steps * rates
    row = lax.broadcasted_iota(jnp.int32, (SPAN, SPAN), 0)
    column = lax.broadcasted_iota(jnp.int32, (SPAN, SPAN), 1)
    lower = (row >= column).astype(bf16)
    logs = running_sum(lower, log_steps)
    last = logs[SPAN - 1 : SPAN]
    entry = jnp.exp(logs) * marks[:, 3:4]
    tail = jnp.exp(last - logs) * marks[:, 4:5]
    through = jnp.exp(last) * marks[SPAN - 1 : SPAN, 3:4]
    entry = jnp.where(live, entry, 0.0)
    tail = jnp.where(live, tail, 0.0)
    through = jnp.where(live, through, 0.0)
    return shifted, steps, log_steps, logs, entry, tail, through, row, column


def linked_mask(row, column, marks, segment_row):
    linked = (row >= column) & (marks[:, 5:6] == segment_row)
    return jnp.where(linked, 0.0, -1e30)


def branch_of(own_ref, other_ref, units):
    width = own_ref.shape[1] - LANES
    own = own_ref[...].astype(f32)
    other = other_ref[...].astype(f32)
    total = own[:, :width] + other[:, :width]
    own_squares = own[:, width : width + 1] + own[:, width + 1 : width + 2]
    other_squares = other[:, width : width + 1] + other[:, width + 1 : width + 2]
    inverse = lax.rsqrt((own_squares + other_squares) / (2 * units) + epsilon)
    return total * inverse, total, inverse


def pieces_of(rows, places):
    half = places // 2
    return ((False, False, 0, places), (True, False, 0, places), (False, True, 0, places), (True, True, 0, half), (True, True, half, places - half))


def load_weights(weights, start, refs, columns, rows, place_ref):
    first, last = columns
    places = weights.shape[0] // (2 * rows)
    mine = place_ref[0]
    size = refs[0].shape[1] // 4
    for index, (moved, turned, base, count) in enumerate(pieces_of(rows, places)):
        if len(refs) == 1:
            if index == 4:
                break
            ref, offset, base, count = refs[0], index * size, 0, places
        else:
            ref, offset = refs[index], 0
        place = 1 - mine if moved else mine
        target = start + (last - first if turned else 0)
        for step in range(count):
            row = pl.multiple_of((2 * (base + step) + place) * rows, 32)
            weights[pl.ds(row, rows), target : target + last - first] = ref[step * rows : (step + 1) * rows, offset + first : offset + last]


def store_grads(refs, columns, acc, start, rows, place_ref, base=0):
    first, last = columns
    places = acc.shape[0] // (2 * rows)
    mine = place_ref[0]
    size = refs[0].shape[1] // 4
    for index, (moved, turned, origin, count) in enumerate(pieces_of(rows, places)):
        if len(refs) == 1:
            if index == 4:
                break
            ref, offset, origin, count = refs[0], index * size + base, 0, places
        else:
            ref, offset = refs[index], 0
        place = 1 - mine if moved else mine
        source = start + (last - first if turned else 0)
        for step in range(count):
            row = pl.multiple_of((2 * (origin + step) + place) * rows, 32)
            block = acc[pl.ds(row, rows), source : source + last - first]
            ref[step * rows : (step + 1) * rows, offset + first : offset + last] = block.astype(bf16)


def scan_forward_kernel(second, heads, rows, pieces, *refs):
    place_ref, refs = refs[0], refs[1:]
    if second:
        (h_ref, own_ref, other_ref), refs = refs[:3], refs[3:]
    else:
        (h_ref,), refs = refs[:1], refs[1:]
    parts, refs = refs[:pieces], refs[pieces:]
    (marks_ref, segment_ref, small_ref, states_small_ref, head_ref, spread_ref), refs = refs[:6], refs[6:]
    if second:
        h_out, refs = refs[0], refs[1:]
    gain_ref, refs = refs[0], refs[1:]
    normed_ref, raw_ref, conv_ref, y_ref, raw_states_ref, conv_states_ref, steps_ref, entry_state_ref = refs[:8]
    state, raw_edge, states_edge, gain, weights = refs[8:]
    units = raw_ref.shape[1]

    @pl.when(pl.program_id(0) == 0)
    def _():
        state[...] = jnp.zeros_like(state)
        raw_edge[...] = jnp.zeros_like(raw_edge)
        states_edge[...] = jnp.zeros_like(states_edge)
        load_weights(weights, 0, parts, (0, units // 2), rows, place_ref)
        load_weights(weights, units, parts, (units // 2, units // 2 + 2 * STATE), rows, place_ref)
        steps_columns = weights[:, units + STATE : units + STATE + LANES].astype(f32)
        gain[...] = jnp.broadcast_to(jnp.transpose(steps_columns)[LANES // 2 : LANES // 2 + 1, :], gain.shape)
        gain_ref[...] = gain[...]

    hidden = h_ref[...].astype(f32)
    if second:
        rounded = (hidden + branch_of(own_ref, other_ref, units)[0]).astype(bf16)
        h_out[...] = rounded
        hidden = rounded.astype(f32)
    scale = lax.rsqrt(jnp.mean(hidden * hidden, axis=1, keepdims=True) + epsilon)
    normed = (hidden * scale * gain[0:1, :]).astype(bf16)
    normed_ref[...] = normed
    projected = nn(normed, weights[...])
    raw = projected[:, :units]
    first, second_part = projected[:, units : units + 2 * STATE], projected[:, units + 2 * STATE :]
    marks = marks_ref[...]
    turned = marks[0:1, 10:11] > 0.5
    raw_states = jnp.concatenate(
        [
            jnp.where(turned, second_part[:, :STATE], first[:, :STATE]),
            jnp.where(turned, first[:, :STATE], second_part[:, :STATE]),
        ],
        axis=1,
    )
    lane = lax.broadcasted_iota(jnp.int32, (1, LANES), 1)
    steps_in = jnp.where(lane < heads // 2, first[:, STATE:], pltpu.roll(second_part[:, STATE:], heads // 2, 1))
    raw_ref[...] = raw
    raw_states_ref[...] = raw_states
    steps_ref[...] = steps_in

    def conv(block, edge, taps):
        total = taps[4:5] + taps[3:4] * block
        for lag in (1, 2, 3):
            total = total + taps[3 - lag : 4 - lag] * (moved_down(block, edge, lag) * marks[:, lag - 1 : lag])
        return total

    taps = small_ref[...]
    conved = conv(raw, raw_edge[...], taps)
    conv_ref[...] = conved
    conved_states = conv(raw_states, states_edge[...], states_small_ref[...])
    conv_states_ref[...] = conved_states
    raw_edge[...] = raw[SPAN - 8 :]
    states_edge[...] = raw_states[SPAN - 8 :]
    values = conved * jax.nn.sigmoid(conved)
    states_in = conved_states * jax.nn.sigmoid(conved_states)
    b_rows = states_in[:, :STATE].astype(bf16)
    c_rows = states_in[:, STATE:].astype(bf16)
    _, steps, _, logs, entry, tail, through, row, column = decay_parts(steps_in, head_ref[...], marks, heads)
    spreader = spread_ref[...]
    scaled = values * spread(steps, spreader)
    mask = linked_mask(row, column, marks, segment_ref[...])
    scores = nt(c_rows, b_rows)
    logs_across = jnp.transpose(logs)
    pieces = []
    for pair in range(heads // 2):
        mixes = []
        for head in (2 * pair, 2 * pair + 1):
            factor = jnp.exp(logs[:, head : head + 1] - logs_across[head : head + 1, :] + mask)
            mixes.append((factor * scores).astype(bf16))
        block = scaled[:, pair * LANES : (pair + 1) * LANES]
        left = jnp.where(lane < HEAD_DIM, block, 0.0).astype(bf16)
        right = jnp.where(lane < HEAD_DIM, 0.0, block).astype(bf16)
        pieces.append(nn(jnp.concatenate(mixes, axis=1), jnp.concatenate([left, right], axis=0)))
    inside = jnp.concatenate(pieces, axis=1)
    held = state[...]
    entry_state_ref[0] = held
    across = nn(c_rows, held.astype(bf16)) * spread(entry, spreader)
    through_row = spread(jnp.broadcast_to(through, (8, LANES)), spreader)[0:1]
    state[...] = through_row * held + tn(b_rows, (spread(tail, spreader) * scaled).astype(bf16))
    y_ref[...] = inside + across + taps[6:7] * values


def gate_forward_kernel(rows, pieces, place_ref, normed_ref, y_ref, *refs):
    parts, refs = refs[:pieces], refs[pieces:]
    small_ref, gate_ref, part_ref, weights, out_weights = refs

    @pl.when(pl.program_id(0) == 0)
    def _():
        half = weights.shape[1] // 2
        load_weights(weights, 0, parts, (0, half), rows, place_ref)
        load_weights(out_weights, 0, parts, (half, 2 * half), rows, place_ref)

    gate = nn(normed_ref[...], weights[...])
    gate_ref[...] = gate
    gated = y_ref[...] * (gate * jax.nn.sigmoid(gate))
    squares = jnp.sum(gated * gated, axis=1, keepdims=True)
    part = nt((gated * small_ref[5:6]).astype(bf16), out_weights[...])
    width = part.shape[1]
    part_ref[:, :width] = part.astype(bf16)
    high, low = high_low(squares)
    lane = lax.broadcasted_iota(jnp.int32, (1, LANES), 1)
    part_ref[:, width:] = jnp.where(lane == 0, high, jnp.where(lane == 1, low, jnp.zeros_like(low)))


def gate_backward_kernel(second, rows, pieces, grad_arrays, base, *refs):
    place_ref, refs = refs[0], refs[1:]
    if second:
        (h_ref, own_ref, other_ref, target_ref), refs = refs[:4], refs[4:]
    else:
        (own_ref, other_ref, next_h_ref, next_out_ref, grad_own_ref, grad_other_ref, next_gain_ref), refs = refs[:7], refs[7:]
    (normed_ref, gate_ref, y_ref), parts, refs = refs[:3], refs[3 : 3 + pieces], refs[3 + pieces :]
    (marks_ref, small_ref), refs = refs[:2], refs[2:]
    if second:
        out_ref, refs = refs[0], refs[1:]
    (grad_out_ref, grad_y_ref, part_ref), refs = refs[:3], refs[3:]
    grads, sums_ref, refs = refs[:grad_arrays], refs[grad_arrays], refs[grad_arrays + 1 :]
    weights, out_weights, acc_z, acc_o, sums = refs
    units = y_ref.shape[1]

    @pl.when(pl.program_id(0) == 0)
    def _():
        load_weights(weights, 0, parts, (0, units // 2), rows, place_ref)
        load_weights(out_weights, 0, parts, (units // 2, units), rows, place_ref)
        for ref in (acc_z, acc_o, sums):
            ref[...] = jnp.zeros_like(ref)

    branch, total, inverse = branch_of(own_ref, other_ref, units)
    if second:
        produced = h_ref[...].astype(f32) + branch
        out_ref[...] = jnp.where(place_ref[3] == 0, h_ref[...].astype(f32), produced).astype(bf16)
        grad_out = marks_ref[:, 9:10] * (produced - target_ref[...])
    else:
        grad_normed = grad_own_ref[...].astype(f32) + grad_other_ref[...].astype(f32)
        grad_out, gain_term = norm_backward(grad_normed, next_h_ref[...].astype(f32), next_out_ref[...], next_gain_ref[0:1, :])
        sums[7:8, :] += jnp.sum(gain_term, axis=0, keepdims=True)
    grad_out_ref[...] = grad_out
    grad = grad_out.astype(bf16)
    inner = jnp.sum(grad.astype(f32) * total, axis=1, keepdims=True) * (inverse * inverse * inverse) / (2 * units)
    gain = small_ref[5:6]
    gate = gate_ref[...]
    y = y_ref[...]
    gate_sig = jax.nn.sigmoid(gate)
    gate_silu = gate * gate_sig
    gated = y * gate_silu
    gated_unit = gated * inverse
    grad_mixed = nn(grad, out_weights[...])
    acc_o[...] += tn(grad, (gated_unit * gain).astype(bf16))
    sums[5:6, :] += jnp.sum(grad_mixed * gated_unit, axis=0, keepdims=True)
    grad_gated = grad_mixed * gain * inverse - gated * inner
    grad_gate = (grad_gated * y * (gate_sig * (1.0 + gate * (1.0 - gate_sig)))).astype(bf16)
    grad_y_ref[...] = (grad_gated * gate_silu).astype(bf16)
    acc_z[...] += tn(normed_ref[...], grad_gate)
    part_ref[...] = nt(grad_gate, weights[...])

    @pl.when(pl.program_id(0) == pl.num_programs(0) - 1)
    def _():
        store_grads(grads, (0, units // 2), acc_z, 0, rows, place_ref, base)
        store_grads(grads, (units // 2, units), acc_o, 0, rows, place_ref, base)
        sums_ref[...] = sums[...]


def scan_backward_kernel(heads, rows, pieces, *refs):
    (place_ref, grad_y_ref, gate_part_ref), parts, refs = refs[:3], refs[3 : 3 + pieces], refs[3 + pieces :]
    (marks_ref, segment_ref, small_ref, states_small_ref, head_ref, spread_ref), refs = refs[:6], refs[6:]
    (raw_ref, conv_ref, y_ref, raw_states_ref, conv_states_ref, steps_ref, entry_state_ref), refs = refs[:7], refs[7:]
    (grads_ref, part_ref, sums_ref, states_sums_ref), refs = refs[:4], refs[4:]
    weights, dstate, next_state, conv_edge, states_edge, sums, states_sums = refs
    step = pl.program_id(0)
    units = raw_ref.shape[1]

    @pl.when(step == 0)
    def _():
        for ref in (dstate, next_state, conv_edge, states_edge, sums, states_sums):
            ref[...] = jnp.zeros_like(ref)
        load_weights(weights, 0, parts, (0, units // 2), rows, place_ref)
        load_weights(weights, units, parts, (units // 2, units // 2 + 2 * STATE), rows, place_ref)

    marks = marks_ref[...]
    taps = small_ref[...]
    y = y_ref[...]
    grad_y_low = grad_y_ref[...]
    grad_y = grad_y_low.astype(f32)
    conved = conv_ref[...]
    value_sig = jax.nn.sigmoid(conved)
    values = conved * value_sig
    conved_states = conv_states_ref[...]
    states_sig = jax.nn.sigmoid(conved_states)
    states_in = conved_states * states_sig
    b_rows = states_in[:, :STATE].astype(bf16)
    c_rows = states_in[:, STATE:].astype(bf16)
    shifted, steps, log_steps, logs, entry, tail, through, row, column = decay_parts(steps_ref[...], head_ref[...], marks, heads)
    spreader = spread_ref[...]
    spread_steps = spread(steps, spreader)
    spread_entry = spread(entry, spreader)
    spread_tail = spread(tail, spreader)
    through_row = spread(jnp.broadcast_to(through, (8, LANES)), spreader)[0:1]
    scaled_low = (values * spread_steps).astype(bf16)
    scaled = scaled_low.astype(f32)
    mask = linked_mask(column, row, marks, segment_ref[...])
    scores = nt(b_rows, c_rows)
    logs_across = jnp.transpose(logs)
    lane = lax.broadcasted_iota(jnp.int32, (1, LANES), 1)
    is_left = lane < HEAD_DIM
    zero = jnp.zeros((), bf16)
    grad_scores = jnp.zeros((SPAN, SPAN), f32)
    pieces = []
    for pair in range(heads // 2):
        columns = slice(pair * LANES, (pair + 1) * LANES)
        block, grad = scaled_low[:, columns], grad_y_low[:, columns]
        grad_left = jnp.where(is_left, grad, zero)
        grad_right = jnp.where(is_left, zero, grad)
        mixes = []
        for head, grad_one in ((2 * pair, grad_left), (2 * pair + 1, grad_right)):
            factor = jnp.exp(logs_across[head : head + 1, :] - logs[:, head : head + 1] + mask)
            mixes.append((factor * scores).astype(bf16))
            grad_scores = grad_scores + nt(block, grad_one) * factor
        pieces.append(nn(jnp.concatenate(mixes, axis=1), jnp.concatenate([grad_left, grad_right], axis=0)))
    held = entry_state_ref[0]
    held_low = held.astype(bf16)
    gradient = dstate[...]
    gradient_low = gradient.astype(bf16)
    grad_scaled = jnp.concatenate(pieces, axis=1) + spread_tail * nn(b_rows, gradient_low)
    grad_entry = (spread_entry * grad_y).astype(bf16)
    grad_scores_low = grad_scores.astype(bf16)
    grad_c = tn(grad_scores_low, b_rows) + nt(grad_entry, held_low)
    grad_b = nn(grad_scores_low, c_rows) + nt((spread_tail * scaled).astype(bf16), gradient_low)
    state_term = jnp.sum(gradient * next_state[...], axis=0, keepdims=True)
    dstate[...] = through_row * gradient + tn(c_rows, grad_entry)
    next_state[...] = held
    skip = taps[6:7]
    sums[6:7, :] += jnp.sum(grad_y * values, axis=0, keepdims=True)
    grad_logs = gathered_heads(grad_y * (y - skip * values) - scaled * grad_scaled, spreader)
    state_heads = gathered_heads(jnp.broadcast_to(state_term, (8, units)), spreader)[0:1]
    last_row = lax.broadcasted_iota(jnp.int32, (SPAN, 1), 0) == SPAN - 1
    grad_logs = grad_logs + jnp.where(last_row, state_heads, 0.0)
    grad_log_steps = running_sum((row <= column).astype(bf16), grad_logs)
    grad_steps = gathered_heads(grad_scaled * values, spreader) - head_ref[1:2, :LANES] * grad_log_steps
    grad_steps_in = jnp.where(lane < heads, grad_steps * jax.nn.sigmoid(shifted), 0.0)
    states_sums[5:6, :] += jnp.concatenate(
        [
            jnp.sum(grad_steps_in, axis=0, keepdims=True),
            jnp.sum(grad_log_steps * log_steps, axis=0, keepdims=True),
        ],
        axis=1,
    )
    grad_values = grad_scaled * spread_steps + skip * grad_y
    grad_conved = grad_values * (value_sig * (1.0 + conved * (1.0 - value_sig)))
    grad_states = jnp.concatenate([grad_b, grad_c], axis=1)
    grad_conved_states = grad_states * (states_sig * (1.0 + conved_states * (1.0 - states_sig)))

    def conv_backward(block, edge, tap_rows, raw, total_ref):
        result = tap_rows[3:4] * block
        total_ref[3:4, :] += jnp.sum(block * raw, axis=0, keepdims=True)
        total_ref[4:5, :] += jnp.sum(block, axis=0, keepdims=True)
        for lag in (1, 2, 3):
            term = moved_up(block, edge, lag) * marks[:, 5 + lag : 6 + lag]
            result = result + tap_rows[3 - lag : 4 - lag] * term
            total_ref[3 - lag : 4 - lag, :] += jnp.sum(term * raw, axis=0, keepdims=True)
        return result

    grad_raw = conv_backward(grad_conved, conv_edge[...], taps, raw_ref[...], sums)
    grad_raw_states = conv_backward(
        grad_conved_states, states_edge[...], states_small_ref[...], raw_states_ref[...], states_sums
    )
    conv_edge[...] = grad_conved[:8]
    states_edge[...] = grad_conved_states[:8]
    turned = marks[0:1, 10:11] > 0.5
    first_states = jnp.where(turned, grad_raw_states[:, STATE:], grad_raw_states[:, :STATE])
    second_states = jnp.where(turned, grad_raw_states[:, :STATE], grad_raw_states[:, STATE:])
    own_steps = jnp.where(lane < heads // 2, grad_steps_in, 0.0)
    other_steps = jnp.where(lane < heads // 2, pltpu.roll(grad_steps_in, LANES - heads // 2, 1), 0.0)
    grads = jnp.concatenate([grad_raw, first_states, own_steps, second_states, other_steps], axis=1).astype(bf16)
    grads_ref[...] = grads
    part_ref[...] = (nt(grads, weights[...]) + gate_part_ref[...]).astype(bf16)

    @pl.when(step == pl.num_programs(0) - 1)
    def _():
        skips = gathered_heads(sums[...], spreader)[6:7]
        states_sums[6:7, :] = jnp.concatenate([skips, jnp.zeros_like(skips)], axis=1)
        sums_ref[...] = sums[...]
        states_sums_ref[...] = states_sums[...]


def scan_grads_kernel(heads, rows, pieces, grad_arrays, *refs):
    normed_ref, refs = refs[0], refs[1:]
    inputs, refs = refs[: 16 + pieces], refs[16 + pieces :]
    outs, refs = refs[:grad_arrays], refs[grad_arrays:]
    results, scratch, grads, acc = refs[:3], refs[3:-2], refs[-2], refs[-1]
    place_ref = inputs[0]
    units = acc.shape[1] - 4 * STATE

    @pl.when(pl.program_id(0) == 0)
    def _():
        acc[...] = jnp.zeros_like(acc)

    scan_backward_kernel(heads, rows, pieces, *inputs, grads, *results, *scratch)
    acc[...] += tn(normed_ref[...], grads[...])

    @pl.when(pl.program_id(0) == pl.num_programs(0) - 1)
    def _():
        store_grads(outs, (0, units // 2), acc, 0, rows, place_ref)
        store_grads(outs, (units // 2, units // 2 + 2 * STATE), acc, units, rows, place_ref)


def second_forward_kernel(heads, rows, *refs):
    inputs, gate_weights, refs = refs[:15], refs[15], refs[16:]
    outputs, (gate_ref, part_ref), refs = refs[:10], refs[10:12], refs[12:]
    scan_forward_kernel(True, heads, rows, 5, *inputs, *outputs, *refs[:5])
    normed_ref, y_ref, small_ref = outputs[2], outputs[5], inputs[11]
    gate_forward_kernel(rows, 1, inputs[0], normed_ref, y_ref, gate_weights, small_ref, gate_ref, part_ref, *refs[5:])


def second_backward_kernel(heads, rows, *refs):
    gate_inputs, refs = refs[:11], refs[11:]
    scan_weights, (segment_ref, states_small_ref, head_ref, spread_ref), refs = refs[:5], refs[5:9], refs[9:]
    (raw_ref, conv_ref, raw_states_ref, conv_states_ref, steps_ref, entry_state_ref), refs = refs[:6], refs[6:]
    (out_ref, grad_out_ref, grads_ref, gate_sums_ref, part_ref, sums_ref, states_sums_ref), refs = refs[:7], refs[7:]
    grad_y, gate_part, refs = refs[0], refs[1], refs[2:]
    gate_scratch, scan_scratch = refs[:5], refs[5:]
    place_ref, normed_ref, y_ref, marks_ref, small_ref = gate_inputs[0], gate_inputs[5], gate_inputs[7], gate_inputs[9], gate_inputs[10]
    base = scan_weights[0].shape[1]
    gate_backward_kernel(
        True, rows, 1, 1, base, *gate_inputs, out_ref, grad_out_ref, grad_y, gate_part, grads_ref, gate_sums_ref, *gate_scratch
    )
    scan_inputs = (place_ref, grad_y, gate_part, *scan_weights, marks_ref, segment_ref, small_ref, states_small_ref, head_ref, spread_ref)
    saved = (raw_ref, conv_ref, y_ref, raw_states_ref, conv_states_ref, steps_ref, entry_state_ref)
    scan_grads_kernel(heads, rows, 5, 1, normed_ref, *scan_inputs, *saved, grads_ref, part_ref, sums_ref, states_sums_ref, *scan_scratch)


def norm_backward(grad_normed, hidden, grad_out, gain):
    scale = lax.rsqrt(jnp.mean(hidden * hidden, axis=1, keepdims=True) + epsilon)
    weighted = grad_normed * gain
    shared = jnp.mean(weighted * hidden, axis=1, keepdims=True) * (scale * scale * scale)
    return grad_out + scale * weighted - hidden * shared, grad_normed * hidden * scale


VMEM_LIMIT = 60 * 1024 * 1024


def spreader_of(units):
    one = (np.arange(LANES)[:, None] == np.arange(units)[None, :] // HEAD_DIM).astype(np.float32)
    return jnp.asarray(np.concatenate([one, one], axis=0), bf16)


def rows_spec(width, last=None):
    if last is None:
        return pl.BlockSpec((SPAN, width), lambda i: (i, 0))
    return pl.BlockSpec((SPAN, width), lambda i: (last - i, 0))


def wide_spec(width):
    return pl.BlockSpec((WIDE, width), lambda i: (i, 0))


def whole_spec(array):
    return pl.BlockSpec(array.shape, lambda i: (0,) * array.ndim)


def call(kernel, inputs, outputs, scratch, chunks, flops):
    return pl.pallas_call(
        kernel,
        grid=(chunks,),
        in_specs=[spec for _, spec in inputs],
        out_specs=[spec for _, _, spec in outputs],
        out_shape=[jax.ShapeDtypeStruct(shape, dtype) for shape, dtype, _ in outputs],
        scratch_shapes=[pltpu.VMEM(shape, dtype) for shape, dtype in scratch],
        compiler_params=pltpu.CompilerParams(vmem_limit_bytes=VMEM_LIMIT, dimension_semantics=("arbitrary",)),
        cost_estimate=pl.CostEstimate(flops=flops, bytes_accessed=500_000, transcendentals=0),
    )(*[array for array, _ in inputs])


def fixed(array):
    return array, whole_spec(array)


def scalars(array):
    return array, pl.BlockSpec(memory_space=pltpu.SMEM)


def grad_outputs(width, rows, columns):
    outputs = []
    for _, _, _, count in pieces_of(rows, width // (2 * rows)):
        shape = (count * rows, columns)
        outputs.append((shape, bf16, pl.BlockSpec(shape, lambda i: (0, 0))))
    return outputs


def awaited(arrays):
    return [(array, pl.BlockSpec(memory_space=pl.ANY)) for array in arrays]


def scan_forward(place, rows, h, parts, weights, marks, segment_row, params):
    length, width = h.shape
    units = params[0].shape[1]
    chunks = length // SPAN
    second = parts is not None
    inputs = [scalars(place), (h, rows_spec(width))]
    outputs = []
    if second:
        inputs += [(part, rows_spec(width + LANES)) for part in parts]
        outputs.append(((length, width), bf16, rows_spec(width)))
    inputs += [fixed(w) for w in weights]
    inputs += [(marks, rows_spec(LANES)), (segment_row, pl.BlockSpec((1, SPAN), lambda i: (0, i)))]
    inputs += [fixed(p) for p in params] + [fixed(spreader_of(units))]
    outputs.append(((8, width), f32, pl.BlockSpec((8, width), lambda i: (0, 0))))
    outputs.append(((length, width), bf16, rows_spec(width)))
    for columns in (units, units, units, 2 * STATE, 2 * STATE, LANES):
        outputs.append(((length, columns), f32, rows_spec(columns)))
    outputs.append(((chunks, STATE, units), f32, pl.BlockSpec((1, STATE, units), lambda i: (i, 0, 0))))
    scratch = [
        ((STATE, units), f32),
        ((8, units), f32),
        ((8, 2 * STATE), f32),
        ((8, width), f32),
        ((width, units + 4 * STATE), bf16),
    ]
    kernel = functools.partial(scan_forward_kernel, second, units // HEAD_DIM, rows, len(weights))
    results = call(kernel, inputs, outputs, scratch, chunks, 2_000_000_000)
    if not second:
        results = [h] + list(results)
    return results[0], results[1], results[2], results[3:]


def gate_forward(place, rows, normed, y, weights, params):
    length, width = normed.shape
    units = params[0].shape[1]
    inputs = [scalars(place), (normed, wide_spec(width)), (y, wide_spec(units))] + [fixed(w) for w in weights] + [fixed(params[0])]
    outputs = [((length, units), f32, wide_spec(units)), ((length, width + LANES), bf16, wide_spec(width + LANES))]
    scratch = [((width, units), bf16)] * 2
    return call(functools.partial(gate_forward_kernel, rows, len(weights)), inputs, outputs, scratch, length // WIDE, 1_000_000_000)


def gate_backward(place, rows, h, parts, extra, normed, gate, y, weights, marks, params):
    length, width = normed.shape
    units = params[0].shape[1]
    second = len(extra) == 1
    inputs = [scalars(place)] + ([(h, rows_spec(width))] if second else [])
    inputs += [(part, rows_spec(width + LANES)) for part in parts]
    inputs += [(array, rows_spec(width)) for array in extra[:4]] + [fixed(gain) for gain in extra[4:]]
    inputs += [(normed, rows_spec(width)), (gate, rows_spec(units)), (y, rows_spec(units))]
    inputs += [fixed(w) for w in weights] + [(marks, rows_spec(LANES)), fixed(params[0])]
    outputs = [((length, width), bf16, rows_spec(width))] if second else []
    outputs += [((length, width), f32, rows_spec(width)), ((length, units), bf16, rows_spec(units)), ((length, width), f32, rows_spec(width))]
    outputs += grad_outputs(width, rows, units)
    outputs.append(((8, units), f32, pl.BlockSpec((8, units), lambda i: (0, 0))))
    scratch = [((width, units), bf16)] * 2 + [((width, units), f32)] * 2 + [((8, units), f32)]
    results = call(functools.partial(gate_backward_kernel, second, rows, len(weights), 5, 0), inputs, outputs, scratch, length // SPAN, 2_000_000_000)
    if not second:
        results = [None] + list(results)
    return results


def scan_scratch(width, units):
    return [
        ((width, units + 4 * STATE), bf16),
        ((STATE, units), f32),
        ((STATE, units), f32),
        ((8, units), f32),
        ((8, 2 * STATE), f32),
        ((8, units), f32),
        ((8, 2 * STATE), f32),
        ((SPAN, units + 4 * STATE), bf16),
        ((width, units + 4 * STATE), f32),
    ]


def scan_backward(place, rows, grad_y, gate_part, normed, weights, marks, segment_row, params, saved):
    length, width = gate_part.shape
    units = params[0].shape[1]
    chunks = length // SPAN
    last = chunks - 1
    inputs = [(normed, rows_spec(width, last)), scalars(place), (grad_y, rows_spec(units, last)), (gate_part, rows_spec(width, last))]
    inputs += [fixed(w) for w in weights]
    inputs += [(marks, rows_spec(LANES, last)), (segment_row, pl.BlockSpec((1, SPAN), lambda i: (0, last - i)))]
    inputs += [fixed(p) for p in params] + [fixed(spreader_of(units))]
    inputs += [(s, rows_spec(s.shape[1], last)) for s in saved[:6]]
    inputs.append((saved[6], pl.BlockSpec((1, STATE, units), lambda i: (last - i, 0, 0))))
    outputs = grad_outputs(width, rows, units // 2 + 2 * STATE)
    outputs.append(((length, width), bf16, rows_spec(width, last)))
    for columns in (units, 2 * STATE):
        outputs.append(((8, columns), f32, pl.BlockSpec((8, columns), lambda i: (0, 0))))
    kernel = functools.partial(scan_grads_kernel, units // HEAD_DIM, rows, len(weights), len(outputs) - 3)
    return call(kernel, inputs, outputs, scan_scratch(width, units), chunks, 3_000_000_000)


def second_forward(place, rows, h, parts, weights, gate_weights, marks, segment_row, params):
    length, width = h.shape
    units = params[0].shape[1]
    chunks = length // SPAN
    inputs = [scalars(place), (h, rows_spec(width))] + [(part, rows_spec(width + LANES)) for part in parts]
    inputs += [fixed(w) for w in weights]
    inputs += [(marks, rows_spec(LANES)), (segment_row, pl.BlockSpec((1, SPAN), lambda i: (0, i)))]
    inputs += [fixed(p) for p in params] + [fixed(spreader_of(units)), fixed(gate_weights)]
    outputs = [((length, width), bf16, rows_spec(width)), ((8, width), f32, pl.BlockSpec((8, width), lambda i: (0, 0)))]
    outputs.append(((length, width), bf16, rows_spec(width)))
    for columns in (units, units, units, 2 * STATE, 2 * STATE, LANES):
        outputs.append(((length, columns), f32, rows_spec(columns)))
    outputs.append(((chunks, STATE, units), f32, pl.BlockSpec((1, STATE, units), lambda i: (i, 0, 0))))
    outputs += [((length, units), f32, rows_spec(units)), ((length, width + LANES), bf16, rows_spec(width + LANES))]
    scratch = [((STATE, units), f32), ((8, units), f32), ((8, 2 * STATE), f32), ((8, width), f32)]
    scratch += [((width, units + 4 * STATE), bf16)] + [((width, units), bf16)] * 2
    kernel = functools.partial(second_forward_kernel, units // HEAD_DIM, rows)
    results = call(kernel, inputs, outputs, scratch, chunks, 3_000_000_000)
    return results[0], results[1], results[2], results[3:10], results[10], results[11]


def second_backward(place, rows, h, parts, target, normed, gate, weights, gate_weights, marks, segment_row, params, saved):
    length, width = normed.shape
    units = params[0].shape[1]
    chunks = length // SPAN
    last = chunks - 1
    inputs = [scalars(place), (h, rows_spec(width, last))] + [(part, rows_spec(width + LANES, last)) for part in parts]
    inputs += [(target, rows_spec(width, last)), (normed, rows_spec(width, last)), (gate, rows_spec(units, last))]
    inputs += [(saved[2], rows_spec(units, last)), fixed(gate_weights), (marks, rows_spec(LANES, last)), fixed(params[0])]
    inputs += [fixed(w) for w in weights] + [(segment_row, pl.BlockSpec((1, SPAN), lambda i: (0, last - i)))]
    inputs += [fixed(params[1]), fixed(params[2]), fixed(spreader_of(units))]
    inputs += [(saved[i], rows_spec(saved[i].shape[1], last)) for i in (0, 1, 3, 4, 5)]
    inputs.append((saved[6], pl.BlockSpec((1, STATE, units), lambda i: (last - i, 0, 0))))

    def sums(columns):
        return (8, columns), f32, pl.BlockSpec((8, columns), lambda i: (0, 0))

    shape = (width // 2, 4 * (units + units // 2 + 2 * STATE))
    outputs = [((length, width), bf16, rows_spec(width, last)), ((length, width), f32, rows_spec(width, last))]
    outputs += [(shape, bf16, pl.BlockSpec(shape, lambda i: (0, 0))), sums(units)]
    outputs += [((length, width), bf16, rows_spec(width, last)), sums(units), sums(2 * STATE)]
    scratch = [((SPAN, units), bf16), ((SPAN, width), f32)]
    scratch += [((width, units), bf16)] * 2 + [((width, units), f32)] * 2 + [((8, units), f32)]
    scratch += scan_scratch(width, units)
    kernel = functools.partial(second_backward_kernel, units // HEAD_DIM, rows)
    return call(kernel, inputs, outputs, scratch, chunks, 4_000_000_000)


def finish_kernel(place_ref, own_ref, other_ref, h_ref, grad_out_ref, gain_ref, *refs):
    grad_ref, low_ref, sums_ref, sums = refs[-4:]

    @pl.when(pl.program_id(0) == 0)
    def _():
        sums[...] = jnp.zeros_like(sums)

    grad_normed = own_ref[...].astype(f32) + other_ref[...].astype(f32)
    next_grad = grad_out_ref[...]
    grad, gain_term = norm_backward(grad_normed, h_ref[...].astype(f32), next_grad.astype(bf16).astype(f32), gain_ref[0:1, :])
    rows = jnp.where(place_ref[3] == 0, grad, next_grad)
    grad_ref[...] = rows
    low_ref[...] = rows.astype(bf16)
    sums[0:1, :] += jnp.sum(gain_term, axis=0, keepdims=True)
    sums_ref[...] = sums[...]


def finish(place, own, other, h, grad_out, gain, ready):
    length, width = h.shape
    inputs = [scalars(place)] + [(rows, rows_spec(width)) for rows in (own, other, h, grad_out)] + [fixed(gain)]
    inputs += awaited(ready)
    outputs = [((length, width), f32, rows_spec(width)), ((length, width), bf16, rows_spec(width))]
    outputs.append(((8, width), f32, pl.BlockSpec((8, width), lambda i: (0, 0))))
    return call(finish_kernel, inputs, outputs, [((8, width), f32)], length // SPAN, 30_000_000)


def placed_kernel(place_ref, own_ref, away_ref, *refs):
    out_ref = refs[-1]
    own = pl.program_id(0) == place_ref[1]
    out_ref[0] = jnp.where(own, own_ref[...].astype(f32), away_ref[...].astype(f32)).astype(out_ref.dtype)


def placed_rows(place, rows, away, ready=()):
    half, width = away.shape
    return pl.pallas_call(
        placed_kernel,
        grid_spec=pltpu.PrefetchScalarGridSpec(
            num_scalar_prefetch=1,
            grid=(2,),
            in_specs=[
                pl.BlockSpec((half, width), lambda m, place: (place[1], 0)),
                pl.BlockSpec((half, width), lambda m, place: (0, 0)),
            ]
            + [pl.BlockSpec(memory_space=pl.ANY)] * len(ready),
            out_specs=pl.BlockSpec((1, half, width), lambda m, place: (m, 0, 0)),
        ),
        out_shape=jax.ShapeDtypeStruct((2, half, width), rows.dtype),
        compiler_params=pltpu.CompilerParams(vmem_limit_bytes=VMEM_LIMIT, dimension_semantics=("arbitrary",)),
        cost_estimate=pl.CostEstimate(flops=0, bytes_accessed=500_000, transcendentals=0),
    )(place, rows, away, *ready)


def marks_kernel(place_ref, lengths_ref, segments_ref, marks_ref, row_ref):
    turn, rank = place_ref[1], place_ref[2]
    micro, sequences = lengths_ref.shape
    length = segments_ref.shape[1]
    total = jnp.int32(0)
    for batch in range(micro):
        total = lax.fori_loop(0, sequences, lambda i, t: t + lengths_ref[batch, i], total)
    weight = 2.0 * (micro * sequences * length) / jnp.full((1, length), total, jnp.int32).astype(f32)
    position = lax.broadcasted_iota(jnp.int32, (1, length), 1)
    segment = jnp.where(turn == 0, segments_ref[0:1, :], segments_ref[1:2, :])
    wide = jnp.broadcast_to(segment, (8, length))

    def same(lag):
        moved = pltpu.roll(wide, lag % length, 1)[0:1]
        inside = (position >= lag) & (position < length + lag)
        return jnp.where(inside & (moved == segment), 1.0, 0.0)

    before = jnp.full((1, length), -1, jnp.int32)
    end = before
    for block in range(length // SPAN):
        here = (position >= block * SPAN) & (position < (block + 1) * SPAN)
        end = jnp.where(here, segment[:, (block + 1) * SPAN - 1 : (block + 1) * SPAN], end)
        if block:
            before = jnp.where(here, segment[:, block * SPAN - 1 : block * SPAN], before)
    as_float = segment.astype(f32)
    rows = [same(1), same(2), same(3)]
    rows += [jnp.where(segment == before, 1.0, 0.0), jnp.where(segment == end, 1.0, 0.0), as_float]
    rows += [same(-1), same(-2), same(-3)]
    rows += [jnp.where(position < lengths_ref[turn, rank], weight, 0.0), jnp.full((1, length), turn, jnp.int32).astype(f32)]
    rows.append(jnp.zeros((LANES - len(rows), length), f32))
    marks_ref[...] = jnp.transpose(jnp.concatenate(rows, axis=0))
    row_ref[...] = as_float


def token_marks(place, lengths, segments):
    length = segments.shape[1]
    return pl.pallas_call(
        marks_kernel,
        in_specs=[pl.BlockSpec(memory_space=pltpu.SMEM)] * 2 + [pl.BlockSpec(memory_space=pltpu.VMEM)],
        out_shape=[jax.ShapeDtypeStruct((length, LANES), f32), jax.ShapeDtypeStruct((1, length), f32)],
        compiler_params=pltpu.CompilerParams(vmem_limit_bytes=VMEM_LIMIT),
        cost_estimate=pl.CostEstimate(flops=0, bytes_accessed=500_000, transcendentals=0),
    )(place, lengths, segments)


def three_parts(value):
    high = value.astype(bf16)
    rest = value - high.astype(f32)
    middle = rest.astype(bf16)
    return high, middle, (rest - middle.astype(f32)).astype(bf16)


PARAM_ROWS = 16


def pack_kernel(
    place_ref, zx_ref, bc_ref, dt_ref, gain_ref, out_ref, conv_ref, gate_gain_ref, states_conv_ref, bias_ref, rate_ref, skip_ref, kept_ref, sent_ref
):
    turn, core = place_ref[1], place_ref[3]
    rows = zx_ref.shape[0]
    half = zx_ref.shape[2] // 2
    heads_half = dt_ref.shape[0] // 2
    lane = lax.broadcasted_iota(jnp.int32, (1, LANES), 1)
    bc = jnp.where(turn == 0, bc_ref[:, :STATE], bc_ref[:, STATE:])
    diagonal = lax.broadcasted_iota(jnp.int32, (rows, rows), 0) == lax.broadcasted_iota(jnp.int32, (rows, rows), 1)
    gain = jnp.sum(jnp.where(diagonal, gain_ref[...].astype(f32), 0.0), axis=1, keepdims=True)
    head = lax.broadcasted_iota(jnp.int32, (2 * heads_half, LANES), 0)
    column = lax.broadcasted_iota(jnp.int32, (2 * heads_half, LANES), 1)
    shared = jnp.concatenate([states_conv_ref[...], jnp.zeros((PARAM_ROWS - 5, 2 * STATE), bf16)], axis=0)
    split = [part.astype(f32) for ref in (bias_ref, rate_ref, skip_ref) for part in three_parts(ref[...])]
    heads = jnp.concatenate(split + [jnp.zeros((PARAM_ROWS - 9, split[0].shape[1]), f32)], axis=0)
    heads = jnp.concatenate([heads, jnp.zeros((PARAM_ROWS, LANES - heads.shape[1]), f32)], axis=1).astype(bf16)
    for ref, part in ((kept_ref, core), (sent_ref, 1 - core)):
        first = part == 0

        def chosen(array, start):
            return jnp.where(first, array[:, start : start + half], array[:, start + half : start + 2 * half])

        ref[:rows, :half] = chosen(zx_ref[:, 1, :], 0)
        ref[:rows, half : half + STATE] = bc
        taken = (head == column + part * heads_half) & (column < heads_half)
        own_steps = tn(dt_ref[...], jnp.where(taken, 1.0, 0.0).astype(bf16))
        ref[:rows, half + STATE : half + 2 * STATE] = jnp.where(lane == LANES // 2, gain, own_steps).astype(bf16)
        ref[:rows, half + 2 * STATE : 2 * half + 2 * STATE] = chosen(zx_ref[:, 0, :], 0)
        ref[:rows, 2 * half + 2 * STATE :] = chosen(out_ref, 0)
        ref[rows:, :] = jnp.zeros((PARAM_ROWS, ref.shape[1]), bf16)
        channels = jnp.concatenate([chosen(conv_ref, 0), chosen(gate_gain_ref, 0)], axis=0)
        ref[rows:, :half] = jnp.concatenate([channels, jnp.zeros((PARAM_ROWS - 6, half), bf16)], axis=0)
        ref[rows:, half : half + 2 * STATE] = shared
        ref[rows:, half + 2 * STATE : half + 2 * STATE + LANES] = heads


def plain_call(kernel, place, inputs, outputs, ready=()):
    count = len(ready)
    body = kernel if not count else lambda place_ref, *refs: kernel(place_ref, *refs[count:])
    return pl.pallas_call(
        body,
        in_specs=[pl.BlockSpec(memory_space=pltpu.SMEM)]
        + [pl.BlockSpec(memory_space=pl.ANY)] * count
        + [pl.BlockSpec(memory_space=pltpu.VMEM)] * len(inputs),
        out_shape=[jax.ShapeDtypeStruct(shape, dtype) for shape, dtype in outputs],
        compiler_params=pltpu.CompilerParams(vmem_limit_bytes=VMEM_LIMIT),
        cost_estimate=pl.CostEstimate(flops=0, bytes_accessed=500_000, transcendentals=0),
    )(place, *ready, *inputs)


def unpack_kernel(place_ref, kept_ref, received_ref, *refs):
    scan_ref, middle_ref, gate_ref, params_ref, channels_ref = refs
    kept_first = place_ref[3] == 0
    kept, received = kept_ref[...], received_ref[...]
    first = jnp.where(kept_first, kept, received)
    second = jnp.where(kept_first, received, kept)
    rows, scan = scan_ref.shape
    half = channels_ref.shape[1]
    scan_ref[...] = first[:rows, :scan]
    middle_ref[:, : 2 * half] = first[:rows, scan:]
    middle_ref[:, 2 * half :] = second[:rows, :scan]
    gate_ref[...] = second[:rows, scan:]
    params_ref[0] = first[rows:, : scan + LANES]
    params_ref[1] = second[rows:, : scan + LANES]
    channels_ref[:PARAM_ROWS] = first[rows:, :half]
    channels_ref[PARAM_ROWS:] = second[rows:, :half]


def params_kernel(heads_half, place_ref, params_ref, channels_ref, spread_ref, *refs):
    turn, core = place_ref[1], place_ref[3]
    half = channels_ref.shape[1]
    lane = lax.broadcasted_iota(jnp.int32, (1, LANES), 1)
    for layer in range(2):
        small_ref, states_ref, head_ref = refs[3 * layer : 3 * layer + 3]
        rows = params_ref[layer].astype(f32)
        split = rows[:, half + 2 * STATE :]
        heads = [split[3 * i : 3 * i + 1] + split[3 * i + 1 : 3 * i + 2] + split[3 * i + 2 : 3 * i + 3] for i in range(3)]
        heads = jnp.concatenate(heads + [jnp.zeros((5, LANES), f32)], axis=0)
        moved = [pltpu.roll(heads, (LANES - start * heads_half) % LANES, 1) for start in range(4)]

        def of(index):
            return jnp.where(index == 0, moved[0], jnp.where(index == 1, moved[1], jnp.where(index == 2, moved[2], moved[3])))

        own, other = of(2 * turn + core), pltpu.roll(of(2 * (1 - turn) + core), heads_half, 1)
        heads = jnp.where(lane < heads_half, own, jnp.where(lane < 2 * heads_half, other, 0.0))
        head_ref[...] = jnp.concatenate([heads[0:1], jnp.exp(heads[1:2]), jnp.zeros((6, LANES), f32)], axis=0)
        high, middle, low = three_parts(jnp.broadcast_to(heads[2:3], (8, LANES)))
        once = spread_ref[:LANES]
        skips = (nn(high, once) + nn(middle, once) + nn(low, once))[0:1]
        own_rows = rows[0:6, :half]
        other_rows = channels_ref[PARAM_ROWS * layer : PARAM_ROWS * layer + 6].astype(f32)
        channels = jnp.concatenate([own_rows, other_rows], axis=1)
        small_ref[...] = jnp.concatenate([channels, skips, jnp.zeros_like(skips)], axis=0)
        states_ref[...] = jnp.concatenate([rows[0:5, half : half + 2 * STATE], jnp.zeros((3, 2 * STATE), f32)], axis=0)


def beside_kernel(place_ref, *refs):
    out = refs[-1]
    start = 0
    for ref in refs[:-1]:
        out[:, start : start + ref.shape[1]] = ref[...]
        start += ref.shape[1]


def split_kernel(place_ref, whole_ref, *outs):
    start = 0
    for out in outs:
        out[...] = whole_ref[:, start : start + out.shape[1]]
        start += out.shape[1]


def cross_kernel(place_ref, *refs):
    over_x, over_tensor = refs[-2:]
    start = 0
    for group in range(len(refs[:-2]) // 4):
        x_ref, y_ref, first_ref, second_ref = refs[4 * group : 4 * group + 4]
        columns = slice(start, start + x_ref.shape[1])
        start += x_ref.shape[1]
        half = first_ref.shape[0]
        over_x[:half, columns] = (x_ref[:half].astype(f32) + first_ref[...].astype(f32)).astype(bf16)
        over_x[half:, columns] = x_ref[half:]
        over_tensor[:half, columns] = y_ref[:half]
        over_tensor[half:, columns] = (y_ref[half:].astype(f32) + second_ref[...].astype(f32)).astype(bf16)


def join_kernel(groups, place_ref, *refs):
    out = refs[-1]
    start = 0
    for own, over_x, over_tensor, offset in groups:
        width = refs[own].shape[1]
        there = slice(offset, offset + width)
        total = refs[own][...].astype(f32) + refs[over_x][:, there].astype(f32) + refs[over_tensor][:, there].astype(f32)
        out[:, start : start + width] = total.astype(bf16)
        start += width


def owned_kernel(place_ref, first_ref, second_ref, beside_ref, across_ref, both_ref, zx_ref, bc_ref, dt_ref, out_ref):
    first = place_ref[3] == 0
    half = out_ref.shape[1] // 2
    heads_half = dt_ref.shape[1] // 2
    mine = jnp.where(first, first_ref[...], second_ref[...]).astype(f32)
    beside = beside_ref[...].astype(f32)
    lower, upper = jnp.where(first, mine, beside), jnp.where(first, beside, mine)
    gate = half + 2 * STATE
    for index, part in enumerate((lower, upper)):
        columns = slice(index * half, (index + 1) * half)
        zx_ref[:, 0, columns] = part[:, gate : gate + half]
        zx_ref[:, 1, columns] = part[:, :half]
        out_ref[:, columns] = part[:, gate + half :]
    own = mine[:, half : half + STATE] + beside[:, half : half + STATE]
    other = across_ref[...].astype(f32) + both_ref[...].astype(f32)
    straight = place_ref[1] == 0
    bc_ref[:, :STATE] = jnp.where(straight, own, other)
    bc_ref[:, STATE:] = jnp.where(straight, other, own)
    lane = lax.broadcasted_iota(jnp.int32, (1, LANES), 1)
    steps = slice(half + STATE, half + 2 * STATE)
    both = jnp.where(lane < heads_half, lower[:, steps], pltpu.roll(upper[:, steps], heads_half, 1))
    dt_ref[...] = both[:, : 2 * heads_half]


def small_kernel(gate0, scan0, states0, gate1, scan1, states1, gain_ref, out_ref):
    for layer, (gate, scan, states, gain) in enumerate(
        ((gate0, scan0, states0, gain_ref[0:1, :]), (gate1, scan1, states1, gate0[7:8, :]))
    ):
        start = 16 * layer
        out_ref[start : start + 5, :] = scan[0:5, :]
        out_ref[start + 5 : start + 6, :] = gate[5:6, :]
        out_ref[start + 6 : start + 7, :] = gain
        out_ref[start + 7 : start + 16, :] = jnp.zeros((9, out_ref.shape[1]), f32)
        out_ref[start + 8 : start + 15, : 2 * STATE] = states[0:7, :]


def fold_kernel(heads_half, place_ref, own_ref, away_ref, mine_ref, others_ref):
    first = place_ref[3] == 0
    half = mine_ref.shape[1]
    folded = []
    for layer in range(2):
        own, away = own_ref[16 * layer : 16 * layer + 16], away_ref[16 * layer : 16 * layer + 16]
        units = own[0:6, :half] + away[0:6, half:]
        gain = own[6:7] + away[6:7]
        total = own[8:16, :half] + away[8:16, :half]
        own_heads = jnp.concatenate([own[14:15, :LANES], own[13:14, : 2 * LANES]], axis=1)
        away_heads = jnp.concatenate([away[14:15, :LANES], away[13:14, : 2 * LANES]], axis=1)
        moved = pltpu.roll(jnp.broadcast_to(away_heads, (8, 3 * LANES)), 3 * LANES - heads_half, 1)[0:1]
        heads = jnp.concatenate([own_heads + moved, jnp.zeros((1, half - 3 * LANES), f32)], axis=1) if half > 3 * LANES else own_heads + moved
        zeros = jnp.zeros((2, half), f32)
        folded.append(jnp.concatenate([units, gain[:, :half], gain[:, half:], total[0:5], heads, zeros], axis=0))
    mine_ref[...] = jnp.where(first, folded[0], folded[1])
    others_ref[...] = jnp.where(first, folded[1], folded[0])


def small_outputs_kernel(heads_half, place_ref, total_ref, conv_ref, states_conv_ref, gate_gain_ref, heads_ref, gain_ref):
    first = place_ref[3] == 0
    half = total_ref.shape[1]
    here, there = total_ref[0:16], total_ref[16:32]
    lower, upper = jnp.where(first, here, there), jnp.where(first, there, here)
    conv_ref[:, :half] = lower[0:5]
    conv_ref[:, half:] = upper[0:5]
    gate_gain_ref[:, :half] = lower[5:6]
    gate_gain_ref[:, half:] = upper[5:6]
    states_conv_ref[...] = here[8:13, : 2 * STATE] + there[8:13, : 2 * STATE]
    lane = lax.broadcasted_iota(jnp.int32, (1, LANES), 1)
    for row in range(3):
        own = lower[13:14, row * LANES : (row + 1) * LANES]
        other = pltpu.roll(jnp.broadcast_to(upper[13:14, row * LANES : (row + 1) * LANES], (8, LANES)), heads_half, 1)[0:1]
        heads_ref[row : row + 1, :] = jnp.where(lane < heads_half, own, other)[:, : 2 * heads_half]
    gain_ref[:, :half] = here[6:7]
    gain_ref[:, half:] = here[7:8]


def tied(*values):
    return lax.optimization_barrier(values)


def swapped(block, axis):
    return lax.ppermute(block, axis, [(0, 1), (1, 0)])


def far_swapped(block):
    size = lax.axis_size("tensor")
    return lax.ppermute(block, ("section", "tensor"), [(i, 2 * size - 1 - i) for i in range(2 * size)])


def body(
    x_input,
    teacher,
    segment_ids,
    valid_len,
    norm_gain,
    w_zx,
    w_bc,
    w_dt,
    conv_x,
    conv_bc,
    dt_bias,
    a_log,
    d_skip,
    gnorm_gain,
    w_out,
):
    local_rows, width = x_input.shape[1:]
    ranks = lax.axis_size("dp")
    places = ranks // 2
    core = lax.axis_index("section")
    turn = lax.axis_index("tensor")
    rank = lax.axis_index("dp")
    place = jnp.stack([rank % 2, turn, rank, core]).astype(jnp.int32)
    on_first = core == 0
    block_rows = w_zx.shape[1]
    half = w_zx.shape[3] // 2
    units = 2 * half
    heads_half = w_dt.shape[2] // 2
    scan_columns = half + 2 * STATE
    line_groups = [[2 * index + start for index in range(places)] for start in range(2)]

    def by_layer(kept, received):
        return jnp.where(on_first, kept, received), jnp.where(on_first, received, kept)

    def x_swapped(block):
        return lax.ppermute(block, "dp", [(i, i ^ 1) for i in range(ranks)])

    def y_swapped(block):
        return swapped(block, "tensor")

    def line_gather(block):
        return lax.all_gather(block, "dp", axis_index_groups=line_groups, axis=0, tiled=True)

    def line_reduce(block):
        return lax.psum_scatter(block, "dp", axis_index_groups=line_groups, scatter_dimension=0, tiled=True)

    def line_total(block):
        if places != 4:
            return lax.psum(block, "dp", axis_index_groups=line_groups)

        def send(rows, moves):
            return lax.ppermute(rows, "dp", [(2 * a + start, 2 * b + start) for a, b in moves for start in range(2)])

        up, down = send(block, [(0, 1), (1, 2), (2, 3)]), send(block, [(1, 0), (2, 1), (3, 2)])
        up2, down2 = send(up, [(1, 2), (2, 3)]), send(down, [(2, 1), (1, 0)])
        far = send(jnp.where(rank // 2 == 1, up, down), [(1, 3), (2, 0)])
        return block + up + down + up2 + down2 + far

    pack_shape = (block_rows + PARAM_ROWS, scan_columns + units)
    kept, sent = plain_call(
        pack_kernel,
        place,
        (w_zx[0], w_bc[0], w_dt[0].T, norm_gain, w_out[0].T, conv_x[0], gnorm_gain, conv_bc[0], dt_bias, a_log, d_skip),
        [(pack_shape, bf16)] * 2,
    )
    received = swapped(sent, "section")
    scan_block, middle_block, gate_block, params_both, channels = plain_call(
        unpack_kernel,
        place,
        (kept, received),
        [
            ((block_rows, scan_columns), bf16),
            ((block_rows, units + scan_columns), bf16),
            ((block_rows, units), bf16),
            ((2, PARAM_ROWS, scan_columns + LANES), bf16),
            ((2 * PARAM_ROWS, half), bf16),
        ],
    )

    def plane_end(block, over_x, over_tensor):
        cut = places // 2 * block_rows
        return block, over_x, over_tensor, y_swapped(over_x[:cut]), x_swapped(over_tensor[cut:])

    def quarter(rows):
        away = lax.dynamic_index_in_dim(rows, 1 - turn, 0, keepdims=False)
        return lax.dynamic_slice_in_dim(away, core * (local_rows // 2), local_rows // 2, 0)

    def whole_rows(rows, here, beside):
        own = lax.dynamic_index_in_dim(rows, turn, 0, keepdims=False)
        other = jnp.concatenate(by_layer(here, beside), axis=0)
        return jnp.where(turn == 0, jnp.concatenate([own, other]), jnp.concatenate([other, own]))

    scan_line, here, channels = tied(line_gather(scan_block), y_swapped(quarter(x_input)), y_swapped(channels))
    scan_line, middle_block = tied(scan_line, middle_block)
    middle_line = line_gather(middle_block)
    scan_half = scan_line, x_swapped(scan_line), y_swapped(scan_line)
    x_rows = whole_rows(x_input, here, swapped(here, "section"))
    params = plain_call(
        functools.partial(params_kernel, heads_half),
        place,
        (params_both, channels, spreader_of(units)),
        [((8, units), f32), ((8, 2 * STATE), f32), ((8, LANES), f32)] * 2,
    )
    params = [params[:3], params[3:]]
    marks, segment_row = token_marks(place, valid_len, segment_ids[:, 0])
    over_x = x_swapped(gate_block)
    side = (gate_block, over_x, y_swapped(gate_block), y_swapped(over_x))
    side = plain_call(beside_kernel, place, side, [((block_rows, 4 * units), bf16)], (x_rows, marks, params[0][0]))[0]
    scan_first, side = tied(plane_end(*scan_half), side)
    middle_line, side = tied(middle_line, side)
    gate_second = line_gather(side)
    gate_line, next_line = plain_call(
        split_kernel,
        place,
        (middle_line,),
        [((places * block_rows, units), bf16), ((places * block_rows, scan_columns), bf16)],
        (scan_first[4],),
    )

    gate_half = gate_line, x_swapped(gate_line), y_swapped(gate_line)
    next_half = next_line, x_swapped(next_line), y_swapped(next_line)
    results = scan_forward(place, block_rows, x_rows, None, scan_first, marks, segment_row, params[0])
    results, gate_half, next_half = tied(results, gate_half, next_half)
    _, gain_first, normed_first, saved_first = results
    gate_first = plane_end(*gate_half)
    results = gate_forward(place, block_rows, normed_first, saved_first[2], gate_first, params[0])
    (gated_first, part), scan_second = tied(results, plane_end(*next_half))
    parts_first = (part, swapped(part, "section"))
    parts_first, teacher, gate_second = tied(parts_first, teacher, gate_second)
    results = second_forward(
        place, block_rows, x_rows, parts_first, scan_second, gate_second, marks, segment_row, params[1]
    )
    results, here = tied(results, y_swapped(quarter(teacher)))
    hidden, gain_second, normed_second, saved_second, gated_second, part = results
    parts_second = (part, swapped(part, "section"))
    target = whole_rows(teacher, here, swapped(here, "section"))

    def add(*blocks):
        return sum(block.astype(f32) for block in blocks).astype(bf16)

    def plane_start(pieces):
        return tuple(pieces[:3]), (y_swapped(pieces[3]), x_swapped(pieces[4]))

    def crossed(*groups):
        arrays = [array for pieces, came in groups for array in pieces[1:] + came]
        columns = sum(pieces[0].shape[1] for pieces, _ in groups)
        over_x, over_tensor = plain_call(cross_kernel, place, arrays, [((places * block_rows, columns), bf16)] * 2)
        return [pieces[0] for pieces, _ in groups], x_swapped(over_x), y_swapped(over_tensor)

    def joined(*groups, ready=()):
        arrays, spans = [], []
        for owns, over_x, over_tensor in groups:
            base = len(arrays)
            arrays += list(owns) + [over_x, over_tensor]
            offset = 0
            for index, own in enumerate(owns):
                spans.append((base + index, base + len(owns), base + len(owns) + 1, offset))
                offset += own.shape[1]
        columns = sum(arrays[span[0]].shape[1] for span in spans)
        kernel = functools.partial(join_kernel, spans)
        return plain_call(kernel, place, arrays, [((places * block_rows, columns), bf16)], ready)[0]

    def away_rows(rows):
        return y_swapped(lax.dynamic_slice_in_dim(rows, (1 - turn) * local_rows, local_rows, 0))

    produced, grad_out, grads, gate_sums, part, sums, states_sums = second_backward(
        place,
        block_rows,
        hidden,
        parts_second,
        target,
        normed_second,
        gated_second,
        scan_second,
        gate_second,
        marks,
        segment_row,
        params[1],
        saved_second,
    )
    quarters = line_reduce(grads)
    sums_second = (gate_sums, sums, states_sums)
    grad_parts = (part, swapped(part, "section"))
    results = gate_backward(
        place,
        block_rows,
        x_rows,
        parts_first,
        (hidden, grad_out) + grad_parts + (gain_second,),
        normed_first,
        gated_first,
        saved_first[2],
        gate_first,
        marks,
        params[0],
    )
    results, produced_away = tied(results[1:], away_rows(produced))
    grad_hidden, grad_y, gate_part = results[:3]
    gate_reduce = plane_start(results[3:8])
    gate_sums_first = results[8]
    results = scan_backward(
        place, block_rows, grad_y, gate_part, normed_first, scan_first, marks, segment_row, params[0], saved_first
    )
    results, gate_reduce = tied(results, gate_reduce)
    scan_reduce = plane_start(results[:5])
    part, sums, states_sums = results[5:]
    sums_first = (gate_sums_first, sums, states_sums)
    crossed_gate = crossed(gate_reduce)
    results = finish(
        place, part, swapped(part, "section"), x_rows, grad_hidden, gain_first, (crossed_gate[0][0],)
    )
    (grad_rows, grad_low, gain_sums), scan_reduce = tied(results, scan_reduce)
    scan_reduce, gain_sums = tied(scan_reduce, gain_sums)
    crossed_scan = crossed(scan_reduce)
    layer_outputs = placed_rows(place, produced, produced_away, (crossed_scan[0][0],))
    blocks = joined(crossed_scan, crossed_gate, ready=(layer_outputs, quarters))
    owned_first = line_reduce(blocks)
    columns = scan_columns + units
    quarters = plain_call(split_kernel, place, (quarters,), [((block_rows, columns), bf16)] * 4, (blocks,))
    both_ways = [(2 * d + t, 2 * (d ^ 1) + 1 - t) for d in range(ranks) for t in range(2)]
    owned_second = add(
        quarters[0],
        x_swapped(quarters[1]),
        y_swapped(quarters[2]),
        lax.ppermute(quarters[3], ("dp", "tensor"), both_ways),
    )
    smalls = plain_call(
        lambda place_ref, *refs: small_kernel(*refs),
        place,
        sums_first + sums_second + (gain_sums,),
        [((32, units), f32)],
    )[0]
    smalls_away = y_swapped(smalls)
    grad_low, smalls = tied(grad_low, smalls)
    mine, others = plain_call(
        functools.partial(fold_kernel, heads_half), place, (smalls, smalls_away), [((16, half), f32)] * 2
    )
    total = jnp.concatenate([mine, swapped(others, "section")])
    total = total + x_swapped(total)
    owned_first, boundary = tied(owned_first, placed_rows(place, grad_rows, away_rows(grad_low)))
    total = line_total(total)
    grad_conv, grad_states_conv, grad_gate_gain, grad_heads, gain_total = plain_call(
        functools.partial(small_outputs_kernel, heads_half),
        place,
        (total,),
        [((5, units), f32), ((5, 2 * STATE), f32), ((1, units), f32), ((3, 2 * heads_half), f32), ((1, width), f32)],
    )

    others = jnp.where(on_first, owned_second, owned_first)
    own_states, other_states = by_layer(owned_first[:, half : half + STATE], owned_second[:, half : half + STATE])
    grad_zx, grad_bc, grad_dt, grad_out_w = plain_call(
        owned_kernel,
        place,
        (owned_first, owned_second, swapped(others, "section"), y_swapped(own_states), far_swapped(other_states)),
        [((block_rows, 2, units), f32)] + [((block_rows, columns), f32) for columns in (2 * STATE, 2 * heads_half, units)],
        (boundary, layer_outputs, grad_conv),
    )
    return (
        layer_outputs[None],
        boundary[None],
        lax.dynamic_slice_in_dim(gain_total, rank * block_rows, block_rows, 1),
        grad_zx[None],
        grad_bc[None],
        grad_dt[None],
        grad_conv[None],
        grad_states_conv[None],
        grad_heads[1:2],
        grad_heads[2:3],
        grad_heads[0:1],
        grad_gate_gain,
        grad_out_w.T[None],
    )


def solution(mesh):
    placed = (
        P(None, ("dp", "tensor"), None),
        P(None, ("dp", "tensor"), None),
        P(None, "dp", None),
        P(),
        P("section", "dp"),
        P("section", "dp", None, "tensor"),
        P("section", "dp", None),
        P("section", "dp", "tensor"),
        P("section", None, "tensor"),
        P("section", None, None),
        P("section", None),
        P("section", None),
        P("section", None),
        P("section", "tensor"),
        P("section", "tensor", "dp"),
    )
    return jax.shard_map(
        body,
        mesh=mesh,
        in_specs=placed,
        out_specs=(
            P("section", None, ("dp", "tensor"), None),
            P("section", None, ("dp", "tensor"), None),
            P("section", "dp"),
            P("section", "dp", None, "tensor"),
            P("section", "dp", None),
            P("section", "dp", "tensor"),
            P("section", None, "tensor"),
            P("section", None, None),
            P("section", "tensor"),
            P("section", "tensor"),
            P("section", "tensor"),
            P("section", "tensor"),
            P("section", "tensor", "dp"),
        ),
        check_vma=False,
    )
```

```python
import functools

import jax
import jax.numpy as jnp
import numpy as np
from jax import lax
from jax.experimental import pallas as pl
from jax.experimental.pallas import tpu as pltpu
from jax.sharding import PartitionSpec as P

HEAD_DIM = 64
STATE = 128
SPAN = 256
WIDE = 512
LANES = 128

epsilon = 1e-05
f32 = jnp.float32
bf16 = jnp.bfloat16


def nn(left, right):
    return lax.dot_general(left, right, (((1,), (0,)), ((), ())), preferred_element_type=f32)


def nt(left, right):
    return lax.dot_general(left, right, (((1,), (1,)), ((), ())), preferred_element_type=f32)


def tn(left, right):
    return lax.dot_general(left, right, (((0,), (0,)), ((), ())), preferred_element_type=f32)


def high_low(value):
    high = value.astype(bf16)
    return high, (value - high.astype(f32)).astype(bf16)


def spread(per_head, spreader):
    return nn(jnp.concatenate(high_low(per_head), axis=1), spreader)


def gathered_heads(units, spreader):
    high, low = high_low(units)
    once = spreader[:LANES]
    return nt(high, once) + nt(low, once)


def running_sum(triangle, value):
    high = value.astype(bf16)
    rest = value - high.astype(f32)
    middle = rest.astype(bf16)
    low = (rest - middle.astype(f32)).astype(bf16)
    sums = nn(triangle, jnp.concatenate([high, middle, low], axis=1))
    return sums[:, :LANES] + sums[:, LANES : 2 * LANES] + sums[:, 2 * LANES :]


def softplus(value):
    return jnp.maximum(value, 0.0) + jnp.log1p(jnp.exp(-jnp.abs(value)))


def moved_down(block, edge, lag):
    return jnp.concatenate([edge, block], axis=0)[8 - lag : 8 - lag + block.shape[0]]


def moved_up(block, edge, lag):
    return jnp.concatenate([block, edge], axis=0)[lag : lag + block.shape[0]]


def decay_parts(steps_in, head_rows, marks, heads):
    lane = lax.broadcasted_iota(jnp.int32, (1, LANES), 1)
    live = lane < heads
    shifted = steps_in + head_rows[0:1, :LANES]
    steps = jnp.where(live, softplus(shifted), 0.0)
    rates = head_rows[1:2, :LANES]
    log_steps = -steps * rates
    row = lax.broadcasted_iota(jnp.int32, (SPAN, SPAN), 0)
    column = lax.broadcasted_iota(jnp.int32, (SPAN, SPAN), 1)
    lower = (row >= column).astype(bf16)
    logs = running_sum(lower, log_steps)
    last = logs[SPAN - 1 : SPAN]
    entry = jnp.exp(logs) * marks[:, 3:4]
    tail = jnp.exp(last - logs) * marks[:, 4:5]
    through = jnp.exp(last) * marks[SPAN - 1 : SPAN, 3:4]
    entry = jnp.where(live, entry, 0.0)
    tail = jnp.where(live, tail, 0.0)
    through = jnp.where(live, through, 0.0)
    return shifted, steps, log_steps, logs, entry, tail, through, row, column


def linked_mask(row, column, marks, segment_row):
    linked = (row >= column) & (marks[:, 5:6] == segment_row)
    return jnp.where(linked, 0.0, -1e30)


def branch_of(own_ref, other_ref, units):
    width = own_ref.shape[1] - LANES
    own = own_ref[...].astype(f32)
    other = other_ref[...].astype(f32)
    total = own[:, :width] + other[:, :width]
    own_squares = own[:, width : width + 1] + own[:, width + 1 : width + 2]
    other_squares = other[:, width : width + 1] + other[:, width + 1 : width + 2]
    inverse = lax.rsqrt((own_squares + other_squares) / (2 * units) + epsilon)
    return total * inverse, total, inverse


PLANE = ((False, False), (True, False), (False, True), (True, True))


def load_weights(weights, start, refs, columns, rows, place_ref):
    first, last = columns
    mine = place_ref[0]
    size = refs[0].shape[1] // 4
    base = 0
    for index in range(len(refs) if len(refs) > 1 else 4):
        moved, turned = PLANE[min(index, 3)]
        ref, offset = (refs[0], index * size) if len(refs) == 1 else (refs[index], 0)
        place = 1 - mine if moved else mine
        target = start + (last - first if turned else 0)
        for step in range(ref.shape[0] // rows):
            row = pl.multiple_of((2 * (base + step) + place) * rows, 32)
            weights[pl.ds(row, rows), target : target + last - first] = ref[step * rows : (step + 1) * rows, offset + first : offset + last]
        base = ref.shape[0] // rows if index == 3 else 0


def store_grads(refs, columns, acc, start, rows, place_ref, base=0):
    first, last = columns
    mine = place_ref[0]
    size = refs[0].shape[1] // 4
    for index, (moved, turned) in enumerate(PLANE):
        ref, offset = (refs[0], index * size + base) if len(refs) == 1 else (refs[index], 0)
        place = 1 - mine if moved else mine
        source = start + (last - first if turned else 0)
        for step in range(ref.shape[0] // rows):
            row = pl.multiple_of((2 * step + place) * rows, 32)
            block = acc[pl.ds(row, rows), source : source + last - first]
            ref[step * rows : (step + 1) * rows, offset + first : offset + last] = block.astype(bf16)


def scan_forward_kernel(second, heads, rows, pieces, *refs):
    place_ref, refs = refs[0], refs[1:]
    if second:
        (h_ref, own_ref, other_ref), refs = refs[:3], refs[3:]
    else:
        (h_ref,), refs = refs[:1], refs[1:]
    parts, refs = refs[:pieces], refs[pieces:]
    (marks_ref, segment_ref, small_ref, states_small_ref, head_ref, spread_ref), refs = refs[:6], refs[6:]
    if second:
        h_out, refs = refs[0], refs[1:]
    gain_ref, refs = refs[0], refs[1:]
    normed_ref, raw_ref, conv_ref, y_ref, raw_states_ref, conv_states_ref, steps_ref, entry_state_ref = refs[:8]
    state, raw_edge, states_edge, gain, weights = refs[8:]
    units = raw_ref.shape[1]

    @pl.when(pl.program_id(0) == 0)
    def _():
        state[...] = jnp.zeros_like(state)
        raw_edge[...] = jnp.zeros_like(raw_edge)
        states_edge[...] = jnp.zeros_like(states_edge)
        load_weights(weights, 0, parts, (0, units // 2), rows, place_ref)
        load_weights(weights, units, parts, (units // 2, units // 2 + 2 * STATE), rows, place_ref)
        steps_columns = weights[:, units + STATE : units + STATE + LANES].astype(f32)
        gain[...] = jnp.broadcast_to(jnp.transpose(steps_columns)[LANES // 2 : LANES // 2 + 1, :], gain.shape)
        gain_ref[...] = gain[...]

    hidden = h_ref[...].astype(f32)
    if second:
        rounded = (hidden + branch_of(own_ref, other_ref, units)[0]).astype(bf16)
        h_out[...] = rounded
        hidden = rounded.astype(f32)
    scale = lax.rsqrt(jnp.mean(hidden * hidden, axis=1, keepdims=True) + epsilon)
    normed = (hidden * scale * gain[0:1, :]).astype(bf16)
    normed_ref[...] = normed
    projected = nn(normed, weights[...])
    raw = projected[:, :units]
    first, second_part = projected[:, units : units + 2 * STATE], projected[:, units + 2 * STATE :]
    marks = marks_ref[...]
    turned = marks[0:1, 10:11] > 0.5
    raw_states = jnp.concatenate(
        [
            jnp.where(turned, second_part[:, :STATE], first[:, :STATE]),
            jnp.where(turned, first[:, :STATE], second_part[:, :STATE]),
        ],
        axis=1,
    )
    lane = lax.broadcasted_iota(jnp.int32, (1, LANES), 1)
    steps_in = jnp.where(lane < heads // 2, first[:, STATE:], pltpu.roll(second_part[:, STATE:], heads // 2, 1))
    raw_ref[...] = raw
    raw_states_ref[...] = raw_states
    steps_ref[...] = steps_in

    def conv(block, edge, taps):
        total = taps[4:5] + taps[3:4] * block
        for lag in (1, 2, 3):
            total = total + taps[3 - lag : 4 - lag] * (moved_down(block, edge, lag) * marks[:, lag - 1 : lag])
        return total

    taps = small_ref[...]
    conved = conv(raw, raw_edge[...], taps)
    conv_ref[...] = conved
    conved_states = conv(raw_states, states_edge[...], states_small_ref[...])
    conv_states_ref[...] = conved_states
    raw_edge[...] = raw[SPAN - 8 :]
    states_edge[...] = raw_states[SPAN - 8 :]
    values = conved * jax.nn.sigmoid(conved)
    states_in = conved_states * jax.nn.sigmoid(conved_states)
    b_rows = states_in[:, :STATE].astype(bf16)
    c_rows = states_in[:, STATE:].astype(bf16)
    _, steps, _, logs, entry, tail, through, row, column = decay_parts(steps_in, head_ref[...], marks, heads)
    spreader = spread_ref[...]
    scaled = values * spread(steps, spreader)
    mask = linked_mask(row, column, marks, segment_ref[...])
    scores = nt(c_rows, b_rows)
    logs_across = jnp.transpose(logs)
    pieces = []
    for pair in range(heads // 2):
        mixes = []
        for head in (2 * pair, 2 * pair + 1):
            factor = jnp.exp(logs[:, head : head + 1] - logs_across[head : head + 1, :] + mask)
            mixes.append((factor * scores).astype(bf16))
        block = scaled[:, pair * LANES : (pair + 1) * LANES]
        left = jnp.where(lane < HEAD_DIM, block, 0.0).astype(bf16)
        right = jnp.where(lane < HEAD_DIM, 0.0, block).astype(bf16)
        pieces.append(nn(jnp.concatenate(mixes, axis=1), jnp.concatenate([left, right], axis=0)))
    inside = jnp.concatenate(pieces, axis=1)
    held = state[...]
    entry_state_ref[0] = held
    across = nn(c_rows, held.astype(bf16)) * spread(entry, spreader)
    through_row = spread(jnp.broadcast_to(through, (8, LANES)), spreader)[0:1]
    state[...] = through_row * held + tn(b_rows, (spread(tail, spreader) * scaled).astype(bf16))
    y_ref[...] = inside + across + taps[6:7] * values


def gate_forward_kernel(rows, pieces, place_ref, normed_ref, y_ref, *refs):
    parts, refs = refs[:pieces], refs[pieces:]
    small_ref, gate_ref, part_ref, weights, out_weights = refs

    @pl.when(pl.program_id(0) == 0)
    def _():
        half = weights.shape[1] // 2
        load_weights(weights, 0, parts, (0, half), rows, place_ref)
        load_weights(out_weights, 0, parts, (half, 2 * half), rows, place_ref)

    gate = nn(normed_ref[...], weights[...])
    gate_ref[...] = gate
    gated = y_ref[...] * (gate * jax.nn.sigmoid(gate))
    squares = jnp.sum(gated * gated, axis=1, keepdims=True)
    part = nt((gated * small_ref[5:6]).astype(bf16), out_weights[...])
    width = part.shape[1]
    part_ref[:, :width] = part.astype(bf16)
    high, low = high_low(squares)
    lane = lax.broadcasted_iota(jnp.int32, (1, LANES), 1)
    part_ref[:, width:] = jnp.where(lane == 0, high, jnp.where(lane == 1, low, jnp.zeros_like(low)))


def gate_backward_kernel(second, rows, pieces, grad_arrays, base, *refs):
    place_ref, refs = refs[0], refs[1:]
    if second:
        (h_ref, own_ref, other_ref, teacher_ref, here_ref, beside_ref), refs = refs[:6], refs[6:]
    else:
        (own_ref, other_ref, next_h_ref, next_out_ref, grad_own_ref, grad_other_ref, next_gain_ref), refs = refs[:7], refs[7:]
    (normed_ref, gate_ref, y_ref), parts, refs = refs[:3], refs[3 : 3 + pieces], refs[3 + pieces :]
    (marks_ref, small_ref), refs = refs[:2], refs[2:]
    if second:
        out_ref, refs = refs[0], refs[1:]
    (grad_out_ref, grad_y_ref, part_ref), refs = refs[:3], refs[3:]
    grads, sums_ref, refs = refs[:grad_arrays], refs[grad_arrays], refs[grad_arrays + 1 :]
    weights, out_weights, acc_z, acc_o, sums = refs
    units = y_ref.shape[1]

    @pl.when(pl.program_id(0) == 0)
    def _():
        load_weights(weights, 0, parts, (0, units // 2), rows, place_ref)
        load_weights(out_weights, 0, parts, (units // 2, units), rows, place_ref)
        for ref in (acc_z, acc_o, sums):
            ref[...] = jnp.zeros_like(ref)

    branch, total, inverse = branch_of(own_ref, other_ref, units)
    if second:
        produced = h_ref[...].astype(f32) + branch
        out_ref[...] = jnp.where(place_ref[3] == 0, h_ref[...].astype(f32), produced).astype(bf16)
        steps = pl.num_programs(0)
        chunk = steps - 1 - pl.program_id(0)
        held = jnp.where(place_ref[1] == 0, teacher_ref[0], teacher_ref[1])
        came = jnp.where(chunk % (steps // 2) == place_ref[3], here_ref[...], beside_ref[...])
        target = jnp.where(chunk // (steps // 2) == place_ref[1], held, came)
        grad_out = marks_ref[:, 9:10] * (produced - target)
    else:
        grad_normed = grad_own_ref[...].astype(f32) + grad_other_ref[...].astype(f32)
        grad_out, gain_term = norm_backward(grad_normed, next_h_ref[...].astype(f32), next_out_ref[...], next_gain_ref[0:1, :])
        sums[7:8, :] += jnp.sum(gain_term, axis=0, keepdims=True)
    grad_out_ref[...] = grad_out
    grad = grad_out.astype(bf16)
    inner = jnp.sum(grad.astype(f32) * total, axis=1, keepdims=True) * (inverse * inverse * inverse) / (2 * units)
    gain = small_ref[5:6]
    gate = gate_ref[...]
    y = y_ref[...]
    gate_sig = jax.nn.sigmoid(gate)
    gate_silu = gate * gate_sig
    gated = y * gate_silu
    gated_unit = gated * inverse
    grad_mixed = nn(grad, out_weights[...])
    acc_o[...] += tn(grad, (gated_unit * gain).astype(bf16))
    sums[5:6, :] += jnp.sum(grad_mixed * gated_unit, axis=0, keepdims=True)
    grad_gated = grad_mixed * gain * inverse - gated * inner
    grad_gate = (grad_gated * y * (gate_sig * (1.0 + gate * (1.0 - gate_sig)))).astype(bf16)
    grad_y_ref[...] = (grad_gated * gate_silu).astype(bf16)
    acc_z[...] += tn(normed_ref[...], grad_gate)
    part_ref[...] = nt(grad_gate, weights[...])

    @pl.when(pl.program_id(0) == pl.num_programs(0) - 1)
    def _():
        store_grads(grads, (0, units // 2), acc_z, 0, rows, place_ref, base)
        store_grads(grads, (units // 2, units), acc_o, 0, rows, place_ref, base)
        sums_ref[...] = sums[...]


def scan_backward_kernel(heads, rows, pieces, *refs):
    (place_ref, grad_y_ref, gate_part_ref), parts, refs = refs[:3], refs[3 : 3 + pieces], refs[3 + pieces :]
    (marks_ref, segment_ref, small_ref, states_small_ref, head_ref, spread_ref), refs = refs[:6], refs[6:]
    (raw_ref, conv_ref, y_ref, raw_states_ref, conv_states_ref, steps_ref, entry_state_ref), refs = refs[:7], refs[7:]
    (grads_ref, part_ref, sums_ref, states_sums_ref), refs = refs[:4], refs[4:]
    weights, dstate, next_state, conv_edge, states_edge, sums, states_sums = refs
    step = pl.program_id(0)
    units = raw_ref.shape[1]

    @pl.when(step == 0)
    def _():
        for ref in (dstate, next_state, conv_edge, states_edge, sums, states_sums):
            ref[...] = jnp.zeros_like(ref)
        load_weights(weights, 0, parts, (0, units // 2), rows, place_ref)
        load_weights(weights, units, parts, (units // 2, units // 2 + 2 * STATE), rows, place_ref)

    marks = marks_ref[...]
    taps = small_ref[...]
    y = y_ref[...]
    grad_y_low = grad_y_ref[...]
    grad_y = grad_y_low.astype(f32)
    conved = conv_ref[...]
    value_sig = jax.nn.sigmoid(conved)
    values = conved * value_sig
    conved_states = conv_states_ref[...]
    states_sig = jax.nn.sigmoid(conved_states)
    states_in = conved_states * states_sig
    b_rows = states_in[:, :STATE].astype(bf16)
    c_rows = states_in[:, STATE:].astype(bf16)
    shifted, steps, log_steps, logs, entry, tail, through, row, column = decay_parts(steps_ref[...], head_ref[...], marks, heads)
    spreader = spread_ref[...]
    spread_steps = spread(steps, spreader)
    spread_entry = spread(entry, spreader)
    spread_tail = spread(tail, spreader)
    through_row = spread(jnp.broadcast_to(through, (8, LANES)), spreader)[0:1]
    scaled_low = (values * spread_steps).astype(bf16)
    scaled = scaled_low.astype(f32)
    mask = linked_mask(column, row, marks, segment_ref[...])
    scores = nt(b_rows, c_rows)
    logs_across = jnp.transpose(logs)
    lane = lax.broadcasted_iota(jnp.int32, (1, LANES), 1)
    is_left = lane < HEAD_DIM
    zero = jnp.zeros((), bf16)
    grad_scores = jnp.zeros((SPAN, SPAN), f32)
    pieces = []
    for pair in range(heads // 2):
        columns = slice(pair * LANES, (pair + 1) * LANES)
        block, grad = scaled_low[:, columns], grad_y_low[:, columns]
        grad_left = jnp.where(is_left, grad, zero)
        grad_right = jnp.where(is_left, zero, grad)
        mixes = []
        for head, grad_one in ((2 * pair, grad_left), (2 * pair + 1, grad_right)):
            factor = jnp.exp(logs_across[head : head + 1, :] - logs[:, head : head + 1] + mask)
            mixes.append((factor * scores).astype(bf16))
            grad_scores = grad_scores + nt(block, grad_one) * factor
        pieces.append(nn(jnp.concatenate(mixes, axis=1), jnp.concatenate([grad_left, grad_right], axis=0)))
    held = entry_state_ref[0]
    held_low = held.astype(bf16)
    gradient = dstate[...]
    gradient_low = gradient.astype(bf16)
    grad_scaled = jnp.concatenate(pieces, axis=1) + spread_tail * nn(b_rows, gradient_low)
    grad_entry = (spread_entry * grad_y).astype(bf16)
    grad_scores_low = grad_scores.astype(bf16)
    grad_c = tn(grad_scores_low, b_rows) + nt(grad_entry, held_low)
    grad_b = nn(grad_scores_low, c_rows) + nt((spread_tail * scaled).astype(bf16), gradient_low)
    state_term = jnp.sum(gradient * next_state[...], axis=0, keepdims=True)
    dstate[...] = through_row * gradient + tn(c_rows, grad_entry)
    next_state[...] = held
    skip = taps[6:7]
    sums[6:7, :] += jnp.sum(grad_y * values, axis=0, keepdims=True)
    grad_logs = gathered_heads(grad_y * (y - skip * values) - scaled * grad_scaled, spreader)
    state_heads = gathered_heads(jnp.broadcast_to(state_term, (8, units)), spreader)[0:1]
    last_row = lax.broadcasted_iota(jnp.int32, (SPAN, 1), 0) == SPAN - 1
    grad_logs = grad_logs + jnp.where(last_row, state_heads, 0.0)
    grad_log_steps = running_sum((row <= column).astype(bf16), grad_logs)
    grad_steps = gathered_heads(grad_scaled * values, spreader) - head_ref[1:2, :LANES] * grad_log_steps
    grad_steps_in = jnp.where(lane < heads, grad_steps * jax.nn.sigmoid(shifted), 0.0)
    states_sums[5:6, :] += jnp.concatenate(
        [
            jnp.sum(grad_steps_in, axis=0, keepdims=True),
            jnp.sum(grad_log_steps * log_steps, axis=0, keepdims=True),
        ],
        axis=1,
    )
    grad_values = grad_scaled * spread_steps + skip * grad_y
    grad_conved = grad_values * (value_sig * (1.0 + conved * (1.0 - value_sig)))
    grad_states = jnp.concatenate([grad_b, grad_c], axis=1)
    grad_conved_states = grad_states * (states_sig * (1.0 + conved_states * (1.0 - states_sig)))

    def conv_backward(block, edge, tap_rows, raw, total_ref):
        result = tap_rows[3:4] * block
        total_ref[3:4, :] += jnp.sum(block * raw, axis=0, keepdims=True)
        total_ref[4:5, :] += jnp.sum(block, axis=0, keepdims=True)
        for lag in (1, 2, 3):
            term = moved_up(block, edge, lag) * marks[:, 5 + lag : 6 + lag]
            result = result + tap_rows[3 - lag : 4 - lag] * term
            total_ref[3 - lag : 4 - lag, :] += jnp.sum(term * raw, axis=0, keepdims=True)
        return result

    grad_raw = conv_backward(grad_conved, conv_edge[...], taps, raw_ref[...], sums)
    grad_raw_states = conv_backward(
        grad_conved_states, states_edge[...], states_small_ref[...], raw_states_ref[...], states_sums
    )
    conv_edge[...] = grad_conved[:8]
    states_edge[...] = grad_conved_states[:8]
    turned = marks[0:1, 10:11] > 0.5
    first_states = jnp.where(turned, grad_raw_states[:, STATE:], grad_raw_states[:, :STATE])
    second_states = jnp.where(turned, grad_raw_states[:, :STATE], grad_raw_states[:, STATE:])
    own_steps = jnp.where(lane < heads // 2, grad_steps_in, 0.0)
    other_steps = jnp.where(lane < heads // 2, pltpu.roll(grad_steps_in, LANES - heads // 2, 1), 0.0)
    grads = jnp.concatenate([grad_raw, first_states, own_steps, second_states, other_steps], axis=1).astype(bf16)
    grads_ref[...] = grads
    part_ref[...] = (nt(grads, weights[...]) + gate_part_ref[...]).astype(bf16)

    @pl.when(step == pl.num_programs(0) - 1)
    def _():
        skips = gathered_heads(sums[...], spreader)[6:7]
        states_sums[6:7, :] = jnp.concatenate([skips, jnp.zeros_like(skips)], axis=1)
        sums_ref[...] = sums[...]
        states_sums_ref[...] = states_sums[...]


def scan_grads_kernel(heads, rows, pieces, grad_arrays, *refs):
    normed_ref, refs = refs[0], refs[1:]
    inputs, refs = refs[: 16 + pieces], refs[16 + pieces :]
    outs, refs = refs[:grad_arrays], refs[grad_arrays:]
    results, scratch, grads, acc = refs[:3], refs[3:-2], refs[-2], refs[-1]
    place_ref = inputs[0]
    units = acc.shape[1] - 4 * STATE

    @pl.when(pl.program_id(0) == 0)
    def _():
        acc[...] = jnp.zeros_like(acc)

    scan_backward_kernel(heads, rows, pieces, *inputs, grads, *results, *scratch)
    acc[...] += tn(normed_ref[...], grads[...])

    @pl.when(pl.program_id(0) == pl.num_programs(0) - 1)
    def _():
        store_grads(outs, (0, units // 2), acc, 0, rows, place_ref)
        store_grads(outs, (units // 2, units // 2 + 2 * STATE), acc, units, rows, place_ref)


def second_forward_kernel(heads, rows, *refs):
    inputs, gate_weights, refs = refs[:15], refs[15], refs[16:]
    outputs, (gate_ref, part_ref), refs = refs[:10], refs[10:12], refs[12:]
    scan_forward_kernel(True, heads, rows, 5, *inputs, *outputs, *refs[:5])
    normed_ref, y_ref, small_ref = outputs[2], outputs[5], inputs[11]
    gate_forward_kernel(rows, 1, inputs[0], normed_ref, y_ref, gate_weights, small_ref, gate_ref, part_ref, *refs[5:])


def second_backward_kernel(heads, rows, *refs):
    gate_inputs, refs = refs[:13], refs[13:]
    scan_weights, (segment_ref, states_small_ref, head_ref, spread_ref), refs = refs[:5], refs[5:9], refs[9:]
    (raw_ref, conv_ref, raw_states_ref, conv_states_ref, steps_ref, entry_state_ref), refs = refs[:6], refs[6:]
    (out_ref, grad_out_ref, grads_ref, gate_sums_ref, part_ref, sums_ref, states_sums_ref), refs = refs[:7], refs[7:]
    grad_y, gate_part, refs = refs[0], refs[1], refs[2:]
    gate_scratch, scan_scratch = refs[:5], refs[5:]
    place_ref, normed_ref, y_ref, marks_ref, small_ref = gate_inputs[0], gate_inputs[7], gate_inputs[9], gate_inputs[11], gate_inputs[12]
    base = scan_weights[0].shape[1]
    gate_backward_kernel(
        True, rows, 1, 1, base, *gate_inputs, out_ref, grad_out_ref, grad_y, gate_part, grads_ref, gate_sums_ref, *gate_scratch
    )
    scan_inputs = (place_ref, grad_y, gate_part, *scan_weights, marks_ref, segment_ref, small_ref, states_small_ref, head_ref, spread_ref)
    saved = (raw_ref, conv_ref, y_ref, raw_states_ref, conv_states_ref, steps_ref, entry_state_ref)
    scan_grads_kernel(heads, rows, 5, 1, normed_ref, *scan_inputs, *saved, grads_ref, part_ref, sums_ref, states_sums_ref, *scan_scratch)


def norm_backward(grad_normed, hidden, grad_out, gain):
    scale = lax.rsqrt(jnp.mean(hidden * hidden, axis=1, keepdims=True) + epsilon)
    weighted = grad_normed * gain
    shared = jnp.mean(weighted * hidden, axis=1, keepdims=True) * (scale * scale * scale)
    return grad_out + scale * weighted - hidden * shared, grad_normed * hidden * scale


VMEM_LIMIT = 60 * 1024 * 1024


def spreader_of(units):
    one = (np.arange(LANES)[:, None] == np.arange(units)[None, :] // HEAD_DIM).astype(np.float32)
    return jnp.asarray(np.concatenate([one, one], axis=0), bf16)


def rows_spec(width, last=None):
    if last is None:
        return pl.BlockSpec((SPAN, width), lambda i: (i, 0))
    return pl.BlockSpec((SPAN, width), lambda i: (last - i, 0))


def wide_spec(width):
    return pl.BlockSpec((WIDE, width), lambda i: (i, 0))


def whole_spec(array):
    return pl.BlockSpec(array.shape, lambda i: (0,) * array.ndim)


def call(kernel, inputs, outputs, scratch, chunks, flops):
    return pl.pallas_call(
        kernel,
        grid=(chunks,),
        in_specs=[spec for _, spec in inputs],
        out_specs=[spec for _, _, spec in outputs],
        out_shape=[jax.ShapeDtypeStruct(shape, dtype) for shape, dtype, _ in outputs],
        scratch_shapes=[pltpu.VMEM(shape, dtype) for shape, dtype in scratch],
        compiler_params=pltpu.CompilerParams(vmem_limit_bytes=VMEM_LIMIT, dimension_semantics=("arbitrary",)),
        cost_estimate=pl.CostEstimate(flops=flops, bytes_accessed=500_000, transcendentals=0),
    )(*[array for array, _ in inputs])


def fixed(array):
    return array, whole_spec(array)


def scalars(array):
    return array, pl.BlockSpec(memory_space=pltpu.SMEM)


def grad_outputs(width, columns):
    shape = (width // 2, columns)
    return [(shape, bf16, pl.BlockSpec(shape, lambda i: (0, 0)))] * 4


def awaited(arrays):
    return [(array, pl.BlockSpec(memory_space=pl.ANY)) for array in arrays]


def scan_forward(place, rows, h, parts, weights, marks, segment_row, params):
    length, width = h.shape
    units = params[0].shape[1]
    chunks = length // SPAN
    second = parts is not None
    inputs = [scalars(place), (h, rows_spec(width))]
    outputs = []
    if second:
        inputs += [(part, rows_spec(width + LANES)) for part in parts]
        outputs.append(((length, width), bf16, rows_spec(width)))
    inputs += [fixed(w) for w in weights]
    inputs += [(marks, rows_spec(LANES)), (segment_row, pl.BlockSpec((1, SPAN), lambda i: (0, i)))]
    inputs += [fixed(p) for p in params] + [fixed(spreader_of(units))]
    outputs.append(((8, width), f32, pl.BlockSpec((8, width), lambda i: (0, 0))))
    outputs.append(((length, width), bf16, rows_spec(width)))
    for columns in (units, units, units, 2 * STATE, 2 * STATE, LANES):
        outputs.append(((length, columns), f32, rows_spec(columns)))
    outputs.append(((chunks, STATE, units), f32, pl.BlockSpec((1, STATE, units), lambda i: (i, 0, 0))))
    scratch = [
        ((STATE, units), f32),
        ((8, units), f32),
        ((8, 2 * STATE), f32),
        ((8, width), f32),
        ((width, units + 4 * STATE), bf16),
    ]
    kernel = functools.partial(scan_forward_kernel, second, units // HEAD_DIM, rows, len(weights))
    results = call(kernel, inputs, outputs, scratch, chunks, 2_000_000_000)
    if not second:
        results = [h] + list(results)
    return results[0], results[1], results[2], results[3:]


def gate_forward(place, rows, normed, y, weights, params):
    length, width = normed.shape
    units = params[0].shape[1]
    inputs = [scalars(place), (normed, wide_spec(width)), (y, wide_spec(units))] + [fixed(w) for w in weights] + [fixed(params[0])]
    outputs = [((length, units), f32, wide_spec(units)), ((length, width + LANES), bf16, wide_spec(width + LANES))]
    scratch = [((width, units), bf16)] * 2
    return call(functools.partial(gate_forward_kernel, rows, len(weights)), inputs, outputs, scratch, length // WIDE, 1_000_000_000)


def gate_backward(place, rows, h, parts, extra, normed, gate, y, weights, marks, params):
    length, width = normed.shape
    units = params[0].shape[1]
    second = len(extra) == 1
    inputs = [scalars(place)] + ([(h, rows_spec(width))] if second else [])
    inputs += [(part, rows_spec(width + LANES)) for part in parts]
    inputs += [(array, rows_spec(width)) for array in extra[:4]] + [fixed(gain) for gain in extra[4:]]
    inputs += [(normed, rows_spec(width)), (gate, rows_spec(units)), (y, rows_spec(units))]
    inputs += [fixed(w) for w in weights] + [(marks, rows_spec(LANES)), fixed(params[0])]
    outputs = [((length, width), bf16, rows_spec(width))] if second else []
    outputs += [((length, width), f32, rows_spec(width)), ((length, units), bf16, rows_spec(units)), ((length, width), f32, rows_spec(width))]
    outputs += grad_outputs(width, units)
    outputs.append(((8, units), f32, pl.BlockSpec((8, units), lambda i: (0, 0))))
    scratch = [((width, units), bf16)] * 2 + [((width, units), f32)] * 2 + [((8, units), f32)]
    results = call(functools.partial(gate_backward_kernel, second, rows, len(weights), 4, 0), inputs, outputs, scratch, length // SPAN, 2_000_000_000)
    if not second:
        results = [None] + list(results)
    return results


def scan_scratch(width, units):
    return [
        ((width, units + 4 * STATE), bf16),
        ((STATE, units), f32),
        ((STATE, units), f32),
        ((8, units), f32),
        ((8, 2 * STATE), f32),
        ((8, units), f32),
        ((8, 2 * STATE), f32),
        ((SPAN, units + 4 * STATE), bf16),
        ((width, units + 4 * STATE), f32),
    ]


def scan_backward(place, rows, grad_y, gate_part, normed, weights, marks, segment_row, params, saved):
    length, width = gate_part.shape
    units = params[0].shape[1]
    chunks = length // SPAN
    last = chunks - 1
    inputs = [(normed, rows_spec(width, last)), scalars(place), (grad_y, rows_spec(units, last)), (gate_part, rows_spec(width, last))]
    inputs += [fixed(w) for w in weights]
    inputs += [(marks, rows_spec(LANES, last)), (segment_row, pl.BlockSpec((1, SPAN), lambda i: (0, last - i)))]
    inputs += [fixed(p) for p in params] + [fixed(spreader_of(units))]
    inputs += [(s, rows_spec(s.shape[1], last)) for s in saved[:6]]
    inputs.append((saved[6], pl.BlockSpec((1, STATE, units), lambda i: (last - i, 0, 0))))
    outputs = grad_outputs(width, units // 2 + 2 * STATE)
    outputs.append(((length, width), bf16, rows_spec(width, last)))
    for columns in (units, 2 * STATE):
        outputs.append(((8, columns), f32, pl.BlockSpec((8, columns), lambda i: (0, 0))))
    kernel = functools.partial(scan_grads_kernel, units // HEAD_DIM, rows, len(weights), len(outputs) - 3)
    return call(kernel, inputs, outputs, scan_scratch(width, units), chunks, 3_000_000_000)


def second_forward(place, rows, h, parts, weights, gate_weights, marks, segment_row, params):
    length, width = h.shape
    units = params[0].shape[1]
    chunks = length // SPAN
    inputs = [scalars(place), (h, rows_spec(width))] + [(part, rows_spec(width + LANES)) for part in parts]
    inputs += [fixed(w) for w in weights]
    inputs += [(marks, rows_spec(LANES)), (segment_row, pl.BlockSpec((1, SPAN), lambda i: (0, i)))]
    inputs += [fixed(p) for p in params] + [fixed(spreader_of(units)), fixed(gate_weights)]
    outputs = [((length, width), bf16, rows_spec(width)), ((8, width), f32, pl.BlockSpec((8, width), lambda i: (0, 0)))]
    outputs.append(((length, width), bf16, rows_spec(width)))
    for columns in (units, units, units, 2 * STATE, 2 * STATE, LANES):
        outputs.append(((length, columns), f32, rows_spec(columns)))
    outputs.append(((chunks, STATE, units), f32, pl.BlockSpec((1, STATE, units), lambda i: (i, 0, 0))))
    outputs += [((length, units), f32, rows_spec(units)), ((length, width + LANES), bf16, rows_spec(width + LANES))]
    scratch = [((STATE, units), f32), ((8, units), f32), ((8, 2 * STATE), f32), ((8, width), f32)]
    scratch += [((width, units + 4 * STATE), bf16)] + [((width, units), bf16)] * 2
    kernel = functools.partial(second_forward_kernel, units // HEAD_DIM, rows)
    results = call(kernel, inputs, outputs, scratch, chunks, 3_000_000_000)
    return results[0], results[1], results[2], results[3:10], results[10], results[11]


def second_backward(place, rows, h, parts, teacher, here, beside, normed, gate, weights, gate_weights, marks, segment_row, params, saved):
    length, width = normed.shape
    units = params[0].shape[1]
    chunks = length // SPAN
    last = chunks - 1
    inputs = [scalars(place), (h, rows_spec(width, last))] + [(part, rows_spec(width + LANES, last)) for part in parts]
    inputs.append((teacher, pl.BlockSpec((2, SPAN, width), lambda i: (0, (last - i) % (chunks // 2), 0))))
    inputs += [fixed(here), fixed(beside), (normed, rows_spec(width, last)), (gate, rows_spec(units, last))]
    inputs += [(saved[2], rows_spec(units, last)), fixed(gate_weights), (marks, rows_spec(LANES, last)), fixed(params[0])]
    inputs += [fixed(w) for w in weights] + [(segment_row, pl.BlockSpec((1, SPAN), lambda i: (0, last - i)))]
    inputs += [fixed(params[1]), fixed(params[2]), fixed(spreader_of(units))]
    inputs += [(saved[i], rows_spec(saved[i].shape[1], last)) for i in (0, 1, 3, 4, 5)]
    inputs.append((saved[6], pl.BlockSpec((1, STATE, units), lambda i: (last - i, 0, 0))))

    def sums(columns):
        return (8, columns), f32, pl.BlockSpec((8, columns), lambda i: (0, 0))

    shape = (width // 2, 4 * (units + units // 2 + 2 * STATE))
    outputs = [((length, width), bf16, rows_spec(width, last)), ((length, width), f32, rows_spec(width, last))]
    outputs += [(shape, bf16, pl.BlockSpec(shape, lambda i: (0, 0))), sums(units)]
    outputs += [((length, width), bf16, rows_spec(width, last)), sums(units), sums(2 * STATE)]
    scratch = [((SPAN, units), bf16), ((SPAN, width), f32)]
    scratch += [((width, units), bf16)] * 2 + [((width, units), f32)] * 2 + [((8, units), f32)]
    scratch += scan_scratch(width, units)
    kernel = functools.partial(second_backward_kernel, units // HEAD_DIM, rows)
    return call(kernel, inputs, outputs, scratch, chunks, 4_000_000_000)


def finish_kernel(
    place_ref, own_ref, other_ref, h_ref, grad_out_ref, gain_ref, rows_ref, away_ref, grad_ref, low_ref, sums_ref, placed_ref, sums
):
    step = pl.program_id(0)

    @pl.when(step == 0)
    def _():
        sums[...] = jnp.zeros_like(sums)

    grad_normed = own_ref[...].astype(f32) + other_ref[...].astype(f32)
    next_grad = grad_out_ref[...]
    grad, gain_term = norm_backward(grad_normed, h_ref[...].astype(f32), next_grad.astype(bf16).astype(f32), gain_ref[0:1, :])
    rows = jnp.where(place_ref[3] == 0, grad, next_grad)
    sums[0:1, :] += jnp.sum(gain_term, axis=0, keepdims=True)
    sums_ref[...] = sums[...]

    @pl.when(step < pl.num_programs(0) // 2)
    def _():
        low_ref[...] = rows.astype(bf16)
        placed_ref[0] = away_ref[...]

    @pl.when(step >= pl.num_programs(0) // 2)
    def _():
        grad_ref[0] = rows
        placed_ref[0] = rows_ref[...]


def finish(place, own, other, h, grad_out, gain, produced, produced_away):
    length, width = h.shape
    steps = length // SPAN
    part = steps // 2

    def rows(i, place):
        return ((i + part * (1 - place[1])) % steps, 0)

    block = pl.BlockSpec((SPAN, width), rows)
    whole = pl.BlockSpec((8, width), lambda i, place: (0, 0))

    def early(i):
        return jnp.minimum(i, part - 1)

    def late(i):
        return jnp.maximum(i - part, 0)

    def placed(i, place):
        return (jnp.where(i < part, 1 - place[1], place[1]), jnp.where(i < part, i, i - part), 0)

    return pl.pallas_call(
        finish_kernel,
        grid_spec=pltpu.PrefetchScalarGridSpec(
            num_scalar_prefetch=1,
            grid=(steps,),
            in_specs=[block] * 4
            + [
                whole,
                pl.BlockSpec((SPAN, width), lambda i, place: (part * place[1] + late(i), 0)),
                pl.BlockSpec((SPAN, width), lambda i, place: (early(i), 0)),
            ],
            out_specs=[
                pl.BlockSpec((1, SPAN, width), lambda i, place: (place[1], late(i), 0)),
                pl.BlockSpec((SPAN, width), lambda i, place: (early(i), 0)),
                whole,
                pl.BlockSpec((1, SPAN, width), placed),
            ],
            scratch_shapes=[pltpu.VMEM((8, width), f32)],
        ),
        out_shape=[
            jax.ShapeDtypeStruct((2, length // 2, width), f32),
            jax.ShapeDtypeStruct((length // 2, width), bf16),
            jax.ShapeDtypeStruct((8, width), f32),
            jax.ShapeDtypeStruct((2, length // 2, width), bf16),
        ],
        compiler_params=pltpu.CompilerParams(vmem_limit_bytes=VMEM_LIMIT, dimension_semantics=("arbitrary",)),
        cost_estimate=pl.CostEstimate(flops=0, bytes_accessed=500_000, transcendentals=0),
    )(place, own, other, h, grad_out, gain, produced, produced_away)


def placed_kernel(place_ref, away_ref, rows_ref, out_ref):
    out_ref[0] = away_ref[...].astype(f32)


def placed_rows(place, rows, away):
    half, width = away.shape
    return pl.pallas_call(
        placed_kernel,
        grid_spec=pltpu.PrefetchScalarGridSpec(
            num_scalar_prefetch=1,
            grid=(half // SPAN,),
            in_specs=[pl.BlockSpec((SPAN, width), lambda i, place: (i, 0)), pl.BlockSpec(memory_space=pl.ANY)],
            out_specs=pl.BlockSpec((1, SPAN, width), lambda i, place: (1 - place[1], i, 0)),
        ),
        out_shape=jax.ShapeDtypeStruct(rows.shape, rows.dtype),
        input_output_aliases={2: 0},
        compiler_params=pltpu.CompilerParams(vmem_limit_bytes=VMEM_LIMIT, dimension_semantics=("arbitrary",)),
        cost_estimate=pl.CostEstimate(flops=0, bytes_accessed=500_000, transcendentals=0),
    )(place, away, rows)


def marks_kernel(place_ref, lengths_ref, segments_ref, marks_ref, row_ref):
    turn, rank = place_ref[1], place_ref[2]
    micro, sequences = lengths_ref.shape
    length = segments_ref.shape[1]
    total = jnp.int32(0)
    for batch in range(micro):
        total = lax.fori_loop(0, sequences, lambda i, t: t + lengths_ref[batch, i], total)
    weight = 2.0 * (micro * sequences * length) / jnp.full((1, length), total, jnp.int32).astype(f32)
    position = lax.broadcasted_iota(jnp.int32, (1, length), 1)
    segment = jnp.where(turn == 0, segments_ref[0:1, :], segments_ref[1:2, :])
    wide = jnp.broadcast_to(segment, (8, length))

    def same(lag):
        moved = pltpu.roll(wide, lag % length, 1)[0:1]
        inside = (position >= lag) & (position < length + lag)
        return jnp.where(inside & (moved == segment), 1.0, 0.0)

    before = jnp.full((1, length), -1, jnp.int32)
    end = before
    for block in range(length // SPAN):
        here = (position >= block * SPAN) & (position < (block + 1) * SPAN)
        end = jnp.where(here, segment[:, (block + 1) * SPAN - 1 : (block + 1) * SPAN], end)
        if block:
            before = jnp.where(here, segment[:, block * SPAN - 1 : block * SPAN], before)
    as_float = segment.astype(f32)
    rows = [same(1), same(2), same(3)]
    rows += [jnp.where(segment == before, 1.0, 0.0), jnp.where(segment == end, 1.0, 0.0), as_float]
    rows += [same(-1), same(-2), same(-3)]
    rows += [jnp.where(position < lengths_ref[turn, rank], weight, 0.0), jnp.full((1, length), turn, jnp.int32).astype(f32)]
    rows.append(jnp.zeros((LANES - len(rows), length), f32))
    marks_ref[...] = jnp.transpose(jnp.concatenate(rows, axis=0))
    row_ref[...] = as_float


def token_marks(place, lengths, segments):
    length = segments.shape[1]
    return pl.pallas_call(
        marks_kernel,
        in_specs=[pl.BlockSpec(memory_space=pltpu.SMEM)] * 2 + [pl.BlockSpec(memory_space=pltpu.VMEM)],
        out_shape=[jax.ShapeDtypeStruct((length, LANES), f32), jax.ShapeDtypeStruct((1, length), f32)],
        compiler_params=pltpu.CompilerParams(vmem_limit_bytes=VMEM_LIMIT),
        cost_estimate=pl.CostEstimate(flops=0, bytes_accessed=500_000, transcendentals=0),
    )(place, lengths, segments)


def three_parts(value):
    high = value.astype(bf16)
    rest = value - high.astype(f32)
    middle = rest.astype(bf16)
    return high, middle, (rest - middle.astype(f32)).astype(bf16)


PARAM_ROWS = 16


def pack_kernel(
    place_ref, zx_ref, bc_ref, dt_ref, gain_ref, out_ref, conv_ref, gate_gain_ref, states_conv_ref, bias_ref, rate_ref, skip_ref, kept_ref, sent_ref
):
    turn, core = place_ref[1], place_ref[3]
    rows = zx_ref.shape[0]
    half = zx_ref.shape[2] // 2
    heads_half = dt_ref.shape[0] // 2
    lane = lax.broadcasted_iota(jnp.int32, (1, LANES), 1)
    bc = jnp.where(turn == 0, bc_ref[:, :STATE], bc_ref[:, STATE:])
    diagonal = lax.broadcasted_iota(jnp.int32, (rows, rows), 0) == lax.broadcasted_iota(jnp.int32, (rows, rows), 1)
    gain = jnp.sum(jnp.where(diagonal, gain_ref[...].astype(f32), 0.0), axis=1, keepdims=True)
    head = lax.broadcasted_iota(jnp.int32, (2 * heads_half, LANES), 0)
    column = lax.broadcasted_iota(jnp.int32, (2 * heads_half, LANES), 1)
    shared = jnp.concatenate([states_conv_ref[...], jnp.zeros((PARAM_ROWS - 5, 2 * STATE), bf16)], axis=0)
    split = [part.astype(f32) for ref in (bias_ref, rate_ref, skip_ref) for part in three_parts(ref[...])]
    heads = jnp.concatenate(split + [jnp.zeros((PARAM_ROWS - 9, split[0].shape[1]), f32)], axis=0)
    heads = jnp.concatenate([heads, jnp.zeros((PARAM_ROWS, LANES - heads.shape[1]), f32)], axis=1).astype(bf16)
    for ref, part in ((kept_ref, core), (sent_ref, 1 - core)):
        first = part == 0

        def chosen(array, start):
            return jnp.where(first, array[:, start : start + half], array[:, start + half : start + 2 * half])

        ref[:rows, :half] = chosen(zx_ref[:, 1, :], 0)
        ref[:rows, half : half + STATE] = bc
        taken = (head == column + part * heads_half) & (column < heads_half)
        own_steps = tn(dt_ref[...], jnp.where(taken, 1.0, 0.0).astype(bf16))
        ref[:rows, half + STATE : half + 2 * STATE] = jnp.where(lane == LANES // 2, gain, own_steps).astype(bf16)
        ref[:rows, half + 2 * STATE : 2 * half + 2 * STATE] = chosen(zx_ref[:, 0, :], 0)
        ref[:rows, 2 * half + 2 * STATE :] = chosen(out_ref, 0)
        ref[rows:, :] = jnp.zeros((PARAM_ROWS, ref.shape[1]), bf16)
        channels = jnp.concatenate([chosen(conv_ref, 0), chosen(gate_gain_ref, 0)], axis=0)
        ref[rows:, :half] = jnp.concatenate([channels, jnp.zeros((PARAM_ROWS - 6, half), bf16)], axis=0)
        ref[rows:, half : half + 2 * STATE] = shared
        ref[rows:, half + 2 * STATE : half + 2 * STATE + LANES] = heads


def plain_call(kernel, place, inputs, outputs, ready=()):
    count = len(ready)
    body = kernel if not count else lambda place_ref, *refs: kernel(place_ref, *refs[count:])
    return pl.pallas_call(
        body,
        in_specs=[pl.BlockSpec(memory_space=pltpu.SMEM)]
        + [pl.BlockSpec(memory_space=pl.ANY)] * count
        + [pl.BlockSpec(memory_space=pltpu.VMEM)] * len(inputs),
        out_shape=[jax.ShapeDtypeStruct(shape, dtype) for shape, dtype in outputs],
        compiler_params=pltpu.CompilerParams(vmem_limit_bytes=VMEM_LIMIT),
        cost_estimate=pl.CostEstimate(flops=0, bytes_accessed=500_000, transcendentals=0),
    )(place, *ready, *inputs)


def unpack_kernel(place_ref, kept_ref, received_ref, *refs):
    scan_ref, middle_ref, gate_ref, params_ref, channels_ref = refs
    kept_first = place_ref[3] == 0
    kept, received = kept_ref[...], received_ref[...]
    first = jnp.where(kept_first, kept, received)
    second = jnp.where(kept_first, received, kept)
    rows, scan = scan_ref.shape
    half = channels_ref.shape[1]
    scan_ref[...] = first[:rows, :scan]
    middle_ref[:, : 2 * half] = first[:rows, scan:]
    middle_ref[:, 2 * half :] = second[:rows, :scan]
    gate_ref[...] = second[:rows, scan:]
    params_ref[0] = first[rows:, : scan + LANES]
    params_ref[1] = second[rows:, : scan + LANES]
    channels_ref[:PARAM_ROWS] = first[rows:, :half]
    channels_ref[PARAM_ROWS:] = second[rows:, :half]


def params_kernel(heads_half, place_ref, params_ref, channels_ref, spread_ref, *refs):
    turn, core = place_ref[1], place_ref[3]
    half = channels_ref.shape[1]
    lane = lax.broadcasted_iota(jnp.int32, (1, LANES), 1)
    for layer in range(2):
        small_ref, states_ref, head_ref = refs[3 * layer : 3 * layer + 3]
        rows = params_ref[layer].astype(f32)
        split = rows[:, half + 2 * STATE :]
        heads = [split[3 * i : 3 * i + 1] + split[3 * i + 1 : 3 * i + 2] + split[3 * i + 2 : 3 * i + 3] for i in range(3)]
        heads = jnp.concatenate(heads + [jnp.zeros((5, LANES), f32)], axis=0)
        moved = [pltpu.roll(heads, (LANES - start * heads_half) % LANES, 1) for start in range(4)]

        def of(index):
            return jnp.where(index == 0, moved[0], jnp.where(index == 1, moved[1], jnp.where(index == 2, moved[2], moved[3])))

        own, other = of(2 * turn + core), pltpu.roll(of(2 * (1 - turn) + core), heads_half, 1)
        heads = jnp.where(lane < heads_half, own, jnp.where(lane < 2 * heads_half, other, 0.0))
        head_ref[...] = jnp.concatenate([heads[0:1], jnp.exp(heads[1:2]), jnp.zeros((6, LANES), f32)], axis=0)
        high, middle, low = three_parts(jnp.broadcast_to(heads[2:3], (8, LANES)))
        once = spread_ref[:LANES]
        skips = (nn(high, once) + nn(middle, once) + nn(low, once))[0:1]
        own_rows = rows[0:6, :half]
        other_rows = channels_ref[PARAM_ROWS * layer : PARAM_ROWS * layer + 6].astype(f32)
        channels = jnp.concatenate([own_rows, other_rows], axis=1)
        small_ref[...] = jnp.concatenate([channels, skips, jnp.zeros_like(skips)], axis=0)
        states_ref[...] = jnp.concatenate([rows[0:5, half : half + 2 * STATE], jnp.zeros((3, 2 * STATE), f32)], axis=0)


def beside_kernel(place_ref, *refs):
    out = refs[-1]
    start = 0
    for ref in refs[:-1]:
        out[:, start : start + ref.shape[1]] = ref[...]
        start += ref.shape[1]


def split_kernel(place_ref, whole_ref, *outs):
    start = 0
    for out in outs:
        out[...] = whole_ref[:, start : start + out.shape[1]]
        start += out.shape[1]


def join_kernel(place_ref, *refs):
    out = refs[-1]
    start = 0
    for group in range(len(refs) // 4):
        parts = refs[4 * group : 4 * group + 4]
        width = parts[0].shape[1]
        total = sum(part[...].astype(f32) for part in parts)
        out[:, start : start + width] = total.astype(bf16)
        start += width


def owned_kernel(place_ref, first_ref, second_ref, beside_ref, across_ref, both_ref, zx_ref, bc_ref, dt_ref, out_ref):
    first = place_ref[3] == 0
    half = out_ref.shape[1] // 2
    heads_half = dt_ref.shape[0] // 2
    mine = jnp.where(first, first_ref[...], second_ref[...]).astype(f32)
    beside = beside_ref[...].astype(f32)
    lower, upper = jnp.where(first, mine, beside), jnp.where(first, beside, mine)
    gate = half + 2 * STATE
    for index, part in enumerate((lower, upper)):
        columns = slice(index * half, (index + 1) * half)
        zx_ref[:, 0, columns] = part[:, gate : gate + half]
        zx_ref[:, 1, columns] = part[:, :half]
        out_ref[:, columns] = part[:, gate + half :]
    own = mine[:, half : half + STATE] + beside[:, half : half + STATE]
    other = across_ref[...].astype(f32) + both_ref[...].astype(f32)
    straight = place_ref[1] == 0
    bc_ref[:, :STATE] = jnp.where(straight, own, other)
    bc_ref[:, STATE:] = jnp.where(straight, other, own)
    lane = lax.broadcasted_iota(jnp.int32, (1, LANES), 1)
    steps = slice(half + STATE, half + 2 * STATE)
    both = jnp.transpose(jnp.where(lane < heads_half, lower[:, steps], pltpu.roll(upper[:, steps], heads_half, 1)))
    for head in range(2 * heads_half):
        dt_ref[head] = both[head : head + 1]


def small_kernel(gate0, scan0, states0, gate1, scan1, states1, gain_ref, out_ref):
    for layer, (gate, scan, states, gain) in enumerate(
        ((gate0, scan0, states0, gain_ref[0:1, :]), (gate1, scan1, states1, gate0[7:8, :]))
    ):
        start = 16 * layer
        out_ref[start : start + 5, :] = scan[0:5, :]
        out_ref[start + 5 : start + 6, :] = gate[5:6, :]
        out_ref[start + 6 : start + 7, :] = gain
        out_ref[start + 7 : start + 16, :] = jnp.zeros((9, out_ref.shape[1]), f32)
        out_ref[start + 8 : start + 15, : 2 * STATE] = states[0:7, :]


def fold_kernel(heads_half, place_ref, own_ref, away_ref, mine_ref, others_ref):
    first = place_ref[3] == 0
    half = mine_ref.shape[1]
    folded = []
    for layer in range(2):
        own, away = own_ref[16 * layer : 16 * layer + 16], away_ref[16 * layer : 16 * layer + 16]
        units = own[0:6, :half] + away[0:6, half:]
        gain = own[6:7] + away[6:7]
        total = own[8:16, :half] + away[8:16, :half]
        own_heads = jnp.concatenate([own[14:15, :LANES], own[13:14, : 2 * LANES]], axis=1)
        away_heads = jnp.concatenate([away[14:15, :LANES], away[13:14, : 2 * LANES]], axis=1)
        moved = pltpu.roll(jnp.broadcast_to(away_heads, (8, 3 * LANES)), 3 * LANES - heads_half, 1)[0:1]
        heads = jnp.concatenate([own_heads + moved, jnp.zeros((1, half - 3 * LANES), f32)], axis=1) if half > 3 * LANES else own_heads + moved
        zeros = jnp.zeros((2, half), f32)
        folded.append(jnp.concatenate([units, gain[:, :half], gain[:, half:], total[0:5], heads, zeros], axis=0))
    mine_ref[...] = jnp.where(first, folded[0], folded[1])
    others_ref[...] = jnp.where(first, folded[1], folded[0])


def small_outputs_kernel(heads_half, place_ref, total_ref, conv_ref, states_conv_ref, gate_gain_ref, heads_ref, gain_ref):
    first = place_ref[3] == 0
    half = total_ref.shape[1]
    here, there = total_ref[0:16], total_ref[16:32]
    lower, upper = jnp.where(first, here, there), jnp.where(first, there, here)
    states = here[8:13, : 2 * STATE] + there[8:13, : 2 * STATE]
    for row in range(5):
        conv_ref[row, :, :half] = lower[row : row + 1]
        conv_ref[row, :, half:] = upper[row : row + 1]
        states_conv_ref[row] = states[row : row + 1]
    gate_gain_ref[:, :half] = lower[5:6]
    gate_gain_ref[:, half:] = upper[5:6]
    lane = lax.broadcasted_iota(jnp.int32, (1, LANES), 1)
    for row in range(3):
        own = lower[13:14, row * LANES : (row + 1) * LANES]
        other = pltpu.roll(jnp.broadcast_to(upper[13:14, row * LANES : (row + 1) * LANES], (8, LANES)), heads_half, 1)[0:1]
        heads_ref[row : row + 1, :] = jnp.where(lane < heads_half, own, other)[:, : 2 * heads_half]
    gain = jnp.concatenate([here[6:7], here[7:8]], axis=1)
    size = gain_ref.shape[1]
    share = jnp.zeros(gain_ref.shape, f32)
    for rank in range(2 * half // size):
        share = jnp.where(place_ref[2] == rank, gain[:, rank * size : (rank + 1) * size], share)
    gain_ref[...] = share


def tied(*values):
    return lax.optimization_barrier(values)


def swapped(block, axis):
    return lax.ppermute(block, axis, [(0, 1), (1, 0)])


def far_swapped(block):
    size = lax.axis_size("tensor")
    return lax.ppermute(block, ("section", "tensor"), [(i, 2 * size - 1 - i) for i in range(2 * size)])


def body(
    x_input,
    teacher,
    segment_ids,
    valid_len,
    norm_gain,
    w_zx,
    w_bc,
    w_dt,
    conv_x,
    conv_bc,
    dt_bias,
    a_log,
    d_skip,
    gnorm_gain,
    w_out,
):
    local_rows, width = x_input.shape[1:]
    ranks = lax.axis_size("dp")
    places = ranks // 2
    core = lax.axis_index("section")
    turn = lax.axis_index("tensor")
    rank = lax.axis_index("dp")
    place = jnp.stack([rank % 2, turn, rank, core]).astype(jnp.int32)
    on_first = core == 0
    block_rows = w_zx.shape[1]
    half = w_zx.shape[3] // 2
    units = 2 * half
    heads_half = w_dt.shape[2] // 2
    scan_columns = half + 2 * STATE
    line_groups = [[2 * index + start for index in range(places)] for start in range(2)]

    def by_layer(kept, received):
        return jnp.where(on_first, kept, received), jnp.where(on_first, received, kept)

    def x_swapped(block):
        return lax.ppermute(block, "dp", [(i, i ^ 1) for i in range(ranks)])

    def y_swapped(block):
        return swapped(block, "tensor")

    def line_gather(block):
        return lax.all_gather(block, "dp", axis_index_groups=line_groups, axis=0, tiled=True)

    def line_reduce(block):
        return lax.psum_scatter(block, "dp", axis_index_groups=line_groups, scatter_dimension=0, tiled=True)

    def line_total(block, beside):
        if places != 4:
            return lax.psum(block, "dp", axis_index_groups=line_groups), beside

        def send(rows, moves):
            return lax.ppermute(rows, "dp", [(2 * a + start, 2 * b + start) for a, b in moves for start in range(2)])

        up, down = send(block, [(0, 1), (1, 2), (2, 3)]), send(block, [(1, 0), (2, 1), (3, 2)])
        up2, down2 = send(up, [(1, 2), (2, 3)]), send(down, [(2, 1), (1, 0)])
        far = send(jnp.where(rank // 2 == 1, up, down), [(1, 3), (2, 0)])
        up2, down2, far, beside = tied(up2, down2, far, beside)
        return block + up + down + up2 + down2 + far, beside

    pack_shape = (block_rows + PARAM_ROWS, scan_columns + units)
    kept, sent = plain_call(
        pack_kernel,
        place,
        (w_zx[0], w_bc[0], w_dt[0].T, norm_gain, w_out[0].T, conv_x[0], gnorm_gain, conv_bc[0], dt_bias, a_log, d_skip),
        [(pack_shape, bf16)] * 2,
    )
    received = swapped(sent, "section")
    scan_block, middle_block, gate_block, params_both, channels = plain_call(
        unpack_kernel,
        place,
        (kept, received),
        [
            ((block_rows, scan_columns), bf16),
            ((block_rows, units + scan_columns), bf16),
            ((block_rows, units), bf16),
            ((2, PARAM_ROWS, scan_columns + LANES), bf16),
            ((2 * PARAM_ROWS, half), bf16),
        ],
    )

    both_ways = [(2 * d + t, 2 * (d ^ 1) + 1 - t) for d in range(ranks) for t in range(2)]

    def over_plane(own, x_block, y_block, far_block):
        far = lax.ppermute(far_block, ("dp", "tensor"), both_ways)
        return own, x_swapped(x_block), y_swapped(y_block), far

    def plane_end(block, over_x, over_tensor):
        cut = places // 2 * block_rows
        return block, over_x, over_tensor, y_swapped(over_x[:cut]), x_swapped(over_tensor[cut:])

    def quarter(rows):
        away = lax.dynamic_index_in_dim(rows, 1 - turn, 0, keepdims=False)
        return lax.dynamic_slice_in_dim(away, core * (local_rows // 2), local_rows // 2, 0)

    def whole_rows(rows, here, beside):
        own = lax.dynamic_index_in_dim(rows, turn, 0, keepdims=False)
        other = jnp.concatenate(by_layer(here, beside), axis=0)
        return jnp.where(turn == 0, jnp.concatenate([own, other]), jnp.concatenate([other, own]))

    scan_line, here, channels = tied(line_gather(scan_block), y_swapped(quarter(x_input)), y_swapped(channels))
    scan_line, middle_block = tied(scan_line, middle_block)
    middle_line = line_gather(middle_block)
    scan_half = scan_line, x_swapped(scan_line), y_swapped(scan_line)
    x_rows = whole_rows(x_input, here, swapped(here, "section"))
    params = plain_call(
        functools.partial(params_kernel, heads_half),
        place,
        (params_both, channels, spreader_of(units)),
        [((8, units), f32), ((8, 2 * STATE), f32), ((8, LANES), f32)] * 2,
    )
    params = [params[:3], params[3:]]
    marks, segment_row = token_marks(place, valid_len, segment_ids[:, 0])
    over_x = x_swapped(gate_block)
    side = (gate_block, over_x, y_swapped(gate_block), y_swapped(over_x))
    side = plain_call(beside_kernel, place, side, [((block_rows, 4 * units), bf16)], (x_rows, marks, params[0][0]))[0]
    scan_first, side = tied(plane_end(*scan_half), side)
    middle_line, side = tied(middle_line, side)
    gate_second = line_gather(side)
    gate_line, next_line = plain_call(
        split_kernel,
        place,
        (middle_line,),
        [((places * block_rows, units), bf16), ((places * block_rows, scan_columns), bf16)],
        (scan_first[4],),
    )

    gate_half = gate_line, x_swapped(gate_line), y_swapped(gate_line)
    next_half = next_line, x_swapped(next_line), y_swapped(next_line)
    results = scan_forward(place, block_rows, x_rows, None, scan_first, marks, segment_row, params[0])
    results, gate_half = tied(results, gate_half)
    _, gain_first, normed_first, saved_first = results
    gate_first = plane_end(*gate_half)
    results = gate_forward(place, block_rows, normed_first, saved_first[2], gate_first, params[0])
    (gated_first, part), scan_second = tied(results, plane_end(*next_half))
    parts_first = (part, swapped(part, "section"))
    parts_first, teacher, gate_second = tied(parts_first, teacher, gate_second)
    results = second_forward(
        place, block_rows, x_rows, parts_first, scan_second, gate_second, marks, segment_row, params[1]
    )
    results, here = tied(results, y_swapped(quarter(teacher)))
    hidden, gain_second, normed_second, saved_second, gated_second, part = results
    parts_second = (part, swapped(part, "section"))
    beside = swapped(here, "section")

    def add(*blocks):
        return sum(block.astype(f32) for block in blocks).astype(bf16)

    def away_rows(rows):
        return y_swapped(lax.dynamic_slice_in_dim(rows, (1 - turn) * local_rows, local_rows, 0))

    produced, grad_out, grads, gate_sums, part, sums, states_sums = second_backward(
        place,
        block_rows,
        hidden,
        parts_second,
        teacher,
        here,
        beside,
        normed_second,
        gated_second,
        scan_second,
        gate_second,
        marks,
        segment_row,
        params[1],
        saved_second,
    )
    quarters = line_reduce(grads)
    sums_second = (gate_sums, sums, states_sums)
    grad_parts = (part, swapped(part, "section"))
    results = gate_backward(
        place,
        block_rows,
        x_rows,
        parts_first,
        (hidden, grad_out) + grad_parts + (gain_second,),
        normed_first,
        gated_first,
        saved_first[2],
        gate_first,
        marks,
        params[0],
    )
    results, produced_away = tied(results[1:], away_rows(produced))
    grad_hidden, grad_y, gate_part = results[:3]
    gate_reduce = over_plane(*results[3:7])
    gate_sums_first = results[7]
    results = scan_backward(
        place, block_rows, grad_y, gate_part, normed_first, scan_first, marks, segment_row, params[0], saved_first
    )
    results, gate_reduce = tied(results, gate_reduce)
    scan_reduce = over_plane(*results[:4])
    part, sums, states_sums = results[4:]
    sums_first = (gate_sums_first, sums, states_sums)
    grad_rows, grad_low, gain_sums, layer_outputs = finish(
        place, part, swapped(part, "section"), x_rows, grad_hidden, gain_first, produced, produced_away
    )
    smalls = plain_call(
        lambda place_ref, *refs: small_kernel(*refs), place, sums_first + sums_second + (gain_sums,), [((32, units), f32)]
    )[0]
    smalls, scan_reduce = line_total(smalls, scan_reduce)
    blocks = plain_call(
        join_kernel,
        place,
        scan_reduce + gate_reduce,
        [((places * block_rows, scan_columns + units), bf16)],
        (quarters,),
    )[0]
    owned_first = line_reduce(blocks)
    quarters = plain_call(
        split_kernel, place, (quarters,), [((block_rows, scan_columns + units), bf16)] * 4, (blocks,)
    )
    owned_second = add(*over_plane(*quarters))
    smalls_away, grad_low = tied(y_swapped(smalls), grad_low)
    mine, others = plain_call(
        functools.partial(fold_kernel, heads_half), place, (smalls, smalls_away), [((16, half), f32)] * 2
    )
    total = jnp.concatenate([mine, swapped(others, "section")])
    owned_first, boundary = tied(owned_first, placed_rows(place, grad_rows, y_swapped(grad_low)))
    total = total + x_swapped(total)
    grad_conv, grad_states_conv, grad_gate_gain, grad_heads, gain_total = plain_call(
        functools.partial(small_outputs_kernel, heads_half),
        place,
        (total,),
        [((5, 1, units), f32), ((5, 1, 2 * STATE), f32), ((1, units), f32), ((3, 2 * heads_half), f32), ((1, block_rows), f32)],
    )

    others = jnp.where(on_first, owned_second, owned_first)
    own_states, other_states = by_layer(owned_first[:, half : half + STATE], owned_second[:, half : half + STATE])
    grad_zx, grad_bc, grad_dt, grad_out_w = plain_call(
        owned_kernel,
        place,
        (owned_first, owned_second, swapped(others, "section"), y_swapped(own_states), far_swapped(other_states)),
        [((block_rows, 2, units), f32), ((block_rows, 2 * STATE), f32), ((2 * heads_half, 1, block_rows), f32), ((block_rows, units), f32)],
        (boundary, layer_outputs, grad_conv),
    )
    return (
        layer_outputs[None],
        boundary[None],
        gain_total,
        grad_zx[None],
        grad_bc[None],
        grad_dt.transpose(1, 2, 0),
        grad_conv.transpose(1, 0, 2),
        grad_states_conv.transpose(1, 0, 2),
        grad_heads[1:2],
        grad_heads[2:3],
        grad_heads[0:1],
        grad_gate_gain,
        grad_out_w.T[None],
    )


def solution(mesh):
    placed = (
        P(None, ("dp", "tensor"), None),
        P(None, ("dp", "tensor"), None),
        P(None, "dp", None),
        P(),
        P("section", "dp"),
        P("section", "dp", None, "tensor"),
        P("section", "dp", None),
        P("section", "dp", "tensor"),
        P("section", None, "tensor"),
        P("section", None, None),
        P("section", None),
        P("section", None),
        P("section", None),
        P("section", "tensor"),
        P("section", "tensor", "dp"),
    )
    return jax.shard_map(
        body,
        mesh=mesh,
        in_specs=placed,
        out_specs=(
            P("section", None, ("dp", "tensor"), None),
            P("section", None, ("dp", "tensor"), None),
            P("section", "dp"),
            P("section", "dp", None, "tensor"),
            P("section", "dp", None),
            P("section", "dp", "tensor"),
            P("section", None, "tensor"),
            P("section", None, None),
            P("section", "tensor"),
            P("section", "tensor"),
            P("section", "tensor"),
            P("section", "tensor"),
            P("section", "tensor", "dp"),
        ),
        check_vma=False,
    )
```

```python
import functools

import jax
import jax.numpy as jnp
import numpy as np
from jax import lax
from jax.experimental import pallas as pl
from jax.experimental.pallas import tpu as pltpu
from jax.sharding import PartitionSpec as P

HEAD_DIM = 64
STATE = 128
SPAN = 256
WIDE = 512
LANES = 128

epsilon = 1e-05
f32 = jnp.float32
bf16 = jnp.bfloat16


def nn(left, right):
    return lax.dot_general(left, right, (((1,), (0,)), ((), ())), preferred_element_type=f32)


def nt(left, right):
    return lax.dot_general(left, right, (((1,), (1,)), ((), ())), preferred_element_type=f32)


def tn(left, right):
    return lax.dot_general(left, right, (((0,), (0,)), ((), ())), preferred_element_type=f32)


def high_low(value):
    high = value.astype(bf16)
    return high, (value - high.astype(f32)).astype(bf16)


def spread(per_head, spreader):
    return nn(jnp.concatenate(high_low(per_head), axis=1), spreader)


def gathered_heads(units, spreader):
    high, low = high_low(units)
    once = spreader[:LANES]
    return nt(high, once) + nt(low, once)


def running_sum(triangle, value):
    high = value.astype(bf16)
    rest = value - high.astype(f32)
    middle = rest.astype(bf16)
    low = (rest - middle.astype(f32)).astype(bf16)
    sums = nn(triangle, jnp.concatenate([high, middle, low], axis=1))
    return sums[:, :LANES] + sums[:, LANES : 2 * LANES] + sums[:, 2 * LANES :]


def softplus(value):
    return jnp.maximum(value, 0.0) + jnp.log1p(jnp.exp(-jnp.abs(value)))


def moved_down(block, edge, lag):
    rolled = pltpu.roll(block, lag, 0)
    row = lax.broadcasted_iota(jnp.int32, (8, 1), 0)
    first = jnp.where(row < lag, pltpu.roll(edge, lag, 0), rolled[:8])
    return jnp.concatenate([first, rolled[8:]], axis=0)


def moved_up(block, edge, lag):
    length = block.shape[0]
    rolled = pltpu.roll(block, length - lag, 0)
    row = lax.broadcasted_iota(jnp.int32, (8, 1), 0)
    last = jnp.where(row >= 8 - lag, pltpu.roll(edge, 8 - lag, 0), rolled[length - 8 :])
    return jnp.concatenate([rolled[: length - 8], last], axis=0)


def decay_parts(steps_in, head_rows, marks, heads):
    lane = lax.broadcasted_iota(jnp.int32, (1, LANES), 1)
    live = lane < heads
    shifted = steps_in + head_rows[0:1, :LANES]
    steps = jnp.where(live, softplus(shifted), 0.0)
    rates = head_rows[1:2, :LANES]
    log_steps = -steps * rates
    row = lax.broadcasted_iota(jnp.int32, (SPAN, SPAN), 0)
    column = lax.broadcasted_iota(jnp.int32, (SPAN, SPAN), 1)
    lower = (row >= column).astype(bf16)
    logs = running_sum(lower, log_steps)
    last = logs[SPAN - 1 : SPAN]
    entry = jnp.exp(logs) * marks[:, 3:4]
    tail = jnp.exp(last - logs) * marks[:, 4:5]
    through = jnp.exp(last) * marks[SPAN - 1 : SPAN, 3:4]
    entry = jnp.where(live, entry, 0.0)
    tail = jnp.where(live, tail, 0.0)
    through = jnp.where(live, through, 0.0)
    return shifted, steps, log_steps, logs, entry, tail, through, row, column


def linked_mask(row, column, marks, segment_row):
    linked = (row >= column) & (marks[:, 5:6] == segment_row)
    return jnp.where(linked, 0.0, -1e30)


def branch_of(own_ref, other_ref, units):
    width = own_ref.shape[1] - LANES
    own = own_ref[...].astype(f32)
    other = other_ref[...].astype(f32)
    total = own[:, :width] + other[:, :width]
    own_squares = own[:, width : width + 1] + own[:, width + 1 : width + 2]
    other_squares = other[:, width : width + 1] + other[:, width + 1 : width + 2]
    inverse = lax.rsqrt((own_squares + other_squares) / (2 * units) + epsilon)
    return total * inverse, total, inverse


PLANE = ((False, False), (True, False), (False, True), (True, True))


def load_weights(weights, start, refs, columns, rows, place_ref):
    first, last = columns
    mine = place_ref[0]
    size = refs[0].shape[1] // 4
    base = 0
    for index in range(len(refs) if len(refs) > 1 else 4):
        moved, turned = PLANE[min(index, 3)]
        ref, offset = (refs[0], index * size) if len(refs) == 1 else (refs[index], 0)
        place = 1 - mine if moved else mine
        target = start + (last - first if turned else 0)
        for step in range(ref.shape[0] // rows):
            row = pl.multiple_of((2 * (base + step) + place) * rows, 32)
            weights[pl.ds(row, rows), target : target + last - first] = ref[step * rows : (step + 1) * rows, offset + first : offset + last]
        base = ref.shape[0] // rows if index == 3 else 0


def store_grads(refs, columns, acc, start, rows, place_ref, base=0):
    first, last = columns
    mine = place_ref[0]
    size = refs[0].shape[1] // 4
    for index, (moved, turned) in enumerate(PLANE):
        ref, offset = (refs[0], index * size + base) if len(refs) == 1 else (refs[index], 0)
        place = 1 - mine if moved else mine
        source = start + (last - first if turned else 0)
        for step in range(ref.shape[0] // rows):
            row = pl.multiple_of((2 * step + place) * rows, 32)
            block = acc[pl.ds(row, rows), source : source + last - first]
            ref[step * rows : (step + 1) * rows, offset + first : offset + last] = block.astype(bf16)


def scan_forward_kernel(second, heads, rows, pieces, *refs):
    place_ref, refs = refs[0], refs[1:]
    if second:
        (h_ref, own_ref, other_ref), refs = refs[:3], refs[3:]
    else:
        (h_ref,), refs = refs[:1], refs[1:]
    parts, refs = refs[:pieces], refs[pieces:]
    (marks_ref, segment_ref, small_ref, states_small_ref, head_ref, spread_ref), refs = refs[:6], refs[6:]
    if second:
        h_out, refs = refs[0], refs[1:]
    gain_ref, refs = refs[0], refs[1:]
    normed_ref, raw_ref, conv_ref, y_ref, raw_states_ref, conv_states_ref, steps_ref, entry_state_ref = refs[:8]
    state, raw_edge, states_edge, gain, weights = refs[8:]
    units = raw_ref.shape[1]

    @pl.when(pl.program_id(0) == 0)
    def _():
        state[...] = jnp.zeros_like(state)
        raw_edge[...] = jnp.zeros_like(raw_edge)
        states_edge[...] = jnp.zeros_like(states_edge)
        load_weights(weights, 0, parts, (0, units // 2), rows, place_ref)
        load_weights(weights, units, parts, (units // 2, units // 2 + 2 * STATE), rows, place_ref)
        steps_columns = weights[:, units + STATE : units + STATE + LANES].astype(f32)
        gain[...] = jnp.broadcast_to(jnp.transpose(steps_columns)[LANES // 2 : LANES // 2 + 1, :], gain.shape)
        gain_ref[...] = gain[...]

    hidden = h_ref[...].astype(f32)
    if second:
        rounded = (hidden + branch_of(own_ref, other_ref, units)[0]).astype(bf16)
        h_out[...] = rounded
        hidden = rounded.astype(f32)
    scale = lax.rsqrt(jnp.mean(hidden * hidden, axis=1, keepdims=True) + epsilon)
    normed = (hidden * scale * gain[0:1, :]).astype(bf16)
    normed_ref[...] = normed
    projected = nn(normed, weights[...])
    raw = projected[:, :units]
    first, second_part = projected[:, units : units + 2 * STATE], projected[:, units + 2 * STATE :]
    marks = marks_ref[...]
    turned = marks[0:1, 10:11] > 0.5
    raw_states = jnp.concatenate(
        [
            jnp.where(turned, second_part[:, :STATE], first[:, :STATE]),
            jnp.where(turned, first[:, :STATE], second_part[:, :STATE]),
        ],
        axis=1,
    )
    lane = lax.broadcasted_iota(jnp.int32, (1, LANES), 1)
    steps_in = jnp.where(lane < heads // 2, first[:, STATE:], pltpu.roll(second_part[:, STATE:], heads // 2, 1))
    raw_ref[...] = raw
    raw_states_ref[...] = raw_states
    steps_ref[...] = steps_in

    def conv(block, edge, taps):
        total = taps[4:5] + taps[3:4] * block
        for lag in (1, 2, 3):
            total = total + taps[3 - lag : 4 - lag] * (moved_down(block, edge, lag) * marks[:, lag - 1 : lag])
        return total

    taps = small_ref[...]
    conved = conv(raw, raw_edge[...], taps)
    conv_ref[...] = conved
    conved_states = conv(raw_states, states_edge[...], states_small_ref[...])
    conv_states_ref[...] = conved_states
    raw_edge[...] = raw[SPAN - 8 :]
    states_edge[...] = raw_states[SPAN - 8 :]
    values = conved * jax.nn.sigmoid(conved)
    states_in = conved_states * jax.nn.sigmoid(conved_states)
    b_rows = states_in[:, :STATE].astype(bf16)
    c_rows = states_in[:, STATE:].astype(bf16)
    _, steps, _, logs, entry, tail, through, row, column = decay_parts(steps_in, head_ref[...], marks, heads)
    spreader = spread_ref[...]
    scaled = values * spread(steps, spreader)
    mask = linked_mask(row, column, marks, segment_ref[...])
    scores = nt(c_rows, b_rows)
    logs_across = jnp.transpose(logs)
    cut = SPAN // 2
    pieces = []
    for pair in range(heads // 2):
        block = scaled[:, pair * LANES : (pair + 1) * LANES]
        left = jnp.where(lane < HEAD_DIM, block, 0.0).astype(bf16)
        right = jnp.where(lane < HEAD_DIM, 0.0, block).astype(bf16)
        halves = []
        for rows_of, seen in ((slice(0, cut), cut), (slice(cut, SPAN), SPAN)):
            mixes = []
            for head in (2 * pair, 2 * pair + 1):
                gap = logs[rows_of, head : head + 1] - logs_across[head : head + 1, :seen]
                mixes.append((jnp.exp(gap + mask[rows_of, :seen]) * scores[rows_of, :seen]).astype(bf16))
            halves.append(nn(jnp.concatenate(mixes, axis=1), jnp.concatenate([left[:seen], right[:seen]], axis=0)))
        pieces.append(jnp.concatenate(halves, axis=0))
    inside = jnp.concatenate(pieces, axis=1)
    held = state[...]
    entry_state_ref[0] = held
    across = nn(c_rows, held.astype(bf16)) * spread(entry, spreader)
    through_row = spread(jnp.broadcast_to(through, (8, LANES)), spreader)[0:1]
    state[...] = through_row * held + tn(b_rows, (spread(tail, spreader) * scaled).astype(bf16))
    y_ref[...] = inside + across + taps[6:7] * values


def gate_forward_kernel(rows, pieces, place_ref, normed_ref, y_ref, *refs):
    parts, refs = refs[:pieces], refs[pieces:]
    small_ref, gate_ref, part_ref, weights, out_weights = refs

    @pl.when(pl.program_id(0) == 0)
    def _():
        half = weights.shape[1] // 2
        load_weights(weights, 0, parts, (0, half), rows, place_ref)
        load_weights(out_weights, 0, parts, (half, 2 * half), rows, place_ref)

    gate = nn(normed_ref[...], weights[...])
    gate_ref[...] = gate
    gated = y_ref[...] * (gate * jax.nn.sigmoid(gate))
    squares = jnp.sum(gated * gated, axis=1, keepdims=True)
    part = nt((gated * small_ref[5:6]).astype(bf16), out_weights[...])
    width = part.shape[1]
    part_ref[:, :width] = part.astype(bf16)
    high, low = high_low(squares)
    lane = lax.broadcasted_iota(jnp.int32, (1, LANES), 1)
    part_ref[:, width:] = jnp.where(lane == 0, high, jnp.where(lane == 1, low, jnp.zeros_like(low)))


def gate_backward_kernel(second, rows, pieces, grad_arrays, base, *refs):
    place_ref, refs = refs[0], refs[1:]
    if second:
        (h_ref, own_ref, other_ref, teacher_ref, here_ref, beside_ref), refs = refs[:6], refs[6:]
    else:
        (own_ref, other_ref, next_h_ref, next_out_ref, grad_own_ref, grad_other_ref, next_gain_ref), refs = refs[:7], refs[7:]
    (normed_ref, gate_ref, y_ref), parts, refs = refs[:3], refs[3 : 3 + pieces], refs[3 + pieces :]
    (marks_ref, small_ref), refs = refs[:2], refs[2:]
    if second:
        out_ref, refs = refs[0], refs[1:]
    (grad_out_ref, grad_y_ref, part_ref), refs = refs[:3], refs[3:]
    grads, sums_ref, refs = refs[:grad_arrays], refs[grad_arrays], refs[grad_arrays + 1 :]
    weights, out_weights, acc_z, acc_o, sums = refs
    units = y_ref.shape[1]

    @pl.when(pl.program_id(0) == 0)
    def _():
        load_weights(weights, 0, parts, (0, units // 2), rows, place_ref)
        load_weights(out_weights, 0, parts, (units // 2, units), rows, place_ref)
        for ref in (acc_z, acc_o, sums):
            ref[...] = jnp.zeros_like(ref)

    branch, total, inverse = branch_of(own_ref, other_ref, units)
    if second:
        produced = h_ref[...].astype(f32) + branch
        out_ref[...] = jnp.where(place_ref[3] == 0, h_ref[...].astype(f32), produced).astype(bf16)
        steps = pl.num_programs(0)
        chunk = steps - 1 - pl.program_id(0)
        held = jnp.where(place_ref[1] == 0, teacher_ref[0], teacher_ref[1])
        came = jnp.where(chunk % (steps // 2) == place_ref[3], here_ref[...], beside_ref[...])
        target = jnp.where(chunk // (steps // 2) == place_ref[1], held, came)
        grad_out = marks_ref[:, 9:10] * (produced - target)
    else:
        grad_normed = grad_own_ref[...].astype(f32) + grad_other_ref[...].astype(f32)
        grad_out, gain_term = norm_backward(grad_normed, next_h_ref[...].astype(f32), next_out_ref[...], next_gain_ref[0:1, :])
        sums[7:8, :] += jnp.sum(gain_term, axis=0, keepdims=True)
    grad_out_ref[...] = grad_out
    grad = grad_out.astype(bf16)
    inner = jnp.sum(grad.astype(f32) * total, axis=1, keepdims=True) * (inverse * inverse * inverse) / (2 * units)
    gain = small_ref[5:6]
    gate = gate_ref[...]
    y = y_ref[...]
    gate_sig = jax.nn.sigmoid(gate)
    gate_silu = gate * gate_sig
    gated = y * gate_silu
    gated_unit = gated * inverse
    grad_mixed = nn(grad, out_weights[...])
    acc_o[...] += tn(grad, (gated_unit * gain).astype(bf16))
    sums[5:6, :] += jnp.sum(grad_mixed * gated_unit, axis=0, keepdims=True)
    grad_gated = grad_mixed * gain * inverse - gated * inner
    grad_gate = (grad_gated * y * (gate_sig * (1.0 + gate * (1.0 - gate_sig)))).astype(bf16)
    grad_y_ref[...] = (grad_gated * gate_silu).astype(bf16)
    acc_z[...] += tn(normed_ref[...], grad_gate)
    part_ref[...] = nt(grad_gate, weights[...])

    @pl.when(pl.program_id(0) == pl.num_programs(0) - 1)
    def _():
        store_grads(grads, (0, units // 2), acc_z, 0, rows, place_ref, base)
        store_grads(grads, (units // 2, units), acc_o, 0, rows, place_ref, base)
        sums_ref[...] = sums[...]


def scan_backward_kernel(heads, rows, pieces, *refs):
    (place_ref, grad_y_ref, gate_part_ref), parts, refs = refs[:3], refs[3 : 3 + pieces], refs[3 + pieces :]
    (marks_ref, segment_ref, small_ref, states_small_ref, head_ref, spread_ref), refs = refs[:6], refs[6:]
    (raw_ref, conv_ref, y_ref, raw_states_ref, conv_states_ref, steps_ref, entry_state_ref), refs = refs[:7], refs[7:]
    (grads_ref, part_ref, sums_ref, states_sums_ref), refs = refs[:4], refs[4:]
    weights, dstate, next_state, conv_edge, states_edge, sums, states_sums = refs
    step = pl.program_id(0)
    units = raw_ref.shape[1]

    @pl.when(step == 0)
    def _():
        for ref in (dstate, next_state, conv_edge, states_edge, sums, states_sums):
            ref[...] = jnp.zeros_like(ref)
        load_weights(weights, 0, parts, (0, units // 2), rows, place_ref)
        load_weights(weights, units, parts, (units // 2, units // 2 + 2 * STATE), rows, place_ref)

    marks = marks_ref[...]
    taps = small_ref[...]
    y = y_ref[...]
    grad_y_low = grad_y_ref[...]
    grad_y = grad_y_low.astype(f32)
    conved = conv_ref[...]
    value_sig = jax.nn.sigmoid(conved)
    values = conved * value_sig
    conved_states = conv_states_ref[...]
    states_sig = jax.nn.sigmoid(conved_states)
    states_in = conved_states * states_sig
    b_rows = states_in[:, :STATE].astype(bf16)
    c_rows = states_in[:, STATE:].astype(bf16)
    shifted, steps, log_steps, logs, entry, tail, through, row, column = decay_parts(steps_ref[...], head_ref[...], marks, heads)
    spreader = spread_ref[...]
    spread_steps = spread(steps, spreader)
    spread_entry = spread(entry, spreader)
    spread_tail = spread(tail, spreader)
    through_row = spread(jnp.broadcast_to(through, (8, LANES)), spreader)[0:1]
    scaled_low = (values * spread_steps).astype(bf16)
    scaled = scaled_low.astype(f32)
    mask = linked_mask(column, row, marks, segment_ref[...])
    scores = nt(b_rows, c_rows)
    logs_across = jnp.transpose(logs)
    lane = lax.broadcasted_iota(jnp.int32, (1, LANES), 1)
    is_left = lane < HEAD_DIM
    zero = jnp.zeros((), bf16)
    cut = SPAN // 2
    spans = ((slice(0, cut), slice(0, SPAN)), (slice(cut, SPAN), slice(cut, SPAN)))
    grad_scores = [jnp.zeros((cut, SPAN), f32), jnp.zeros((cut, cut), f32)]
    pieces = []
    for pair in range(heads // 2):
        columns = slice(pair * LANES, (pair + 1) * LANES)
        block, grad = scaled_low[:, columns], grad_y_low[:, columns]
        grad_left = jnp.where(is_left, grad, zero)
        grad_right = jnp.where(is_left, zero, grad)
        halves = []
        for index, (rows_of, seen) in enumerate(spans):
            mixes = []
            for head, grad_one in ((2 * pair, grad_left), (2 * pair + 1, grad_right)):
                gap = logs_across[head : head + 1, seen] - logs[rows_of, head : head + 1]
                factor = jnp.exp(gap + mask[rows_of, seen])
                mixes.append((factor * scores[rows_of, seen]).astype(bf16))
                grad_scores[index] = grad_scores[index] + nt(block[rows_of], grad_one[seen]) * factor
            halves.append(nn(jnp.concatenate(mixes, axis=1), jnp.concatenate([grad_left[seen], grad_right[seen]], axis=0)))
        pieces.append(jnp.concatenate(halves, axis=0))
    lower_scores = jnp.concatenate([jnp.zeros((cut, cut), f32), grad_scores[1]], axis=1)
    grad_scores = jnp.concatenate([grad_scores[0], lower_scores], axis=0)
    held = entry_state_ref[0]
    held_low = held.astype(bf16)
    gradient = dstate[...]
    gradient_low = gradient.astype(bf16)
    grad_scaled = jnp.concatenate(pieces, axis=1) + spread_tail * nn(b_rows, gradient_low)
    grad_entry = (spread_entry * grad_y).astype(bf16)
    grad_scores_low = grad_scores.astype(bf16)
    grad_c = tn(grad_scores_low, b_rows) + nt(grad_entry, held_low)
    grad_b = nn(grad_scores_low, c_rows) + nt((spread_tail * scaled).astype(bf16), gradient_low)
    state_term = jnp.sum(gradient * next_state[...], axis=0, keepdims=True)
    dstate[...] = through_row * gradient + tn(c_rows, grad_entry)
    next_state[...] = held
    skip = taps[6:7]
    sums[6:7, :] += jnp.sum(grad_y * values, axis=0, keepdims=True)
    grad_logs = gathered_heads(grad_y * (y - skip * values) - scaled * grad_scaled, spreader)
    state_heads = gathered_heads(jnp.broadcast_to(state_term, (8, units)), spreader)[0:1]
    last_row = lax.broadcasted_iota(jnp.int32, (SPAN, 1), 0) == SPAN - 1
    grad_logs = grad_logs + jnp.where(last_row, state_heads, 0.0)
    grad_log_steps = running_sum((row <= column).astype(bf16), grad_logs)
    grad_steps = nt((grad_scaled * values).astype(bf16), spreader[:LANES]) - head_ref[1:2, :LANES] * grad_log_steps
    grad_steps_in = jnp.where(lane < heads, grad_steps * jax.nn.sigmoid(shifted), 0.0)
    states_sums[5:6, :] += jnp.concatenate(
        [
            jnp.sum(grad_steps_in, axis=0, keepdims=True),
            jnp.sum(grad_log_steps * log_steps, axis=0, keepdims=True),
        ],
        axis=1,
    )
    grad_values = grad_scaled * spread_steps + skip * grad_y
    grad_conved = grad_values * (value_sig * (1.0 + conved * (1.0 - value_sig)))
    grad_states = jnp.concatenate([grad_b, grad_c], axis=1)
    grad_conved_states = grad_states * (states_sig * (1.0 + conved_states * (1.0 - states_sig)))

    def conv_backward(block, edge, tap_rows, raw, total_ref):
        result = tap_rows[3:4] * block
        total_ref[3:4, :] += jnp.sum(block * raw, axis=0, keepdims=True)
        total_ref[4:5, :] += jnp.sum(block, axis=0, keepdims=True)
        for lag in (1, 2, 3):
            term = moved_up(block, edge, lag) * marks[:, 5 + lag : 6 + lag]
            result = result + tap_rows[3 - lag : 4 - lag] * term
            total_ref[3 - lag : 4 - lag, :] += jnp.sum(term * raw, axis=0, keepdims=True)
        return result

    grad_raw = conv_backward(grad_conved, conv_edge[...], taps, raw_ref[...], sums)
    grad_raw_states = conv_backward(
        grad_conved_states, states_edge[...], states_small_ref[...], raw_states_ref[...], states_sums
    )
    conv_edge[...] = grad_conved[:8]
    states_edge[...] = grad_conved_states[:8]
    turned = marks[0:1, 10:11] > 0.5
    first_states = jnp.where(turned, grad_raw_states[:, STATE:], grad_raw_states[:, :STATE])
    second_states = jnp.where(turned, grad_raw_states[:, :STATE], grad_raw_states[:, STATE:])
    own_steps = jnp.where(lane < heads // 2, grad_steps_in, 0.0)
    other_steps = jnp.where(lane < heads // 2, pltpu.roll(grad_steps_in, LANES - heads // 2, 1), 0.0)
    grads = jnp.concatenate([grad_raw, first_states, own_steps, second_states, other_steps], axis=1).astype(bf16)
    grads_ref[...] = grads
    part_ref[...] = (nt(grads, weights[...]) + gate_part_ref[...]).astype(bf16)

    @pl.when(step == pl.num_programs(0) - 1)
    def _():
        skips = gathered_heads(sums[...], spreader)[6:7]
        states_sums[6:7, :] = jnp.concatenate([skips, jnp.zeros_like(skips)], axis=1)
        sums_ref[...] = sums[...]
        states_sums_ref[...] = states_sums[...]


def scan_grads_kernel(heads, rows, pieces, grad_arrays, *refs):
    normed_ref, refs = refs[0], refs[1:]
    inputs, refs = refs[: 16 + pieces], refs[16 + pieces :]
    outs, refs = refs[:grad_arrays], refs[grad_arrays:]
    results, scratch, grads, kept, acc = refs[:3], refs[3:-3], refs[-3], refs[-2], refs[-1]
    place_ref = inputs[0]
    units = acc.shape[1] - 4 * STATE

    step = pl.program_id(0)
    here = pl.ds(pl.multiple_of(step * SPAN, SPAN), SPAN)
    scan_backward_kernel(heads, rows, pieces, *inputs, grads.at[here], *results, *scratch)
    kept[here] = normed_ref[...]

    @pl.when(step == pl.num_programs(0) - 1)
    def _():
        acc[...] = tn(kept[...], grads[...])
        store_grads(outs, (0, units // 2), acc, 0, rows, place_ref)
        store_grads(outs, (units // 2, units // 2 + 2 * STATE), acc, units, rows, place_ref)


def second_forward_kernel(heads, rows, *refs):
    inputs, gate_weights, refs = refs[:15], refs[15], refs[16:]
    outputs, (gate_ref, part_ref), refs = refs[:10], refs[10:12], refs[12:]
    scan_forward_kernel(True, heads, rows, 5, *inputs, *outputs, *refs[:5])
    normed_ref, y_ref, small_ref = outputs[2], outputs[5], inputs[11]
    gate_forward_kernel(rows, 1, inputs[0], normed_ref, y_ref, gate_weights, small_ref, gate_ref, part_ref, *refs[5:])


def second_backward_kernel(heads, rows, *refs):
    gate_inputs, refs = refs[:13], refs[13:]
    scan_weights, (segment_ref, states_small_ref, head_ref, spread_ref), refs = refs[:5], refs[5:9], refs[9:]
    (raw_ref, conv_ref, raw_states_ref, conv_states_ref, steps_ref, entry_state_ref), refs = refs[:6], refs[6:]
    (out_ref, grad_out_ref, grads_ref, gate_sums_ref, part_ref, sums_ref, states_sums_ref), refs = refs[:7], refs[7:]
    grad_y, gate_part, refs = refs[0], refs[1], refs[2:]
    gate_scratch, scan_scratch = refs[:5], refs[5:]
    place_ref, normed_ref, y_ref, marks_ref, small_ref = gate_inputs[0], gate_inputs[7], gate_inputs[9], gate_inputs[11], gate_inputs[12]
    base = scan_weights[0].shape[1]
    gate_backward_kernel(
        True, rows, 1, 1, base, *gate_inputs, out_ref, grad_out_ref, grad_y, gate_part, grads_ref, gate_sums_ref, *gate_scratch
    )
    scan_inputs = (place_ref, grad_y, gate_part, *scan_weights, marks_ref, segment_ref, small_ref, states_small_ref, head_ref, spread_ref)
    saved = (raw_ref, conv_ref, y_ref, raw_states_ref, conv_states_ref, steps_ref, entry_state_ref)
    scan_grads_kernel(heads, rows, 5, 1, normed_ref, *scan_inputs, *saved, grads_ref, part_ref, sums_ref, states_sums_ref, *scan_scratch)


def norm_backward(grad_normed, hidden, grad_out, gain):
    scale = lax.rsqrt(jnp.mean(hidden * hidden, axis=1, keepdims=True) + epsilon)
    weighted = grad_normed * gain
    shared = jnp.mean(weighted * hidden, axis=1, keepdims=True) * (scale * scale * scale)
    return grad_out + scale * weighted - hidden * shared, grad_normed * hidden * scale


VMEM_LIMIT = 60 * 1024 * 1024


def spreader_of(units):
    one = (np.arange(LANES)[:, None] == np.arange(units)[None, :] // HEAD_DIM).astype(np.float32)
    return jnp.asarray(np.concatenate([one, one], axis=0), bf16)


def rows_spec(width, last=None):
    if last is None:
        return pl.BlockSpec((SPAN, width), lambda i: (i, 0))
    return pl.BlockSpec((SPAN, width), lambda i: (last - i, 0))


def wide_spec(width):
    return pl.BlockSpec((WIDE, width), lambda i: (i, 0))


def whole_spec(array):
    return pl.BlockSpec(array.shape, lambda i: (0,) * array.ndim)


def call(kernel, inputs, outputs, scratch, chunks, flops):
    return pl.pallas_call(
        kernel,
        grid=(chunks,),
        in_specs=[spec for _, spec in inputs],
        out_specs=[spec for _, _, spec in outputs],
        out_shape=[jax.ShapeDtypeStruct(shape, dtype) for shape, dtype, _ in outputs],
        scratch_shapes=[pltpu.VMEM(shape, dtype) for shape, dtype in scratch],
        compiler_params=pltpu.CompilerParams(vmem_limit_bytes=VMEM_LIMIT, dimension_semantics=("arbitrary",)),
        cost_estimate=pl.CostEstimate(flops=flops, bytes_accessed=500_000, transcendentals=0),
    )(*[array for array, _ in inputs])


def fixed(array):
    return array, whole_spec(array)


def scalars(array):
    return array, pl.BlockSpec(memory_space=pltpu.SMEM)


def grad_outputs(width, columns):
    shape = (width // 2, columns)
    return [(shape, bf16, pl.BlockSpec(shape, lambda i: (0, 0)))] * 4


def awaited(arrays):
    return [(array, pl.BlockSpec(memory_space=pl.ANY)) for array in arrays]


def scan_forward(place, rows, h, parts, weights, marks, segment_row, params):
    length, width = h.shape
    units = params[0].shape[1]
    chunks = length // SPAN
    second = parts is not None
    inputs = [scalars(place), (h, rows_spec(width))]
    outputs = []
    if second:
        inputs += [(part, rows_spec(width + LANES)) for part in parts]
        outputs.append(((length, width), bf16, rows_spec(width)))
    inputs += [fixed(w) for w in weights]
    inputs += [(marks, rows_spec(LANES)), (segment_row, pl.BlockSpec((1, SPAN), lambda i: (0, i)))]
    inputs += [fixed(p) for p in params] + [fixed(spreader_of(units))]
    outputs.append(((8, width), f32, pl.BlockSpec((8, width), lambda i: (0, 0))))
    outputs.append(((length, width), bf16, rows_spec(width)))
    for columns in (units, units, units, 2 * STATE, 2 * STATE, LANES):
        outputs.append(((length, columns), f32, rows_spec(columns)))
    outputs.append(((chunks, STATE, units), f32, pl.BlockSpec((1, STATE, units), lambda i: (i, 0, 0))))
    scratch = [
        ((STATE, units), f32),
        ((8, units), f32),
        ((8, 2 * STATE), f32),
        ((8, width), f32),
        ((width, units + 4 * STATE), bf16),
    ]
    kernel = functools.partial(scan_forward_kernel, second, units // HEAD_DIM, rows, len(weights))
    results = call(kernel, inputs, outputs, scratch, chunks, 2_000_000_000)
    if not second:
        results = [h] + list(results)
    return results[0], results[1], results[2], results[3:]


def gate_forward(place, rows, normed, y, weights, params):
    length, width = normed.shape
    units = params[0].shape[1]
    inputs = [scalars(place), (normed, wide_spec(width)), (y, wide_spec(units))] + [fixed(w) for w in weights] + [fixed(params[0])]
    outputs = [((length, units), f32, wide_spec(units)), ((length, width + LANES), bf16, wide_spec(width + LANES))]
    scratch = [((width, units), bf16)] * 2
    return call(functools.partial(gate_forward_kernel, rows, len(weights)), inputs, outputs, scratch, length // WIDE, 1_000_000_000)


def gate_backward(place, rows, h, parts, extra, normed, gate, y, weights, marks, params):
    length, width = normed.shape
    units = params[0].shape[1]
    second = len(extra) == 1
    inputs = [scalars(place)] + ([(h, rows_spec(width))] if second else [])
    inputs += [(part, rows_spec(width + LANES)) for part in parts]
    inputs += [(array, rows_spec(width)) for array in extra[:4]] + [fixed(gain) for gain in extra[4:]]
    inputs += [(normed, rows_spec(width)), (gate, rows_spec(units)), (y, rows_spec(units))]
    inputs += [fixed(w) for w in weights] + [(marks, rows_spec(LANES)), fixed(params[0])]
    outputs = [((length, width), bf16, rows_spec(width))] if second else []
    outputs += [((length, width), f32, rows_spec(width)), ((length, units), bf16, rows_spec(units)), ((length, width), f32, rows_spec(width))]
    outputs += grad_outputs(width, units)
    outputs.append(((8, units), f32, pl.BlockSpec((8, units), lambda i: (0, 0))))
    scratch = [((width, units), bf16)] * 2 + [((width, units), f32)] * 2 + [((8, units), f32)]
    results = call(functools.partial(gate_backward_kernel, second, rows, len(weights), 4, 0), inputs, outputs, scratch, length // SPAN, 2_000_000_000)
    if not second:
        results = [None] + list(results)
    return results


def scan_scratch(length, width, units):
    return [
        ((width, units + 4 * STATE), bf16),
        ((STATE, units), f32),
        ((STATE, units), f32),
        ((8, units), f32),
        ((8, 2 * STATE), f32),
        ((8, units), f32),
        ((8, 2 * STATE), f32),
        ((length, units + 4 * STATE), bf16),
        ((length, width), bf16),
        ((width, units + 4 * STATE), f32),
    ]


def scan_backward(place, rows, grad_y, gate_part, normed, weights, marks, segment_row, params, saved):
    length, width = gate_part.shape
    units = params[0].shape[1]
    chunks = length // SPAN
    last = chunks - 1
    inputs = [(normed, rows_spec(width, last)), scalars(place), (grad_y, rows_spec(units, last)), (gate_part, rows_spec(width, last))]
    inputs += [fixed(w) for w in weights]
    inputs += [(marks, rows_spec(LANES, last)), (segment_row, pl.BlockSpec((1, SPAN), lambda i: (0, last - i)))]
    inputs += [fixed(p) for p in params] + [fixed(spreader_of(units))]
    inputs += [(s, rows_spec(s.shape[1], last)) for s in saved[:6]]
    inputs.append((saved[6], pl.BlockSpec((1, STATE, units), lambda i: (last - i, 0, 0))))
    outputs = grad_outputs(width, units // 2 + 2 * STATE)
    outputs.append(((length, width), bf16, rows_spec(width, last)))
    for columns in (units, 2 * STATE):
        outputs.append(((8, columns), f32, pl.BlockSpec((8, columns), lambda i: (0, 0))))
    kernel = functools.partial(scan_grads_kernel, units // HEAD_DIM, rows, len(weights), len(outputs) - 3)
    return call(kernel, inputs, outputs, scan_scratch(length, width, units), chunks, 3_000_000_000)


def second_forward(place, rows, h, parts, weights, gate_weights, marks, segment_row, params):
    length, width = h.shape
    units = params[0].shape[1]
    chunks = length // SPAN
    inputs = [scalars(place), (h, rows_spec(width))] + [(part, rows_spec(width + LANES)) for part in parts]
    inputs += [fixed(w) for w in weights]
    inputs += [(marks, rows_spec(LANES)), (segment_row, pl.BlockSpec((1, SPAN), lambda i: (0, i)))]
    inputs += [fixed(p) for p in params] + [fixed(spreader_of(units)), fixed(gate_weights)]
    outputs = [((length, width), bf16, rows_spec(width)), ((8, width), f32, pl.BlockSpec((8, width), lambda i: (0, 0)))]
    outputs.append(((length, width), bf16, rows_spec(width)))
    for columns in (units, units, units, 2 * STATE, 2 * STATE, LANES):
        outputs.append(((length, columns), f32, rows_spec(columns)))
    outputs.append(((chunks, STATE, units), f32, pl.BlockSpec((1, STATE, units), lambda i: (i, 0, 0))))
    outputs += [((length, units), f32, rows_spec(units)), ((length, width + LANES), bf16, rows_spec(width + LANES))]
    scratch = [((STATE, units), f32), ((8, units), f32), ((8, 2 * STATE), f32), ((8, width), f32)]
    scratch += [((width, units + 4 * STATE), bf16)] + [((width, units), bf16)] * 2
    kernel = functools.partial(second_forward_kernel, units // HEAD_DIM, rows)
    results = call(kernel, inputs, outputs, scratch, chunks, 3_000_000_000)
    return results[0], results[1], results[2], results[3:10], results[10], results[11]


def second_backward(place, rows, h, parts, teacher, here, beside, normed, gate, weights, gate_weights, marks, segment_row, params, saved):
    length, width = normed.shape
    units = params[0].shape[1]
    chunks = length // SPAN
    last = chunks - 1
    inputs = [scalars(place), (h, rows_spec(width, last))] + [(part, rows_spec(width + LANES, last)) for part in parts]
    inputs.append((teacher, pl.BlockSpec((2, SPAN, width), lambda i: (0, (last - i) % (chunks // 2), 0))))
    inputs += [fixed(here), fixed(beside), (normed, rows_spec(width, last)), (gate, rows_spec(units, last))]
    inputs += [(saved[2], rows_spec(units, last)), fixed(gate_weights), (marks, rows_spec(LANES, last)), fixed(params[0])]
    inputs += [fixed(w) for w in weights] + [(segment_row, pl.BlockSpec((1, SPAN), lambda i: (0, last - i)))]
    inputs += [fixed(params[1]), fixed(params[2]), fixed(spreader_of(units))]
    inputs += [(saved[i], rows_spec(saved[i].shape[1], last)) for i in (0, 1, 3, 4, 5)]
    inputs.append((saved[6], pl.BlockSpec((1, STATE, units), lambda i: (last - i, 0, 0))))

    def sums(columns):
        return (8, columns), f32, pl.BlockSpec((8, columns), lambda i: (0, 0))

    shape = (width // 2, 4 * (units + units // 2 + 2 * STATE))
    outputs = [((length, width), bf16, rows_spec(width, last)), ((length, width), f32, rows_spec(width, last))]
    outputs += [(shape, bf16, pl.BlockSpec(shape, lambda i: (0, 0))), sums(units)]
    outputs += [((length, width), bf16, rows_spec(width, last)), sums(units), sums(2 * STATE)]
    scratch = [((SPAN, units), bf16), ((SPAN, width), f32)]
    scratch += [((width, units), bf16)] * 2 + [((width, units), f32)] * 2 + [((8, units), f32)]
    scratch += scan_scratch(length, width, units)
    kernel = functools.partial(second_backward_kernel, units // HEAD_DIM, rows)
    return call(kernel, inputs, outputs, scratch, chunks, 4_000_000_000)


def finish_kernel(
    place_ref, own_ref, other_ref, h_ref, grad_out_ref, gain_ref, rows_ref, away_ref, grad_ref, low_ref, sums_ref, placed_ref, sums
):
    step = pl.program_id(0)

    @pl.when(step == 0)
    def _():
        sums[...] = jnp.zeros_like(sums)

    grad_normed = own_ref[...].astype(f32) + other_ref[...].astype(f32)
    next_grad = grad_out_ref[...]
    grad, gain_term = norm_backward(grad_normed, h_ref[...].astype(f32), next_grad.astype(bf16).astype(f32), gain_ref[0:1, :])
    rows = jnp.where(place_ref[3] == 0, grad, next_grad)
    sums[0:1, :] += jnp.sum(gain_term, axis=0, keepdims=True)
    sums_ref[...] = sums[...]

    @pl.when(step < pl.num_programs(0) // 2)
    def _():
        low_ref[...] = rows.astype(bf16)
        placed_ref[0] = away_ref[...]

    @pl.when(step >= pl.num_programs(0) // 2)
    def _():
        grad_ref[0] = rows
        placed_ref[0] = rows_ref[...]


def finish(place, own, other, h, grad_out, gain, produced, produced_away):
    length, width = h.shape
    steps = length // SPAN
    part = steps // 2

    def rows(i, place):
        return ((i + part * (1 - place[1])) % steps, 0)

    block = pl.BlockSpec((SPAN, width), rows)
    whole = pl.BlockSpec((8, width), lambda i, place: (0, 0))

    def early(i):
        return jnp.minimum(i, part - 1)

    def late(i):
        return jnp.maximum(i - part, 0)

    def placed(i, place):
        return (jnp.where(i < part, 1 - place[1], place[1]), jnp.where(i < part, i, i - part), 0)

    return pl.pallas_call(
        finish_kernel,
        grid_spec=pltpu.PrefetchScalarGridSpec(
            num_scalar_prefetch=1,
            grid=(steps,),
            in_specs=[block] * 4
            + [
                whole,
                pl.BlockSpec((SPAN, width), lambda i, place: (part * place[1] + late(i), 0)),
                pl.BlockSpec((SPAN, width), lambda i, place: (early(i), 0)),
            ],
            out_specs=[
                pl.BlockSpec((1, SPAN, width), lambda i, place: (place[1], late(i), 0)),
                pl.BlockSpec((SPAN, width), lambda i, place: (early(i), 0)),
                whole,
                pl.BlockSpec((1, SPAN, width), placed),
            ],
            scratch_shapes=[pltpu.VMEM((8, width), f32)],
        ),
        out_shape=[
            jax.ShapeDtypeStruct((2, length // 2, width), f32),
            jax.ShapeDtypeStruct((length // 2, width), bf16),
            jax.ShapeDtypeStruct((8, width), f32),
            jax.ShapeDtypeStruct((2, length // 2, width), bf16),
        ],
        compiler_params=pltpu.CompilerParams(vmem_limit_bytes=VMEM_LIMIT, dimension_semantics=("arbitrary",)),
        cost_estimate=pl.CostEstimate(flops=0, bytes_accessed=500_000, transcendentals=0),
    )(place, own, other, h, grad_out, gain, produced, produced_away)


def placed_kernel(place_ref, away_ref, rows_ref, out_ref):
    out_ref[0] = away_ref[...].astype(f32)


def placed_rows(place, rows, away):
    half, width = away.shape
    return pl.pallas_call(
        placed_kernel,
        grid_spec=pltpu.PrefetchScalarGridSpec(
            num_scalar_prefetch=1,
            grid=(half // SPAN,),
            in_specs=[pl.BlockSpec((SPAN, width), lambda i, place: (i, 0)), pl.BlockSpec(memory_space=pl.ANY)],
            out_specs=pl.BlockSpec((1, SPAN, width), lambda i, place: (1 - place[1], i, 0)),
        ),
        out_shape=jax.ShapeDtypeStruct(rows.shape, rows.dtype),
        input_output_aliases={2: 0},
        compiler_params=pltpu.CompilerParams(vmem_limit_bytes=VMEM_LIMIT, dimension_semantics=("arbitrary",)),
        cost_estimate=pl.CostEstimate(flops=0, bytes_accessed=500_000, transcendentals=0),
    )(place, away, rows)


def marks_kernel(place_ref, lengths_ref, segments_ref, marks_ref, row_ref):
    turn, rank = place_ref[1], place_ref[2]
    micro, sequences = lengths_ref.shape
    length = segments_ref.shape[1]
    total = jnp.int32(0)
    for batch in range(micro):
        total = lax.fori_loop(0, sequences, lambda i, t: t + lengths_ref[batch, i], total)
    weight = 2.0 * (micro * sequences * length) / jnp.full((1, length), total, jnp.int32).astype(f32)
    position = lax.broadcasted_iota(jnp.int32, (1, length), 1)
    segment = jnp.where(turn == 0, segments_ref[0:1, :], segments_ref[1:2, :])
    wide = jnp.broadcast_to(segment, (8, length))

    def same(lag):
        moved = pltpu.roll(wide, lag % length, 1)[0:1]
        inside = (position >= lag) & (position < length + lag)
        return jnp.where(inside & (moved == segment), 1.0, 0.0)

    before = jnp.full((1, length), -1, jnp.int32)
    end = before
    for block in range(length // SPAN):
        here = (position >= block * SPAN) & (position < (block + 1) * SPAN)
        end = jnp.where(here, segment[:, (block + 1) * SPAN - 1 : (block + 1) * SPAN], end)
        if block:
            before = jnp.where(here, segment[:, block * SPAN - 1 : block * SPAN], before)
    as_float = segment.astype(f32)
    rows = [same(1), same(2), same(3)]
    rows += [jnp.where(segment == before, 1.0, 0.0), jnp.where(segment == end, 1.0, 0.0), as_float]
    rows += [same(-1), same(-2), same(-3)]
    rows += [jnp.where(position < lengths_ref[turn, rank], weight, 0.0), jnp.full((1, length), turn, jnp.int32).astype(f32)]
    rows.append(jnp.zeros((LANES - len(rows), length), f32))
    marks_ref[...] = jnp.transpose(jnp.concatenate(rows, axis=0))
    row_ref[...] = as_float


def token_marks(place, lengths, segments):
    length = segments.shape[1]
    return pl.pallas_call(
        marks_kernel,
        in_specs=[pl.BlockSpec(memory_space=pltpu.SMEM)] * 2 + [pl.BlockSpec(memory_space=pltpu.VMEM)],
        out_shape=[jax.ShapeDtypeStruct((length, LANES), f32), jax.ShapeDtypeStruct((1, length), f32)],
        compiler_params=pltpu.CompilerParams(vmem_limit_bytes=VMEM_LIMIT),
        cost_estimate=pl.CostEstimate(flops=0, bytes_accessed=500_000, transcendentals=0),
    )(place, lengths, segments)


def three_parts(value):
    high = value.astype(bf16)
    rest = value - high.astype(f32)
    middle = rest.astype(bf16)
    return high, middle, (rest - middle.astype(f32)).astype(bf16)


PARAM_ROWS = 16


def pack_kernel(
    place_ref, zx_ref, bc_ref, dt_ref, gain_ref, out_ref, conv_ref, gate_gain_ref, states_conv_ref, bias_ref, rate_ref, skip_ref, kept_ref, sent_ref
):
    turn, core = place_ref[1], place_ref[3]
    rows = zx_ref.shape[0]
    half = zx_ref.shape[2] // 2
    heads_half = dt_ref.shape[0] // 2
    lane = lax.broadcasted_iota(jnp.int32, (1, LANES), 1)
    bc = jnp.where(turn == 0, bc_ref[:, :STATE], bc_ref[:, STATE:])
    diagonal = lax.broadcasted_iota(jnp.int32, (rows, rows), 0) == lax.broadcasted_iota(jnp.int32, (rows, rows), 1)
    gain = jnp.sum(jnp.where(diagonal, gain_ref[...].astype(f32), 0.0), axis=1, keepdims=True)
    head = lax.broadcasted_iota(jnp.int32, (2 * heads_half, LANES), 0)
    column = lax.broadcasted_iota(jnp.int32, (2 * heads_half, LANES), 1)
    shared = jnp.concatenate([states_conv_ref[...], jnp.zeros((PARAM_ROWS - 5, 2 * STATE), bf16)], axis=0)
    split = [part.astype(f32) for ref in (bias_ref, rate_ref, skip_ref) for part in three_parts(ref[...])]
    heads = jnp.concatenate(split + [jnp.zeros((PARAM_ROWS - 9, split[0].shape[1]), f32)], axis=0)
    heads = jnp.concatenate([heads, jnp.zeros((PARAM_ROWS, LANES - heads.shape[1]), f32)], axis=1).astype(bf16)
    for ref, part in ((kept_ref, core), (sent_ref, 1 - core)):
        first = part == 0

        def chosen(array, start):
            return jnp.where(first, array[:, start : start + half], array[:, start + half : start + 2 * half])

        ref[:rows, :half] = chosen(zx_ref[:, 1, :], 0)
        ref[:rows, half : half + STATE] = bc
        taken = (head == column + part * heads_half) & (column < heads_half)
        own_steps = tn(dt_ref[...], jnp.where(taken, 1.0, 0.0).astype(bf16))
        ref[:rows, half + STATE : half + 2 * STATE] = jnp.where(lane == LANES // 2, gain, own_steps).astype(bf16)
        ref[:rows, half + 2 * STATE : 2 * half + 2 * STATE] = chosen(zx_ref[:, 0, :], 0)
        ref[:rows, 2 * half + 2 * STATE :] = chosen(out_ref, 0)
        ref[rows:, :] = jnp.zeros((PARAM_ROWS, ref.shape[1]), bf16)
        channels = jnp.concatenate([chosen(conv_ref, 0), chosen(gate_gain_ref, 0)], axis=0)
        ref[rows:, :half] = jnp.concatenate([channels, jnp.zeros((PARAM_ROWS - 6, half), bf16)], axis=0)
        ref[rows:, half : half + 2 * STATE] = shared
        ref[rows:, half + 2 * STATE : half + 2 * STATE + LANES] = heads


def plain_call(kernel, place, inputs, outputs, ready=()):
    count = len(ready)
    body = kernel if not count else lambda place_ref, *refs: kernel(place_ref, *refs[count:])
    return pl.pallas_call(
        body,
        in_specs=[pl.BlockSpec(memory_space=pltpu.SMEM)]
        + [pl.BlockSpec(memory_space=pl.ANY)] * count
        + [pl.BlockSpec(memory_space=pltpu.VMEM)] * len(inputs),
        out_shape=[jax.ShapeDtypeStruct(shape, dtype) for shape, dtype in outputs],
        compiler_params=pltpu.CompilerParams(vmem_limit_bytes=VMEM_LIMIT),
        cost_estimate=pl.CostEstimate(flops=0, bytes_accessed=500_000, transcendentals=0),
    )(place, *ready, *inputs)


def unpack_kernel(place_ref, kept_ref, received_ref, *refs):
    scan_ref, middle_ref, gate_ref, params_ref, channels_ref = refs
    kept_first = place_ref[3] == 0
    kept, received = kept_ref[...], received_ref[...]
    first = jnp.where(kept_first, kept, received)
    second = jnp.where(kept_first, received, kept)
    rows, scan = scan_ref.shape
    half = channels_ref.shape[1]
    scan_ref[...] = first[:rows, :scan]
    middle_ref[:, : 2 * half] = first[:rows, scan:]
    middle_ref[:, 2 * half :] = second[:rows, :scan]
    gate_ref[...] = second[:rows, scan:]
    params_ref[0] = first[rows:, : scan + LANES]
    params_ref[1] = second[rows:, : scan + LANES]
    channels_ref[:PARAM_ROWS] = first[rows:, :half]
    channels_ref[PARAM_ROWS:] = second[rows:, :half]


def params_kernel(heads_half, place_ref, params_ref, channels_ref, spread_ref, *refs):
    turn, core = place_ref[1], place_ref[3]
    half = channels_ref.shape[1]
    lane = lax.broadcasted_iota(jnp.int32, (1, LANES), 1)
    for layer in range(2):
        small_ref, states_ref, head_ref = refs[3 * layer : 3 * layer + 3]
        rows = params_ref[layer].astype(f32)
        split = rows[:, half + 2 * STATE :]
        heads = [split[3 * i : 3 * i + 1] + split[3 * i + 1 : 3 * i + 2] + split[3 * i + 2 : 3 * i + 3] for i in range(3)]
        heads = jnp.concatenate(heads + [jnp.zeros((5, LANES), f32)], axis=0)
        moved = [pltpu.roll(heads, (LANES - start * heads_half) % LANES, 1) for start in range(4)]

        def of(index):
            return jnp.where(index == 0, moved[0], jnp.where(index == 1, moved[1], jnp.where(index == 2, moved[2], moved[3])))

        own, other = of(2 * turn + core), pltpu.roll(of(2 * (1 - turn) + core), heads_half, 1)
        heads = jnp.where(lane < heads_half, own, jnp.where(lane < 2 * heads_half, other, 0.0))
        head_ref[...] = jnp.concatenate([heads[0:1], jnp.exp(heads[1:2]), jnp.zeros((6, LANES), f32)], axis=0)
        high, middle, low = three_parts(jnp.broadcast_to(heads[2:3], (8, LANES)))
        once = spread_ref[:LANES]
        skips = (nn(high, once) + nn(middle, once) + nn(low, once))[0:1]
        own_rows = rows[0:6, :half]
        other_rows = channels_ref[PARAM_ROWS * layer : PARAM_ROWS * layer + 6].astype(f32)
        channels = jnp.concatenate([own_rows, other_rows], axis=1)
        small_ref[...] = jnp.concatenate([channels, skips, jnp.zeros_like(skips)], axis=0)
        states_ref[...] = jnp.concatenate([rows[0:5, half : half + 2 * STATE], jnp.zeros((3, 2 * STATE), f32)], axis=0)


def beside_kernel(place_ref, *refs):
    out = refs[-1]
    start = 0
    for ref in refs[:-1]:
        out[:, start : start + ref.shape[1]] = ref[...]
        start += ref.shape[1]


def split_kernel(place_ref, whole_ref, *outs):
    start = 0
    for out in outs:
        out[...] = whole_ref[:, start : start + out.shape[1]]
        start += out.shape[1]


def join_kernel(place_ref, *refs):
    out = refs[-1]
    start = 0
    for group in range(len(refs) // 4):
        parts = refs[4 * group : 4 * group + 4]
        width = parts[0].shape[1]
        total = sum(part[...].astype(f32) for part in parts)
        out[:, start : start + width] = total.astype(bf16)
        start += width


def owned_kernel(place_ref, first_ref, second_ref, beside_ref, across_ref, both_ref, zx_ref, bc_ref, dt_ref, out_ref):
    first = place_ref[3] == 0
    half = out_ref.shape[1] // 2
    heads_half = dt_ref.shape[0] // 2
    mine = jnp.where(first, first_ref[...], second_ref[...]).astype(f32)
    beside = beside_ref[...].astype(f32)
    lower, upper = jnp.where(first, mine, beside), jnp.where(first, beside, mine)
    gate = half + 2 * STATE
    for index, part in enumerate((lower, upper)):
        columns = slice(index * half, (index + 1) * half)
        zx_ref[:, 0, columns] = part[:, gate : gate + half]
        zx_ref[:, 1, columns] = part[:, :half]
        out_ref[:, columns] = part[:, gate + half :]
    own = mine[:, half : half + STATE] + beside[:, half : half + STATE]
    other = across_ref[...].astype(f32) + both_ref[...].astype(f32)
    straight = place_ref[1] == 0
    bc_ref[:, :STATE] = jnp.where(straight, own, other)
    bc_ref[:, STATE:] = jnp.where(straight, other, own)
    lane = lax.broadcasted_iota(jnp.int32, (1, LANES), 1)
    steps = slice(half + STATE, half + 2 * STATE)
    both = jnp.transpose(jnp.where(lane < heads_half, lower[:, steps], pltpu.roll(upper[:, steps], heads_half, 1)))
    for head in range(2 * heads_half):
        dt_ref[head] = both[head : head + 1]


def small_kernel(gate0, scan0, states0, gate1, scan1, states1, gain_ref, out_ref):
    for layer, (gate, scan, states, gain) in enumerate(
        ((gate0, scan0, states0, gain_ref[0:1, :]), (gate1, scan1, states1, gate0[7:8, :]))
    ):
        start = 16 * layer
        out_ref[start : start + 5, :] = scan[0:5, :]
        out_ref[start + 5 : start + 6, :] = gate[5:6, :]
        out_ref[start + 6 : start + 7, :] = gain
        out_ref[start + 7 : start + 16, :] = jnp.zeros((9, out_ref.shape[1]), f32)
        out_ref[start + 8 : start + 15, : 2 * STATE] = states[0:7, :]


def fold_kernel(heads_half, place_ref, own_ref, away_ref, mine_ref, others_ref):
    first = place_ref[3] == 0
    half = mine_ref.shape[1]
    folded = []
    for layer in range(2):
        own, away = own_ref[16 * layer : 16 * layer + 16], away_ref[16 * layer : 16 * layer + 16]
        units = own[0:6, :half] + away[0:6, half:]
        gain = own[6:7] + away[6:7]
        total = own[8:16, :half] + away[8:16, :half]
        own_heads = jnp.concatenate([own[14:15, :LANES], own[13:14, : 2 * LANES]], axis=1)
        away_heads = jnp.concatenate([away[14:15, :LANES], away[13:14, : 2 * LANES]], axis=1)
        moved = pltpu.roll(jnp.broadcast_to(away_heads, (8, 3 * LANES)), 3 * LANES - heads_half, 1)[0:1]
        heads = jnp.concatenate([own_heads + moved, jnp.zeros((1, half - 3 * LANES), f32)], axis=1) if half > 3 * LANES else own_heads + moved
        zeros = jnp.zeros((2, half), f32)
        folded.append(jnp.concatenate([units, gain[:, :half], gain[:, half:], total[0:5], heads, zeros], axis=0))
    mine_ref[...] = jnp.where(first, folded[0], folded[1])
    others_ref[...] = jnp.where(first, folded[1], folded[0])


def small_outputs_kernel(heads_half, place_ref, total_ref, conv_ref, states_conv_ref, gate_gain_ref, heads_ref, gain_ref):
    first = place_ref[3] == 0
    half = total_ref.shape[1]
    here, there = total_ref[0:16], total_ref[16:32]
    lower, upper = jnp.where(first, here, there), jnp.where(first, there, here)
    states = here[8:13, : 2 * STATE] + there[8:13, : 2 * STATE]
    for row in range(5):
        conv_ref[row, :, :half] = lower[row : row + 1]
        conv_ref[row, :, half:] = upper[row : row + 1]
        states_conv_ref[row] = states[row : row + 1]
    gate_gain_ref[:, :half] = lower[5:6]
    gate_gain_ref[:, half:] = upper[5:6]
    lane = lax.broadcasted_iota(jnp.int32, (1, LANES), 1)
    for row in range(3):
        own = lower[13:14, row * LANES : (row + 1) * LANES]
        other = pltpu.roll(jnp.broadcast_to(upper[13:14, row * LANES : (row + 1) * LANES], (8, LANES)), heads_half, 1)[0:1]
        heads_ref[row : row + 1, :] = jnp.where(lane < heads_half, own, other)[:, : 2 * heads_half]
    gain = jnp.concatenate([here[6:7], here[7:8]], axis=1)
    size = gain_ref.shape[1]
    share = jnp.zeros(gain_ref.shape, f32)
    for rank in range(2 * half // size):
        share = jnp.where(place_ref[2] == rank, gain[:, rank * size : (rank + 1) * size], share)
    gain_ref[...] = share


def tied(*values):
    return lax.optimization_barrier(values)


def swapped(block, axis):
    return lax.ppermute(block, axis, [(0, 1), (1, 0)])


def far_swapped(block):
    size = lax.axis_size("tensor")
    return lax.ppermute(block, ("section", "tensor"), [(i, 2 * size - 1 - i) for i in range(2 * size)])


def body(
    x_input,
    teacher,
    segment_ids,
    valid_len,
    norm_gain,
    w_zx,
    w_bc,
    w_dt,
    conv_x,
    conv_bc,
    dt_bias,
    a_log,
    d_skip,
    gnorm_gain,
    w_out,
):
    local_rows, width = x_input.shape[1:]
    ranks = lax.axis_size("dp")
    places = ranks // 2
    core = lax.axis_index("section")
    turn = lax.axis_index("tensor")
    rank = lax.axis_index("dp")
    place = jnp.stack([rank % 2, turn, rank, core]).astype(jnp.int32)
    on_first = core == 0
    block_rows = w_zx.shape[1]
    half = w_zx.shape[3] // 2
    units = 2 * half
    heads_half = w_dt.shape[2] // 2
    scan_columns = half + 2 * STATE
    line_groups = [[2 * index + start for index in range(places)] for start in range(2)]

    def by_layer(kept, received):
        return jnp.where(on_first, kept, received), jnp.where(on_first, received, kept)

    def x_swapped(block):
        return lax.ppermute(block, "dp", [(i, i ^ 1) for i in range(ranks)])

    def y_swapped(block):
        return swapped(block, "tensor")

    def line_gather(block):
        return lax.all_gather(block, "dp", axis_index_groups=line_groups, axis=0, tiled=True)

    def line_reduce(block):
        return lax.psum_scatter(block, "dp", axis_index_groups=line_groups, scatter_dimension=0, tiled=True)

    def line_total(block, beside):
        if places != 4:
            return lax.psum(block, "dp", axis_index_groups=line_groups), beside

        def send(rows, moves):
            return lax.ppermute(rows, "dp", [(2 * a + start, 2 * b + start) for a, b in moves for start in range(2)])

        up, down = send(block, [(0, 1), (1, 2), (2, 3)]), send(block, [(1, 0), (2, 1), (3, 2)])
        up2, down2 = send(up, [(1, 2), (2, 3)]), send(down, [(2, 1), (1, 0)])
        far = send(jnp.where(rank // 2 == 1, up, down), [(1, 3), (2, 0)])
        up2, down2, far, beside = tied(up2, down2, far, beside)
        return block + up + down + up2 + down2 + far, beside

    pack_shape = (block_rows + PARAM_ROWS, scan_columns + units)
    kept, sent = plain_call(
        pack_kernel,
        place,
        (w_zx[0], w_bc[0], w_dt[0].T, norm_gain, w_out[0].T, conv_x[0], gnorm_gain, conv_bc[0], dt_bias, a_log, d_skip),
        [(pack_shape, bf16)] * 2,
    )
    received = swapped(sent, "section")
    scan_block, middle_block, gate_block, params_both, channels = plain_call(
        unpack_kernel,
        place,
        (kept, received),
        [
            ((block_rows, scan_columns), bf16),
            ((block_rows, units + scan_columns), bf16),
            ((block_rows, units), bf16),
            ((2, PARAM_ROWS, scan_columns + LANES), bf16),
            ((2 * PARAM_ROWS, half), bf16),
        ],
    )

    both_ways = [(2 * d + t, 2 * (d ^ 1) + 1 - t) for d in range(ranks) for t in range(2)]

    def over_plane(own, x_block, y_block, far_block):
        far = lax.ppermute(far_block, ("dp", "tensor"), both_ways)
        return own, x_swapped(x_block), y_swapped(y_block), far

    def plane_end(block, over_x, over_tensor):
        cut = places // 2 * block_rows
        return block, over_x, over_tensor, y_swapped(over_x[:cut]), x_swapped(over_tensor[cut:])

    def quarter(rows):
        away = lax.dynamic_index_in_dim(rows, 1 - turn, 0, keepdims=False)
        return lax.dynamic_slice_in_dim(away, core * (local_rows // 2), local_rows // 2, 0)

    def whole_rows(rows, here, beside):
        own = lax.dynamic_index_in_dim(rows, turn, 0, keepdims=False)
        other = jnp.concatenate(by_layer(here, beside), axis=0)
        return jnp.where(turn == 0, jnp.concatenate([own, other]), jnp.concatenate([other, own]))

    scan_line, here, channels = tied(line_gather(scan_block), y_swapped(quarter(x_input)), y_swapped(channels))
    scan_line, middle_block = tied(scan_line, middle_block)
    middle_line = line_gather(middle_block)
    scan_half = scan_line, x_swapped(scan_line), y_swapped(scan_line)
    x_rows = whole_rows(x_input, here, swapped(here, "section"))
    params = plain_call(
        functools.partial(params_kernel, heads_half),
        place,
        (params_both, channels, spreader_of(units)),
        [((8, units), f32), ((8, 2 * STATE), f32), ((8, LANES), f32)] * 2,
    )
    params = [params[:3], params[3:]]
    marks, segment_row = token_marks(place, valid_len, segment_ids[:, 0])
    over_x = x_swapped(gate_block)
    side = (gate_block, over_x, y_swapped(gate_block), y_swapped(over_x))
    side = plain_call(beside_kernel, place, side, [((block_rows, 4 * units), bf16)], (x_rows, marks, params[0][0]))[0]
    scan_first, side = tied(plane_end(*scan_half), side)
    middle_line, side = tied(middle_line, side)
    gate_second = line_gather(side)
    gate_line, next_line = plain_call(
        split_kernel,
        place,
        (middle_line,),
        [((places * block_rows, units), bf16), ((places * block_rows, scan_columns), bf16)],
        (scan_first[4],),
    )

    gate_half = gate_line, x_swapped(gate_line), y_swapped(gate_line)
    next_half = next_line, x_swapped(next_line), y_swapped(next_line)
    results = scan_forward(place, block_rows, x_rows, None, scan_first, marks, segment_row, params[0])
    results, gate_half = tied(results, gate_half)
    _, gain_first, normed_first, saved_first = results
    gate_first = plane_end(*gate_half)
    results = gate_forward(place, block_rows, normed_first, saved_first[2], gate_first, params[0])
    (gated_first, part), scan_second = tied(results, plane_end(*next_half))
    parts_first = (part, swapped(part, "section"))
    parts_first, teacher, gate_second = tied(parts_first, teacher, gate_second)
    results = second_forward(
        place, block_rows, x_rows, parts_first, scan_second, gate_second, marks, segment_row, params[1]
    )
    results, here = tied(results, y_swapped(quarter(teacher)))
    hidden, gain_second, normed_second, saved_second, gated_second, part = results
    parts_second = (part, swapped(part, "section"))
    beside = swapped(here, "section")

    def add(*blocks):
        return sum(block.astype(f32) for block in blocks).astype(bf16)

    def away_rows(rows):
        return y_swapped(lax.dynamic_slice_in_dim(rows, (1 - turn) * local_rows, local_rows, 0))

    produced, grad_out, grads, gate_sums, part, sums, states_sums = second_backward(
        place,
        block_rows,
        hidden,
        parts_second,
        teacher,
        here,
        beside,
        normed_second,
        gated_second,
        scan_second,
        gate_second,
        marks,
        segment_row,
        params[1],
        saved_second,
    )
    quarters = line_reduce(grads)
    sums_second = (gate_sums, sums, states_sums)
    grad_parts = (part, swapped(part, "section"))
    results = gate_backward(
        place,
        block_rows,
        x_rows,
        parts_first,
        (hidden, grad_out) + grad_parts + (gain_second,),
        normed_first,
        gated_first,
        saved_first[2],
        gate_first,
        marks,
        params[0],
    )
    results, produced_away = tied(results[1:], away_rows(produced))
    grad_hidden, grad_y, gate_part = results[:3]
    gate_reduce = over_plane(*results[3:7])
    gate_sums_first = results[7]
    results = scan_backward(
        place, block_rows, grad_y, gate_part, normed_first, scan_first, marks, segment_row, params[0], saved_first
    )
    results, gate_reduce = tied(results, gate_reduce)
    scan_reduce = over_plane(*results[:4])
    part, sums, states_sums = results[4:]
    sums_first = (gate_sums_first, sums, states_sums)
    grad_rows, grad_low, gain_sums, layer_outputs = finish(
        place, part, swapped(part, "section"), x_rows, grad_hidden, gain_first, produced, produced_away
    )
    smalls = plain_call(
        lambda place_ref, *refs: small_kernel(*refs), place, sums_first + sums_second + (gain_sums,), [((32, units), f32)]
    )[0]
    smalls, scan_reduce = line_total(smalls, scan_reduce)
    blocks = plain_call(
        join_kernel,
        place,
        scan_reduce + gate_reduce,
        [((places * block_rows, scan_columns + units), bf16)],
        (quarters,),
    )[0]
    owned_first = line_reduce(blocks)
    quarters = plain_call(
        split_kernel, place, (quarters,), [((block_rows, scan_columns + units), bf16)] * 4, (blocks,)
    )
    owned_second = add(*over_plane(*quarters))
    smalls_away, grad_low = tied(y_swapped(smalls), grad_low)
    mine, others = plain_call(
        functools.partial(fold_kernel, heads_half), place, (smalls, smalls_away), [((16, half), f32)] * 2
    )
    total = jnp.concatenate([mine, swapped(others, "section")])
    owned_first, boundary = tied(owned_first, placed_rows(place, grad_rows, y_swapped(grad_low)))
    total = total + x_swapped(total)
    grad_conv, grad_states_conv, grad_gate_gain, grad_heads, gain_total = plain_call(
        functools.partial(small_outputs_kernel, heads_half),
        place,
        (total,),
        [((5, 1, units), f32), ((5, 1, 2 * STATE), f32), ((1, units), f32), ((3, 2 * heads_half), f32), ((1, block_rows), f32)],
    )

    others = jnp.where(on_first, owned_second, owned_first)
    own_states, other_states = by_layer(owned_first[:, half : half + STATE], owned_second[:, half : half + STATE])
    grad_zx, grad_bc, grad_dt, grad_out_w = plain_call(
        owned_kernel,
        place,
        (owned_first, owned_second, swapped(others, "section"), y_swapped(own_states), far_swapped(other_states)),
        [((block_rows, 2, units), f32), ((block_rows, 2 * STATE), f32), ((2 * heads_half, 1, block_rows), f32), ((block_rows, units), f32)],
        (boundary, layer_outputs, grad_conv),
    )
    return (
        layer_outputs[None],
        boundary[None],
        gain_total,
        grad_zx[None],
        grad_bc[None],
        grad_dt.transpose(1, 2, 0),
        grad_conv.transpose(1, 0, 2),
        grad_states_conv.transpose(1, 0, 2),
        grad_heads[1:2],
        grad_heads[2:3],
        grad_heads[0:1],
        grad_gate_gain,
        grad_out_w.T[None],
    )


def solution(mesh):
    placed = (
        P(None, ("dp", "tensor"), None),
        P(None, ("dp", "tensor"), None),
        P(None, "dp", None),
        P(),
        P("section", "dp"),
        P("section", "dp", None, "tensor"),
        P("section", "dp", None),
        P("section", "dp", "tensor"),
        P("section", None, "tensor"),
        P("section", None, None),
        P("section", None),
        P("section", None),
        P("section", None),
        P("section", "tensor"),
        P("section", "tensor", "dp"),
    )
    return jax.shard_map(
        body,
        mesh=mesh,
        in_specs=placed,
        out_specs=(
            P("section", None, ("dp", "tensor"), None),
            P("section", None, ("dp", "tensor"), None),
            P("section", "dp"),
            P("section", "dp", None, "tensor"),
            P("section", "dp", None),
            P("section", "dp", "tensor"),
            P("section", None, "tensor"),
            P("section", None, None),
            P("section", "tensor"),
            P("section", "tensor"),
            P("section", "tensor"),
            P("section", "tensor"),
            P("section", "tensor", "dp"),
        ),
        check_vma=False,
    )
```

```python
import functools

import jax
import jax.numpy as jnp
import numpy as np
from jax import lax
from jax.experimental import pallas as pl
from jax.experimental.pallas import tpu as pltpu
from jax.sharding import PartitionSpec as P

HEAD_DIM = 64
STATE = 128
SPAN = 256
WIDE = 512
LANES = 128

epsilon = 1e-05
f32 = jnp.float32
bf16 = jnp.bfloat16


def nn(left, right):
    return lax.dot_general(left, right, (((1,), (0,)), ((), ())), preferred_element_type=f32)


def nt(left, right):
    return lax.dot_general(left, right, (((1,), (1,)), ((), ())), preferred_element_type=f32)


def tn(left, right):
    return lax.dot_general(left, right, (((0,), (0,)), ((), ())), preferred_element_type=f32)


def high_low(value):
    high = value.astype(bf16)
    return high, (value - high.astype(f32)).astype(bf16)


def spread(per_head, spreader):
    return nn(jnp.concatenate(high_low(per_head), axis=1), spreader)


def gathered_heads(units, spreader):
    high, low = high_low(units)
    once = spreader[:LANES]
    return nt(high, once) + nt(low, once)


def running_sum(triangle, value):
    high = value.astype(bf16)
    rest = value - high.astype(f32)
    middle = rest.astype(bf16)
    low = (rest - middle.astype(f32)).astype(bf16)
    sums = nn(triangle, jnp.concatenate([high, middle, low], axis=1))
    return sums[:, :LANES] + sums[:, LANES : 2 * LANES] + sums[:, 2 * LANES :]


def softplus(value):
    return jnp.maximum(value, 0.0) + jnp.log1p(jnp.exp(-jnp.abs(value)))


def moved_down(block, edge, lag):
    rolled = pltpu.roll(block, lag, 0)
    row = lax.broadcasted_iota(jnp.int32, (8, 1), 0)
    first = jnp.where(row < lag, pltpu.roll(edge, lag, 0), rolled[:8])
    return jnp.concatenate([first, rolled[8:]], axis=0)


def moved_up(block, edge, lag):
    length = block.shape[0]
    rolled = pltpu.roll(block, length - lag, 0)
    row = lax.broadcasted_iota(jnp.int32, (8, 1), 0)
    last = jnp.where(row >= 8 - lag, pltpu.roll(edge, 8 - lag, 0), rolled[length - 8 :])
    return jnp.concatenate([rolled[: length - 8], last], axis=0)


def decay_parts(steps_in, head_rows, marks, heads):
    lane = lax.broadcasted_iota(jnp.int32, (1, LANES), 1)
    live = lane < heads
    shifted = steps_in + head_rows[0:1, :LANES]
    steps = jnp.where(live, softplus(shifted), 0.0)
    rates = head_rows[1:2, :LANES]
    log_steps = -steps * rates
    row = lax.broadcasted_iota(jnp.int32, (SPAN, SPAN), 0)
    column = lax.broadcasted_iota(jnp.int32, (SPAN, SPAN), 1)
    lower = (row >= column).astype(bf16)
    logs = running_sum(lower, log_steps)
    last = logs[SPAN - 1 : SPAN]
    entry = jnp.exp(logs) * marks[:, 3:4]
    tail = jnp.exp(last - logs) * marks[:, 4:5]
    through = jnp.exp(last) * marks[SPAN - 1 : SPAN, 3:4]
    entry = jnp.where(live, entry, 0.0)
    tail = jnp.where(live, tail, 0.0)
    through = jnp.where(live, through, 0.0)
    return shifted, steps, log_steps, logs, entry, tail, through, row, column


def linked_mask(row, column, marks, segment_row):
    linked = (row >= column) & (marks[:, 5:6] == segment_row)
    return jnp.where(linked, 0.0, -1e30)


def branch_of(own_ref, other_ref, units):
    width = own_ref.shape[1] - LANES
    own = own_ref[...].astype(f32)
    other = other_ref[...].astype(f32)
    total = own[:, :width] + other[:, :width]
    own_squares = own[:, width : width + 1] + own[:, width + 1 : width + 2]
    other_squares = other[:, width : width + 1] + other[:, width + 1 : width + 2]
    inverse = lax.rsqrt((own_squares + other_squares) / (2 * units) + epsilon)
    return total * inverse, total, inverse


PLANE = ((False, False), (True, False), (False, True), (True, True))


def load_weights(weights, start, refs, columns, rows, place_ref):
    first, last = columns
    mine = place_ref[0]
    size = refs[0].shape[1] // 4
    if rows % 32:

        def piece(index, step):
            ref, offset = (refs[0], index * size) if len(refs) == 1 else (refs[index], 0)
            if index == 3 and len(refs) == 5 and step >= ref.shape[0] // rows:
                ref, step = refs[4], step - ref.shape[0] // rows
            return ref[step * rows : (step + 1) * rows, offset + first : offset + last]

        for turned in range(2):
            target = start + turned * (last - first)
            for step in range(weights.shape[0] // (2 * rows)):
                own, moved = piece(2 * turned, step), piece(2 * turned + 1, step)
                row = 2 * step * rows
                weights[row : row + rows, target : target + last - first] = jnp.where(mine == 0, own, moved)
                weights[row + rows : row + 2 * rows, target : target + last - first] = jnp.where(mine == 0, moved, own)
        return
    base = 0
    for index in range(len(refs) if len(refs) > 1 else 4):
        moved, turned = PLANE[min(index, 3)]
        ref, offset = (refs[0], index * size) if len(refs) == 1 else (refs[index], 0)
        place = 1 - mine if moved else mine
        target = start + (last - first if turned else 0)
        for step in range(ref.shape[0] // rows):
            row = pl.multiple_of((2 * (base + step) + place) * rows, 32)
            weights[pl.ds(row, rows), target : target + last - first] = ref[step * rows : (step + 1) * rows, offset + first : offset + last]
        base = ref.shape[0] // rows if index == 3 else 0


def store_grads(refs, columns, acc, start, rows, place_ref, base=0):
    first, last = columns
    mine = place_ref[0]
    size = refs[0].shape[1] // 4
    if rows % 32:
        for index, (moved, turned) in enumerate(PLANE):
            ref, offset = (refs[0], index * size + base) if len(refs) == 1 else (refs[index], 0)
            source = start + (last - first if turned else 0)
            for step in range(ref.shape[0] // rows):
                row = 2 * step * rows
                upper = acc[row : row + rows, source : source + last - first]
                lower = acc[row + rows : row + 2 * rows, source : source + last - first]
                block = jnp.where(mine == 0, lower, upper) if moved else jnp.where(mine == 0, upper, lower)
                ref[step * rows : (step + 1) * rows, offset + first : offset + last] = block.astype(bf16)
        return
    for index, (moved, turned) in enumerate(PLANE):
        ref, offset = (refs[0], index * size + base) if len(refs) == 1 else (refs[index], 0)
        place = 1 - mine if moved else mine
        source = start + (last - first if turned else 0)
        for step in range(ref.shape[0] // rows):
            row = pl.multiple_of((2 * step + place) * rows, 32)
            block = acc[pl.ds(row, rows), source : source + last - first]
            ref[step * rows : (step + 1) * rows, offset + first : offset + last] = block.astype(bf16)


def scan_forward_kernel(second, heads, rows, pieces, *refs):
    place_ref, refs = refs[0], refs[1:]
    if second:
        (h_ref, own_ref, other_ref), refs = refs[:3], refs[3:]
    else:
        (h_ref,), refs = refs[:1], refs[1:]
    parts, refs = refs[:pieces], refs[pieces:]
    (marks_ref, segment_ref, small_ref, states_small_ref, head_ref, spread_ref), refs = refs[:6], refs[6:]
    if second:
        h_out, refs = refs[0], refs[1:]
    gain_ref, refs = refs[0], refs[1:]
    normed_ref, raw_ref, conv_ref, y_ref, raw_states_ref, conv_states_ref, steps_ref, entry_state_ref = refs[:8]
    state, raw_edge, states_edge, gain, weights = refs[8:]
    units = raw_ref.shape[1]

    @pl.when(pl.program_id(0) == 0)
    def _():
        state[...] = jnp.zeros_like(state)
        raw_edge[...] = jnp.zeros_like(raw_edge)
        states_edge[...] = jnp.zeros_like(states_edge)
        load_weights(weights, 0, parts, (0, units // 2), rows, place_ref)
        load_weights(weights, units, parts, (units // 2, units // 2 + 2 * STATE), rows, place_ref)
        steps_columns = weights[:, units + STATE : units + STATE + LANES].astype(f32)
        gain[...] = jnp.broadcast_to(jnp.transpose(steps_columns)[LANES // 2 : LANES // 2 + 1, :], gain.shape)
        gain_ref[...] = gain[...]

    hidden = h_ref[...].astype(f32)
    if second:
        rounded = (hidden + branch_of(own_ref, other_ref, units)[0]).astype(bf16)
        h_out[...] = rounded
        hidden = rounded.astype(f32)
    scale = lax.rsqrt(jnp.mean(hidden * hidden, axis=1, keepdims=True) + epsilon)
    normed = (hidden * scale * gain[0:1, :]).astype(bf16)
    normed_ref[...] = normed
    projected = nn(normed, weights[...])
    raw = projected[:, :units]
    first, second_part = projected[:, units : units + 2 * STATE], projected[:, units + 2 * STATE :]
    marks = marks_ref[...]
    turned = marks[0:1, 10:11] > 0.5
    raw_states = jnp.concatenate(
        [
            jnp.where(turned, second_part[:, :STATE], first[:, :STATE]),
            jnp.where(turned, first[:, :STATE], second_part[:, :STATE]),
        ],
        axis=1,
    )
    lane = lax.broadcasted_iota(jnp.int32, (1, LANES), 1)
    steps_in = jnp.where(lane < heads // 2, first[:, STATE:], pltpu.roll(second_part[:, STATE:], heads // 2, 1))
    raw_ref[...] = raw
    raw_states_ref[...] = raw_states
    steps_ref[...] = steps_in

    def conv(block, edge, taps):
        total = taps[4:5] + taps[3:4] * block
        for lag in (1, 2, 3):
            total = total + taps[3 - lag : 4 - lag] * (moved_down(block, edge, lag) * marks[:, lag - 1 : lag])
        return total

    taps = small_ref[...]
    conved = conv(raw, raw_edge[...], taps)
    conv_ref[...] = conved
    conved_states = conv(raw_states, states_edge[...], states_small_ref[...])
    conv_states_ref[...] = conved_states
    raw_edge[...] = raw[SPAN - 8 :]
    states_edge[...] = raw_states[SPAN - 8 :]
    values = conved * jax.nn.sigmoid(conved)
    states_in = conved_states * jax.nn.sigmoid(conved_states)
    b_rows = states_in[:, :STATE].astype(bf16)
    c_rows = states_in[:, STATE:].astype(bf16)
    _, steps, _, logs, entry, tail, through, row, column = decay_parts(steps_in, head_ref[...], marks, heads)
    spreader = spread_ref[...]
    scaled = values * spread(steps, spreader)
    mask = linked_mask(row, column, marks, segment_ref[...])
    scores = nt(c_rows, b_rows)
    logs_across = jnp.transpose(logs)
    cut = SPAN // 2
    pieces = []
    for pair in range(heads // 2):
        block = scaled[:, pair * LANES : (pair + 1) * LANES]
        left = jnp.where(lane < HEAD_DIM, block, 0.0).astype(bf16)
        right = jnp.where(lane < HEAD_DIM, 0.0, block).astype(bf16)
        halves = []
        for rows_of, seen in ((slice(0, cut), cut), (slice(cut, SPAN), SPAN)):
            mixes = []
            for head in (2 * pair, 2 * pair + 1):
                gap = logs[rows_of, head : head + 1] - logs_across[head : head + 1, :seen]
                mixes.append((jnp.exp(gap + mask[rows_of, :seen]) * scores[rows_of, :seen]).astype(bf16))
            halves.append(nn(jnp.concatenate(mixes, axis=1), jnp.concatenate([left[:seen], right[:seen]], axis=0)))
        pieces.append(jnp.concatenate(halves, axis=0))
    inside = jnp.concatenate(pieces, axis=1)
    held = state[...]
    entry_state_ref[0] = held
    across = nn(c_rows, held.astype(bf16)) * spread(entry, spreader)
    through_row = spread(jnp.broadcast_to(through, (8, LANES)), spreader)[0:1]
    state[...] = through_row * held + tn(b_rows, (spread(tail, spreader) * scaled).astype(bf16))
    y_ref[...] = inside + across + taps[6:7] * values


def gate_forward_kernel(rows, pieces, place_ref, normed_ref, y_ref, *refs):
    parts, refs = refs[:pieces], refs[pieces:]
    small_ref, gate_ref, part_ref, weights, out_weights = refs

    @pl.when(pl.program_id(0) == 0)
    def _():
        half = weights.shape[1] // 2
        load_weights(weights, 0, parts, (0, half), rows, place_ref)
        load_weights(out_weights, 0, parts, (half, 2 * half), rows, place_ref)

    gate = nn(normed_ref[...], weights[...])
    gate_ref[...] = gate
    gated = y_ref[...] * (gate * jax.nn.sigmoid(gate))
    squares = jnp.sum(gated * gated, axis=1, keepdims=True)
    part = nt((gated * small_ref[5:6]).astype(bf16), out_weights[...])
    width = part.shape[1]
    part_ref[:, :width] = part.astype(bf16)
    high, low = high_low(squares)
    lane = lax.broadcasted_iota(jnp.int32, (1, LANES), 1)
    part_ref[:, width:] = jnp.where(lane == 0, high, jnp.where(lane == 1, low, jnp.zeros_like(low)))


def gate_backward_kernel(second, rows, pieces, grad_arrays, base, *refs):
    place_ref, refs = refs[0], refs[1:]
    if second:
        (h_ref, own_ref, other_ref, teacher_ref, here_ref, beside_ref), refs = refs[:6], refs[6:]
    else:
        (own_ref, other_ref, next_h_ref, next_out_ref, grad_own_ref, grad_other_ref, next_gain_ref), refs = refs[:7], refs[7:]
    (normed_ref, gate_ref, y_ref), parts, refs = refs[:3], refs[3 : 3 + pieces], refs[3 + pieces :]
    (marks_ref, small_ref), refs = refs[:2], refs[2:]
    if second:
        out_ref, refs = refs[0], refs[1:]
    (grad_out_ref, grad_y_ref, part_ref), refs = refs[:3], refs[3:]
    grads, sums_ref, refs = refs[:grad_arrays], refs[grad_arrays], refs[grad_arrays + 1 :]
    weights, out_weights, acc_z, acc_o, sums = refs
    units = y_ref.shape[1]

    @pl.when(pl.program_id(0) == 0)
    def _():
        load_weights(weights, 0, parts, (0, units // 2), rows, place_ref)
        load_weights(out_weights, 0, parts, (units // 2, units), rows, place_ref)
        for ref in (acc_z, acc_o, sums):
            ref[...] = jnp.zeros_like(ref)

    branch, total, inverse = branch_of(own_ref, other_ref, units)
    if second:
        produced = h_ref[...].astype(f32) + branch
        out_ref[...] = jnp.where(place_ref[3] == 0, h_ref[...].astype(f32), produced).astype(bf16)
        steps = pl.num_programs(0)
        chunk = steps - 1 - pl.program_id(0)
        held = jnp.where(place_ref[1] == 0, teacher_ref[0], teacher_ref[1])
        came = jnp.where(chunk % (steps // 2) == place_ref[3], here_ref[...], beside_ref[...])
        target = jnp.where(chunk // (steps // 2) == place_ref[1], held, came)
        grad_out = marks_ref[:, 9:10] * (produced - target)
    else:
        grad_normed = grad_own_ref[...].astype(f32) + grad_other_ref[...].astype(f32)
        grad_out, gain_term = norm_backward(grad_normed, next_h_ref[...].astype(f32), next_out_ref[...], next_gain_ref[0:1, :])
        sums[7:8, :] += jnp.sum(gain_term, axis=0, keepdims=True)
    grad_out_ref[...] = grad_out
    grad = grad_out.astype(bf16)
    inner = jnp.sum(grad.astype(f32) * total, axis=1, keepdims=True) * (inverse * inverse * inverse) / (2 * units)
    gain = small_ref[5:6]
    gate = gate_ref[...]
    y = y_ref[...]
    gate_sig = jax.nn.sigmoid(gate)
    gate_silu = gate * gate_sig
    gated = y * gate_silu
    gated_unit = gated * inverse
    grad_mixed = nn(grad, out_weights[...])
    acc_o[...] += tn(grad, (gated_unit * gain).astype(bf16))
    sums[5:6, :] += jnp.sum(grad_mixed * gated_unit, axis=0, keepdims=True)
    grad_gated = grad_mixed * gain * inverse - gated * inner
    grad_gate = (grad_gated * y * (gate_sig * (1.0 + gate * (1.0 - gate_sig)))).astype(bf16)
    grad_y_ref[...] = (grad_gated * gate_silu).astype(bf16)
    acc_z[...] += tn(normed_ref[...], grad_gate)
    part_ref[...] = nt(grad_gate, weights[...])

    @pl.when(pl.program_id(0) == pl.num_programs(0) - 1)
    def _():
        store_grads(grads, (0, units // 2), acc_z, 0, rows, place_ref, base)
        store_grads(grads, (units // 2, units), acc_o, 0, rows, place_ref, base)
        sums_ref[...] = sums[...]


def scan_backward_kernel(heads, rows, pieces, *refs):
    (place_ref, grad_y_ref, gate_part_ref), parts, refs = refs[:3], refs[3 : 3 + pieces], refs[3 + pieces :]
    (marks_ref, segment_ref, small_ref, states_small_ref, head_ref, spread_ref), refs = refs[:6], refs[6:]
    (raw_ref, conv_ref, y_ref, raw_states_ref, conv_states_ref, steps_ref, entry_state_ref), refs = refs[:7], refs[7:]
    (grads_ref, part_ref, sums_ref, states_sums_ref), refs = refs[:4], refs[4:]
    weights, dstate, next_state, conv_edge, states_edge, sums, states_sums = refs
    step = pl.program_id(0)
    units = raw_ref.shape[1]

    @pl.when(step == 0)
    def _():
        for ref in (dstate, next_state, conv_edge, states_edge, sums, states_sums):
            ref[...] = jnp.zeros_like(ref)
        load_weights(weights, 0, parts, (0, units // 2), rows, place_ref)
        load_weights(weights, units, parts, (units // 2, units // 2 + 2 * STATE), rows, place_ref)

    marks = marks_ref[...]
    taps = small_ref[...]
    y = y_ref[...]
    grad_y_low = grad_y_ref[...]
    grad_y = grad_y_low.astype(f32)
    conved = conv_ref[...]
    value_sig = jax.nn.sigmoid(conved)
    values = conved * value_sig
    conved_states = conv_states_ref[...]
    states_sig = jax.nn.sigmoid(conved_states)
    states_in = conved_states * states_sig
    b_rows = states_in[:, :STATE].astype(bf16)
    c_rows = states_in[:, STATE:].astype(bf16)
    shifted, steps, log_steps, logs, entry, tail, through, row, column = decay_parts(steps_ref[...], head_ref[...], marks, heads)
    spreader = spread_ref[...]
    spread_steps = spread(steps, spreader)
    spread_entry = spread(entry, spreader)
    spread_tail = spread(tail, spreader)
    through_row = spread(jnp.broadcast_to(through, (8, LANES)), spreader)[0:1]
    scaled_low = (values * spread_steps).astype(bf16)
    scaled = scaled_low.astype(f32)
    mask = linked_mask(column, row, marks, segment_ref[...])
    scores = nt(b_rows, c_rows)
    logs_across = jnp.transpose(logs)
    lane = lax.broadcasted_iota(jnp.int32, (1, LANES), 1)
    is_left = lane < HEAD_DIM
    zero = jnp.zeros((), bf16)
    cut = SPAN // 2
    spans = ((slice(0, cut), slice(0, SPAN)), (slice(cut, SPAN), slice(cut, SPAN)))
    grad_scores = [jnp.zeros((cut, SPAN), f32), jnp.zeros((cut, cut), f32)]
    pieces = []
    for pair in range(heads // 2):
        columns = slice(pair * LANES, (pair + 1) * LANES)
        block, grad = scaled_low[:, columns], grad_y_low[:, columns]
        grad_left = jnp.where(is_left, grad, zero)
        grad_right = jnp.where(is_left, zero, grad)
        halves = []
        for index, (rows_of, seen) in enumerate(spans):
            mixes = []
            for head, grad_one in ((2 * pair, grad_left), (2 * pair + 1, grad_right)):
                gap = logs_across[head : head + 1, seen] - logs[rows_of, head : head + 1]
                factor = jnp.exp(gap + mask[rows_of, seen])
                mixes.append((factor * scores[rows_of, seen]).astype(bf16))
                grad_scores[index] = grad_scores[index] + nt(block[rows_of], grad_one[seen]) * factor
            halves.append(nn(jnp.concatenate(mixes, axis=1), jnp.concatenate([grad_left[seen], grad_right[seen]], axis=0)))
        pieces.append(jnp.concatenate(halves, axis=0))
    lower_scores = jnp.concatenate([jnp.zeros((cut, cut), f32), grad_scores[1]], axis=1)
    grad_scores = jnp.concatenate([grad_scores[0], lower_scores], axis=0)
    held = entry_state_ref[0]
    held_low = held.astype(bf16)
    gradient = dstate[...]
    gradient_low = gradient.astype(bf16)
    grad_scaled = jnp.concatenate(pieces, axis=1) + spread_tail * nn(b_rows, gradient_low)
    grad_entry = (spread_entry * grad_y).astype(bf16)
    grad_scores_low = grad_scores.astype(bf16)
    grad_c = tn(grad_scores_low, b_rows) + nt(grad_entry, held_low)
    grad_b = nn(grad_scores_low, c_rows) + nt((spread_tail * scaled).astype(bf16), gradient_low)
    state_term = jnp.sum(gradient * next_state[...], axis=0, keepdims=True)
    dstate[...] = through_row * gradient + tn(c_rows, grad_entry)
    next_state[...] = held
    skip = taps[6:7]
    sums[6:7, :] += jnp.sum(grad_y * values, axis=0, keepdims=True)
    grad_logs = gathered_heads(grad_y * (y - skip * values) - scaled * grad_scaled, spreader)
    state_heads = gathered_heads(jnp.broadcast_to(state_term, (8, units)), spreader)[0:1]
    last_row = lax.broadcasted_iota(jnp.int32, (SPAN, 1), 0) == SPAN - 1
    grad_logs = grad_logs + jnp.where(last_row, state_heads, 0.0)
    grad_log_steps = running_sum((row <= column).astype(bf16), grad_logs)
    grad_steps = nt((grad_scaled * values).astype(bf16), spreader[:LANES]) - head_ref[1:2, :LANES] * grad_log_steps
    grad_steps_in = jnp.where(lane < heads, grad_steps * jax.nn.sigmoid(shifted), 0.0)
    states_sums[5:6, :] += jnp.concatenate(
        [
            jnp.sum(grad_steps_in, axis=0, keepdims=True),
            jnp.sum(grad_log_steps * log_steps, axis=0, keepdims=True),
        ],
        axis=1,
    )
    grad_values = grad_scaled * spread_steps + skip * grad_y
    grad_conved = grad_values * (value_sig * (1.0 + conved * (1.0 - value_sig)))
    grad_states = jnp.concatenate([grad_b, grad_c], axis=1)
    grad_conved_states = grad_states * (states_sig * (1.0 + conved_states * (1.0 - states_sig)))

    def conv_backward(block, edge, tap_rows, raw, total_ref):
        result = tap_rows[3:4] * block
        total_ref[3:4, :] += jnp.sum(block * raw, axis=0, keepdims=True)
        total_ref[4:5, :] += jnp.sum(block, axis=0, keepdims=True)
        for lag in (1, 2, 3):
            term = moved_up(block, edge, lag) * marks[:, 5 + lag : 6 + lag]
            result = result + tap_rows[3 - lag : 4 - lag] * term
            total_ref[3 - lag : 4 - lag, :] += jnp.sum(term * raw, axis=0, keepdims=True)
        return result

    grad_raw = conv_backward(grad_conved, conv_edge[...], taps, raw_ref[...], sums)
    grad_raw_states = conv_backward(
        grad_conved_states, states_edge[...], states_small_ref[...], raw_states_ref[...], states_sums
    )
    conv_edge[...] = grad_conved[:8]
    states_edge[...] = grad_conved_states[:8]
    turned = marks[0:1, 10:11] > 0.5
    first_states = jnp.where(turned, grad_raw_states[:, STATE:], grad_raw_states[:, :STATE])
    second_states = jnp.where(turned, grad_raw_states[:, :STATE], grad_raw_states[:, STATE:])
    own_steps = jnp.where(lane < heads // 2, grad_steps_in, 0.0)
    other_steps = jnp.where(lane < heads // 2, pltpu.roll(grad_steps_in, LANES - heads // 2, 1), 0.0)
    grads = jnp.concatenate([grad_raw, first_states, own_steps, second_states, other_steps], axis=1).astype(bf16)
    grads_ref[...] = grads
    part_ref[...] = (nt(grads, weights[...]) + gate_part_ref[...]).astype(bf16)

    @pl.when(step == pl.num_programs(0) - 1)
    def _():
        skips = gathered_heads(sums[...], spreader)[6:7]
        states_sums[6:7, :] = jnp.concatenate([skips, jnp.zeros_like(skips)], axis=1)
        sums_ref[...] = sums[...]
        states_sums_ref[...] = states_sums[...]


def scan_grads_kernel(heads, rows, pieces, grad_arrays, *refs):
    normed_ref, refs = refs[0], refs[1:]
    inputs, refs = refs[: 16 + pieces], refs[16 + pieces :]
    outs, refs = refs[:grad_arrays], refs[grad_arrays:]
    results, scratch, grads, kept, acc = refs[:3], refs[3:-3], refs[-3], refs[-2], refs[-1]
    place_ref = inputs[0]
    units = acc.shape[1] - 4 * STATE

    step = pl.program_id(0)
    here = pl.ds(pl.multiple_of(step * SPAN, SPAN), SPAN)
    scan_backward_kernel(heads, rows, pieces, *inputs, grads.at[here], *results, *scratch)
    kept[here] = normed_ref[...]

    @pl.when(step == pl.num_programs(0) - 1)
    def _():
        acc[...] = tn(kept[...], grads[...])
        store_grads(outs, (0, units // 2), acc, 0, rows, place_ref)
        store_grads(outs, (units // 2, units // 2 + 2 * STATE), acc, units, rows, place_ref)


def second_forward_kernel(heads, rows, *refs):
    inputs, gate_weights, refs = refs[:15], refs[15], refs[16:]
    outputs, (gate_ref, part_ref), refs = refs[:10], refs[10:12], refs[12:]
    scan_forward_kernel(True, heads, rows, 5, *inputs, *outputs, *refs[:5])
    normed_ref, y_ref, small_ref = outputs[2], outputs[5], inputs[11]
    gate_forward_kernel(rows, 1, inputs[0], normed_ref, y_ref, gate_weights, small_ref, gate_ref, part_ref, *refs[5:])


def second_backward_kernel(heads, rows, *refs):
    gate_inputs, refs = refs[:13], refs[13:]
    scan_weights, (segment_ref, states_small_ref, head_ref, spread_ref), refs = refs[:5], refs[5:9], refs[9:]
    (raw_ref, conv_ref, raw_states_ref, conv_states_ref, steps_ref, entry_state_ref), refs = refs[:6], refs[6:]
    (out_ref, grad_out_ref, grads_ref, gate_sums_ref, part_ref, sums_ref, states_sums_ref), refs = refs[:7], refs[7:]
    grad_y, gate_part, refs = refs[0], refs[1], refs[2:]
    gate_scratch, scan_scratch = refs[:5], refs[5:]
    place_ref, normed_ref, y_ref, marks_ref, small_ref = gate_inputs[0], gate_inputs[7], gate_inputs[9], gate_inputs[11], gate_inputs[12]
    base = scan_weights[0].shape[1]
    gate_backward_kernel(
        True, rows, 1, 1, base, *gate_inputs, out_ref, grad_out_ref, grad_y, gate_part, grads_ref, gate_sums_ref, *gate_scratch
    )
    scan_inputs = (place_ref, grad_y, gate_part, *scan_weights, marks_ref, segment_ref, small_ref, states_small_ref, head_ref, spread_ref)
    saved = (raw_ref, conv_ref, y_ref, raw_states_ref, conv_states_ref, steps_ref, entry_state_ref)
    scan_grads_kernel(heads, rows, 5, 1, normed_ref, *scan_inputs, *saved, grads_ref, part_ref, sums_ref, states_sums_ref, *scan_scratch)


def norm_backward(grad_normed, hidden, grad_out, gain):
    scale = lax.rsqrt(jnp.mean(hidden * hidden, axis=1, keepdims=True) + epsilon)
    weighted = grad_normed * gain
    shared = jnp.mean(weighted * hidden, axis=1, keepdims=True) * (scale * scale * scale)
    return grad_out + scale * weighted - hidden * shared, grad_normed * hidden * scale


VMEM_LIMIT = 60 * 1024 * 1024


def spreader_of(units):
    one = (np.arange(LANES)[:, None] == np.arange(units)[None, :] // HEAD_DIM).astype(np.float32)
    return jnp.asarray(np.concatenate([one, one], axis=0), bf16)


def rows_spec(width, last=None):
    if last is None:
        return pl.BlockSpec((SPAN, width), lambda i: (i, 0))
    return pl.BlockSpec((SPAN, width), lambda i: (last - i, 0))


def wide_spec(width):
    return pl.BlockSpec((WIDE, width), lambda i: (i, 0))


def whole_spec(array):
    return pl.BlockSpec(array.shape, lambda i: (0,) * array.ndim)


def call(kernel, inputs, outputs, scratch, chunks, flops):
    return pl.pallas_call(
        kernel,
        grid=(chunks,),
        in_specs=[spec for _, spec in inputs],
        out_specs=[spec for _, _, spec in outputs],
        out_shape=[jax.ShapeDtypeStruct(shape, dtype) for shape, dtype, _ in outputs],
        scratch_shapes=[pltpu.VMEM(shape, dtype) for shape, dtype in scratch],
        compiler_params=pltpu.CompilerParams(vmem_limit_bytes=VMEM_LIMIT, dimension_semantics=("arbitrary",)),
        cost_estimate=pl.CostEstimate(flops=flops, bytes_accessed=500_000, transcendentals=0),
    )(*[array for array, _ in inputs])


def fixed(array):
    return array, whole_spec(array)


def scalars(array):
    return array, pl.BlockSpec(memory_space=pltpu.SMEM)


def grad_outputs(width, columns):
    shape = (width // 2, columns)
    return [(shape, bf16, pl.BlockSpec(shape, lambda i: (0, 0)))] * 4


def awaited(arrays):
    return [(array, pl.BlockSpec(memory_space=pl.ANY)) for array in arrays]


def scan_forward(place, rows, h, parts, weights, marks, segment_row, params):
    length, width = h.shape
    units = params[0].shape[1]
    chunks = length // SPAN
    second = parts is not None
    inputs = [scalars(place), (h, rows_spec(width))]
    outputs = []
    if second:
        inputs += [(part, rows_spec(width + LANES)) for part in parts]
        outputs.append(((length, width), bf16, rows_spec(width)))
    inputs += [fixed(w) for w in weights]
    inputs += [(marks, rows_spec(LANES)), (segment_row, pl.BlockSpec((1, SPAN), lambda i: (0, i)))]
    inputs += [fixed(p) for p in params] + [fixed(spreader_of(units))]
    outputs.append(((8, width), f32, pl.BlockSpec((8, width), lambda i: (0, 0))))
    outputs.append(((length, width), bf16, rows_spec(width)))
    for columns in (units, units, units, 2 * STATE, 2 * STATE, LANES):
        outputs.append(((length, columns), f32, rows_spec(columns)))
    outputs.append(((chunks, STATE, units), f32, pl.BlockSpec((1, STATE, units), lambda i: (i, 0, 0))))
    scratch = [
        ((STATE, units), f32),
        ((8, units), f32),
        ((8, 2 * STATE), f32),
        ((8, width), f32),
        ((width, units + 4 * STATE), bf16),
    ]
    kernel = functools.partial(scan_forward_kernel, second, units // HEAD_DIM, rows, len(weights))
    results = call(kernel, inputs, outputs, scratch, chunks, 2_000_000_000)
    if not second:
        results = [h] + list(results)
    return results[0], results[1], results[2], results[3:]


def gate_forward(place, rows, normed, y, weights, params):
    length, width = normed.shape
    units = params[0].shape[1]
    inputs = [scalars(place), (normed, wide_spec(width)), (y, wide_spec(units))] + [fixed(w) for w in weights] + [fixed(params[0])]
    outputs = [((length, units), f32, wide_spec(units)), ((length, width + LANES), bf16, wide_spec(width + LANES))]
    scratch = [((width, units), bf16)] * 2
    return call(functools.partial(gate_forward_kernel, rows, len(weights)), inputs, outputs, scratch, length // WIDE, 1_000_000_000)


def gate_backward(place, rows, h, parts, extra, normed, gate, y, weights, marks, params):
    length, width = normed.shape
    units = params[0].shape[1]
    second = len(extra) == 1
    inputs = [scalars(place)] + ([(h, rows_spec(width))] if second else [])
    inputs += [(part, rows_spec(width + LANES)) for part in parts]
    inputs += [(array, rows_spec(width)) for array in extra[:4]] + [fixed(gain) for gain in extra[4:]]
    inputs += [(normed, rows_spec(width)), (gate, rows_spec(units)), (y, rows_spec(units))]
    inputs += [fixed(w) for w in weights] + [(marks, rows_spec(LANES)), fixed(params[0])]
    outputs = [((length, width), bf16, rows_spec(width))] if second else []
    outputs += [((length, width), f32, rows_spec(width)), ((length, units), bf16, rows_spec(units)), ((length, width), f32, rows_spec(width))]
    outputs += grad_outputs(width, units)
    outputs.append(((8, units), f32, pl.BlockSpec((8, units), lambda i: (0, 0))))
    scratch = [((width, units), bf16)] * 2 + [((width, units), f32)] * 2 + [((8, units), f32)]
    results = call(functools.partial(gate_backward_kernel, second, rows, len(weights), 4, 0), inputs, outputs, scratch, length // SPAN, 2_000_000_000)
    if not second:
        results = [None] + list(results)
    return results


def scan_scratch(length, width, units):
    return [
        ((width, units + 4 * STATE), bf16),
        ((STATE, units), f32),
        ((STATE, units), f32),
        ((8, units), f32),
        ((8, 2 * STATE), f32),
        ((8, units), f32),
        ((8, 2 * STATE), f32),
        ((length, units + 4 * STATE), bf16),
        ((length, width), bf16),
        ((width, units + 4 * STATE), f32),
    ]


def scan_backward(place, rows, grad_y, gate_part, normed, weights, marks, segment_row, params, saved):
    length, width = gate_part.shape
    units = params[0].shape[1]
    chunks = length // SPAN
    last = chunks - 1
    inputs = [(normed, rows_spec(width, last)), scalars(place), (grad_y, rows_spec(units, last)), (gate_part, rows_spec(width, last))]
    inputs += [fixed(w) for w in weights]
    inputs += [(marks, rows_spec(LANES, last)), (segment_row, pl.BlockSpec((1, SPAN), lambda i: (0, last - i)))]
    inputs += [fixed(p) for p in params] + [fixed(spreader_of(units))]
    inputs += [(s, rows_spec(s.shape[1], last)) for s in saved[:6]]
    inputs.append((saved[6], pl.BlockSpec((1, STATE, units), lambda i: (last - i, 0, 0))))
    outputs = grad_outputs(width, units // 2 + 2 * STATE)
    outputs.append(((length, width), bf16, rows_spec(width, last)))
    for columns in (units, 2 * STATE):
        outputs.append(((8, columns), f32, pl.BlockSpec((8, columns), lambda i: (0, 0))))
    kernel = functools.partial(scan_grads_kernel, units // HEAD_DIM, rows, len(weights), len(outputs) - 3)
    return call(kernel, inputs, outputs, scan_scratch(length, width, units), chunks, 3_000_000_000)


def second_forward(place, rows, h, parts, weights, gate_weights, marks, segment_row, params):
    length, width = h.shape
    units = params[0].shape[1]
    chunks = length // SPAN
    inputs = [scalars(place), (h, rows_spec(width))] + [(part, rows_spec(width + LANES)) for part in parts]
    inputs += [fixed(w) for w in weights]
    inputs += [(marks, rows_spec(LANES)), (segment_row, pl.BlockSpec((1, SPAN), lambda i: (0, i)))]
    inputs += [fixed(p) for p in params] + [fixed(spreader_of(units)), fixed(gate_weights)]
    outputs = [((length, width), bf16, rows_spec(width)), ((8, width), f32, pl.BlockSpec((8, width), lambda i: (0, 0)))]
    outputs.append(((length, width), bf16, rows_spec(width)))
    for columns in (units, units, units, 2 * STATE, 2 * STATE, LANES):
        outputs.append(((length, columns), f32, rows_spec(columns)))
    outputs.append(((chunks, STATE, units), f32, pl.BlockSpec((1, STATE, units), lambda i: (i, 0, 0))))
    outputs += [((length, units), f32, rows_spec(units)), ((length, width + LANES), bf16, rows_spec(width + LANES))]
    scratch = [((STATE, units), f32), ((8, units), f32), ((8, 2 * STATE), f32), ((8, width), f32)]
    scratch += [((width, units + 4 * STATE), bf16)] + [((width, units), bf16)] * 2
    kernel = functools.partial(second_forward_kernel, units // HEAD_DIM, rows)
    results = call(kernel, inputs, outputs, scratch, chunks, 3_000_000_000)
    return results[0], results[1], results[2], results[3:10], results[10], results[11]


def second_backward(place, rows, h, parts, teacher, here, beside, normed, gate, weights, gate_weights, marks, segment_row, params, saved):
    length, width = normed.shape
    units = params[0].shape[1]
    chunks = length // SPAN
    last = chunks - 1
    inputs = [scalars(place), (h, rows_spec(width, last))] + [(part, rows_spec(width + LANES, last)) for part in parts]
    inputs.append((teacher, pl.BlockSpec((2, SPAN, width), lambda i: (0, (last - i) % (chunks // 2), 0))))
    inputs += [fixed(here), fixed(beside), (normed, rows_spec(width, last)), (gate, rows_spec(units, last))]
    inputs += [(saved[2], rows_spec(units, last)), fixed(gate_weights), (marks, rows_spec(LANES, last)), fixed(params[0])]
    inputs += [fixed(w) for w in weights] + [(segment_row, pl.BlockSpec((1, SPAN), lambda i: (0, last - i)))]
    inputs += [fixed(params[1]), fixed(params[2]), fixed(spreader_of(units))]
    inputs += [(saved[i], rows_spec(saved[i].shape[1], last)) for i in (0, 1, 3, 4, 5)]
    inputs.append((saved[6], pl.BlockSpec((1, STATE, units), lambda i: (last - i, 0, 0))))

    def sums(columns):
        return (8, columns), f32, pl.BlockSpec((8, columns), lambda i: (0, 0))

    shape = (width // 2, 4 * (units + units // 2 + 2 * STATE))
    outputs = [((length, width), bf16, rows_spec(width, last)), ((length, width), f32, rows_spec(width, last))]
    outputs += [(shape, bf16, pl.BlockSpec(shape, lambda i: (0, 0))), sums(units)]
    outputs += [((length, width), bf16, rows_spec(width, last)), sums(units), sums(2 * STATE)]
    scratch = [((SPAN, units), bf16), ((SPAN, width), f32)]
    scratch += [((width, units), bf16)] * 2 + [((width, units), f32)] * 2 + [((8, units), f32)]
    scratch += scan_scratch(length, width, units)
    kernel = functools.partial(second_backward_kernel, units // HEAD_DIM, rows)
    return call(kernel, inputs, outputs, scratch, chunks, 4_000_000_000)


def finish_kernel(
    place_ref, own_ref, other_ref, h_ref, grad_out_ref, gain_ref, rows_ref, away_ref, *refs
):
    small_refs, (grad_ref, low_ref, smalls_ref, placed_ref, sums) = refs[:6], refs[6:]
    step = pl.program_id(0)

    @pl.when(step == 0)
    def _():
        sums[...] = jnp.zeros_like(sums)

    grad_normed = own_ref[...].astype(f32) + other_ref[...].astype(f32)
    next_grad = grad_out_ref[...]
    grad, gain_term = norm_backward(grad_normed, h_ref[...].astype(f32), next_grad.astype(bf16).astype(f32), gain_ref[0:1, :])
    rows = jnp.where(place_ref[3] == 0, grad, next_grad)
    sums[0:1, :] += jnp.sum(gain_term, axis=0, keepdims=True)

    @pl.when(step == pl.num_programs(0) - 1)
    def _():
        small_kernel(*small_refs, sums, smalls_ref)

    @pl.when(step < pl.num_programs(0) // 2)
    def _():
        low_ref[...] = rows.astype(bf16)
        placed_ref[0] = away_ref[...]

    @pl.when(step >= pl.num_programs(0) // 2)
    def _():
        grad_ref[0] = rows
        placed_ref[0] = rows_ref[...]


def finish(place, own, other, h, grad_out, gain, produced, produced_away, smalls):
    length, width = h.shape
    steps = length // SPAN
    units = smalls[0].shape[1]
    part = steps // 2

    def rows(i, place):
        return ((i + part * (1 - place[1])) % steps, 0)

    block = pl.BlockSpec((SPAN, width), rows)
    whole = pl.BlockSpec((8, width), lambda i, place: (0, 0))

    def early(i):
        return jnp.minimum(i, part - 1)

    def late(i):
        return jnp.maximum(i - part, 0)

    def placed(i, place):
        return (jnp.where(i < part, 1 - place[1], place[1]), jnp.where(i < part, i, i - part), 0)

    return pl.pallas_call(
        finish_kernel,
        grid_spec=pltpu.PrefetchScalarGridSpec(
            num_scalar_prefetch=1,
            grid=(steps,),
            in_specs=[block] * 4
            + [
                whole,
                pl.BlockSpec((SPAN, width), lambda i, place: (part * place[1] + late(i), 0)),
                pl.BlockSpec((SPAN, width), lambda i, place: (early(i), 0)),
            ]
            + [pl.BlockSpec(array.shape, lambda i, place: (0, 0)) for array in smalls],
            out_specs=[
                pl.BlockSpec((1, SPAN, width), lambda i, place: (place[1], late(i), 0)),
                pl.BlockSpec((SPAN, width), lambda i, place: (early(i), 0)),
                pl.BlockSpec((32, units), lambda i, place: (0, 0)),
                pl.BlockSpec((1, SPAN, width), placed),
            ],
            scratch_shapes=[pltpu.VMEM((8, width), f32)],
        ),
        out_shape=[
            jax.ShapeDtypeStruct((2, length // 2, width), f32),
            jax.ShapeDtypeStruct((length // 2, width), bf16),
            jax.ShapeDtypeStruct((32, units), f32),
            jax.ShapeDtypeStruct((2, length // 2, width), bf16),
        ],
        compiler_params=pltpu.CompilerParams(vmem_limit_bytes=VMEM_LIMIT, dimension_semantics=("arbitrary",)),
        cost_estimate=pl.CostEstimate(flops=0, bytes_accessed=500_000, transcendentals=0),
    )(place, own, other, h, grad_out, gain, produced, produced_away, *smalls)


def placed_kernel(place_ref, away_ref, rows_ref, out_ref):
    out_ref[0] = away_ref[...].astype(f32)


def placed_rows(place, rows, away):
    half, width = away.shape
    return pl.pallas_call(
        placed_kernel,
        grid_spec=pltpu.PrefetchScalarGridSpec(
            num_scalar_prefetch=1,
            grid=(half // SPAN,),
            in_specs=[pl.BlockSpec((SPAN, width), lambda i, place: (i, 0)), pl.BlockSpec(memory_space=pl.ANY)],
            out_specs=pl.BlockSpec((1, SPAN, width), lambda i, place: (1 - place[1], i, 0)),
        ),
        out_shape=jax.ShapeDtypeStruct(rows.shape, rows.dtype),
        input_output_aliases={2: 0},
        compiler_params=pltpu.CompilerParams(vmem_limit_bytes=VMEM_LIMIT, dimension_semantics=("arbitrary",)),
        cost_estimate=pl.CostEstimate(flops=0, bytes_accessed=500_000, transcendentals=0),
    )(place, away, rows)


def marks_kernel(place_ref, lengths_ref, segments_ref, marks_ref, row_ref):
    turn, rank = place_ref[1], place_ref[2]
    micro, sequences = lengths_ref.shape
    length = segments_ref.shape[1]
    total = jnp.int32(0)
    for batch in range(micro):
        total = lax.fori_loop(0, sequences, lambda i, t: t + lengths_ref[batch, i], total)
    weight = 2.0 * (micro * sequences * length) / jnp.full((1, length), total, jnp.int32).astype(f32)
    position = lax.broadcasted_iota(jnp.int32, (1, length), 1)
    segment = jnp.where(turn == 0, segments_ref[0:1, :], segments_ref[1:2, :])
    wide = jnp.broadcast_to(segment, (8, length))

    def same(lag):
        moved = pltpu.roll(wide, lag % length, 1)[0:1]
        inside = (position >= lag) & (position < length + lag)
        return jnp.where(inside & (moved == segment), 1.0, 0.0)

    before = jnp.full((1, length), -1, jnp.int32)
    end = before
    for block in range(length // SPAN):
        here = (position >= block * SPAN) & (position < (block + 1) * SPAN)
        end = jnp.where(here, segment[:, (block + 1) * SPAN - 1 : (block + 1) * SPAN], end)
        if block:
            before = jnp.where(here, segment[:, block * SPAN - 1 : block * SPAN], before)
    as_float = segment.astype(f32)
    rows = [same(1), same(2), same(3)]
    rows += [jnp.where(segment == before, 1.0, 0.0), jnp.where(segment == end, 1.0, 0.0), as_float]
    rows += [same(-1), same(-2), same(-3)]
    rows += [jnp.where(position < lengths_ref[turn, rank], weight, 0.0), jnp.full((1, length), turn, jnp.int32).astype(f32)]
    rows.append(jnp.zeros((LANES - len(rows), length), f32))
    marks_ref[...] = jnp.transpose(jnp.concatenate(rows, axis=0))
    row_ref[...] = as_float


def token_marks(place, lengths, segments):
    length = segments.shape[1]
    return pl.pallas_call(
        marks_kernel,
        in_specs=[pl.BlockSpec(memory_space=pltpu.SMEM)] * 2 + [pl.BlockSpec(memory_space=pltpu.VMEM)],
        out_shape=[jax.ShapeDtypeStruct((length, LANES), f32), jax.ShapeDtypeStruct((1, length), f32)],
        compiler_params=pltpu.CompilerParams(vmem_limit_bytes=VMEM_LIMIT),
        cost_estimate=pl.CostEstimate(flops=0, bytes_accessed=500_000, transcendentals=0),
    )(place, lengths, segments)


def three_parts(value):
    high = value.astype(bf16)
    rest = value - high.astype(f32)
    middle = rest.astype(bf16)
    return high, middle, (rest - middle.astype(f32)).astype(bf16)


PARAM_ROWS = 16


def pack_kernel(
    place_ref, zx_ref, bc_ref, dt_ref, gain_ref, out_ref, conv_ref, gate_gain_ref, states_conv_ref, bias_ref, rate_ref, skip_ref, kept_ref, sent_ref
):
    turn, core = place_ref[1], place_ref[3]
    rows = zx_ref.shape[0]
    half = zx_ref.shape[2] // 2
    heads_half = dt_ref.shape[0] // 2
    lane = lax.broadcasted_iota(jnp.int32, (1, LANES), 1)
    bc = jnp.where(turn == 0, bc_ref[:, :STATE], bc_ref[:, STATE:])
    diagonal = lax.broadcasted_iota(jnp.int32, (rows, rows), 0) == lax.broadcasted_iota(jnp.int32, (rows, rows), 1)
    gain = jnp.sum(jnp.where(diagonal, gain_ref[...].astype(f32), 0.0), axis=1, keepdims=True)
    head = lax.broadcasted_iota(jnp.int32, (2 * heads_half, LANES), 0)
    column = lax.broadcasted_iota(jnp.int32, (2 * heads_half, LANES), 1)
    shared = jnp.concatenate([states_conv_ref[...], jnp.zeros((PARAM_ROWS - 5, 2 * STATE), bf16)], axis=0)
    split = [part.astype(f32) for ref in (bias_ref, rate_ref, skip_ref) for part in three_parts(ref[...])]
    heads = jnp.concatenate(split + [jnp.zeros((PARAM_ROWS - 9, split[0].shape[1]), f32)], axis=0)
    heads = jnp.concatenate([heads, jnp.zeros((PARAM_ROWS, LANES - heads.shape[1]), f32)], axis=1).astype(bf16)
    for ref, part in ((kept_ref, core), (sent_ref, 1 - core)):
        first = part == 0

        def chosen(array, start):
            return jnp.where(first, array[:, start : start + half], array[:, start + half : start + 2 * half])

        ref[:rows, :half] = chosen(zx_ref[:, 1, :], 0)
        ref[:rows, half : half + STATE] = bc
        taken = (head == column + part * heads_half) & (column < heads_half)
        own_steps = tn(dt_ref[...], jnp.where(taken, 1.0, 0.0).astype(bf16))
        ref[:rows, half + STATE : half + 2 * STATE] = jnp.where(lane == LANES // 2, gain, own_steps).astype(bf16)
        ref[:rows, half + 2 * STATE : 2 * half + 2 * STATE] = chosen(zx_ref[:, 0, :], 0)
        ref[:rows, 2 * half + 2 * STATE :] = chosen(out_ref, 0)
        ref[rows:, :] = jnp.zeros((PARAM_ROWS, ref.shape[1]), bf16)
        channels = jnp.concatenate([chosen(conv_ref, 0), chosen(gate_gain_ref, 0)], axis=0)
        ref[rows:, :half] = jnp.concatenate([channels, jnp.zeros((PARAM_ROWS - 6, half), bf16)], axis=0)
        ref[rows:, half : half + 2 * STATE] = shared
        ref[rows:, half + 2 * STATE : half + 2 * STATE + LANES] = heads


def plain_call(kernel, place, inputs, outputs, ready=()):
    count = len(ready)
    body = kernel if not count else lambda place_ref, *refs: kernel(place_ref, *refs[count:])
    return pl.pallas_call(
        body,
        in_specs=[pl.BlockSpec(memory_space=pltpu.SMEM)]
        + [pl.BlockSpec(memory_space=pl.ANY)] * count
        + [pl.BlockSpec(memory_space=pltpu.VMEM)] * len(inputs),
        out_shape=[jax.ShapeDtypeStruct(shape, dtype) for shape, dtype in outputs],
        compiler_params=pltpu.CompilerParams(vmem_limit_bytes=VMEM_LIMIT),
        cost_estimate=pl.CostEstimate(flops=0, bytes_accessed=500_000, transcendentals=0),
    )(place, *ready, *inputs)


def unpack_kernel(place_ref, kept_ref, received_ref, *refs):
    scan_ref, middle_ref, gate_ref, params_ref, channels_ref = refs
    kept_first = place_ref[3] == 0
    kept, received = kept_ref[...], received_ref[...]
    first = jnp.where(kept_first, kept, received)
    second = jnp.where(kept_first, received, kept)
    rows, scan = scan_ref.shape
    half = channels_ref.shape[1]
    scan_ref[...] = first[:rows, :scan]
    middle_ref[:, : 2 * half] = first[:rows, scan:]
    middle_ref[:, 2 * half :] = second[:rows, :scan]
    gate_ref[...] = second[:rows, scan:]
    params_ref[0] = first[rows:, : scan + LANES]
    params_ref[1] = second[rows:, : scan + LANES]
    channels_ref[:PARAM_ROWS] = first[rows:, :half]
    channels_ref[PARAM_ROWS:] = second[rows:, :half]


def params_kernel(heads_half, place_ref, params_ref, channels_ref, spread_ref, *refs):
    turn, core = place_ref[1], place_ref[3]
    half = channels_ref.shape[1]
    lane = lax.broadcasted_iota(jnp.int32, (1, LANES), 1)
    for layer in range(2):
        small_ref, states_ref, head_ref = refs[3 * layer : 3 * layer + 3]
        rows = params_ref[layer].astype(f32)
        split = rows[:, half + 2 * STATE :]
        heads = [split[3 * i : 3 * i + 1] + split[3 * i + 1 : 3 * i + 2] + split[3 * i + 2 : 3 * i + 3] for i in range(3)]
        heads = jnp.concatenate(heads + [jnp.zeros((5, LANES), f32)], axis=0)
        moved = [pltpu.roll(heads, (LANES - start * heads_half) % LANES, 1) for start in range(4)]

        def of(index):
            return jnp.where(index == 0, moved[0], jnp.where(index == 1, moved[1], jnp.where(index == 2, moved[2], moved[3])))

        own, other = of(2 * turn + core), pltpu.roll(of(2 * (1 - turn) + core), heads_half, 1)
        heads = jnp.where(lane < heads_half, own, jnp.where(lane < 2 * heads_half, other, 0.0))
        head_ref[...] = jnp.concatenate([heads[0:1], jnp.exp(heads[1:2]), jnp.zeros((6, LANES), f32)], axis=0)
        high, middle, low = three_parts(jnp.broadcast_to(heads[2:3], (8, LANES)))
        once = spread_ref[:LANES]
        skips = (nn(high, once) + nn(middle, once) + nn(low, once))[0:1]
        own_rows = rows[0:6, :half]
        other_rows = channels_ref[PARAM_ROWS * layer : PARAM_ROWS * layer + 6].astype(f32)
        channels = jnp.concatenate([own_rows, other_rows], axis=1)
        small_ref[...] = jnp.concatenate([channels, skips, jnp.zeros_like(skips)], axis=0)
        states_ref[...] = jnp.concatenate([rows[0:5, half : half + 2 * STATE], jnp.zeros((3, 2 * STATE), f32)], axis=0)


def beside_kernel(place_ref, *refs):
    out = refs[-1]
    start = 0
    for ref in refs[:-1]:
        out[:, start : start + ref.shape[1]] = ref[...]
        start += ref.shape[1]


def split_kernel(place_ref, whole_ref, *outs):
    start = 0
    for out in outs:
        out[...] = whole_ref[:, start : start + out.shape[1]]
        start += out.shape[1]


def join_kernel(place_ref, *refs):
    out = refs[-1]
    start = 0
    for group in range(len(refs) // 4):
        parts = refs[4 * group : 4 * group + 4]
        width = parts[0].shape[1]
        total = sum(part[...].astype(f32) for part in parts)
        out[:, start : start + width] = total.astype(bf16)
        start += width


def owned_kernel(place_ref, first_ref, second_ref, beside_ref, across_ref, both_ref, zx_ref, bc_ref, dt_ref, out_ref):
    first = place_ref[3] == 0
    half = out_ref.shape[1] // 2
    heads_half = dt_ref.shape[0] // 2
    mine = jnp.where(first, first_ref[...], second_ref[...]).astype(f32)
    beside = beside_ref[...].astype(f32)
    lower, upper = jnp.where(first, mine, beside), jnp.where(first, beside, mine)
    gate = half + 2 * STATE
    for index, part in enumerate((lower, upper)):
        columns = slice(index * half, (index + 1) * half)
        zx_ref[:, 0, columns] = part[:, gate : gate + half]
        zx_ref[:, 1, columns] = part[:, :half]
        out_ref[:, columns] = part[:, gate + half :]
    own = mine[:, half : half + STATE] + beside[:, half : half + STATE]
    other = across_ref[...].astype(f32) + both_ref[...].astype(f32)
    straight = place_ref[1] == 0
    bc_ref[:, :STATE] = jnp.where(straight, own, other)
    bc_ref[:, STATE:] = jnp.where(straight, other, own)
    lane = lax.broadcasted_iota(jnp.int32, (1, LANES), 1)
    steps = slice(half + STATE, half + 2 * STATE)
    both = jnp.transpose(jnp.where(lane < heads_half, lower[:, steps], pltpu.roll(upper[:, steps], heads_half, 1)))
    for head in range(2 * heads_half):
        dt_ref[head] = both[head : head + 1]


def small_kernel(gate0, scan0, states0, gate1, scan1, states1, gain_ref, out_ref):
    for layer, (gate, scan, states, gain) in enumerate(
        ((gate0, scan0, states0, gain_ref[0:1, :]), (gate1, scan1, states1, gate0[7:8, :]))
    ):
        start = 16 * layer
        out_ref[start : start + 5, :] = scan[0:5, :]
        out_ref[start + 5 : start + 6, :] = gate[5:6, :]
        out_ref[start + 6 : start + 7, :] = gain
        out_ref[start + 7 : start + 16, :] = jnp.zeros((9, out_ref.shape[1]), f32)
        out_ref[start + 8 : start + 15, : 2 * STATE] = states[0:7, :]


def fold_kernel(heads_half, place_ref, own_ref, away_ref, mine_ref, others_ref):
    first = place_ref[3] == 0
    half = mine_ref.shape[1]
    folded = []
    for layer in range(2):
        own, away = own_ref[16 * layer : 16 * layer + 16], away_ref[16 * layer : 16 * layer + 16]
        units = own[0:6, :half] + away[0:6, half:]
        gain = own[6:7] + away[6:7]
        total = own[8:16, :half] + away[8:16, :half]
        own_heads = jnp.concatenate([own[14:15, :LANES], own[13:14, : 2 * LANES]], axis=1)
        away_heads = jnp.concatenate([away[14:15, :LANES], away[13:14, : 2 * LANES]], axis=1)
        moved = pltpu.roll(jnp.broadcast_to(away_heads, (8, 3 * LANES)), 3 * LANES - heads_half, 1)[0:1]
        heads = jnp.concatenate([own_heads + moved, jnp.zeros((1, half - 3 * LANES), f32)], axis=1) if half > 3 * LANES else own_heads + moved
        zeros = jnp.zeros((2, half), f32)
        folded.append(jnp.concatenate([units, gain[:, :half], gain[:, half:], total[0:5], heads, zeros], axis=0))
    mine_ref[...] = jnp.where(first, folded[0], folded[1])
    others_ref[...] = jnp.where(first, folded[1], folded[0])


def small_outputs_kernel(heads_half, place_ref, total_ref, conv_ref, states_conv_ref, gate_gain_ref, heads_ref, gain_ref):
    first = place_ref[3] == 0
    half = total_ref.shape[1]
    here, there = total_ref[0:16], total_ref[16:32]
    lower, upper = jnp.where(first, here, there), jnp.where(first, there, here)
    states = here[8:13, : 2 * STATE] + there[8:13, : 2 * STATE]
    for row in range(5):
        conv_ref[row, :, :half] = lower[row : row + 1]
        conv_ref[row, :, half:] = upper[row : row + 1]
        states_conv_ref[row] = states[row : row + 1]
    gate_gain_ref[:, :half] = lower[5:6]
    gate_gain_ref[:, half:] = upper[5:6]
    lane = lax.broadcasted_iota(jnp.int32, (1, LANES), 1)
    for row in range(3):
        own = lower[13:14, row * LANES : (row + 1) * LANES]
        other = pltpu.roll(jnp.broadcast_to(upper[13:14, row * LANES : (row + 1) * LANES], (8, LANES)), heads_half, 1)[0:1]
        heads_ref[row : row + 1, :] = jnp.where(lane < heads_half, own, other)[:, : 2 * heads_half]
    gain = jnp.concatenate([here[6:7], here[7:8]], axis=1)
    size = gain_ref.shape[1]
    share = jnp.zeros(gain_ref.shape, f32)
    for rank in range(2 * half // size):
        share = jnp.where(place_ref[2] == rank, gain[:, rank * size : (rank + 1) * size], share)
    gain_ref[...] = share


def tied(*values):
    return lax.optimization_barrier(values)


def swapped(block, axis):
    return lax.ppermute(block, axis, [(0, 1), (1, 0)])


def far_swapped(block):
    size = lax.axis_size("tensor")
    return lax.ppermute(block, ("section", "tensor"), [(i, 2 * size - 1 - i) for i in range(2 * size)])


def body(
    x_input,
    teacher,
    segment_ids,
    valid_len,
    norm_gain,
    w_zx,
    w_bc,
    w_dt,
    conv_x,
    conv_bc,
    dt_bias,
    a_log,
    d_skip,
    gnorm_gain,
    w_out,
):
    local_rows, width = x_input.shape[1:]
    ranks = lax.axis_size("dp")
    places = ranks // 2
    core = lax.axis_index("section")
    turn = lax.axis_index("tensor")
    rank = lax.axis_index("dp")
    place = jnp.stack([rank % 2, turn, rank, core]).astype(jnp.int32)
    on_first = core == 0
    block_rows = w_zx.shape[1]
    half = w_zx.shape[3] // 2
    units = 2 * half
    heads_half = w_dt.shape[2] // 2
    scan_columns = half + 2 * STATE
    line_groups = [[2 * index + start for index in range(places)] for start in range(2)]

    def by_layer(kept, received):
        return jnp.where(on_first, kept, received), jnp.where(on_first, received, kept)

    def x_swapped(block):
        return lax.ppermute(block, "dp", [(i, i ^ 1) for i in range(ranks)])

    def y_swapped(block):
        return swapped(block, "tensor")

    def line_gather(block):
        return lax.all_gather(block, "dp", axis_index_groups=line_groups, axis=0, tiled=True)

    def line_reduce(block):
        return lax.psum_scatter(block, "dp", axis_index_groups=line_groups, scatter_dimension=0, tiled=True)

    def line_total(block, beside):
        if places != 4:
            return lax.psum(block, "dp", axis_index_groups=line_groups), beside

        def send(rows, moves):
            return lax.ppermute(rows, "dp", [(2 * a + start, 2 * b + start) for a, b in moves for start in range(2)])

        up, down = send(block, [(0, 1), (1, 2), (2, 3)]), send(block, [(1, 0), (2, 1), (3, 2)])
        up2, down2 = send(up, [(1, 2), (2, 3)]), send(down, [(2, 1), (1, 0)])
        far = send(jnp.where(rank // 2 == 1, up, down), [(1, 3), (2, 0)])
        up2, down2, far, beside = tied(up2, down2, far, beside)
        return block + up + down + up2 + down2 + far, beside

    pack_shape = (block_rows + PARAM_ROWS, scan_columns + units)
    kept, sent = plain_call(
        pack_kernel,
        place,
        (w_zx[0], w_bc[0], w_dt[0].T, norm_gain, w_out[0].T, conv_x[0], gnorm_gain, conv_bc[0], dt_bias, a_log, d_skip),
        [(pack_shape, bf16)] * 2,
    )
    received = swapped(sent, "section")
    scan_block, middle_block, gate_block, params_both, channels = plain_call(
        unpack_kernel,
        place,
        (kept, received),
        [
            ((block_rows, scan_columns), bf16),
            ((block_rows, units + scan_columns), bf16),
            ((block_rows, units), bf16),
            ((2, PARAM_ROWS, scan_columns + LANES), bf16),
            ((2 * PARAM_ROWS, half), bf16),
        ],
    )

    both_ways = [(2 * d + t, 2 * (d ^ 1) + 1 - t) for d in range(ranks) for t in range(2)]

    def over_plane(own, x_block, y_block, far_block):
        far = lax.ppermute(far_block, ("dp", "tensor"), both_ways)
        return own, x_swapped(x_block), y_swapped(y_block), far

    def plane_end(block, over_x, over_tensor):
        cut = places // 2 * block_rows
        return block, over_x, over_tensor, y_swapped(over_x[:cut]), x_swapped(over_tensor[cut:])

    def quarter(rows):
        away = lax.dynamic_index_in_dim(rows, 1 - turn, 0, keepdims=False)
        return lax.dynamic_slice_in_dim(away, core * (local_rows // 2), local_rows // 2, 0)

    def whole_rows(rows, here, beside):
        own = lax.dynamic_index_in_dim(rows, turn, 0, keepdims=False)
        other = jnp.concatenate(by_layer(here, beside), axis=0)
        return jnp.where(turn == 0, jnp.concatenate([own, other]), jnp.concatenate([other, own]))

    scan_line, here, channels = tied(line_gather(scan_block), y_swapped(quarter(x_input)), y_swapped(channels))
    scan_line, middle_block = tied(scan_line, middle_block)
    middle_line = line_gather(middle_block)
    scan_half = scan_line, x_swapped(scan_line), y_swapped(scan_line)
    x_rows = whole_rows(x_input, here, swapped(here, "section"))
    params = plain_call(
        functools.partial(params_kernel, heads_half),
        place,
        (params_both, channels, spreader_of(units)),
        [((8, units), f32), ((8, 2 * STATE), f32), ((8, LANES), f32)] * 2,
    )
    params = [params[:3], params[3:]]
    marks, segment_row = token_marks(place, valid_len, segment_ids[:, 0])
    over_x = x_swapped(gate_block)
    side = (gate_block, over_x, y_swapped(gate_block), y_swapped(over_x))
    side = plain_call(beside_kernel, place, side, [((block_rows, 4 * units), bf16)], (x_rows, marks, params[0][0]))[0]
    scan_first, side = tied(plane_end(*scan_half), side)
    middle_line, side = tied(middle_line, side)
    gate_second = line_gather(side)
    gate_line, next_line = plain_call(
        split_kernel,
        place,
        (middle_line,),
        [((places * block_rows, units), bf16), ((places * block_rows, scan_columns), bf16)],
        (scan_first[4],),
    )

    gate_half = gate_line, x_swapped(gate_line), y_swapped(gate_line)
    next_half = next_line, x_swapped(next_line), y_swapped(next_line)
    results = scan_forward(place, block_rows, x_rows, None, scan_first, marks, segment_row, params[0])
    results, gate_half = tied(results, gate_half)
    _, gain_first, normed_first, saved_first = results
    gate_first = plane_end(*gate_half)
    results = gate_forward(place, block_rows, normed_first, saved_first[2], gate_first, params[0])
    (gated_first, part), scan_second = tied(results, plane_end(*next_half))
    part, teacher = tied(part, teacher)
    parts_first = (part, swapped(part, "section"))
    parts_first, gate_second = tied(parts_first, gate_second)
    results = second_forward(
        place, block_rows, x_rows, parts_first, scan_second, gate_second, marks, segment_row, params[1]
    )
    results, here = tied(results, y_swapped(quarter(teacher)))
    hidden, gain_second, normed_second, saved_second, gated_second, part = results
    parts_second = (part, swapped(part, "section"))
    beside = swapped(here, "section")

    def add(*blocks):
        return sum(block.astype(f32) for block in blocks).astype(bf16)

    def away_rows(rows):
        return y_swapped(lax.dynamic_slice_in_dim(rows, (1 - turn) * local_rows, local_rows, 0))

    produced, grad_out, grads, gate_sums, part, sums, states_sums = second_backward(
        place,
        block_rows,
        hidden,
        parts_second,
        teacher,
        here,
        beside,
        normed_second,
        gated_second,
        scan_second,
        gate_second,
        marks,
        segment_row,
        params[1],
        saved_second,
    )
    quarters = line_reduce(grads)
    sums_second = (gate_sums, sums, states_sums)
    grad_parts = (part, swapped(part, "section"))
    results = gate_backward(
        place,
        block_rows,
        x_rows,
        parts_first,
        (hidden, grad_out) + grad_parts + (gain_second,),
        normed_first,
        gated_first,
        saved_first[2],
        gate_first,
        marks,
        params[0],
    )
    results, produced_away = tied(results[1:], away_rows(produced))
    grad_hidden, grad_y, gate_part = results[:3]
    gate_reduce = over_plane(*results[3:7])
    gate_sums_first = results[7]
    results = scan_backward(
        place, block_rows, grad_y, gate_part, normed_first, scan_first, marks, segment_row, params[0], saved_first
    )
    results, gate_reduce = tied(results, gate_reduce)
    scan_reduce = over_plane(*results[:4])
    part, sums, states_sums = results[4:]
    sums_first = (gate_sums_first, sums, states_sums)
    grad_rows, grad_low, smalls, layer_outputs = finish(
        place,
        part,
        swapped(part, "section"),
        x_rows,
        grad_hidden,
        gain_first,
        produced,
        produced_away,
        sums_first + sums_second,
    )
    smalls, scan_reduce = line_total(smalls, scan_reduce)
    blocks = plain_call(
        join_kernel,
        place,
        scan_reduce + gate_reduce,
        [((places * block_rows, scan_columns + units), bf16)],
        (quarters,),
    )[0]
    owned_first = line_reduce(blocks)
    quarters = plain_call(
        split_kernel, place, (quarters,), [((block_rows, scan_columns + units), bf16)] * 4, (blocks,)
    )
    owned_second = add(*over_plane(*quarters))
    smalls_away, grad_low = tied(y_swapped(smalls), grad_low)
    mine, others = plain_call(
        functools.partial(fold_kernel, heads_half), place, (smalls, smalls_away), [((16, half), f32)] * 2
    )
    total = jnp.concatenate([mine, swapped(others, "section")])
    owned_first, boundary = tied(owned_first, placed_rows(place, grad_rows, y_swapped(grad_low)))
    total = total + x_swapped(total)
    grad_conv, grad_states_conv, grad_gate_gain, grad_heads, gain_total = plain_call(
        functools.partial(small_outputs_kernel, heads_half),
        place,
        (total,),
        [((5, 1, units), f32), ((5, 1, 2 * STATE), f32), ((1, units), f32), ((3, 2 * heads_half), f32), ((1, block_rows), f32)],
    )

    others = jnp.where(on_first, owned_second, owned_first)
    own_states, other_states = by_layer(owned_first[:, half : half + STATE], owned_second[:, half : half + STATE])
    grad_zx, grad_bc, grad_dt, grad_out_w = plain_call(
        owned_kernel,
        place,
        (owned_first, owned_second, swapped(others, "section"), y_swapped(own_states), far_swapped(other_states)),
        [((block_rows, 2, units), f32), ((block_rows, 2 * STATE), f32), ((2 * heads_half, 1, block_rows), f32), ((block_rows, units), f32)],
        (boundary, layer_outputs, grad_conv),
    )
    return (
        layer_outputs[None],
        boundary[None],
        gain_total,
        grad_zx[None],
        grad_bc[None],
        grad_dt.transpose(1, 2, 0),
        grad_conv.transpose(1, 0, 2),
        grad_states_conv.transpose(1, 0, 2),
        grad_heads[1:2],
        grad_heads[2:3],
        grad_heads[0:1],
        grad_gate_gain,
        grad_out_w.T[None],
    )


def solution(mesh):
    placed = (
        P(None, ("dp", "tensor"), None),
        P(None, ("dp", "tensor"), None),
        P(None, "dp", None),
        P(),
        P("section", "dp"),
        P("section", "dp", None, "tensor"),
        P("section", "dp", None),
        P("section", "dp", "tensor"),
        P("section", None, "tensor"),
        P("section", None, None),
        P("section", None),
        P("section", None),
        P("section", None),
        P("section", "tensor"),
        P("section", "tensor", "dp"),
    )
    return jax.shard_map(
        body,
        mesh=mesh,
        in_specs=placed,
        out_specs=(
            P("section", None, ("dp", "tensor"), None),
            P("section", None, ("dp", "tensor"), None),
            P("section", "dp"),
            P("section", "dp", None, "tensor"),
            P("section", "dp", None),
            P("section", "dp", "tensor"),
            P("section", None, "tensor"),
            P("section", None, None),
            P("section", "tensor"),
            P("section", "tensor"),
            P("section", "tensor"),
            P("section", "tensor"),
            P("section", "tensor", "dp"),
        ),
        check_vma=False,
    )
```
